32 devices in a mesh: exp: 8 (over y, x, core), head: 4 (over z).
Axes of the slice: x: 2, y: 2, z: 4, core: 2. Of those that a mesh axis runs over, the one named last changes fastest.
Arguments:
- tokens: bfloat16 [13824, 768], P('exp'), may hold values from -6 to 6
- segments: int32 [24, 576], P('exp'), may hold values from 0 to 3, never falling along the last dimension, each value on 1 to 288 neighbouring positions
- live_mask: int32 [24, 576], P('exp'), may hold values 0 or 1
- routes: int32 [13824, 2], P('exp'), may hold values from 0 to 7, all different within a row
- priority: int32 [8, 1728], P('exp'), may hold values from 0 to 1727, each once within a row
- norm1_gain: bfloat16 [768], replicated, may hold values from 0.5 to 1.5
- norm1_bias: bfloat16 [768], replicated, may hold values from -1.1953125 to 1.1953125
- qkv_weight: bfloat16 [768, 3, 768], P(None, None, 'head'), may hold values from -0.21875 to 0.21875
- qv_bias: bfloat16 [2, 768], P(None, 'head'), may hold values from -1.796875 to 1.796875
- out_weight: bfloat16 [768, 768], P('head'), may hold values from -1 to 1
- out_bias: bfloat16 [768], replicated, may hold values from -1.1953125 to 1.1953125
- norm2_gain: bfloat16 [768], replicated, may hold values from 0.5 to 1.5
- norm2_bias: bfloat16 [768], replicated, may hold values from -1.1953125 to 1.1953125
- router: bfloat16 [768, 8], replicated, may hold values from -0.15625 to 0.15625
- up_weight: bfloat16 [8, 768, 3072], P('exp', None, 'head'), may hold values from -0.21875 to 0.21875
- up_bias: bfloat16 [8, 3072], P('exp', 'head'), may hold values from -1.796875 to 1.796875
- down_weight: bfloat16 [8, 3072, 768], P('exp', 'head'), may hold values from -1.75 to 1.75
- down_bias: bfloat16 [8, 768], P('exp', 'head'), may hold values from -6 to 6
- cotangent: bfloat16 [13824, 768], P('exp', 'head'), may hold values from -6 to 6
Outputs:
- block_out: bfloat16 [13824, 768], P('exp', 'head')
- grad_tokens: float32 [13824, 768], P('exp')
- grad_norm1_gain: float32 [768], replicated
- grad_norm1_bias: float32 [768], replicated
- grad_qkv_weight: float32 [768, 3, 768], P(None, None, 'head')
- grad_qv_bias: float32 [2, 768], P(None, 'head')
- grad_out_weight: float32 [768, 768], P('head')
- grad_out_bias: float32 [768], replicated
- grad_norm2_gain: float32 [768], replicated
- grad_norm2_bias: float32 [768], replicated
- grad_router: float32 [768, 8], replicated
- grad_up_weight: float32 [8, 768, 3072], P('exp', None, 'head')
- grad_up_bias: float32 [8, 3072], P('exp', 'head')
- grad_down_weight: float32 [8, 3072, 768], P('exp', 'head')
- grad_down_bias: float32 [8, 768], P('exp', 'head')
The draws below stay inside these ranges and needn't reach their ends.
Inputs may be any that keep to these rules, and one draw needn't show every extreme that they name: `segments`: segment numbers never fall along a sequence; each segment has at most 288 patches. `routes`: the two experts of a patch differ. `priority`: each row is a permutation.
All inputs are finite; a program needn't handle non-finite values. No bound on the sum of `live_mask` on one device may be relied on, other than what follows from the above.
Results may differ from the reference program's by a relative error of at most 0.015.
Values may be sent and summed in bfloat16 or wider, within the bound.
A program may use at most 192 MiB of HBM per device.

```python
import math
import jax
import jax.numpy as jnp
import numpy as np
from jax import lax

D = 768
HEADS = 12
HEAD_DIM = 64
FF = 3072
LEN = 576
SEQ_DEV = 3
E = 8
HD = 768
GROUPS = 8
SEQS = 24
TOK_DEV = 1728
TOKENS = 13824
CAP = 454


def touch_ends(entries, stream_key, smallest, high):
    longest = entries.shape.index(max(entries.shape))
    spots = []
    for shift in (0, 1):
        where = [jax.random.randint(jax.random.fold_in(stream_key, axis), (), 0, length) for axis, length in enumerate(entries.shape)]
        where[longest] = (where[longest] + shift) % entries.shape[longest]
        spots.append(tuple(where))
    return entries.at[spots[0]].set(smallest).at[spots[1]].set(high)


def block_levels(key, extent, cuts, smallest, high):
    level = 1.0
    for position, shards_of in cuts:
        steps = jax.random.uniform(jax.random.fold_in(jax.random.fold_in(key, 6), position), (shards_of,), jnp.float32, smallest / len(cuts), high / len(cuts))
        level = level * jnp.repeat(jnp.exp(steps), extent[position] // shards_of).reshape((-1,) + (1,) * (len(extent) - 1 - position))
    return level


def picks_of(rng, rows, amount, top, lift):
    sequence = jax.random.permutation(jax.random.fold_in(rng, 1), amount)
    pull = sequence
    for power in range(3):
        pull = pull * pull // amount
    pull = pull * lift // amount
    lots = jax.random.randint(jax.random.fold_in(rng, 2), (rows, amount), 0, 4096) + pull
    holders = jax.random.permutation(jax.random.fold_in(rng, 3), rows)[jnp.arange(amount) % rows]
    lots = jnp.where(jnp.arange(rows)[:, None] == holders[None, :], 1 << 14, lots)
    score = lots * amount + jnp.arange(amount)
    return lax.top_k(score.astype(jnp.int32), top)[1].astype(jnp.int32)


def profile(count, total, bound, lean):
    portions = [(1 << 20) // math.isqrt(grade ** lean) + 1 for grade in range(2, count + 1)]
    spare, counts = total - bound - (count - 1), [1] * (count - 1)
    while spare > 0:
        free = [i for i in range(count - 1) if counts[i] < bound]
        pool, budget = sum([portions[i] for i in free]), spare
        for i in free:
            addition = min(bound - counts[i], max(1, budget * portions[i] // pool), spare)
            counts[i] = counts[i] + addition
            spare = spare - addition
    return np.array([bound] + counts)


def uneven_parts(own_key, number_of, total, reach, slope):
    if number_of == 2:
        one = jax.random.randint(own_key, (), max(1, total - reach), min(reach, total - 1) + 1)
        return jnp.stack([one, total - one])
    tallies = jnp.asarray(profile(number_of, total, reach, slope), jnp.int32)
    couples = (number_of - 1) // 2
    source_of, taker = tallies[1:1 + 2 * couples:2], tallies[2:2 + 2 * couples:2]
    slack = jnp.minimum(source_of - 1, reach - taker)
    shifted = jax.random.randint(jax.random.fold_in(own_key, 1), (couples,), 0, 1 << 20) % (slack + 1)
    tallies = tallies.at[1:1 + 2 * couples:2].set(source_of - shifted).at[2:2 + 2 * couples:2].set(taker + shifted)
    return tallies[jax.random.permutation(jax.random.fold_in(own_key, 2), number_of)]


def bell_draw(own_key, extent, width, most, pieces=(), held_as=jnp.bfloat16):
    drawn = width * jax.random.normal(own_key, extent, jnp.float32)
    if pieces:
        drawn = drawn * block_levels(own_key, extent, pieces, -0.22, 0.18)
    return jnp.clip(drawn, -most, most).astype(held_as)


def setup_inputs(seed: int = 0) -> dict:
    key_of = jax.random.split(jax.random.key(seed), 20)
    tokens = bell_draw(key_of[0], (TOKENS, D), 1.0, 6.0, ((0, 8),))
    segments = jax.vmap(lambda own: jnp.searchsorted(jnp.cumsum(uneven_parts(own, 4, LEN, LEN // 2, 0)), jnp.arange(LEN), side="right"))(jax.random.split(key_of[1], SEQS)).reshape((SEQS, LEN)).astype(jnp.int32)
    live_mask = touch_ends((jax.random.randint(key_of[2], (SEQS, LEN), 0, 8) < 7).astype(jnp.int32), jax.random.fold_in(key_of[2], 1), 0, 1)
    routes = picks_of(key_of[3], TOKENS, E, 2, 2048)
    priority = jax.vmap(lambda own: jax.random.permutation(own, TOK_DEV))(jax.random.split(key_of[4], GROUPS)).reshape((GROUPS, TOK_DEV)).astype(jnp.int32)
    norm1_gain = jnp.clip(1.0 + 0.1 * jax.random.normal(key_of[5], (D,), jnp.float32), 0.5, 1.5).astype(jnp.bfloat16)
    norm1_bias = bell_draw(key_of[6], (D,), 0.2, 1.1953125)
    qkv_weight = bell_draw(key_of[7], (D, 3, HD), D ** -0.5, 0.21875, ((2, 4),))
    qv_bias = bell_draw(key_of[8], (2, HD), 0.3, 1.796875, ((1, 4),))
    out_weight = bell_draw(key_of[9], (HD, D), (HD // 24) ** -0.5, 1.0, ((0, 4),))
    out_bias = bell_draw(key_of[10], (D,), 0.2, 1.1953125)
    norm2_gain = jnp.clip(1.0 + 0.1 * jax.random.normal(key_of[11], (D,), jnp.float32), 0.5, 1.5).astype(jnp.bfloat16)
    norm2_bias = bell_draw(key_of[12], (D,), 0.2, 1.1953125)
    router = bell_draw(key_of[13], (D, E), (2 * D) ** -0.5, 0.15625)
    up_weight = bell_draw(key_of[14], (E, D, FF), D ** -0.5, 0.21875, ((0, 8), (2, 4)))
    up_bias = bell_draw(key_of[15], (E, FF), 0.3, 1.796875, ((0, 8), (1, 4)))
    down_weight = bell_draw(key_of[16], (E, FF, D), (max(FF // 256, 1)) ** -0.5, 1.75, ((0, 8), (1, 4)))
    down_bias = bell_draw(key_of[17], (E, D), 1.0, 6.0, ((0, 8), (1, 4)))
    cotangent = bell_draw(key_of[18], (TOKENS, D), 1.0, 6.0, ((0, 8), (1, 4)))
    return dict(tokens=tokens, segments=segments, live_mask=live_mask, routes=routes, priority=priority, norm1_gain=norm1_gain, norm1_bias=norm1_bias, qkv_weight=qkv_weight, qv_bias=qv_bias, out_weight=out_weight, out_bias=out_bias, norm2_gain=norm2_gain, norm2_bias=norm2_bias, router=router, up_weight=up_weight, up_bias=up_bias, down_weight=down_weight, down_bias=down_bias, cotangent=cotangent)


@jax.custom_vjp
def low(v):
    return lax.optimization_barrier(v.astype(jnp.bfloat16)).astype(jnp.float32)

@jax.custom_vjp
def low_back(v):
    return v

def low_keep(v):
    return (low(v), None)

def low_pass(kept, grad):
    return (grad,)

def back_keep(v):
    return (v, None)

def back_low(kept, grad):
    return (low(grad),)
low.defvjp(low_keep, low_pass)
low_back.defvjp(back_keep, back_low)
EPSILON = 1e-06
NEGATIVE = -1e+30
HIGHEST = lax.Precision.HIGHEST

def norm_rows(values, gain_row, shift_row):
    row_mean = lax.optimization_barrier(jnp.mean(values, axis=-1, keepdims=True))
    centred = values - row_mean
    spread = lax.optimization_barrier(jnp.mean(centred * centred, axis=-1, keepdims=True))
    return centred * lax.rsqrt(spread + EPSILON) * gain_row + shift_row

def attend_group(params, block_rows, seg_rows, live_rows):
    norm1_gain, norm1_bias, qkv_weight, qv_bias, out_weight, out_bias = params
    seq_total = seg_rows.shape[0]
    normed = low(norm_rows(block_rows, norm1_gain, norm1_bias))
    projected = jnp.dot(normed, qkv_weight.reshape(D, 3 * HD), precision=HIGHEST).reshape(-1, 3, HD)
    shape_four = (seq_total, LEN, HEADS, HEAD_DIM)
    queries = low_back(low(projected[:, 0] + qv_bias[0])).reshape(shape_four)
    key_rows = low_back(low(projected[:, 1])).reshape(shape_four)
    value_rows = low_back(low(projected[:, 2] + qv_bias[1])).reshape(shape_four)
    same_segment = seg_rows[:, :, None] == seg_rows[:, None, :]
    diagonal = jnp.eye(LEN, dtype=bool)
    allowed = same_segment & ((live_rows[:, None, :] > 0) | diagonal[None])
    scores = jnp.einsum('sqhd,skhd->shqk', queries, key_rows, precision=HIGHEST) / math.sqrt(HEAD_DIM)
    scores = low_back(scores)
    masked = jnp.where(allowed[:, None], scores, NEGATIVE)
    chances = low(jax.nn.softmax(masked, axis=-1))
    context = jnp.einsum('shqk,skhd->sqhd', chances, value_rows, precision=HIGHEST)
    context = low_back(low(context)).reshape(seq_total * LEN, HD)
    branch = low_back(jnp.dot(context, out_weight, precision=HIGHEST))
    return block_rows + branch + out_bias

def run_expert(expert_item):
    rows_in, weight_in, bias_in, weight_back, bias_back = expert_item
    rows_in = low_back(rows_in)
    before = low_back(jnp.dot(rows_in, weight_in, precision=HIGHEST) + bias_in)
    hidden = low(jax.nn.gelu(before))
    return low(jnp.dot(hidden, weight_back, precision=HIGHEST) + bias_back)

def slot_positions(routes, live_mask, priority):
    pair_rows = routes.reshape(GROUPS, TOK_DEV, 2)
    alive_rows = live_mask.reshape(GROUPS, TOK_DEV)
    expert_ids = jnp.arange(E, dtype=jnp.int32)

    def one_group(group_pairs, group_alive, group_rank):
        by_rank = jnp.argsort(group_rank).astype(jnp.int32)

        def before_count(onehot):
            ordered = onehot[by_rank]
            earlier = jnp.cumsum(ordered, axis=0, dtype=jnp.int32) - ordered
            return lax.optimization_barrier(jnp.sum(earlier * ordered, axis=1, dtype=jnp.int32))[group_rank]
        first_hot = (group_pairs[:, 0:1] == expert_ids[None, :]).astype(jnp.int32) * group_alive[:, None]
        second_hot = (group_pairs[:, 1:2] == expert_ids[None, :]).astype(jnp.int32) * group_alive[:, None]
        totals = lax.optimization_barrier(jnp.sum(first_hot, axis=0, dtype=jnp.int32))
        pos_first = before_count(first_hot)
        pos_second = before_count(second_hot) + lax.optimization_barrier(jnp.sum(second_hot * totals[None, :], axis=1, dtype=jnp.int32))
        return jnp.stack([pos_first, pos_second], axis=1)
    positions = jax.vmap(one_group)(pair_rows, alive_rows, priority).reshape(TOKENS, 2)
    kept_pairs = (positions < CAP) & (live_mask.reshape(TOKENS, 1) > 0)
    return (jnp.minimum(positions, CAP - 1).astype(jnp.int32), kept_pairs)

def reference(tokens, segments, live_mask, routes, priority, norm1_gain, norm1_bias, qkv_weight, qv_bias, out_weight, out_bias, norm2_gain, norm2_bias, router, up_weight, up_bias, down_weight, down_bias, cotangent):
    slot_at, kept_pairs = slot_positions(routes, live_mask, priority)
    kept_float = kept_pairs.astype(jnp.float32)
    group_of = (jnp.arange(TOKENS, dtype=jnp.int32) // TOK_DEV).astype(jnp.int32)
    seg_groups = segments.reshape(GROUPS, SEQ_DEV, LEN)
    live_groups = live_mask.reshape(GROUPS, SEQ_DEV, LEN)

    def forward(inputs, gain_one, bias_one, weight_qkv, bias_qv, weight_out, bias_out, gain_two, bias_two, router_weight, weight_up, bias_up, weight_down, bias_down):
        params = (gain_one, bias_one, weight_qkv, bias_qv, weight_out, bias_out)

        def one_group(group_item):
            return attend_group(params, group_item[0], group_item[1], group_item[2])
        residual = lax.map(jax.checkpoint(one_group), (inputs.reshape(GROUPS, TOK_DEV, D), seg_groups, live_groups)).reshape(TOKENS, D)
        normed = low(norm_rows(residual, gain_two, bias_two))
        logits = low_back(jnp.dot(normed, router_weight, precision=HIGHEST))
        chances = jax.nn.softmax(logits, axis=-1)
        buffer = jnp.zeros((E, GROUPS, CAP, D), jnp.float32)
        for route_pick in range(2):
            buffer = buffer.at[routes[:, route_pick], group_of, slot_at[:, route_pick]].add(normed * kept_float[:, route_pick:route_pick + 1])
        expert_out = lax.map(jax.checkpoint(run_expert), (buffer.reshape(E, GROUPS * CAP, D), weight_up, bias_up, weight_down, bias_down))
        expert_out = expert_out.reshape(E, GROUPS, CAP, D)
        combined = residual
        for route_pick in range(2):
            gate_col = jnp.take_along_axis(chances, routes[:, route_pick:route_pick + 1], axis=1) * kept_float[:, route_pick:route_pick + 1]
            chosen = low_back(expert_out[routes[:, route_pick], group_of, slot_at[:, route_pick]])
            combined = combined + gate_col * chosen
        return combined
    result, pullback = jax.vjp(forward, tokens.astype(jnp.float32), norm1_gain.astype(jnp.float32), norm1_bias.astype(jnp.float32), qkv_weight.astype(jnp.float32), qv_bias.astype(jnp.float32), out_weight.astype(jnp.float32), out_bias.astype(jnp.float32), norm2_gain.astype(jnp.float32), norm2_bias.astype(jnp.float32), router.astype(jnp.float32), up_weight.astype(jnp.float32), up_bias.astype(jnp.float32), down_weight.astype(jnp.float32), down_bias.astype(jnp.float32))
    gradients = pullback(cotangent.astype(jnp.float32))
    return (result.astype(jnp.bfloat16), gradients[0], gradients[1], gradients[2], gradients[3], gradients[4], gradients[5], gradients[6], gradients[7], gradients[8], gradients[9], gradients[10], gradients[11], gradients[12], gradients[13])
```

```python
from functools import partial
import math

import jax
import jax.numpy as jnp
from jax import lax
from jax.sharding import PartitionSpec as P

HEAD_DIM = 64


EPSILON = 1e-06
NEGATIVE = -1e30
CONTRACT_FIRST = (((0,), (0,)), ((), ()))
CONTRACT_LAST = (((1,), (1,)), ((), ()))


def norm_rows(values, gain_row, shift_row):
    row_mean = jnp.mean(values, axis=-1, keepdims=True)
    centred = values - row_mean
    spread = jnp.mean(centred * centred, axis=-1, keepdims=True)
    return centred * lax.rsqrt(spread + EPSILON) * gain_row + shift_row


def masked_scores(query_rows, key_rows, seg_row, live_row, factor):
    scores = (
        jnp.einsum("qhd,khd->hqk", query_rows, key_rows, preferred_element_type=jnp.float32)
        * factor
    )
    same_segment = seg_row[:, None] == seg_row[None, :]
    diagonal = jnp.eye(seg_row.shape[0], dtype=bool)
    allowed = same_segment & ((live_row[None, :] > 0) | diagonal)
    return jnp.where(allowed[None], scores, NEGATIVE)


def attend_sequence(block_item, factor):
    query_rows, key_rows, value_rows, seg_row, live_row = block_item
    masked = masked_scores(query_rows, key_rows, seg_row, live_row, factor)
    largest = jnp.max(masked, axis=-1, keepdims=True)
    weights = jnp.exp(masked - largest)
    totals = jnp.sum(weights, axis=-1, keepdims=True)
    context = jnp.einsum(
        "hqk,khd->qhd",
        (weights / totals).astype(jnp.bfloat16),
        value_rows,
        preferred_element_type=jnp.float32,
    )
    return (context.astype(jnp.bfloat16), largest + jnp.log(totals))


def attend_backward(block_item, factor):
    query_rows, key_rows, value_rows, seg_row, live_row, context_grad, log_total = block_item
    masked = masked_scores(query_rows, key_rows, seg_row, live_row, factor)
    weights = jnp.exp(masked - log_total)
    value_grad = jnp.einsum(
        "hqk,qhd->khd",
        weights.astype(jnp.bfloat16),
        context_grad,
        preferred_element_type=jnp.float32,
    )
    weight_grad = jnp.einsum(
        "qhd,khd->hqk", context_grad, value_rows, preferred_element_type=jnp.float32
    )
    score_grad = (
        weights * (weight_grad - jnp.sum(weights * weight_grad, axis=-1, keepdims=True))
    ).astype(jnp.bfloat16)
    query_grad = (
        jnp.einsum("hqk,khd->qhd", score_grad, key_rows, preferred_element_type=jnp.float32)
        * factor
    )
    key_grad = (
        jnp.einsum("hqk,qhd->khd", score_grad, query_rows, preferred_element_type=jnp.float32)
        * factor
    )
    return (
        query_grad.astype(jnp.bfloat16),
        key_grad.astype(jnp.bfloat16),
        value_grad.astype(jnp.bfloat16),
    )


def slot_tables(routes, live_mask, priority, seqlen, experts, capacity, stride):
    tok_count = routes.shape[0]
    expert_ids = jnp.arange(experts, dtype=jnp.int32)
    live_column = live_mask.reshape(tok_count, 1) > 0
    first_hot = ((routes[:, 0:1] == expert_ids[None, :]) & live_column).astype(jnp.bfloat16)
    second_hot = ((routes[:, 1:2] == expert_ids[None, :]) & live_column).astype(jnp.bfloat16)
    both_hot = jnp.concatenate([first_hot, second_hot], axis=1)
    rank_all = priority.reshape(tok_count)

    def count_block(rank_block):
        earlier = (rank_all[None, :] < rank_block[:, None]).astype(jnp.bfloat16)
        return jnp.dot(earlier, both_hot, preferred_element_type=jnp.float32)

    counts = lax.map(count_block, rank_all.reshape(-1, seqlen)).reshape(tok_count, 2 * experts)
    first_float = first_hot.astype(jnp.float32)
    second_float = second_hot.astype(jnp.float32)
    pos_first = jnp.sum(counts[:, :experts] * first_float, axis=1)
    pos_second = jnp.sum(counts[:, experts:] * second_float, axis=1) + jnp.sum(
        second_float * jnp.sum(first_float, axis=0)[None, :], axis=1
    )
    positions = jnp.stack([pos_first, pos_second], axis=1).astype(jnp.int32)
    kept_pairs = (positions < capacity) & live_column
    return (jnp.where(kept_pairs, routes * stride + positions, -1), kept_pairs)


def round_up(number, step):
    return (number + step - 1) // step * step


def exchange(slot_rows, experts):
    blocks = slot_rows.reshape(experts, slot_rows.shape[0] // experts, *slot_rows.shape[1:])
    moved = lax.all_to_all(blocks, "exp", split_axis=0, concat_axis=0, tiled=True)
    return moved.reshape(slot_rows.shape)


def to_slots(slot_ids, rows, slot_count):
    numbers = jnp.arange(slot_count, dtype=jnp.int32)[:, None]
    onehot = (slot_ids[None, :, 0] == numbers) | (slot_ids[None, :, 1] == numbers)
    return jnp.dot(onehot.astype(jnp.bfloat16), rows, preferred_element_type=jnp.float32).astype(
        jnp.bfloat16
    )


def body(
    tokens,
    segments,
    live_mask,
    routes,
    priority,
    norm1_gain,
    norm1_bias,
    qkv_weight,
    qv_bias,
    out_weight,
    out_bias,
    norm2_gain,
    norm2_bias,
    router,
    up_weight,
    up_bias,
    down_weight,
    down_bias,
    cotangent,
):
    tok_count, model_width = tokens.shape
    seq_count, seqlen = segments.shape
    experts = lax.axis_size("exp")
    head_parts = lax.axis_size("head")
    head_index = lax.axis_index("head")
    quarter = model_width // head_parts
    tok_part = tok_count // head_parts
    capacity = (21 * tok_count + 10 * experts - 1) // (10 * experts)
    stride = round_up(capacity, 16)
    slot_count = experts * stride
    local_width = qkv_weight.shape[2]
    head_count = local_width // HEAD_DIM
    factor = 1.0 / math.sqrt(HEAD_DIM)
    f32 = jnp.float32
    bf16 = jnp.bfloat16

    def my_rows(rows):
        return lax.dynamic_slice_in_dim(rows, head_index * tok_part, tok_part, 0)

    out_full_weight = lax.all_gather(out_weight, "head", axis=0, tiled=True)
    slot_ids, kept_pairs = slot_tables(
        routes, live_mask, priority, seqlen, experts, capacity, stride
    )
    kept_float = kept_pairs.astype(f32)
    out_slots = to_slots(slot_ids, cotangent, slot_count)
    out_rows = lax.all_gather(exchange(out_slots, experts), "head", axis=1, tiled=True)

    inputs = tokens.astype(f32)
    gain_one, bias_one = norm1_gain.astype(f32), norm1_bias.astype(f32)
    gain_two, bias_two = norm2_gain.astype(f32), norm2_bias.astype(f32)
    first_in = norm_rows(inputs, gain_one, bias_one).astype(bf16)
    flat_qkv = qkv_weight.reshape(model_width, 3 * local_width)
    projected = jnp.dot(first_in, flat_qkv, preferred_element_type=f32).reshape(
        tok_count, 3, local_width
    )
    bias_rows = qv_bias.astype(f32)
    shape_four = (seq_count, seqlen, head_count, HEAD_DIM)
    query_rows = (projected[:, 0] + bias_rows[0]).astype(bf16).reshape(shape_four)
    key_rows = projected[:, 1].astype(bf16).reshape(shape_four)
    value_rows = (projected[:, 2] + bias_rows[1]).astype(bf16).reshape(shape_four)
    context, log_total = lax.map(
        partial(attend_sequence, factor=factor),
        (query_rows, key_rows, value_rows, segments, live_mask),
    )
    context_flat = context.reshape(tok_count, local_width)
    context_full = lax.all_gather(context_flat, "head", axis=1, tiled=True)
    residual = (
        inputs
        + jnp.dot(context_full, out_full_weight, preferred_element_type=f32)
        + out_bias.astype(f32)
    )
    second_in = norm_rows(residual, gain_two, bias_two).astype(bf16)
    logits = jnp.dot(second_in, router, preferred_element_type=f32)
    chances = jax.nn.softmax(logits, axis=-1)
    expert_ids = jnp.arange(experts, dtype=jnp.int32)
    chosen = (routes[:, :, None] == expert_ids[None, None, :]).astype(f32)
    gate_values = jnp.sum(chosen * chances[:, None, :], axis=2) * kept_float
    numbers = jnp.arange(slot_count, dtype=jnp.int32)[:, None]
    gate_slots = jnp.sum(
        jnp.where(slot_ids[None, :, 0] == numbers, gate_values[None, :, 0], 0.0)
        + jnp.where(slot_ids[None, :, 1] == numbers, gate_values[None, :, 1], 0.0),
        axis=1,
    )
    expert_rows = exchange(to_slots(slot_ids, second_in, slot_count), experts)
    gate_rows = exchange(gate_slots, experts)

    pre_act = jnp.dot(expert_rows, up_weight[0], preferred_element_type=f32) + up_bias[0].astype(
        f32
    )
    filled = lax.rem(jnp.arange(slot_count, dtype=jnp.int32), stride) < capacity
    gelu_value, gelu_back = jax.vjp(jax.nn.gelu, pre_act)
    hidden = gelu_value.astype(bf16)
    bias_full = lax.dynamic_update_slice_in_dim(
        jnp.zeros((model_width,), f32), down_bias[0].astype(f32), head_index * quarter, 0
    )
    partial_expert = jnp.dot(hidden, down_weight[0], preferred_element_type=f32) + bias_full
    gate_grad_rows = jnp.sum(partial_expert * out_rows.astype(f32), axis=1)
    grad_full = (gate_rows[:, None] * out_rows.astype(f32)).astype(bf16)
    hidden_grad = lax.dot_general(
        grad_full, down_weight[0], CONTRACT_LAST, preferred_element_type=f32
    )
    pre_grad = gelu_back(hidden_grad)[0].astype(bf16)
    rows_grad = lax.dot_general(
        pre_grad, up_weight[0], CONTRACT_LAST, preferred_element_type=f32
    ).astype(bf16)
    home_grad = exchange(rows_grad, experts)
    home_gate = exchange(lax.psum(gate_grad_rows, "head"), experts)
    home_out = exchange(partial_expert.astype(bf16), experts)
    grad_down_bias = jnp.sum(
        lax.dynamic_slice_in_dim(grad_full, head_index * quarter, quarter, 1), axis=0, dtype=f32
    )[None]
    grad_down_weight = lax.dot_general(
        hidden, grad_full, CONTRACT_FIRST, preferred_element_type=f32
    )[None]
    grad_up_weight = lax.dot_general(
        expert_rows, pre_grad, CONTRACT_FIRST, preferred_element_type=f32
    )[None]
    grad_up_bias = jnp.sum(pre_grad, axis=0, dtype=f32)[None]

    first_hit = slot_ids[:, 0:1] == numbers.T
    second_hit = slot_ids[:, 1:2] == numbers.T
    back_sum = jnp.dot(
        (first_hit | second_hit).astype(bf16), home_grad, preferred_element_type=f32
    ).astype(bf16)
    back_rows = lax.psum_scatter(back_sum, "head", scatter_dimension=0, tiled=True)
    my_ids = my_rows(slot_ids)
    gate_grad = jnp.stack(
        [
            jnp.sum(jnp.where(my_ids[:, 0:1] == numbers.T, home_gate[None, :], 0.0), axis=1),
            jnp.sum(jnp.where(my_ids[:, 1:2] == numbers.T, home_gate[None, :], 0.0), axis=1),
        ],
        axis=1,
    )
    my_chances = my_rows(chances)
    my_second = my_rows(second_in)
    route_grad = jnp.sum(my_rows(chosen) * gate_grad[:, :, None], axis=1)
    logit_grad = (
        my_chances * (route_grad - jnp.sum(my_chances * route_grad, axis=1, keepdims=True))
    ).astype(bf16)
    grad_router = lax.dot_general(
        my_second, logit_grad, CONTRACT_FIRST, preferred_element_type=f32
    )
    normed_two_grad = back_rows.astype(f32) + lax.dot_general(
        logit_grad, router, CONTRACT_LAST, preferred_element_type=f32
    )
    ignored, norm_two_back = jax.vjp(norm_rows, my_rows(residual), gain_two, bias_two)
    residual_norm, grad_norm2_gain, grad_norm2_bias = norm_two_back(normed_two_grad)
    cotangent_rows = lax.all_to_all(
        cotangent, "head", split_axis=0, concat_axis=1, tiled=True
    )
    residual_grad = cotangent_rows.astype(f32) + residual_norm
    grad_out_bias = jnp.sum(residual_grad, axis=0)
    residual_half = lax.all_gather(residual_grad.astype(bf16), "head", axis=0, tiled=True)

    moe_sum = jnp.dot(
        jnp.where(first_hit, gate_values[:, 0:1], jnp.where(second_hit, gate_values[:, 1:2], 0.0)).astype(bf16),
        home_out,
        preferred_element_type=f32,
    ).astype(bf16)
    moe_cols = lax.psum_scatter(moe_sum, "head", scatter_dimension=1, tiled=True)
    block_out = (
        lax.dynamic_slice_in_dim(residual, head_index * quarter, quarter, 1) + moe_cols.astype(f32)
    ).astype(bf16)

    grad_out_weight = lax.dot_general(
        context_flat, residual_half, CONTRACT_FIRST, preferred_element_type=f32
    )
    context_grad = (
        lax.dot_general(residual_half, out_weight, CONTRACT_LAST, preferred_element_type=f32)
        .astype(bf16)
        .reshape(shape_four)
    )
    query_grad, key_grad, value_grad = lax.map(
        partial(attend_backward, factor=factor),
        (query_rows, key_rows, value_rows, segments, live_mask, context_grad, log_total),
    )
    query_flat = query_grad.reshape(tok_count, local_width)
    value_flat = value_grad.reshape(tok_count, local_width)
    qkv_grad = jnp.stack(
        [query_flat, key_grad.reshape(tok_count, local_width), value_flat], axis=1
    ).reshape(tok_count, 3 * local_width)
    normed_one_grad = lax.psum_scatter(
        lax.dot_general(qkv_grad, flat_qkv, CONTRACT_LAST, preferred_element_type=f32).astype(bf16),
        "head",
        scatter_dimension=0,
        tiled=True,
    ).astype(f32)
    grad_qkv_weight = lax.dot_general(
        first_in, qkv_grad, CONTRACT_FIRST, preferred_element_type=f32
    ).reshape(model_width, 3, local_width)
    grad_qv_bias = jnp.stack(
        [jnp.sum(query_flat, axis=0, dtype=f32), jnp.sum(value_flat, axis=0, dtype=f32)], axis=0
    )
    ignored, norm_one_back = jax.vjp(norm_rows, my_rows(inputs), gain_one, bias_one)
    inputs_norm, grad_norm1_gain, grad_norm1_bias = norm_one_back(normed_one_grad)
    grad_tokens = lax.all_gather(
        (residual_grad + inputs_norm).astype(bf16), "head", axis=0, tiled=True
    ).astype(f32)
    sums_all = lax.psum(
        (
            grad_norm1_gain,
            grad_norm1_bias,
            grad_out_bias,
            grad_norm2_gain,
            grad_norm2_bias,
            grad_router,
        ),
        ("exp", "head"),
    )
    grad_out_weight = lax.psum(grad_out_weight, "exp")
    grad_qkv_weight, grad_qv_bias = lax.psum((grad_qkv_weight, grad_qv_bias), "exp")
    return (
        block_out,
        grad_tokens,
        sums_all[0],
        sums_all[1],
        grad_qkv_weight,
        grad_qv_bias,
        grad_out_weight,
        sums_all[2],
        sums_all[3],
        sums_all[4],
        sums_all[5],
        grad_up_weight,
        grad_up_bias,
        grad_down_weight,
        grad_down_bias,
    )


def solution(mesh):
    in_specs = (
        P("exp", None),
        P("exp", None),
        P("exp", None),
        P("exp", None),
        P("exp", None),
        P(),
        P(),
        P(None, None, "head"),
        P(None, "head"),
        P("head", None),
        P(),
        P(),
        P(),
        P(),
        P("exp", None, "head"),
        P("exp", "head"),
        P("exp", "head", None),
        P("exp", "head"),
        P("exp", "head"),
    )
    out_specs = (
        P("exp", "head"),
        P("exp", None),
        P(),
        P(),
        P(None, None, "head"),
        P(None, "head"),
        P("head", None),
        P(),
        P(),
        P(),
        P(),
        P("exp", None, "head"),
        P("exp", "head"),
        P("exp", "head", None),
        P("exp", "head"),
    )
    return jax.shard_map(body, mesh=mesh, in_specs=in_specs, out_specs=out_specs, check_vma=False)
```

```python
from functools import partial
import math

import jax
import jax.numpy as jnp
from jax import lax
from jax.experimental import pallas as pl
from jax.experimental.pallas import tpu as pltpu
from jax.sharding import PartitionSpec as P

HEAD_DIM = 64
LANES = 128
EPSILON = 1e-06
NEGATIVE = -1e30
CONTRACT_FIRST = (((0,), (0,)), ((), ()))
CONTRACT_LAST = (((1,), (1,)), ((), ()))
F32 = jnp.float32
BF16 = jnp.bfloat16
MESH = pl.DeviceIdType.MESH
VMEM_LIMIT = 48 * 1024 * 1024


def round_up(number, step):
    return (number + step - 1) // step * step


def whole():
    return pl.BlockSpec(memory_space=pltpu.VMEM)


def anywhere():
    return pl.BlockSpec(memory_space=pl.ANY)


def shaped(shape, dtype):
    return jax.ShapeDtypeStruct(shape, dtype)


def params(**more):
    return pltpu.CompilerParams(vmem_limit_bytes=VMEM_LIMIT, **more)


def cost(flops, moved):
    return pl.CostEstimate(flops=int(flops), bytes_accessed=int(moved), transcendentals=0)


def dot(left, right):
    return jnp.dot(left, right, preferred_element_type=F32)


def dot_last(left, right):
    return lax.dot_general(left, right, CONTRACT_LAST, preferred_element_type=F32)


def dot_first(left, right):
    return lax.dot_general(left, right, CONTRACT_FIRST, preferred_element_type=F32)


def standard(values):
    centred = values - jnp.mean(values, axis=-1, keepdims=True)
    scale = lax.rsqrt(jnp.mean(centred * centred, axis=-1, keepdims=True) + EPSILON)
    return centred * scale, scale


def norm_back(grad_rows, gain_row, normal, scale):
    inner = grad_rows * gain_row
    return scale * (
        inner
        - jnp.mean(inner, axis=-1, keepdims=True)
        - normal * jnp.mean(inner * normal, axis=-1, keepdims=True)
    )


def mask_penalty(seg_col, seg_row, live_row):
    shape = (seg_col.shape[0], seg_row.shape[1])
    diagonal = lax.broadcasted_iota(jnp.int32, shape, 0) == lax.broadcasted_iota(
        jnp.int32, shape, 1
    )
    allowed = (seg_col == seg_row) & ((live_row > 0) | diagonal)
    return jnp.where(allowed, 0.0, NEGATIVE)


def pack_rows(rows, half):
    count = rows.shape[0]
    third = rows[:, LANES:]
    return rows[:, :LANES], jnp.concatenate([third[:half], third[count - half :]], axis=1)


def unpack_rows(parts_of, into, head_parts, count, half):
    extra = HEAD_DIM
    width = LANES + extra
    for z in range(head_parts):
        packed = parts_of(z)
        into[:, z * width : z * width + LANES] = packed[:count]
        tail = packed[count : count + half]
        into[:half, z * width + LANES : (z + 1) * width] = tail[:, :extra]
        into[half:, z * width + LANES : (z + 1) * width] = tail[2 * half - count :, extra:]


def attend_kernel(
    tokens_ref, norm_ref, weight_ref, bias_ref, segc_ref, segr_ref, live_ref,
    first_ref, qkv_ref, context_ref, packed_ref, total_ref,
):
    normal, ignored = standard(tokens_ref[...].astype(F32))
    first = (normal * norm_ref[0:1] + norm_ref[1:2]).astype(BF16)
    first_ref[...] = first
    rows = (dot(first, weight_ref[...]) + bias_ref[...]).astype(BF16)
    qkv_ref[...] = rows
    penalty = mask_penalty(segc_ref[0], segr_ref[0], live_ref[0])
    seqlen = rows.shape[0]
    width = rows.shape[1] // 3
    parts = []
    for head in range(width // HEAD_DIM):
        lo = head * HEAD_DIM
        hi = lo + HEAD_DIM
        query = rows[:, lo:hi] * BF16(1.0 / math.sqrt(HEAD_DIM))
        scores = dot_last(query, rows[:, width + lo : width + hi]) + penalty
        largest = jnp.max(scores, axis=-1, keepdims=True)
        weights = jnp.exp(scores - largest)
        total = jnp.sum(weights, axis=-1, keepdims=True)
        values = rows[:, 2 * width + lo : 2 * width + hi]
        parts.append((dot(weights.astype(BF16), values) / total).astype(BF16))
        total_ref[:, head : head + 1] = largest + jnp.log(total)
    context = jnp.concatenate(parts, axis=1)
    context_ref[...] = context
    wide, tail = pack_rows(context, seqlen // 2)
    packed_ref[0, :seqlen] = wide
    packed_ref[0, seqlen:] = tail


def attend(tokens, norm_rows, flat_qkv, bias_row, seg_cols, seg_rows, live_rows):
    tok_count, model_width = tokens.shape
    seq_count, seqlen = seg_rows.shape[0], seg_rows.shape[2]
    wide = flat_qkv.shape[1]
    width = wide // 3
    step = lambda i: (i, 0)
    fixed = lambda i: (0, 0)
    deep = lambda i: (i, 0, 0)
    return pl.pallas_call(
        attend_kernel,
        grid=(seq_count,),
        in_specs=[
            pl.BlockSpec((seqlen, model_width), step),
            pl.BlockSpec((8, model_width), fixed),
            pl.BlockSpec((model_width, wide), fixed),
            pl.BlockSpec((1, wide), fixed),
            pl.BlockSpec((1, seqlen, 1), deep),
            pl.BlockSpec((1, 1, seqlen), deep),
            pl.BlockSpec((1, 1, seqlen), deep),
        ],
        out_specs=[
            pl.BlockSpec((seqlen, model_width), step),
            pl.BlockSpec((seqlen, wide), step),
            pl.BlockSpec((seqlen, width), step),
            pl.BlockSpec((1, seqlen + seqlen // 2, LANES), deep),
            pl.BlockSpec((seqlen, LANES), step),
        ],
        out_shape=[
            shaped((tok_count, model_width), BF16),
            shaped((tok_count, wide), BF16),
            shaped((tok_count, width), BF16),
            shaped((seq_count, seqlen + seqlen // 2, LANES), BF16),
            shaped((tok_count, LANES), F32),
        ],
        compiler_params=params(),
        cost_estimate=cost(4e9, 1e7),
        name="attend",
    )(tokens, norm_rows, flat_qkv, bias_row, seg_cols, seg_rows, live_rows)


def table_kernel(experts, capacity, stride, half, chunk, prio_ref, rows_ref, cot_ref, ids_ref, out_ref):
    tok_count = rows_ref.shape[1]
    numbers = lax.broadcasted_iota(jnp.int32, (experts, 1), 0)

    def hot(rows):
        live = rows[2:3] > 0
        first = jnp.where((rows[0:1] == numbers) & live, 1.0, 0.0)
        second = jnp.where((rows[1:2] == numbers) & live, 1.0, 0.0)
        return first, second

    rank_row = rows_ref[3:4]
    counts = jnp.zeros((2 * experts, tok_count), F32)
    for start in range(0, tok_count, chunk):
        first, second = hot(rows_ref[:, start : start + chunk])
        earlier = jnp.where(prio_ref[start : start + chunk] < rank_row, 1.0, 0.0).astype(BF16)
        counts = counts + dot(jnp.concatenate([first, second], axis=0).astype(BF16), earlier)
    first, second = hot(rows_ref[...])
    total = jnp.sum(first, axis=1, keepdims=True)
    places = [
        jnp.sum(first * counts[:experts], axis=0, keepdims=True),
        jnp.sum(second * (counts[experts:] + total), axis=0, keepdims=True),
    ]
    ids = []
    for pick in range(2):
        place = places[pick].astype(jnp.int32)
        kept = (place < capacity) & (rows_ref[2:3] > 0)
        ids.append(jnp.where(kept, rows_ref[pick : pick + 1] * stride + place, -1))
        ids_ref[pick : pick + 1] = ids[pick]
    ids_ref[2:8] = jnp.full((6, tok_count), -1, jnp.int32)

    def one(expert, carry):
        slots = expert * stride + lax.broadcasted_iota(jnp.int32, (stride, 1), 0)
        hit = (ids_ref[0:1] == slots) | (ids_ref[1:2] == slots)
        block = dot(jnp.where(hit, 1.0, 0.0).astype(BF16), cot_ref[...]).astype(BF16)
        wide, tail = pack_rows(block, half)
        out_ref[expert, :stride] = wide
        out_ref[expert, stride:] = tail
        return carry

    lax.fori_loop(0, experts, one, 0)


def tables(prio_col, rows, cotangent, experts, capacity, stride, half, chunk):
    tok_count = rows.shape[1]
    return pl.pallas_call(
        partial(table_kernel, experts, capacity, stride, half, chunk),
        in_specs=[whole()] * 3,
        out_specs=[whole()] * 2,
        out_shape=[
            shaped((8, tok_count), jnp.int32),
            shaped((experts, stride + half, LANES), BF16),
        ],
        compiler_params=params(),
        cost_estimate=cost(1e10, 1e7),
        name="tables",
    )(prio_col, rows, cotangent)


def gelu_parts(pre):
    root = math.sqrt(2.0 / math.pi)
    square = pre * pre
    wave = jnp.tanh(root * (pre + 0.044715 * pre * square))
    half_sum = 0.5 * (1.0 + wave)
    slope = half_sum + 0.5 * pre * (1.0 - wave * wave) * (
        root * (1.0 + 3.0 * 0.044715 * square)
    )
    return pre * half_sum, slope


def greet(peers):
    barrier = pltpu.get_barrier_semaphore()
    me = lax.axis_index("exp")
    here = lax.axis_index("head")

    def call(step, carry):
        other = lax.rem(me + step, peers)
        pl.semaphore_signal(barrier, inc=1, device_id=(other, here), device_id_type=MESH)
        return carry

    lax.fori_loop(1, peers, call, 0)
    return barrier


def forward_kernel(
    experts, stride, seq_count, head_parts,
    gathered_ref, tokens_ref, vectors_ref, out_weight_ref, router_ref, rows_ref, ids_ref,
    up_ref, up_bias_ref, down_ref, down_bias_ref,
    residual_ref, own_residual_ref, own_second_ref, gates_ref, arrived_ref, hidden_ref, result_ref,
    gate_col_ref, context_scr, second_scr, logit_scr, send_scr, gate_send, gate_recv,
    send_sem, recv_sem, gate_send_sem, gate_recv_sem,
):
    me = lax.axis_index("exp")
    here = lax.axis_index("head")
    barrier = greet(experts)
    tok_count = tokens_ref.shape[0]
    seqlen = tok_count // seq_count
    tok_part = tok_count // head_parts
    for seq in range(seq_count):
        span = slice(seq * seqlen, (seq + 1) * seqlen)
        unpack_rows(lambda z: gathered_ref[z, seq], context_scr, head_parts, seqlen, seqlen // 2)
        residual = (
            tokens_ref[span].astype(F32)
            + dot(context_scr[...], out_weight_ref[...])
            + vectors_ref[0:1]
        )
        residual_ref[span] = residual
        normal, ignored = standard(residual)
        second = (normal * vectors_ref[1:2] + vectors_ref[2:3]).astype(BF16)
        second_scr[span] = second
        logit_scr[:, span] = dot(second, router_ref[...]).T[:experts]
    own = pl.ds(pl.multiple_of(here * tok_part, tok_part), tok_part)
    own_residual_ref[...] = residual_ref[own]
    own_second_ref[...] = second_scr[own]

    logits = logit_scr[...]
    powers = jnp.exp(logits - jnp.max(logits, axis=0, keepdims=True))
    chances = powers / jnp.sum(powers, axis=0, keepdims=True)
    numbers = lax.broadcasted_iota(jnp.int32, (experts, 1), 0)
    for pick in range(2):
        chosen = jnp.where(rows_ref[pick : pick + 1] == numbers, chances, 0.0)
        gate = jnp.where(ids_ref[pick : pick + 1] >= 0, jnp.sum(chosen, axis=0, keepdims=True), 0.0)
        gates_ref[pick : pick + 1] = gate
    gates_ref[2:8] = jnp.zeros((6, tok_count), F32)
    pl.semaphore_wait(barrier, experts - 1)

    def copies(target, step):
        to = dict(device_id=(target, here), device_id_type=MESH)
        return (
            pltpu.make_async_remote_copy(
                src_ref=send_scr.at[step],
                dst_ref=arrived_ref.at[me],
                send_sem=send_sem.at[step],
                recv_sem=recv_sem.at[step],
                **to,
            ),
            pltpu.make_async_remote_copy(
                src_ref=gate_send.at[step],
                dst_ref=gate_recv.at[me],
                send_sem=gate_send_sem.at[step],
                recv_sem=gate_recv_sem.at[step],
                **to,
            ),
        )

    def fill(target):
        slots = target * stride + lax.broadcasted_iota(jnp.int32, (stride, 1), 0)
        first = ids_ref[0:1] == slots
        second = ids_ref[1:2] == slots
        block = dot(jnp.where(first | second, 1.0, 0.0).astype(BF16), second_scr[...]).astype(BF16)
        gate = jnp.sum(
            jnp.where(first, gates_ref[0:1], jnp.where(second, gates_ref[1:2], 0.0)),
            axis=1,
            keepdims=True,
        )
        return block, jnp.broadcast_to(gate, (stride, LANES)).T[:8]

    def send(step, carry):
        target = lax.rem(me + step, experts)
        block, gate = fill(target)
        send_scr[step] = block
        gate_send[step] = gate
        for copy in copies(target, step):
            copy.start()
        return carry

    lax.fori_loop(1, experts, send, 0)
    block, gate = fill(me)
    arrived_ref[me] = block
    gate_recv[me] = gate

    def work(source):
        pre = dot(arrived_ref[source], up_ref[...]) + up_bias_ref[...]
        hidden = gelu_parts(pre)[0].astype(BF16)
        hidden_ref[source] = hidden
        result_ref[source] = (dot(hidden, down_ref[...]) + down_bias_ref[...]).astype(BF16)

    work(me)

    def receive(step, carry):
        source = lax.rem(me + experts - step, experts)
        wide, narrow = copies(source, step)
        wide.wait_recv()
        narrow.wait_recv()
        work(source)
        return carry

    lax.fori_loop(1, experts, receive, 0)

    def finish(step, carry):
        for copy in copies(lax.rem(me + step, experts), step):
            copy.wait_send()
        return carry

    lax.fori_loop(1, experts, finish, 0)
    lane = lax.broadcasted_iota(jnp.int32, (LANES, stride), 0)
    square = jnp.zeros((LANES, stride), F32)
    for source in range(experts):
        square = jnp.where(lane == source, gate_recv[source, 0:1], square)
    gate_col_ref[...] = square.T


def forward(
    gathered, tokens, vectors, out_weight, router, rows, ids, up, up_bias, down, down_bias,
    experts, stride, seq_count, head_parts,
):
    tok_count, model_width = tokens.shape
    tok_part = tok_count // head_parts
    seqlen = tok_count // seq_count
    return pl.pallas_call(
        partial(forward_kernel, experts, stride, seq_count, head_parts),
        in_specs=[whole()] * 11,
        out_specs=[whole()] * 8,
        out_shape=[
            shaped((tok_count, model_width), F32),
            shaped((tok_part, model_width), F32),
            shaped((tok_part, model_width), BF16),
            shaped((8, tok_count), F32),
            shaped((experts, stride, model_width), BF16),
            shaped((experts, stride, up.shape[1]), BF16),
            shaped((experts, stride, model_width), BF16),
            shaped((stride, LANES), F32),
        ],
        scratch_shapes=[
            pltpu.VMEM((seqlen, model_width), BF16),
            pltpu.VMEM((tok_count, model_width), BF16),
            pltpu.VMEM((experts, tok_count), F32),
            pltpu.VMEM((experts, stride, model_width), BF16),
            pltpu.VMEM((experts, 8, stride), F32),
            pltpu.VMEM((experts, 8, stride), F32),
            pltpu.SemaphoreType.DMA((experts,)),
            pltpu.SemaphoreType.DMA((experts,)),
            pltpu.SemaphoreType.DMA((experts,)),
            pltpu.SemaphoreType.DMA((experts,)),
        ],
        compiler_params=params(collective_id=0, has_side_effects=True),
        cost_estimate=cost(8e10, 1e8),
        name="forward",
    )(gathered, tokens, vectors, out_weight, router, rows, ids, up, up_bias, down, down_bias)


def backward_kernel(
    experts, stride, half, head_parts, chunk,
    arrived_hbm, hidden_hbm, result_hbm, cot_hbm, gate_col_ref, ids_ref, up_ref, up_bias_ref, down_ref,
    sums_ref, grad_up_ref, grad_up_bias_ref, grad_down_ref, grad_down_bias_ref,
    rows_scr, result_scr, cot_scr, cot_wide, hidden_scr, pre_grad_scr, out_grad_scr,
    send_scr, recv_scr, gate_send, gate_recv, total_scr, gate_total,
    load_sem, send_sem, recv_sem, gate_send_sem, gate_recv_sem,
):
    me = lax.axis_index("exp")
    here = lax.axis_index("head")
    barrier = greet(experts)
    tok_count = ids_ref.shape[0]
    model_width = up_ref.shape[0]

    def loads(step):
        home = lax.rem(me + step, experts)
        slot = lax.rem(step, 2)
        return (
            pltpu.make_async_copy(arrived_hbm.at[home], rows_scr.at[slot], load_sem.at[slot, 0]),
            pltpu.make_async_copy(result_hbm.at[home], result_scr.at[slot], load_sem.at[slot, 1]),
            pltpu.make_async_copy(cot_hbm.at[:, home], cot_scr.at[slot], load_sem.at[slot, 2]),
        )

    def copies(target, step):
        to = dict(device_id=(target, here), device_id_type=MESH)
        return (
            pltpu.make_async_remote_copy(
                src_ref=send_scr.at[step],
                dst_ref=recv_scr.at[me],
                send_sem=send_sem.at[step],
                recv_sem=recv_sem.at[step],
                **to,
            ),
            pltpu.make_async_remote_copy(
                src_ref=gate_send.at[step],
                dst_ref=gate_recv.at[me],
                send_sem=gate_send_sem.at[step],
                recv_sem=gate_recv_sem.at[step],
                **to,
            ),
        )

    for copy in loads(1):
        copy.start()
    grad_up_ref[...] = jnp.zeros_like(grad_up_ref)
    grad_down_ref[...] = jnp.zeros_like(grad_down_ref)
    grad_up_bias_ref[...] = jnp.zeros_like(grad_up_bias_ref)
    grad_down_bias_ref[...] = jnp.zeros_like(grad_down_bias_ref)
    total_scr[...] = jnp.zeros_like(total_scr)
    gate_total[...] = jnp.zeros_like(gate_total)
    pl.semaphore_wait(barrier, experts - 1)

    def work(step):
        home = lax.rem(me + step, experts)
        slot = lax.rem(step, 2)
        for copy in loads(step):
            copy.wait()
        unpack_rows(lambda z: cot_scr[slot, z], cot_wide, head_parts, stride, half)
        out_rows = cot_wide[...].astype(F32)
        pre = dot(rows_scr[slot], up_ref[...]) + up_bias_ref[...]
        slope = gelu_parts(pre)[1]
        lane = lax.broadcasted_iota(jnp.int32, (stride, LANES), 1)
        gate = jnp.sum(jnp.where(lane == home, gate_col_ref[...], 0.0), axis=1, keepdims=True)
        out_grad = (gate * out_rows).astype(BF16)
        out_grad_scr[step] = out_grad
        grad_down_bias_ref[0:1] += jnp.sum(out_grad.astype(F32), axis=0, keepdims=True)
        pre_grad = (dot_last(out_grad, down_ref[...]) * slope).astype(BF16)
        pre_grad_scr[step] = pre_grad
        grad_up_bias_ref[0:1] += jnp.sum(pre_grad.astype(F32), axis=0, keepdims=True)
        gate_grad = jnp.sum(result_scr[slot].astype(F32) * out_rows, axis=1, keepdims=True)
        return (
            dot_last(pre_grad, up_ref[...]).astype(BF16),
            jnp.broadcast_to(gate_grad, (stride, LANES)).T[:8],
        )

    def send(step, carry):
        for copy in loads(lax.rem(step + 1, experts)):
            copy.start()
        block, gate = work(step)
        send_scr[step] = block
        gate_send[step] = gate
        for copy in copies(lax.rem(me + step, experts), step):
            copy.start()
        return carry

    lax.fori_loop(1, experts, send, 0)
    block, gate = work(0)
    recv_scr[me] = block
    gate_recv[me] = gate

    def row_loads(step):
        home = lax.rem(me + step, experts)
        slot = lax.rem(step, 2)
        return (
            pltpu.make_async_copy(arrived_hbm.at[home], rows_scr.at[slot], load_sem.at[slot, 0]),
            pltpu.make_async_copy(hidden_hbm.at[home], hidden_scr.at[slot], load_sem.at[slot, 1]),
        )

    def weigh(step):
        slot = lax.rem(step, 2)
        for copy in row_loads(step):
            copy.wait()
        grad_up_ref[...] += dot_first(rows_scr[slot], pre_grad_scr[step])
        grad_down_ref[...] += dot_first(hidden_scr[slot], out_grad_scr[step])

    def weigh_some(step, carry):
        for copy in row_loads(step + 1):
            copy.start()
        weigh(step)
        return carry

    for copy in row_loads(0):
        copy.start()
    lax.fori_loop(0, experts - 1, weigh_some, 0)
    weigh(experts - 1)

    def gather(source):
        slots = source * stride + lax.broadcasted_iota(jnp.int32, (1, stride), 1)
        lane = lax.broadcasted_iota(jnp.int32, (chunk, LANES), 1)

        def part(index, carry):
            span = pl.ds(pl.multiple_of(index * chunk, chunk), chunk)
            hit = (ids_ref[span, 0:1] == slots) | (ids_ref[span, 1:2] == slots)
            total_scr[span] += dot(jnp.where(hit, 1.0, 0.0).astype(BF16), recv_scr[source])
            gate = jnp.sum(jnp.where(hit, gate_recv[source, 0:1], 0.0), axis=1, keepdims=True)
            gate_total[span] = jnp.where(lane == source, gate, gate_total[span])
            return carry

        lax.fori_loop(0, tok_count // chunk, part, 0)

    gather(me)

    def receive(step, carry):
        source = lax.rem(me + experts - step, experts)
        for copy in copies(source, step):
            copy.wait_recv()
        gather(source)
        return carry

    lax.fori_loop(1, experts, receive, 0)

    def finish(step, carry):
        for copy in copies(lax.rem(me + step, experts), step):
            copy.wait_send()
        return carry

    lax.fori_loop(1, experts, finish, 0)
    sums_ref[:, :model_width] = total_scr[...].astype(BF16)
    sums_ref[:, model_width:] = gate_total[...].astype(BF16)


def backward(
    arrived, hidden, result, cot_rows, gate_col, id_cols, up, up_bias, down, half, head_parts, chunk
):
    experts, stride, model_width = arrived.shape
    tok_count = id_cols.shape[0]
    inner = up.shape[1]
    rows = (experts, stride, model_width)
    return pl.pallas_call(
        partial(backward_kernel, experts, stride, half, head_parts, chunk),
        in_specs=[anywhere()] * 4 + [whole()] * 5,
        out_specs=[whole()] * 5,
        out_shape=[
            shaped((tok_count, model_width + LANES), BF16),
            shaped((model_width, inner), F32),
            shaped((8, inner), F32),
            shaped((inner, model_width), F32),
            shaped((8, model_width), F32),
        ],
        scratch_shapes=[
            pltpu.VMEM((2, stride, model_width), BF16),
            pltpu.VMEM((2, stride, model_width), BF16),
            pltpu.VMEM((2, head_parts, stride + half, LANES), BF16),
            pltpu.VMEM((stride, model_width), BF16),
            pltpu.VMEM((2, stride, inner), BF16),
            pltpu.VMEM((experts, stride, inner), BF16),
            pltpu.VMEM(rows, BF16),
            pltpu.VMEM(rows, BF16),
            pltpu.VMEM(rows, BF16),
            pltpu.VMEM((experts, 8, stride), F32),
            pltpu.VMEM((experts, 8, stride), F32),
            pltpu.VMEM((tok_count, model_width), F32),
            pltpu.VMEM((tok_count, LANES), F32),
            pltpu.SemaphoreType.DMA((2, 3)),
            pltpu.SemaphoreType.DMA((experts,)),
            pltpu.SemaphoreType.DMA((experts,)),
            pltpu.SemaphoreType.DMA((experts,)),
            pltpu.SemaphoreType.DMA((experts,)),
        ],
        compiler_params=params(collective_id=1, has_side_effects=True),
        cost_estimate=cost(8e10, 1e8),
        name="backward",
    )(arrived, hidden, result, cot_rows, gate_col, id_cols, up, up_bias, down)


def middle_kernel(
    experts, sums_ref, residual_ref, second_ref, cot_ref, router_ref, vectors_ref,
    grad_ref, half_ref, router_grad_ref, rows_ref,
):
    model_width = residual_ref.shape[1]
    second = second_ref[...]
    lane = lax.broadcasted_iota(jnp.int32, (second.shape[0], LANES), 1)
    logits = jnp.where(lane < experts, dot(second, router_ref[...]), NEGATIVE)
    powers = jnp.exp(logits - jnp.max(logits, axis=1, keepdims=True))
    chances = powers / jnp.sum(powers, axis=1, keepdims=True)
    route_grad = sums_ref[:, model_width:].astype(F32)
    logit_grad = (
        chances * (route_grad - jnp.sum(chances * route_grad, axis=1, keepdims=True))
    ).astype(BF16)
    router_grad_ref[...] = dot_first(second, logit_grad)
    grad = sums_ref[:, :model_width].astype(F32) + dot_last(logit_grad, router_ref[...])
    normal, scale = standard(residual_ref[...])
    rows_ref[0:1] = jnp.sum(grad * normal, axis=0, keepdims=True)
    rows_ref[1:2] = jnp.sum(grad, axis=0, keepdims=True)
    total = cot_ref[...].astype(F32) + norm_back(grad, vectors_ref[1:2], normal, scale)
    grad_ref[...] = total
    half_ref[...] = total.astype(BF16)
    rows_ref[2:3] = jnp.sum(total, axis=0, keepdims=True)
    rows_ref[3:8] = jnp.zeros((5, model_width), F32)


def middle(sums, residual, second, cot_rows, router, vectors, experts):
    rows, model_width = residual.shape
    return pl.pallas_call(
        partial(middle_kernel, experts),
        in_specs=[whole()] * 6,
        out_specs=[whole()] * 4,
        out_shape=[
            shaped((rows, model_width), F32),
            shaped((rows, model_width), BF16),
            shaped((model_width, LANES), F32),
            shaped((8, model_width), F32),
        ],
        compiler_params=params(),
        cost_estimate=cost(5e9, 1e7),
        name="middle",
    )(sums, residual, second, cot_rows, router, vectors)


def attend_back_kernel(
    grad_ref, context_ref, first_ref, qkv_ref, total_ref, weight_ref, out_weight_ref,
    segc_ref, segr_ref, live_ref,
    first_grad_ref, weight_grad_ref, bias_grad_ref, out_grad_ref,
):
    rows = qkv_ref[...]
    width = rows.shape[1] // 3
    grad = grad_ref[...]
    context_grad = dot_last(grad, out_weight_ref[...]).astype(BF16)
    penalty = mask_penalty(segc_ref[0], segr_ref[0], live_ref[0])
    context = context_ref[...]
    query_parts, key_parts, value_parts = [], [], []
    factor = 1.0 / math.sqrt(HEAD_DIM)
    for head in range(width // HEAD_DIM):
        lo = head * HEAD_DIM
        hi = lo + HEAD_DIM
        query = rows[:, lo:hi] * BF16(factor)
        keys = rows[:, width + lo : width + hi]
        values = rows[:, 2 * width + lo : 2 * width + hi]
        back = context_grad[:, lo:hi]
        weights = jnp.exp(dot_last(query, keys) + penalty - total_ref[:, head : head + 1])
        value_parts.append(dot_first(weights.astype(BF16), back))
        weight_grad = dot_last(back, values)
        inner = jnp.sum(
            back.astype(F32) * context[:, lo:hi].astype(F32), axis=-1, keepdims=True
        )
        score_grad = (weights * (weight_grad - inner)).astype(BF16)
        query_parts.append(dot(score_grad, keys) * factor)
        key_parts.append(dot_first(score_grad, query))
    joined = jnp.concatenate(query_parts + key_parts + value_parts, axis=1).astype(BF16)
    first_grad_ref[...] = dot_last(joined, weight_ref[...]).astype(BF16)
    weight_grad = dot_first(first_ref[...], joined)
    out_grad = dot_first(context, grad)
    bias_grad = jnp.sum(joined.astype(F32), axis=0, keepdims=True)

    @pl.when(pl.program_id(0) == 0)
    def start():
        weight_grad_ref[...] = weight_grad
        out_grad_ref[...] = out_grad
        bias_grad_ref[...] = jnp.broadcast_to(bias_grad, bias_grad_ref.shape)

    @pl.when(pl.program_id(0) > 0)
    def more():
        weight_grad_ref[...] += weight_grad
        out_grad_ref[...] += out_grad
        bias_grad_ref[...] += jnp.broadcast_to(bias_grad, bias_grad_ref.shape)


def attend_back(
    grad, context, first, qkv, totals, flat_qkv, out_weight, seg_cols, seg_rows, live_rows
):
    tok_count, model_width = first.shape
    seq_count, seqlen = seg_rows.shape[0], seg_rows.shape[2]
    wide = flat_qkv.shape[1]
    width = wide // 3
    step = lambda i: (i, 0)
    fixed = lambda i: (0, 0)
    deep = lambda i: (i, 0, 0)
    return pl.pallas_call(
        attend_back_kernel,
        grid=(seq_count,),
        in_specs=[
            pl.BlockSpec((seqlen, model_width), step),
            pl.BlockSpec((seqlen, width), step),
            pl.BlockSpec((seqlen, model_width), step),
            pl.BlockSpec((seqlen, wide), step),
            pl.BlockSpec((seqlen, LANES), step),
            pl.BlockSpec((model_width, wide), fixed),
            pl.BlockSpec((width, model_width), fixed),
            pl.BlockSpec((1, seqlen, 1), deep),
            pl.BlockSpec((1, 1, seqlen), deep),
            pl.BlockSpec((1, 1, seqlen), deep),
        ],
        out_specs=[
            pl.BlockSpec((seqlen, model_width), step),
            pl.BlockSpec((model_width, wide), fixed),
            pl.BlockSpec((8, wide), fixed),
            pl.BlockSpec((width, model_width), fixed),
        ],
        out_shape=[
            shaped((tok_count, model_width), BF16),
            shaped((model_width, wide), F32),
            shaped((8, wide), F32),
            shaped((width, model_width), F32),
        ],
        compiler_params=params(),
        cost_estimate=cost(1e10, 1e7),
        name="attend_back",
    )(grad, context, first, qkv, totals, flat_qkv, out_weight, seg_cols, seg_rows, live_rows)


def last_kernel(grad_ref, tokens_ref, residual_grad_ref, norm_ref, out_ref, rows_ref):
    grad = grad_ref[...].astype(F32)
    normal, scale = standard(tokens_ref[...].astype(F32))
    rows_ref[0:1] = jnp.sum(grad * normal, axis=0, keepdims=True)
    rows_ref[1:2] = jnp.sum(grad, axis=0, keepdims=True)
    rows_ref[2:8] = jnp.zeros((6, grad.shape[1]), F32)
    total = residual_grad_ref[...] + norm_back(grad, norm_ref[0:1], normal, scale)
    out_ref[...] = total.astype(BF16)


def last(grad, tokens, residual_grad, norm_rows):
    rows, model_width = tokens.shape
    return pl.pallas_call(
        last_kernel,
        in_specs=[whole()] * 4,
        out_specs=[whole()] * 2,
        out_shape=[shaped((rows, model_width), BF16), shaped((8, model_width), F32)],
        compiler_params=params(),
        cost_estimate=cost(1e9, 1e7),
        name="last",
    )(grad, tokens, residual_grad, norm_rows)


def combine_kernel(stride, share, chunk, ids_ref, gates_ref, home_ref, residual_ref, out_ref, total_scr):
    experts = home_ref.shape[0]
    total_scr[...] = residual_ref[...] * share

    def one(source, carry):
        slots = source * stride + lax.broadcasted_iota(jnp.int32, (1, stride), 1)

        def part(index, carry):
            span = pl.ds(pl.multiple_of(index * chunk, chunk), chunk)
            weights = jnp.where(
                ids_ref[span, 0:1] == slots,
                gates_ref[span, 0:1],
                jnp.where(ids_ref[span, 1:2] == slots, gates_ref[span, 1:2], 0.0),
            ).astype(BF16)
            total_scr[span] += dot(weights, home_ref[source])
            return carry

        return lax.fori_loop(0, total_scr.shape[0] // chunk, part, carry)

    lax.fori_loop(0, experts, one, 0)
    out_ref[...] = total_scr[...].astype(BF16)


def combine(id_cols, gate_cols, home, residual, stride, share, chunk):
    return pl.pallas_call(
        partial(combine_kernel, stride, share, chunk),
        in_specs=[whole()] * 4,
        out_specs=whole(),
        out_shape=shaped(residual.shape, BF16),
        scratch_shapes=[pltpu.VMEM(residual.shape, F32)],
        compiler_params=params(),
        cost_estimate=cost(1.2e10, 1e7),
        name="combine",
    )(id_cols, gate_cols, home, residual)


def body(
    tokens,
    segments,
    live_mask,
    routes,
    priority,
    norm1_gain,
    norm1_bias,
    qkv_weight,
    qv_bias,
    out_weight,
    out_bias,
    norm2_gain,
    norm2_bias,
    router,
    up_weight,
    up_bias,
    down_weight,
    down_bias,
    cotangent,
):
    tok_count, model_width = tokens.shape
    seq_count, seqlen = segments.shape
    experts = lax.axis_size("exp")
    head_parts = lax.axis_size("head")
    head_index = lax.axis_index("head")
    quarter = model_width // head_parts
    tok_part = tok_count // head_parts
    capacity = (21 * tok_count + 10 * experts - 1) // (10 * experts)
    stride = round_up(capacity, 16)
    half = round_up(stride // 2, 16)
    local_width = qkv_weight.shape[2]

    def vector_rows(*vectors):
        rows = [v.astype(F32).reshape(1, -1) for v in vectors]
        rows.append(jnp.zeros((8 - len(rows), model_width), F32))
        return jnp.concatenate(rows, axis=0)

    norm_rows = vector_rows(norm1_gain, norm1_bias)
    vectors = vector_rows(out_bias, norm2_gain, norm2_bias)
    flat_qkv = qkv_weight.reshape(model_width, 3 * local_width)
    bias_row = jnp.concatenate(
        [qv_bias[0], jnp.zeros((local_width,), qv_bias.dtype), qv_bias[1]]
    ).astype(F32)[None]
    router_wide = jnp.pad(router, ((0, 0), (0, LANES - experts)))
    seg_rows = segments.reshape(seq_count, 1, seqlen)
    live_rows = live_mask.reshape(seq_count, 1, seqlen)
    seg_cols = segments.reshape(seq_count, seqlen, 1)
    down_bias_row = lax.dynamic_update_slice_in_dim(
        jnp.zeros((1, model_width), F32), down_bias.astype(F32), head_index * quarter, 1
    )
    up, down = up_weight[0], down_weight[0]
    up_bias_row = up_bias.astype(F32)

    out_full_weight = lax.all_gather(out_weight, "head", axis=0, tiled=True)
    first, qkv, context, packed, totals = attend(
        tokens, norm_rows, flat_qkv, bias_row, seg_cols, seg_rows, live_rows
    )
    gathered = lax.all_gather(packed, "head", axis=0)

    int_rows = jnp.concatenate(
        [
            routes.T,
            live_mask.reshape(1, tok_count),
            priority,
            jnp.zeros((4, tok_count), jnp.int32),
        ],
        axis=0,
    )
    ids, cot_slots = tables(
        priority.reshape(tok_count, 1), int_rows, cotangent, experts, capacity, stride, half, seqlen
    )
    id_cols = ids.T
    cot_moved = lax.all_to_all(cot_slots, "exp", split_axis=0, concat_axis=0, tiled=True)
    cot_rows = lax.all_gather(cot_moved, "head", axis=0)
    cot_own = lax.all_to_all(cotangent, "head", split_axis=0, concat_axis=1, tiled=True)

    residual, own_residual, own_second, gates, arrived, hidden, result, gate_col = forward(
        gathered, tokens, vectors, out_full_weight, router_wide, int_rows, ids,
        up, up_bias_row, down, down_bias_row, experts, stride, seq_count, head_parts,
    )
    sums, grad_up, grad_up_bias, grad_down, grad_down_bias = backward(
        arrived, hidden, result, cot_rows, gate_col, id_cols, up, up_bias_row, down, half, head_parts,
        seqlen,
    )
    own_sums = lax.psum_scatter(sums, "head", scatter_dimension=0, tiled=True)
    residual_grad, residual_half, router_grad, second_rows = middle(
        own_sums, own_residual, own_second, cot_own, router_wide, vectors, experts
    )
    grad_full = lax.all_gather(residual_half, "head", axis=0, tiled=True)

    home_out = lax.all_to_all(result, "exp", split_axis=0, concat_axis=0, tiled=True)
    block_sum = combine(id_cols, gates.T, home_out, residual, stride, 1.0 / head_parts, seqlen)
    block_out = lax.psum_scatter(block_sum, "head", scatter_dimension=1, tiled=True)

    first_grad, qkv_grad, bias_grad, out_grad = attend_back(
        grad_full, context, first, qkv, totals, flat_qkv, out_weight, seg_cols, seg_rows, live_rows
    )
    own_first = lax.psum_scatter(first_grad, "head", scatter_dimension=0, tiled=True)
    own_tokens = lax.dynamic_slice_in_dim(tokens, head_index * tok_part, tok_part, 0)
    own_grad, first_rows = last(own_first, own_tokens, residual_grad, norm_rows)
    grad_tokens = lax.all_gather(own_grad, "head", axis=0, tiled=True).astype(F32)

    small = lax.psum(
        jnp.concatenate([second_rows, first_rows, router_grad[:, :experts].T], axis=0),
        ("exp", "head"),
    )
    qkv_grad, bias_grad, out_grad = lax.psum((qkv_grad, bias_grad[0:1], out_grad), "exp")
    grad_qv_bias = jnp.concatenate(
        [bias_grad[:, :local_width], bias_grad[:, 2 * local_width :]], axis=0
    )
    return (
        block_out,
        grad_tokens,
        small[8],
        small[9],
        qkv_grad.reshape(model_width, 3, local_width),
        grad_qv_bias,
        out_grad,
        small[2],
        small[0],
        small[1],
        small[16 : 16 + experts].T,
        grad_up[None],
        grad_up_bias[0:1],
        grad_down[None],
        lax.dynamic_slice_in_dim(grad_down_bias[0:1], head_index * quarter, quarter, 1),
    )


def solution(mesh):
    in_specs = (
        P("exp", None),
        P("exp", None),
        P("exp", None),
        P("exp", None),
        P("exp", None),
        P(),
        P(),
        P(None, None, "head"),
        P(None, "head"),
        P("head", None),
        P(),
        P(),
        P(),
        P(),
        P("exp", None, "head"),
        P("exp", "head"),
        P("exp", "head", None),
        P("exp", "head"),
        P("exp", "head"),
    )
    out_specs = (
        P("exp", "head"),
        P("exp", None),
        P(),
        P(),
        P(None, None, "head"),
        P(None, "head"),
        P("head", None),
        P(),
        P(),
        P(),
        P(),
        P("exp", None, "head"),
        P("exp", "head"),
        P("exp", "head", None),
        P("exp", "head"),
    )
    return jax.shard_map(body, mesh=mesh, in_specs=in_specs, out_specs=out_specs, check_vma=False)
```

```python
from functools import partial
import math

import jax
import jax.numpy as jnp
from jax import lax
from jax.experimental import pallas as pl
from jax.experimental.pallas import tpu as pltpu
from jax.sharding import PartitionSpec as P

HEAD_DIM = 64
LANES = 128
EPSILON = 1e-06
NEGATIVE = -1e30
CONTRACT_FIRST = (((0,), (0,)), ((), ()))
CONTRACT_LAST = (((1,), (1,)), ((), ()))
F32 = jnp.float32
BF16 = jnp.bfloat16
MESH = pl.DeviceIdType.MESH
VMEM_LIMIT = 54 * 1024 * 1024


def round_up(number, step):
    return (number + step - 1) // step * step


def whole():
    return pl.BlockSpec(memory_space=pltpu.VMEM)


def anywhere():
    return pl.BlockSpec(memory_space=pl.ANY)


def shaped(shape, dtype):
    return jax.ShapeDtypeStruct(shape, dtype)


def params(**more):
    return pltpu.CompilerParams(vmem_limit_bytes=VMEM_LIMIT, **more)


def cost(flops, moved):
    return pl.CostEstimate(flops=int(flops), bytes_accessed=int(moved), transcendentals=0)


def dot(left, right):
    return jnp.dot(left, right, preferred_element_type=F32)


def dot_last(left, right):
    return lax.dot_general(left, right, CONTRACT_LAST, preferred_element_type=F32)


def dot_first(left, right):
    return lax.dot_general(left, right, CONTRACT_FIRST, preferred_element_type=F32)


def standard(values):
    centred = values - jnp.mean(values, axis=-1, keepdims=True)
    scale = lax.rsqrt(jnp.mean(centred * centred, axis=-1, keepdims=True) + EPSILON)
    return centred * scale, scale


def norm_back(grad_rows, gain_row, normal, scale):
    inner = grad_rows * gain_row
    return scale * (
        inner
        - jnp.mean(inner, axis=-1, keepdims=True)
        - normal * jnp.mean(inner * normal, axis=-1, keepdims=True)
    )


def mask_penalty(seg_col, seg_row, live_row):
    shape = (seg_col.shape[0], seg_row.shape[1])
    diagonal = lax.broadcasted_iota(jnp.int32, shape, 0) == lax.broadcasted_iota(
        jnp.int32, shape, 1
    )
    allowed = (seg_col == seg_row) & ((live_row > 0) | diagonal)
    return jnp.where(allowed, 0.0, NEGATIVE)


def pack_rows(rows, half):
    count = rows.shape[0]
    third = rows[:, LANES:]
    return rows[:, :LANES], jnp.concatenate([third[:half], third[count - half :]], axis=1)


def unpack_rows(parts_of, into, head_parts, count, half):
    extra = HEAD_DIM
    width = LANES + extra
    for z in range(head_parts):
        packed = parts_of(z)
        into[:, z * width : z * width + LANES] = packed[:count]
        tail = packed[count : count + half]
        into[:half, z * width + LANES : (z + 1) * width] = tail[:, :extra]
        into[half:, z * width + LANES : (z + 1) * width] = tail[2 * half - count :, extra:]


def attend_kernel(
    tokens_ref, norm_ref, weight_ref, bias_ref, segc_ref, segr_ref, live_ref,
    first_ref, qkv_ref, context_ref, packed_ref, total_ref,
):
    normal, ignored = standard(tokens_ref[...].astype(F32))
    first = (normal * norm_ref[0:1] + norm_ref[1:2]).astype(BF16)
    first_ref[...] = first
    rows = (dot(first, weight_ref[...]) + bias_ref[...]).astype(BF16)
    qkv_ref[...] = rows
    penalty = mask_penalty(segc_ref[0], segr_ref[0], live_ref[0])
    seqlen = rows.shape[0]
    width = rows.shape[1] // 3
    parts = []
    for head in range(width // HEAD_DIM):
        lo = head * HEAD_DIM
        hi = lo + HEAD_DIM
        query = rows[:, lo:hi] * BF16(1.0 / math.sqrt(HEAD_DIM))
        scores = dot_last(query, rows[:, width + lo : width + hi]) + penalty
        largest = jnp.max(scores, axis=-1, keepdims=True)
        weights = jnp.exp(scores - largest)
        total = jnp.sum(weights, axis=-1, keepdims=True)
        values = rows[:, 2 * width + lo : 2 * width + hi]
        parts.append((dot(weights.astype(BF16), values) / total).astype(BF16))
        total_ref[:, head : head + 1] = largest + jnp.log(total)
    context = jnp.concatenate(parts, axis=1)
    context_ref[...] = context
    wide, tail = pack_rows(context, seqlen // 2)
    packed_ref[0, :seqlen] = wide
    packed_ref[0, seqlen:] = tail


def attend(tokens, norm_rows, flat_qkv, bias_row, seg_cols, seg_rows, live_rows):
    tok_count, model_width = tokens.shape
    seq_count, seqlen = seg_rows.shape[0], seg_rows.shape[2]
    wide = flat_qkv.shape[1]
    width = wide // 3
    step = lambda i: (i, 0)
    fixed = lambda i: (0, 0)
    deep = lambda i: (i, 0, 0)
    return pl.pallas_call(
        attend_kernel,
        grid=(seq_count,),
        in_specs=[
            pl.BlockSpec((seqlen, model_width), step),
            pl.BlockSpec((8, model_width), fixed),
            pl.BlockSpec((model_width, wide), fixed),
            pl.BlockSpec((1, wide), fixed),
            pl.BlockSpec((1, seqlen, 1), deep),
            pl.BlockSpec((1, 1, seqlen), deep),
            pl.BlockSpec((1, 1, seqlen), deep),
        ],
        out_specs=[
            pl.BlockSpec((seqlen, model_width), step),
            pl.BlockSpec((seqlen, wide), step),
            pl.BlockSpec((seqlen, width), step),
            pl.BlockSpec((1, seqlen + seqlen // 2, LANES), deep),
            pl.BlockSpec((seqlen, LANES), step),
        ],
        out_shape=[
            shaped((tok_count, model_width), BF16),
            shaped((tok_count, wide), BF16),
            shaped((tok_count, width), BF16),
            shaped((seq_count, seqlen + seqlen // 2, LANES), BF16),
            shaped((tok_count, LANES), F32),
        ],
        compiler_params=params(),
        cost_estimate=cost(4e9, 1e7),
        name="attend",
    )(tokens, norm_rows, flat_qkv, bias_row, seg_cols, seg_rows, live_rows)


def table_kernel(experts, capacity, stride, half, chunk, prio_ref, rows_ref, cot_ref, ids_ref, out_ref):
    tok_count = rows_ref.shape[1]
    numbers = lax.broadcasted_iota(jnp.int32, (experts, 1), 0)

    def hot(rows):
        live = rows[2:3] > 0
        first = jnp.where((rows[0:1] == numbers) & live, 1.0, 0.0)
        second = jnp.where((rows[1:2] == numbers) & live, 1.0, 0.0)
        return first, second

    rank_row = rows_ref[3:4]
    counts = jnp.zeros((2 * experts, tok_count), F32)
    for start in range(0, tok_count, chunk):
        first, second = hot(rows_ref[:, start : start + chunk])
        earlier = jnp.where(prio_ref[start : start + chunk] < rank_row, 1.0, 0.0).astype(BF16)
        counts = counts + dot(jnp.concatenate([first, second], axis=0).astype(BF16), earlier)
    first, second = hot(rows_ref[...])
    total = jnp.sum(first, axis=1, keepdims=True)
    places = [
        jnp.sum(first * counts[:experts], axis=0, keepdims=True),
        jnp.sum(second * (counts[experts:] + total), axis=0, keepdims=True),
    ]
    ids = []
    for pick in range(2):
        place = places[pick].astype(jnp.int32)
        kept = (place < capacity) & (rows_ref[2:3] > 0)
        ids.append(jnp.where(kept, rows_ref[pick : pick + 1] * stride + place, -1))
        ids_ref[pick : pick + 1] = ids[pick]
    ids_ref[2:8] = jnp.full((6, tok_count), -1, jnp.int32)

    def one(expert, carry):
        slots = expert * stride + lax.broadcasted_iota(jnp.int32, (stride, 1), 0)
        hit = (ids_ref[0:1] == slots) | (ids_ref[1:2] == slots)
        block = dot(jnp.where(hit, 1.0, 0.0).astype(BF16), cot_ref[...]).astype(BF16)
        wide, tail = pack_rows(block, half)
        out_ref[expert, :stride] = wide
        out_ref[expert, stride:] = tail
        return carry

    lax.fori_loop(0, experts, one, 0)


def tables(prio_col, rows, cotangent, experts, capacity, stride, half, chunk):
    tok_count = rows.shape[1]
    return pl.pallas_call(
        partial(table_kernel, experts, capacity, stride, half, chunk),
        in_specs=[whole()] * 3,
        out_specs=[whole()] * 2,
        out_shape=[
            shaped((8, tok_count), jnp.int32),
            shaped((experts, stride + half, LANES), BF16),
        ],
        compiler_params=params(),
        cost_estimate=cost(1e10, 1e7),
        name="tables",
    )(prio_col, rows, cotangent)


def gelu_parts(pre):
    root = math.sqrt(2.0 / math.pi)
    square = pre * pre
    wave = jnp.tanh(root * (pre + 0.044715 * pre * square))
    half_sum = 0.5 * (1.0 + wave)
    slope = half_sum + 0.5 * pre * (1.0 - wave * wave) * (
        root * (1.0 + 3.0 * 0.044715 * square)
    )
    return pre * half_sum, slope


def greet(peers):
    barrier = pltpu.get_barrier_semaphore()
    me = lax.axis_index("exp")
    here = lax.axis_index("head")

    def call(step, carry):
        other = lax.rem(me + step, peers)
        pl.semaphore_signal(barrier, inc=1, device_id=(other, here), device_id_type=MESH)
        return carry

    lax.fori_loop(1, peers, call, 0)
    return barrier


def forward_kernel(
    experts, stride, half, seq_count, head_parts,
    gathered_ref, tokens_ref, vectors_ref, out_weight_ref, router_ref, rows_ref, ids_ref,
    up_ref, up_bias_ref, down_ref, down_bias_ref,
    own_residual_ref, own_second_ref, own_columns_ref, gates_ref, arrived_ref, hidden_ref, result_ref,
    gate_col_ref, residual_ref, context_scr, second_scr, logit_scr, send_scr, gate_send, gate_recv,
    send_sem, recv_sem, gate_send_sem, gate_recv_sem,
):
    me = lax.axis_index("exp")
    here = lax.axis_index("head")
    barrier = greet(experts)
    tok_count = tokens_ref.shape[0]
    seqlen = tok_count // seq_count
    for seq in range(seq_count):
        span = slice(seq * seqlen, (seq + 1) * seqlen)
        unpack_rows(lambda z: gathered_ref[z, seq], context_scr, head_parts, seqlen, seqlen // 2)
        residual = (
            tokens_ref[span].astype(F32)
            + dot(context_scr[...], out_weight_ref[...])
            + vectors_ref[0:1]
        )
        residual_ref[span] = residual
        normal, ignored = standard(residual)
        second = (normal * vectors_ref[1:2] + vectors_ref[2:3]).astype(BF16)
        second_scr[span] = second
        logit_scr[:, span] = dot(second, router_ref[...]).T[:experts]
    part = seqlen // head_parts
    for seq in range(seq_count):
        own = pl.ds(pl.multiple_of(seq * seqlen + here * part, part), part)
        own_residual_ref[seq] = residual_ref[own]
        own_second_ref[seq] = second_scr[own]
    width = residual_ref.shape[1] // head_parts
    for z in range(head_parts):

        @pl.when(here == z)
        def columns():
            own_columns_ref[...] = residual_ref[:, z * width : (z + 1) * width]


    logits = logit_scr[...]
    powers = jnp.exp(logits - jnp.max(logits, axis=0, keepdims=True))
    chances = powers / jnp.sum(powers, axis=0, keepdims=True)
    numbers = lax.broadcasted_iota(jnp.int32, (experts, 1), 0)
    for pick in range(2):
        chosen = jnp.where(rows_ref[pick : pick + 1] == numbers, chances, 0.0)
        gate = jnp.where(ids_ref[pick : pick + 1] >= 0, jnp.sum(chosen, axis=0, keepdims=True), 0.0)
        gates_ref[pick : pick + 1] = gate
    gates_ref[2:8] = jnp.zeros((6, tok_count), F32)
    pl.semaphore_wait(barrier, experts - 1)

    def copies(target, step):
        to = dict(device_id=(target, here), device_id_type=MESH)
        return (
            pltpu.make_async_remote_copy(
                src_ref=send_scr.at[step],
                dst_ref=arrived_ref.at[me],
                send_sem=send_sem.at[step],
                recv_sem=recv_sem.at[step],
                **to,
            ),
            pltpu.make_async_remote_copy(
                src_ref=gate_send.at[step],
                dst_ref=gate_recv.at[me],
                send_sem=gate_send_sem.at[step],
                recv_sem=gate_recv_sem.at[step],
                **to,
            ),
        )

    def fill(target):
        slots = target * stride + lax.broadcasted_iota(jnp.int32, (stride, 1), 0)
        first = ids_ref[0:1] == slots
        second = ids_ref[1:2] == slots
        block = dot(jnp.where(first | second, 1.0, 0.0).astype(BF16), second_scr[...]).astype(BF16)
        gate = jnp.sum(
            jnp.where(first, gates_ref[0:1], jnp.where(second, gates_ref[1:2], 0.0)),
            axis=1,
            keepdims=True,
        )
        return block, jnp.broadcast_to(gate, (stride, LANES)).T[:8]

    def send(step, carry):
        target = lax.rem(me + step, experts)
        block, gate = fill(target)
        send_scr[step] = block
        gate_send[step] = gate
        for copy in copies(target, step):
            copy.start()
        return carry

    lax.fori_loop(1, experts, send, 0)
    block, gate = fill(me)
    arrived_ref[me] = block
    gate_recv[me] = gate

    def work(source):
        pre = dot(arrived_ref[source], up_ref[...]) + up_bias_ref[...]
        hidden = gelu_parts(pre)[0].astype(BF16)
        hidden_ref[source] = hidden
        result = (dot(hidden, down_ref[...]) + down_bias_ref[...]).astype(BF16)
        for z in range(head_parts):
            wide, tail = pack_rows(result[:, z * width : (z + 1) * width], half)
            result_ref[z, source, :stride] = wide
            result_ref[z, source, stride:] = tail

    work(me)

    def receive(step, carry):
        source = lax.rem(me + experts - step, experts)
        wide, narrow = copies(source, step)
        wide.wait_recv()
        narrow.wait_recv()
        work(source)
        return carry

    lax.fori_loop(1, experts, receive, 0)

    def finish(step, carry):
        for copy in copies(lax.rem(me + step, experts), step):
            copy.wait_send()
        return carry

    lax.fori_loop(1, experts, finish, 0)
    lane = lax.broadcasted_iota(jnp.int32, (LANES, stride), 0)
    square = jnp.zeros((LANES, stride), F32)
    for source in range(experts):
        square = jnp.where(lane == source, gate_recv[source, 0:1], square)
    gate_col_ref[...] = square.T


def forward(
    gathered, tokens, vectors, out_weight, router, rows, ids, up, up_bias, down, down_bias,
    experts, stride, half, seq_count, head_parts,
):
    tok_count, model_width = tokens.shape
    seqlen = tok_count // seq_count
    part = seqlen // head_parts
    return pl.pallas_call(
        partial(forward_kernel, experts, stride, half, seq_count, head_parts),
        in_specs=[whole()] * 11,
        out_specs=[whole()] * 8,
        out_shape=[
            shaped((seq_count, part, model_width), F32),
            shaped((seq_count, part, model_width), BF16),
            shaped((tok_count, model_width // head_parts), F32),
            shaped((8, tok_count), F32),
            shaped((experts, stride, model_width), BF16),
            shaped((experts, stride, up.shape[1]), BF16),
            shaped((head_parts, experts, stride + half, LANES), BF16),
            shaped((stride, LANES), F32),
        ],
        scratch_shapes=[
            pltpu.VMEM((tok_count, model_width), F32),
            pltpu.VMEM((seqlen, model_width), BF16),
            pltpu.VMEM((tok_count, model_width), BF16),
            pltpu.VMEM((experts, tok_count), F32),
            pltpu.VMEM((experts, stride, model_width), BF16),
            pltpu.VMEM((experts, 8, stride), F32),
            pltpu.VMEM((experts, 8, stride), F32),
            pltpu.SemaphoreType.DMA((experts,)),
            pltpu.SemaphoreType.DMA((experts,)),
            pltpu.SemaphoreType.DMA((experts,)),
            pltpu.SemaphoreType.DMA((experts,)),
        ],
        compiler_params=params(collective_id=0, has_side_effects=True),
        cost_estimate=cost(8e10, 1e8),
        name="forward",
    )(gathered, tokens, vectors, out_weight, router, rows, ids, up, up_bias, down, down_bias)


def backward_kernel(
    experts, stride, half, head_parts, chunk,
    arrived_hbm, hidden_hbm, result_hbm, cot_hbm, gate_col_ref, ids_ref, up_ref, up_bias_ref, down_ref,
    sums_ref, grad_up_ref, grad_up_bias_ref, grad_down_ref, grad_down_bias_ref,
    rows_scr, result_scr, cot_scr, cot_wide, result_wide, hidden_scr, pre_grad_scr, out_grad_scr,
    send_scr, recv_scr, gate_send, gate_recv, total_scr,
    load_sem, send_sem, recv_sem, gate_send_sem, gate_recv_sem,
):
    me = lax.axis_index("exp")
    here = lax.axis_index("head")
    barrier = greet(experts)
    tok_count = ids_ref.shape[0]
    model_width = up_ref.shape[0]

    def loads(step):
        home = lax.rem(me + step, experts)
        slot = lax.rem(step, 2)
        return (
            pltpu.make_async_copy(arrived_hbm.at[home], rows_scr.at[slot], load_sem.at[slot, 0]),
            pltpu.make_async_copy(result_hbm.at[:, home], result_scr.at[slot], load_sem.at[slot, 1]),
            pltpu.make_async_copy(cot_hbm.at[:, home], cot_scr.at[slot], load_sem.at[slot, 2]),
        )

    def copies(target, step):
        to = dict(device_id=(target, here), device_id_type=MESH)
        return (
            pltpu.make_async_remote_copy(
                src_ref=send_scr.at[step],
                dst_ref=recv_scr.at[me],
                send_sem=send_sem.at[step],
                recv_sem=recv_sem.at[step],
                **to,
            ),
            pltpu.make_async_remote_copy(
                src_ref=gate_send.at[step],
                dst_ref=gate_recv.at[me],
                send_sem=gate_send_sem.at[step],
                recv_sem=gate_recv_sem.at[step],
                **to,
            ),
        )

    for copy in loads(1):
        copy.start()
    grad_up_ref[...] = jnp.zeros_like(grad_up_ref)
    grad_down_ref[...] = jnp.zeros_like(grad_down_ref)
    grad_up_bias_ref[...] = jnp.zeros_like(grad_up_bias_ref)
    grad_down_bias_ref[...] = jnp.zeros_like(grad_down_bias_ref)
    total_scr[...] = jnp.zeros_like(total_scr)
    pl.semaphore_wait(barrier, experts - 1)

    def work(step):
        home = lax.rem(me + step, experts)
        slot = lax.rem(step, 2)
        for copy in loads(step):
            copy.wait()
        unpack_rows(lambda z: cot_scr[slot, z], cot_wide, head_parts, stride, half)
        unpack_rows(lambda z: result_scr[slot, z], result_wide, head_parts, stride, half)
        out_rows = cot_wide[...].astype(F32)
        pre = dot(rows_scr[slot], up_ref[...]) + up_bias_ref[...]
        slope = gelu_parts(pre)[1]
        lane = lax.broadcasted_iota(jnp.int32, (stride, LANES), 1)
        gate = jnp.sum(jnp.where(lane == home, gate_col_ref[...], 0.0), axis=1, keepdims=True)
        out_grad = (gate * out_rows).astype(BF16)
        out_grad_scr[step] = out_grad
        grad_down_bias_ref[0:1] += jnp.sum(out_grad.astype(F32), axis=0, keepdims=True)
        pre_grad = (dot_last(out_grad, down_ref[...]) * slope).astype(BF16)
        pre_grad_scr[step] = pre_grad
        grad_up_bias_ref[0:1] += jnp.sum(pre_grad.astype(F32), axis=0, keepdims=True)
        gate_grad = jnp.sum(result_wide[...].astype(F32) * out_rows, axis=1, keepdims=True)
        return (
            dot_last(pre_grad, up_ref[...]).astype(BF16),
            jnp.broadcast_to(gate_grad, (stride, LANES)).T[:8],
        )

    def send(step, carry):
        for copy in loads(lax.rem(step + 1, experts)):
            copy.start()
        block, gate = work(step)
        send_scr[step] = block
        gate_send[step] = gate
        for copy in copies(lax.rem(me + step, experts), step):
            copy.start()
        return carry

    lax.fori_loop(1, experts, send, 0)
    block, gate = work(0)
    recv_scr[me] = block
    gate_recv[me] = gate

    def row_loads(step):
        home = lax.rem(me + step, experts)
        slot = lax.rem(step, 2)
        return (
            pltpu.make_async_copy(arrived_hbm.at[home], rows_scr.at[slot], load_sem.at[slot, 0]),
            pltpu.make_async_copy(hidden_hbm.at[home], hidden_scr.at[slot], load_sem.at[slot, 1]),
        )

    def weigh(step):
        slot = lax.rem(step, 2)
        for copy in row_loads(step):
            copy.wait()
        grad_up_ref[...] += dot_first(rows_scr[slot], pre_grad_scr[step])
        grad_down_ref[...] += dot_first(hidden_scr[slot], out_grad_scr[step])

    def weigh_some(step, carry):
        for copy in row_loads(step + 1):
            copy.start()
        weigh(step)
        return carry

    for copy in row_loads(0):
        copy.start()
    lax.fori_loop(0, experts - 1, weigh_some, 0)
    weigh(experts - 1)

    def gather(source):
        slots = source * stride + lax.broadcasted_iota(jnp.int32, (1, stride), 1)
        lane = lax.broadcasted_iota(jnp.int32, (chunk, LANES), 1)

        def part(index, carry):
            span = pl.ds(pl.multiple_of(index * chunk, chunk), chunk)
            hit = (ids_ref[span, 0:1] == slots) | (ids_ref[span, 1:2] == slots)
            total_scr[span, :model_width] += dot(
                jnp.where(hit, 1.0, 0.0).astype(BF16), recv_scr[source]
            )
            gate = jnp.sum(jnp.where(hit, gate_recv[source, 0:1], 0.0), axis=1, keepdims=True)
            total_scr[span, model_width:] = jnp.where(
                lane == source, gate, total_scr[span, model_width:]
            )
            return carry

        lax.fori_loop(0, tok_count // chunk, part, 0)

    gather(me)

    def receive(step, carry):
        source = lax.rem(me + experts - step, experts)
        for copy in copies(source, step):
            copy.wait_recv()
        gather(source)
        return carry

    lax.fori_loop(1, experts, receive, 0)
    sums_ref[...] = total_scr[...].astype(BF16)

    def finish(step, carry):
        for copy in copies(lax.rem(me + step, experts), step):
            copy.wait_send()
        return carry

    lax.fori_loop(1, experts, finish, 0)


def backward(
    arrived, hidden, result, cot_rows, gate_col, id_cols, up, up_bias, down, half, head_parts, chunk
):
    tok_count = id_cols.shape[0]
    experts, stride, model_width = arrived.shape
    inner = up.shape[1]
    rows = (experts, stride, model_width)
    return pl.pallas_call(
        partial(backward_kernel, experts, stride, half, head_parts, chunk),
        in_specs=[anywhere()] * 4 + [whole()] * 5,
        out_specs=[whole()] * 5,
        out_shape=[
            shaped((tok_count, model_width + LANES), BF16),
            shaped((model_width, inner), F32),
            shaped((8, inner), F32),
            shaped((inner, model_width), F32),
            shaped((8, model_width), F32),
        ],
        scratch_shapes=[
            pltpu.VMEM((2, stride, model_width), BF16),
            pltpu.VMEM((2, head_parts, stride + half, LANES), BF16),
            pltpu.VMEM((2, head_parts, stride + half, LANES), BF16),
            pltpu.VMEM((stride, model_width), BF16),
            pltpu.VMEM((stride, model_width), BF16),
            pltpu.VMEM((2, stride, inner), BF16),
            pltpu.VMEM((experts, stride, inner), BF16),
            pltpu.VMEM(rows, BF16),
            pltpu.VMEM(rows, BF16),
            pltpu.VMEM(rows, BF16),
            pltpu.VMEM((experts, 8, stride), F32),
            pltpu.VMEM((experts, 8, stride), F32),
            pltpu.VMEM((tok_count, model_width + LANES), F32),
            pltpu.SemaphoreType.DMA((2, 3)),
            pltpu.SemaphoreType.DMA((experts,)),
            pltpu.SemaphoreType.DMA((experts,)),
            pltpu.SemaphoreType.DMA((experts,)),
            pltpu.SemaphoreType.DMA((experts,)),
        ],
        compiler_params=params(collective_id=1, has_side_effects=True),
        cost_estimate=cost(8e10, 1e8),
        name="backward",
    )(arrived, hidden, result, cot_rows, gate_col, id_cols, up, up_bias, down)


def tail_kernel(
    experts, stride, half, seq_count, head_parts,
    sums_ref, id_cols_ref, gate_cols_ref, own_residual_ref, own_second_ref, cot_own_ref,
    own_columns_hbm, router_ref, vectors_ref, own_tokens_ref, norm_ref, result_ref,
    context_hbm, first_hbm, qkv_hbm, totals_hbm, weight_ref, out_weight_ref,
    segc_ref, segr_ref, live_ref,
    tokens_hbm, block_ref, qkv_sum_ref, out_sum_ref, bias_sum_ref, small_ref,
    columns_scr, part_two, down_one, up_one, down_two, up_two, own_scr,
    full_one, full_two, grad_scr,
    context_scr, first_scr, qkv_scr, totals_scr, back_scr, penalty_scr, joined_scr,
    qkv_grad, out_grad, bias_grad, rows_acc, router_acc,
    result_home, result_wide,
    qkv_send, qkv_recv, qkv_all, out_send, out_recv, out_all, bias_recv, small_head, small_recv,
    columns_sem, load_sem, stage_sem, result_send_sem, result_recv_sem,
    down_one_sem, up_one_sem, down_two_sem, up_two_sem, down_one_out, up_one_out, down_two_out, up_two_out,
    full_one_sem, full_two_sem, full_one_out, full_two_out,
    sum_send_sem, sum_recv_sem, all_send_sem, all_recv_sem,
    bias_send_sem, bias_recv_sem, head_send_sem, head_recv_sem, small_send_sem, small_recv_sem,
):
    me = lax.axis_index("exp")
    here = lax.axis_index("head")
    ends = head_parts - 1
    seqlen = segr_ref.shape[2]
    part = seqlen // head_parts
    model_width = vectors_ref.shape[1]
    width = out_weight_ref.shape[0]
    factor = 1.0 / math.sqrt(HEAD_DIM)

    barrier = greet(experts)

    def call(step, carry):
        other = lax.rem(here + step, head_parts)
        pl.semaphore_signal(barrier, inc=1, device_id=(me, other), device_id_type=MESH)
        return carry

    lax.fori_loop(1, head_parts, call, 0)

    def chunk_loads(seq):
        span = pl.ds(pl.multiple_of(seq * seqlen, seqlen), seqlen)
        return (
            pltpu.make_async_copy(context_hbm.at[span], context_scr, load_sem.at[0]),
            pltpu.make_async_copy(first_hbm.at[span], first_scr, load_sem.at[1]),
            pltpu.make_async_copy(qkv_hbm.at[span], qkv_scr, load_sem.at[2]),
            pltpu.make_async_copy(totals_hbm.at[span], totals_scr, load_sem.at[3]),
        )

    for copy in chunk_loads(0):
        copy.start()
    qkv_grad[...] = jnp.zeros_like(qkv_grad)
    out_grad[...] = jnp.zeros_like(out_grad)
    bias_grad[...] = jnp.zeros_like(bias_grad)
    rows_acc[...] = jnp.zeros_like(rows_acc)
    router_acc[...] = jnp.zeros_like(router_acc)
    pl.semaphore_wait(barrier, experts - 1 + ends)

    def to_exp(target):
        return dict(device_id=(target, here), device_id_type=MESH)

    def to_head(target):
        return dict(device_id=(me, target), device_id_type=MESH)

    def each_peer(action):
        def one(step, carry):
            action(step, lax.rem(me + step, experts), lax.rem(me + experts - step, experts))
            return carry

        lax.fori_loop(1, experts, one, 0)

    def result_copy(step, target):
        return pltpu.make_async_remote_copy(
            src_ref=result_ref.at[target],
            dst_ref=result_home.at[me],
            send_sem=result_send_sem.at[step],
            recv_sem=result_recv_sem.at[step],
            **to_exp(target),
        )

    each_peer(lambda step, target, source: result_copy(step, target).start())
    result_home[me] = result_ref[me]

    def down_copy(buffer, sems, outs, seq, shard):
        return pltpu.make_async_remote_copy(
            src_ref=buffer.at[seq, shard],
            dst_ref=buffer.at[seq, shard],
            send_sem=outs.at[seq, shard],
            recv_sem=sems.at[seq, shard],
            **to_head(here - 1),
        )

    def up_copy(buffer, sems, outs, seq, shard):
        return pltpu.make_async_remote_copy(
            src_ref=buffer.at[seq, shard - 1],
            dst_ref=buffer.at[seq, shard - 1],
            send_sem=outs.at[seq, shard - 1],
            recv_sem=sems.at[seq, shard - 1],
            **to_head(here + 1),
        )

    one_down = (down_one, down_one_sem, down_one_out)
    one_up = (up_one, up_one_sem, up_one_out)
    two_down = (down_two, down_two_sem, down_two_out)
    two_up = (up_two, up_two_sem, up_two_out)

    def reduce_hop(partial_ref, base, down, up, seq, hop):
        low = hop - ends + here
        high = ends - hop + here

        @pl.when((low >= 0) & (low < here))
        def downward():
            rows = partial_ref[pl.ds(pl.multiple_of(base + low * part, part), part)]

            @pl.when(here < ends)
            def add():
                down_copy(*down, seq, low).wait_recv()
                down[0][seq, low] = (down[0][seq, low].astype(F32) + rows.astype(F32)).astype(BF16)

            @pl.when(here == ends)
            def begin():
                down[0][seq, low] = rows

            down_copy(*down, seq, low).start()

        @pl.when((high > here) & (high <= ends))
        def upward():
            rows = partial_ref[pl.ds(pl.multiple_of(base + high * part, part), part)]

            @pl.when(here > 0)
            def add():
                up_copy(*up, seq, high).wait_recv()
                up[0][seq, high - 1] = (
                    up[0][seq, high - 1].astype(F32) + rows.astype(F32)
                ).astype(BF16)

            @pl.when(here == 0)
            def begin():
                up[0][seq, high - 1] = rows

            up_copy(*up, seq, high).start()

    def reduce_end(partial_ref, base, down, up, seq, columns):
        own = pl.ds(pl.multiple_of(base + here * part, part), part)
        own_scr[:, :columns] = partial_ref[own].astype(F32)

        @pl.when(here < ends)
        def below():
            down_copy(*down, seq, here).wait_recv()
            own_scr[:, :columns] += down[0][seq, here].astype(F32)

        @pl.when(here > 0)
        def above():
            up_copy(*up, seq, here).wait_recv()
            own_scr[:, :columns] += up[0][seq, here - 1].astype(F32)

    def reduce_drain(down, up, seq):
        for shard in range(ends):

            @pl.when(shard < here)
            def downward():
                down_copy(*down, seq, shard).wait_send()

            @pl.when(shard + 1 > here)
            def upward():
                up_copy(*up, seq, shard + 1).wait_send()

    def full_copy(buffer, sems, outs, seq, shard, side):
        rows = pl.ds(pl.multiple_of(shard * part, part), part)
        return pltpu.make_async_remote_copy(
            src_ref=buffer.at[seq, rows],
            dst_ref=buffer.at[seq, rows],
            send_sem=outs.at[seq, shard, side],
            recv_sem=sems.at[seq, shard],
            **to_head(here + 1 - 2 * side),
        )

    one_full = (full_one, full_one_sem, full_one_out)
    two_full = (full_two, full_two_sem, full_two_out)

    def spread_hop(full, seq, hop):
        for side in range(2):
            shard = here - hop if side == 0 else here + hop
            there = shard >= 0 if side == 0 else shard <= ends
            onward = here < ends if side == 0 else here > 0

            @pl.when(there)
            def arrived():
                if hop > 0:
                    full_copy(*full, seq, shard, side).wait_recv()
                if hop < ends:

                    @pl.when(onward)
                    def pass_on():
                        full_copy(*full, seq, shard, side).start()

    def spread_drain(full, seq):
        for hop in range(ends):
            for side in range(2):
                shard = here - hop if side == 0 else here + hop
                there = shard >= 0 if side == 0 else shard <= ends
                onward = here < ends if side == 0 else here > 0

                @pl.when(there & onward)
                def sent():
                    full_copy(*full, seq, shard, side).wait_send()

    def middle(seq):
        second = own_second_ref[seq]
        lane = lax.broadcasted_iota(jnp.int32, (part, LANES), 1)
        logits = jnp.where(lane < experts, dot(second, router_ref[...]), NEGATIVE)
        powers = jnp.exp(logits - jnp.max(logits, axis=1, keepdims=True))
        chances = powers / jnp.sum(powers, axis=1, keepdims=True)
        route_grad = own_scr[:, model_width:]
        logit_grad = (
            chances * (route_grad - jnp.sum(chances * route_grad, axis=1, keepdims=True))
        ).astype(BF16)
        router_acc[...] += dot_first(second, logit_grad)
        grad = own_scr[:, :model_width] + dot_last(logit_grad, router_ref[...])
        normal, scale = standard(own_residual_ref[seq])
        rows_acc[0:1] += jnp.sum(grad * normal, axis=0, keepdims=True)
        rows_acc[1:2] += jnp.sum(grad, axis=0, keepdims=True)
        total = cot_own_ref[seq].astype(F32) + norm_back(grad, vectors_ref[1:2], normal, scale)
        rows_acc[2:3] += jnp.sum(total, axis=0, keepdims=True)
        grad_scr[seq] = total
        full_one[seq, pl.ds(pl.multiple_of(here * part, part), part)] = total.astype(BF16)

    def attend_start(seq):
        for copy in chunk_loads(seq):
            copy.wait()
        grad = full_one[seq]
        back_scr[...] = dot_last(grad, out_weight_ref[...]).astype(BF16)
        out_grad[...] += dot_first(context_scr[...], grad)
        penalty_scr[...] = mask_penalty(segc_ref[seq], segr_ref[seq], live_ref[seq]).astype(BF16)

    def attend_head(head):
        lo = head * HEAD_DIM
        hi = lo + HEAD_DIM
        query = qkv_scr[:, lo:hi] * BF16(factor)
        keys = qkv_scr[:, width + lo : width + hi]
        values = qkv_scr[:, 2 * width + lo : 2 * width + hi]
        back = back_scr[:, lo:hi]
        weights = jnp.exp(
            dot_last(query, keys) + penalty_scr[...].astype(F32) - totals_scr[:, head : head + 1]
        )
        joined_scr[:, 2 * width + lo : 2 * width + hi] = dot_first(
            weights.astype(BF16), back
        ).astype(BF16)
        inner = jnp.sum(
            back.astype(F32) * context_scr[:, lo:hi].astype(F32), axis=-1, keepdims=True
        )
        score_grad = (weights * (dot_last(back, values) - inner)).astype(BF16)
        joined_scr[:, lo:hi] = (dot(score_grad, keys) * factor).astype(BF16)
        joined_scr[:, width + lo : width + hi] = dot_first(score_grad, query).astype(BF16)

    def attend_end(seq):
        joined = joined_scr[...]
        part_two[...] = dot_last(joined, weight_ref[...]).astype(BF16)
        qkv_grad[...] += dot_first(first_scr[...], joined)
        bias_grad[0:1] += jnp.sum(joined.astype(F32), axis=0, keepdims=True)

        @pl.when(seq + 1 < seq_count)
        def more():
            for copy in chunk_loads(seq + 1):
                copy.start()

    def last(seq):
        grad = own_scr[:, :model_width]
        normal, scale = standard(own_tokens_ref[seq].astype(F32))
        rows_acc[3:4] += jnp.sum(grad * normal, axis=0, keepdims=True)
        rows_acc[4:5] += jnp.sum(grad, axis=0, keepdims=True)
        total = grad_scr[seq] + norm_back(grad, norm_ref[0:1], normal, scale)
        full_two[seq, pl.ds(pl.multiple_of(here * part, part), part)] = total.astype(BF16)

    def stage_copy(seq):
        span = pl.ds(pl.multiple_of(seq * seqlen, seqlen), seqlen)
        return pltpu.make_async_copy(full_two.at[seq], tokens_hbm.at[span], stage_sem.at[seq])

    def open_results():
        each_peer(lambda step, target, source: result_copy(step, target).wait_recv())

        def one(expert, carry):
            packed = result_home[expert]
            result_wide[expert, :, :LANES] = packed[:stride]
            tail = packed[stride:]
            result_wide[expert, :half, LANES:] = tail[:, :HEAD_DIM]
            result_wide[expert, half:, LANES:] = tail[2 * half - stride :, HEAD_DIM:]
            return carry

        lax.fori_loop(0, experts, one, 0)

    def combine(seq):
        span = pl.ds(pl.multiple_of(seq * seqlen, seqlen), seqlen)
        first = id_cols_ref[span, 0:1]
        second = id_cols_ref[span, 1:2]
        pltpu.make_async_copy(own_columns_hbm.at[span], columns_scr, columns_sem.at[0]).start()
        pltpu.make_async_copy(own_columns_hbm.at[span], columns_scr, columns_sem.at[0]).wait()
        first_gate = gate_cols_ref[span, 0:1]
        second_gate = gate_cols_ref[span, 1:2]

        def one(expert, total):
            slots = expert * stride + lax.broadcasted_iota(jnp.int32, (1, stride), 1)
            weights = jnp.where(
                first == slots, first_gate, jnp.where(second == slots, second_gate, 0.0)
            )
            return total + dot(weights.astype(BF16), result_wide[expert])

        block_ref[span] = lax.fori_loop(0, experts, one, columns_scr[...]).astype(BF16)

    qkv_rows = qkv_grad.shape[0] // experts
    out_rows = out_grad.shape[0] // experts

    def sum_copies(step, target):
        return (
            pltpu.make_async_remote_copy(
                src_ref=qkv_send.at[target],
                dst_ref=qkv_recv.at[me],
                send_sem=sum_send_sem.at[step, 0],
                recv_sem=sum_recv_sem.at[step, 0],
                **to_exp(target),
            ),
            pltpu.make_async_remote_copy(
                src_ref=out_send.at[target],
                dst_ref=out_recv.at[me],
                send_sem=sum_send_sem.at[step, 1],
                recv_sem=sum_recv_sem.at[step, 1],
                **to_exp(target),
            ),
        )

    def all_copies(step, target):
        return (
            pltpu.make_async_remote_copy(
                src_ref=qkv_all.at[me],
                dst_ref=qkv_all.at[me],
                send_sem=all_send_sem.at[step, 0],
                recv_sem=all_recv_sem.at[step, 0],
                **to_exp(target),
            ),
            pltpu.make_async_remote_copy(
                src_ref=out_all.at[me],
                dst_ref=out_all.at[me],
                send_sem=all_send_sem.at[step, 1],
                recv_sem=all_recv_sem.at[step, 1],
                **to_exp(target),
            ),
        )

    def all_arrivals(step, source):
        return (
            pltpu.make_async_remote_copy(
                src_ref=qkv_all.at[source],
                dst_ref=qkv_all.at[source],
                send_sem=all_send_sem.at[step, 0],
                recv_sem=all_recv_sem.at[step, 0],
                **to_exp(source),
            ),
            pltpu.make_async_remote_copy(
                src_ref=out_all.at[source],
                dst_ref=out_all.at[source],
                send_sem=all_send_sem.at[step, 1],
                recv_sem=all_recv_sem.at[step, 1],
                **to_exp(source),
            ),
        )

    def bias_copy(step, target):
        return pltpu.make_async_remote_copy(
            src_ref=bias_grad,
            dst_ref=bias_recv.at[me],
            send_sem=bias_send_sem.at[step],
            recv_sem=bias_recv_sem.at[step],
            **to_exp(target),
        )

    def start_sums():
        for block in range(experts):
            qkv_send[block] = qkv_grad[block * qkv_rows : (block + 1) * qkv_rows].astype(BF16)
            out_send[block] = out_grad[block * out_rows : (block + 1) * out_rows].astype(BF16)

        def begin(step, target, source):
            for copy in sum_copies(step, target):
                copy.start()
            bias_copy(step, target).start()

        each_peer(begin)
        qkv_recv[me] = qkv_send[me]
        out_recv[me] = out_send[me]
        bias_recv[me] = bias_grad[...]

    def spread_sums():
        def arrive(step, target, source):
            for copy in sum_copies(step, target):
                copy.wait_recv()
            bias_copy(step, target).wait_recv()

        each_peer(arrive)

        def add(source, totals):
            return (
                totals[0] + qkv_recv[source].astype(F32),
                totals[1] + out_recv[source].astype(F32),
                totals[2] + bias_recv[source],
            )

        qkv_total, out_total, bias_total = lax.fori_loop(
            1,
            experts,
            add,
            (qkv_recv[0].astype(F32), out_recv[0].astype(F32), bias_recv[0]),
        )
        qkv_all[me] = qkv_total.astype(BF16)
        out_all[me] = out_total.astype(BF16)
        bias_sum_ref[...] = bias_total

        def begin(step, target, source):
            for copy in all_copies(step, target):
                copy.start()

        each_peer(begin)

    def end_sums():
        def arrive(step, target, source):
            for copy in all_arrivals(step, source):
                copy.wait_recv()

        each_peer(arrive)
        for block in range(experts):
            qkv_sum_ref[block * qkv_rows : (block + 1) * qkv_rows] = qkv_all[block].astype(F32)
            out_sum_ref[block * out_rows : (block + 1) * out_rows] = out_all[block].astype(F32)

    def head_copy(step):
        return pltpu.make_async_remote_copy(
            src_ref=small_head.at[here],
            dst_ref=small_head.at[here],
            send_sem=head_send_sem.at[step],
            recv_sem=head_recv_sem.at[step],
            **to_head(lax.rem(here + step, head_parts)),
        )

    def head_arrival(step):
        source = lax.rem(here + head_parts - step, head_parts)
        return pltpu.make_async_remote_copy(
            src_ref=small_head.at[source],
            dst_ref=small_head.at[source],
            send_sem=head_send_sem.at[step],
            recv_sem=head_recv_sem.at[step],
            **to_head(source),
        )

    def small_copy(step, target):
        return pltpu.make_async_remote_copy(
            src_ref=small_recv.at[me],
            dst_ref=small_recv.at[me],
            send_sem=small_send_sem.at[step],
            recv_sem=small_recv_sem.at[step],
            **to_exp(target),
        )

    def small_arrival(step, source):
        return pltpu.make_async_remote_copy(
            src_ref=small_recv.at[source],
            dst_ref=small_recv.at[source],
            send_sem=small_send_sem.at[step],
            recv_sem=small_recv_sem.at[step],
            **to_exp(source),
        )

    heads = width // HEAD_DIM
    router_rows = small_head.shape[1] - 8

    def at(step, offset, action):
        seq = step - offset

        @pl.when((seq >= 0) & (seq < seq_count))
        def run():
            action(seq)

    def time_step(step, carry):
        at(step, 2, attend_start)
        for hop in range(max(ends, heads)):
            if hop < ends:
                at(
                    step,
                    0,
                    lambda seq: reduce_hop(sums_ref, seq * seqlen, one_down, one_up, seq, hop),
                )
                at(step, 3, lambda seq: reduce_hop(part_two, 0, two_down, two_up, seq, hop))
                at(step, 1, lambda seq: spread_hop(one_full, seq, hop))
                at(step, 4, lambda seq: spread_hop(two_full, seq, hop))
            if hop < heads:
                at(step, 2, lambda seq: attend_head(hop))

        def first_end(seq):
            reduce_end(sums_ref, seq * seqlen, one_down, one_up, seq, model_width + LANES)
            middle(seq)

        def second_end(seq):
            reduce_end(part_two, 0, two_down, two_up, seq, model_width)
            last(seq)

        def tokens_end(seq):
            spread_hop(two_full, seq, ends)
            stage_copy(seq).start()

        at(step, 0, first_end)
        at(step, 3, second_end)
        at(step, 2, attend_end)
        at(step, 1, lambda seq: spread_hop(one_full, seq, ends))

        @pl.when(step == seq_count + 1)
        def sums():
            start_sums()
            open_results()

        at(step, 4, combine)

        @pl.when(step == seq_count + 2)
        def small():
            small_head[here, :8] = rows_acc[...]
            small_head[here, 8:] = router_acc[...].T[:router_rows]
            for other in range(1, head_parts):
                head_copy(other).start()
            spread_sums()

        at(step, 4, tokens_end)
        return carry

    lax.fori_loop(0, seq_count + 4, time_step, 0)

    for other in range(1, head_parts):
        head_arrival(other).wait_recv()
    total = small_head[0]
    for other in range(1, head_parts):
        total = total + small_head[other]
    small_recv[me] = total
    each_peer(lambda step, target, source: small_copy(step, target).start())
    end_sums()
    each_peer(lambda step, target, source: small_arrival(step, source).wait_recv())
    small_ref[...] = lax.fori_loop(
        1, experts, lambda source, total: total + small_recv[source], small_recv[0]
    )
    for seq in range(seq_count):
        stage_copy(seq).wait()
        reduce_drain(one_down, one_up, seq)
        reduce_drain(two_down, two_up, seq)
        spread_drain(one_full, seq)
        spread_drain(two_full, seq)
    for other in range(1, head_parts):
        head_copy(other).wait_send()

    def sent(step, target, source):
        result_copy(step, target).wait_send()
        for copy in sum_copies(step, target):
            copy.wait_send()
        bias_copy(step, target).wait_send()
        for copy in all_copies(step, target):
            copy.wait_send()
        small_copy(step, target).wait_send()

    each_peer(sent)


def tail(
    sums, id_cols, gate_cols, own_residual, own_second, cot_own, own_columns, router, vectors,
    own_tokens, norm_rows, result, context, first, qkv, totals, flat_qkv, out_weight,
    seg_cols, seg_rows, live_rows, stride, half, head_parts,
):
    experts = result.shape[0]
    model_width = first.shape[1]
    seq_count, part = own_residual.shape[:2]
    seqlen = part * head_parts
    tok_count = seq_count * seqlen
    wide = flat_qkv.shape[1]
    width = wide // 3
    ends = head_parts - 1
    small_rows = 8 + round_up(experts, 8)
    dma = pltpu.SemaphoreType.DMA
    return pl.pallas_call(
        partial(tail_kernel, experts, stride, half, seq_count, head_parts),
        in_specs=[whole()] * 6 + [anywhere()] + [whole()] * 5 + [anywhere()] * 4 + [whole()] * 5,
        out_specs=[anywhere()] + [whole()] * 5,
        out_shape=[
            shaped((tok_count, model_width), BF16),
            shaped((tok_count, width), BF16),
            shaped((model_width, wide), F32),
            shaped((width, model_width), F32),
            shaped((8, wide), F32),
            shaped((small_rows, model_width), F32),
        ],
        scratch_shapes=[
            pltpu.VMEM((seqlen, width), F32),
            pltpu.VMEM((seqlen, model_width), BF16),
            pltpu.VMEM((seq_count, ends, part, model_width + LANES), BF16),
            pltpu.VMEM((seq_count, ends, part, model_width + LANES), BF16),
            pltpu.VMEM((seq_count, ends, part, model_width), BF16),
            pltpu.VMEM((seq_count, ends, part, model_width), BF16),
            pltpu.VMEM((part, model_width + LANES), F32),
            pltpu.VMEM((seq_count, seqlen, model_width), BF16),
            pltpu.VMEM((seq_count, seqlen, model_width), BF16),
            pltpu.VMEM((seq_count, part, model_width), F32),
            pltpu.VMEM((seqlen, width), BF16),
            pltpu.VMEM((seqlen, model_width), BF16),
            pltpu.VMEM((seqlen, wide), BF16),
            pltpu.VMEM((seqlen, LANES), F32),
            pltpu.VMEM((seqlen, width), BF16),
            pltpu.VMEM((seqlen, seqlen), BF16),
            pltpu.VMEM((seqlen, wide), BF16),
            pltpu.VMEM((model_width, wide), F32),
            pltpu.VMEM((width, model_width), F32),
            pltpu.VMEM((8, wide), F32),
            pltpu.VMEM((8, model_width), F32),
            pltpu.VMEM((model_width, LANES), F32),
            pltpu.VMEM((experts, stride + half, LANES), BF16),
            pltpu.VMEM((experts, stride, width), BF16),
            pltpu.VMEM((experts, model_width // experts, wide), BF16),
            pltpu.VMEM((experts, model_width // experts, wide), BF16),
            pltpu.VMEM((experts, model_width // experts, wide), BF16),
            pltpu.VMEM((experts, width // experts, model_width), BF16),
            pltpu.VMEM((experts, width // experts, model_width), BF16),
            pltpu.VMEM((experts, width // experts, model_width), BF16),
            pltpu.VMEM((experts, 8, wide), F32),
            pltpu.VMEM((head_parts, small_rows, model_width), F32),
            pltpu.VMEM((experts, small_rows, model_width), F32),
            dma((1,)),
            dma((4,)),
            dma((seq_count,)),
            dma((experts,)),
            dma((experts,)),
        ]
        + [dma((seq_count, ends))] * 8
        + [dma((seq_count, head_parts))] * 2
        + [dma((seq_count, head_parts, 2))] * 2
        + [dma((experts, 2))] * 4
        + [dma((experts,))] * 2
        + [dma((head_parts,))] * 2
        + [dma((experts,))] * 2,
        compiler_params=params(collective_id=2, has_side_effects=True),
        cost_estimate=cost(1e11, 1e8),
        name="tail",
    )(
        sums, id_cols, gate_cols, own_residual, own_second, cot_own, own_columns, router, vectors,
        own_tokens, norm_rows, result, context, first, qkv, totals, flat_qkv, out_weight,
        seg_cols, seg_rows, live_rows,
    )


def body(
    tokens,
    segments,
    live_mask,
    routes,
    priority,
    norm1_gain,
    norm1_bias,
    qkv_weight,
    qv_bias,
    out_weight,
    out_bias,
    norm2_gain,
    norm2_bias,
    router,
    up_weight,
    up_bias,
    down_weight,
    down_bias,
    cotangent,
):
    tok_count, model_width = tokens.shape
    seq_count, seqlen = segments.shape
    experts = lax.axis_size("exp")
    head_parts = lax.axis_size("head")
    head_index = lax.axis_index("head")
    quarter = model_width // head_parts
    capacity = (21 * tok_count + 10 * experts - 1) // (10 * experts)
    stride = round_up(capacity, 16)
    half = round_up(stride // 2, 16)
    local_width = qkv_weight.shape[2]

    def vector_rows(*vectors):
        rows = [v.astype(F32).reshape(1, -1) for v in vectors]
        rows.append(jnp.zeros((8 - len(rows), model_width), F32))
        return jnp.concatenate(rows, axis=0)

    norm_rows = vector_rows(norm1_gain, norm1_bias)
    vectors = vector_rows(out_bias, norm2_gain, norm2_bias)
    flat_qkv = qkv_weight.reshape(model_width, 3 * local_width)
    bias_row = jnp.concatenate(
        [qv_bias[0], jnp.zeros((local_width,), qv_bias.dtype), qv_bias[1]]
    ).astype(F32)[None]
    router_wide = jnp.pad(router, ((0, 0), (0, LANES - experts)))
    seg_rows = segments.reshape(seq_count, 1, seqlen)
    live_rows = live_mask.reshape(seq_count, 1, seqlen)
    seg_cols = segments.reshape(seq_count, seqlen, 1)
    down_bias_row = lax.dynamic_update_slice_in_dim(
        jnp.zeros((1, model_width), F32), down_bias.astype(F32), head_index * quarter, 1
    )
    up, down = up_weight[0], down_weight[0]
    up_bias_row = up_bias.astype(F32)

    out_full_weight = lax.all_gather(out_weight, "head", axis=0, tiled=True)
    first, qkv, context, packed, totals = attend(
        tokens, norm_rows, flat_qkv, bias_row, seg_cols, seg_rows, live_rows
    )
    gathered = lax.all_gather(packed, "head", axis=0)

    int_rows = jnp.concatenate(
        [
            routes.T,
            live_mask.reshape(1, tok_count),
            priority,
            jnp.zeros((4, tok_count), jnp.int32),
        ],
        axis=0,
    )
    ids, cot_slots = tables(
        priority.reshape(tok_count, 1), int_rows, cotangent, experts, capacity, stride, half, seqlen
    )
    id_cols = ids.T
    cot_moved = lax.all_to_all(cot_slots, "exp", split_axis=0, concat_axis=0, tiled=True)
    cot_rows = lax.all_gather(cot_moved, "head", axis=0)
    part = seqlen // head_parts
    cot_own = lax.all_to_all(
        cotangent.reshape(seq_count, head_parts, part, quarter),
        "head",
        split_axis=1,
        concat_axis=3,
        tiled=True,
    ).reshape(seq_count, part, model_width)
    own_tokens = lax.dynamic_slice_in_dim(
        tokens.reshape(seq_count, seqlen, model_width), head_index * part, part, 1
    )

    own_residual, own_second, own_columns, gates, arrived, hidden, result, gate_col = forward(
        gathered, tokens, vectors, out_full_weight, router_wide, int_rows, ids,
        up, up_bias_row, down, down_bias_row, experts, stride, half, seq_count, head_parts,
    )
    gate_cols = gates.T
    own_result = lax.psum_scatter(result, "head", scatter_dimension=0, tiled=True)[0]
    sums, grad_up, grad_up_bias, grad_down, grad_down_bias = backward(
        arrived, hidden, result, cot_rows, gate_col, id_cols, up, up_bias_row, down, half, head_parts,
        seqlen,
    )
    grad_tokens, block_out, qkv_grad, out_grad, bias_grad, small = tail(
        sums, id_cols, gate_cols, own_residual, own_second, cot_own, own_columns,
        router_wide, vectors, own_tokens, norm_rows, own_result, context, first, qkv, totals,
        flat_qkv, out_weight, seg_cols, seg_rows, live_rows, stride, half, head_parts,
    )
    grad_qv_bias = jnp.concatenate(
        [bias_grad[0:1, :local_width], bias_grad[0:1, 2 * local_width :]], axis=0
    )
    return (
        block_out,
        grad_tokens.astype(F32),
        small[3],
        small[4],
        qkv_grad.reshape(model_width, 3, local_width),
        grad_qv_bias,
        out_grad,
        small[2],
        small[0],
        small[1],
        small[8 : 8 + experts].T,
        grad_up[None],
        grad_up_bias[0:1],
        grad_down[None],
        lax.dynamic_slice_in_dim(grad_down_bias[0:1], head_index * quarter, quarter, 1),
    )


def solution(mesh):
    in_specs = (
        P("exp", None),
        P("exp", None),
        P("exp", None),
        P("exp", None),
        P("exp", None),
        P(),
        P(),
        P(None, None, "head"),
        P(None, "head"),
        P("head", None),
        P(),
        P(),
        P(),
        P(),
        P("exp", None, "head"),
        P("exp", "head"),
        P("exp", "head", None),
        P("exp", "head"),
        P("exp", "head"),
    )
    out_specs = (
        P("exp", "head"),
        P("exp", None),
        P(),
        P(),
        P(None, None, "head"),
        P(None, "head"),
        P("head", None),
        P(),
        P(),
        P(),
        P(),
        P("exp", None, "head"),
        P("exp", "head"),
        P("exp", "head", None),
        P("exp", "head"),
    )
    return jax.shard_map(body, mesh=mesh, in_specs=in_specs, out_specs=out_specs, check_vma=False)
```

```python
from functools import partial
import math

import jax
import jax.numpy as jnp
from jax import lax
from jax.experimental import pallas as pl
from jax.experimental.pallas import tpu as pltpu
from jax.sharding import PartitionSpec as P

HEAD_DIM = 64
LANES = 128
EPSILON = 1e-06
NEGATIVE = -1e30
CONTRACT_FIRST = (((0,), (0,)), ((), ()))
CONTRACT_LAST = (((1,), (1,)), ((), ()))
F32 = jnp.float32
BF16 = jnp.bfloat16
MESH = pl.DeviceIdType.MESH
VMEM_LIMIT = 54 * 1024 * 1024


def round_up(number, step):
    return (number + step - 1) // step * step


def whole():
    return pl.BlockSpec(memory_space=pltpu.VMEM)


def anywhere():
    return pl.BlockSpec(memory_space=pl.ANY)


def shaped(shape, dtype):
    return jax.ShapeDtypeStruct(shape, dtype)


def params(**more):
    return pltpu.CompilerParams(vmem_limit_bytes=VMEM_LIMIT, **more)


def cost(flops, moved):
    return pl.CostEstimate(flops=int(flops), bytes_accessed=int(moved), transcendentals=0)


def dot(left, right):
    return jnp.dot(left, right, preferred_element_type=F32)


def dot_last(left, right):
    return lax.dot_general(left, right, CONTRACT_LAST, preferred_element_type=F32)


def dot_first(left, right):
    return lax.dot_general(left, right, CONTRACT_FIRST, preferred_element_type=F32)


def standard(values):
    centred = values - jnp.mean(values, axis=-1, keepdims=True)
    scale = lax.rsqrt(jnp.mean(centred * centred, axis=-1, keepdims=True) + EPSILON)
    return centred * scale, scale


def norm_back(grad_rows, gain_row, normal, scale):
    inner = grad_rows * gain_row
    return scale * (
        inner
        - jnp.mean(inner, axis=-1, keepdims=True)
        - normal * jnp.mean(inner * normal, axis=-1, keepdims=True)
    )


def mask_penalty(seg_row, live_row):
    count = seg_row.shape[1]
    diagonal = lax.broadcasted_iota(jnp.int32, (count, count), 0) == lax.broadcasted_iota(
        jnp.int32, (count, count), 1
    )
    number = seg_row.astype(F32)
    column = jnp.sum(jnp.where(diagonal, number, 0.0), axis=1, keepdims=True)
    allowed = (column == number) & ((live_row > 0) | diagonal)
    return jnp.where(allowed, 0.0, NEGATIVE)


def pack_rows(rows, half):
    count = rows.shape[0]
    third = rows[:, LANES:]
    return rows[:, :LANES], jnp.concatenate([third[:half], third[count - half :]], axis=1)


def unpack_rows(parts_of, into, head_parts, count, half):
    extra = HEAD_DIM
    width = LANES + extra
    for z in range(head_parts):
        packed = parts_of(z)
        into[:, z * width : z * width + LANES] = packed[:count]
        tail = packed[count : count + half]
        into[:half, z * width + LANES : (z + 1) * width] = tail[:, :extra]
        into[half:, z * width + LANES : (z + 1) * width] = tail[2 * half - count :, extra:]


def greet(peers):
    barrier = pltpu.get_barrier_semaphore()
    me = lax.axis_index("exp")
    here = lax.axis_index("head")

    def call(step, carry):
        other = lax.rem(me + step, peers)
        pl.semaphore_signal(barrier, inc=1, device_id=(other, here), device_id_type=MESH)
        return carry

    lax.fori_loop(1, peers, call, 0)
    return barrier


def greet_both(peers, head_parts):
    barrier = greet(peers)
    me = lax.axis_index("exp")
    here = lax.axis_index("head")

    def call(step, carry):
        other = lax.rem(here + step, head_parts)
        pl.semaphore_signal(barrier, inc=1, device_id=(me, other), device_id_type=MESH)
        return carry

    lax.fori_loop(1, head_parts, call, 0)
    return barrier


def head_kernel(
    experts, capacity, stride, half, part_half, seq_count, head_parts,
    tokens_ref, norm_ref, weight_ref, bias_ref, seg_ref, live_ref, prio_ref, rows_ref, cot_ref,
    first_ref, qkv_ref, context_ref, total_ref, gathered_ref, ids_ref, cot_recv, own_send, own_tokens_ref,
    cot_send,
    gather_sem, gather_out, cot_send_sem, cot_recv_sem,
):
    me = lax.axis_index("exp")
    here = lax.axis_index("head")
    barrier = greet_both(experts, head_parts)
    ends = head_parts - 1
    tok_count = tokens_ref.shape[0]
    seqlen = tok_count // seq_count
    part = seqlen // head_parts
    pl.semaphore_wait(barrier, experts - 1 + ends)

    def own_rows():
        for seq in range(seq_count):
            own = pl.ds(pl.multiple_of(seq * seqlen + here * part, part), part)
            own_tokens_ref[seq] = tokens_ref[own]
            for z in range(head_parts):
                start = seq * seqlen + z * part
                wide, tail = pack_rows(cot_ref[start : start + part], part_half)
                own_send[z, seq, :part] = wide
                own_send[z, seq, part:] = tail

    def attend(seq):
        span = pl.ds(pl.multiple_of(seq * seqlen, seqlen), seqlen)
        normal, ignored = standard(tokens_ref[span].astype(F32))
        first = (normal * norm_ref[0:1] + norm_ref[1:2]).astype(BF16)
        first_ref[span] = first
        rows = (dot(first, weight_ref[...]) + bias_ref[...]).astype(BF16)
        qkv_ref[span] = rows
        penalty = mask_penalty(seg_ref[pl.ds(seq, 1)], live_ref[pl.ds(seq, 1)])
        width = rows.shape[1] // 3
        parts = []
        for head in range(width // HEAD_DIM):
            lo = head * HEAD_DIM
            hi = lo + HEAD_DIM
            query = rows[:, lo:hi] * BF16(1.0 / math.sqrt(HEAD_DIM))
            scores = dot_last(query, rows[:, width + lo : width + hi]) + penalty
            largest = jnp.max(scores, axis=-1, keepdims=True)
            weights = jnp.exp(scores - largest)
            total = jnp.sum(weights, axis=-1, keepdims=True)
            values = rows[:, 2 * width + lo : 2 * width + hi]
            parts.append((dot(weights.astype(BF16), values) / total).astype(BF16))
            total_ref[span, head : head + 1] = largest + jnp.log(total)
        context = jnp.concatenate(parts, axis=1)
        context_ref[span] = context
        wide, tail = pack_rows(context, seqlen // 2)
        gathered_ref[here, seq, :seqlen] = wide
        gathered_ref[here, seq, seqlen:] = tail

    def full_copy(seq, shard, side):
        return pltpu.make_async_remote_copy(
            src_ref=gathered_ref.at[shard, seq],
            dst_ref=gathered_ref.at[shard, seq],
            send_sem=gather_out.at[seq, shard, side],
            recv_sem=gather_sem.at[seq, shard],
            device_id=(me, here + 1 - 2 * side),
            device_id_type=MESH,
        )

    def each_side(hop, action):
        for side in range(2):
            shard = here - hop if side == 0 else here + hop
            there = shard >= 0 if side == 0 else shard <= ends
            onward = here < ends if side == 0 else here > 0
            action(side, shard, there, onward)

    def spread_hop(seq, hop):
        def one(side, shard, there, onward):
            @pl.when(there)
            def arrived():
                if hop > 0:
                    full_copy(seq, shard, side).wait_recv()
                if hop < ends:

                    @pl.when(onward)
                    def pass_on():
                        full_copy(seq, shard, side).start()

        each_side(hop, one)

    def spread_drain(seq):
        def one(side, shard, there, onward):
            @pl.when(there & onward)
            def sent():
                full_copy(seq, shard, side).wait_send()

        for hop in range(ends):
            each_side(hop, one)

    numbers = lax.broadcasted_iota(jnp.int32, (experts, 1), 0)

    def hot(rows):
        live = rows[2:3] > 0
        first = jnp.where((rows[0:1] == numbers) & live, 1.0, 0.0)
        second = jnp.where((rows[1:2] == numbers) & live, 1.0, 0.0)
        return first, second

    def tables():
        rank_row = rows_ref[3:4]
        counts = jnp.zeros((2 * experts, tok_count), F32)
        for start in range(0, tok_count, seqlen):
            first, second = hot(rows_ref[:, start : start + seqlen])
            earlier = jnp.where(prio_ref[start : start + seqlen] < rank_row, 1.0, 0.0)
            both = jnp.concatenate([first, second], axis=0)
            counts = counts + dot(both.astype(BF16), earlier.astype(BF16))
        first, second = hot(rows_ref[...])
        total = jnp.sum(first, axis=1, keepdims=True)
        places = [
            jnp.sum(first * counts[:experts], axis=0, keepdims=True),
            jnp.sum(second * (counts[experts:] + total), axis=0, keepdims=True),
        ]
        for pick in range(2):
            place = places[pick].astype(jnp.int32)
            kept = (place < capacity) & (rows_ref[2:3] > 0)
            ids_ref[pick : pick + 1] = jnp.where(
                kept, rows_ref[pick : pick + 1] * stride + place, -1
            )
        ids_ref[2:8] = jnp.full((6, tok_count), -1, jnp.int32)

    def cot_copy(step, target):
        return pltpu.make_async_remote_copy(
            src_ref=cot_send.at[target],
            dst_ref=cot_recv.at[me],
            send_sem=cot_send_sem.at[step],
            recv_sem=cot_recv_sem.at[step],
            device_id=(target, here),
            device_id_type=MESH,
        )

    def fill(target):
        slots = target * stride + lax.broadcasted_iota(jnp.int32, (stride, 1), 0)
        hit = (ids_ref[0:1] == slots) | (ids_ref[1:2] == slots)
        block = dot(jnp.where(hit, 1.0, 0.0).astype(BF16), cot_ref[...]).astype(BF16)
        return pack_rows(block, half)

    def dispatch():
        def one(step, carry):
            target = lax.rem(me + step, experts)
            wide, tail = fill(target)
            cot_send[target, :stride] = wide
            cot_send[target, stride:] = tail
            cot_copy(step, target).start()
            return carry

        lax.fori_loop(1, experts, one, 0)
        wide, tail = fill(me)
        cot_recv[me, :stride] = wide
        cot_recv[me, stride:] = tail

    def time_step(step, carry):
        @pl.when(step == seq_count + 1)
        def send():
            dispatch()

        for hop in range(ends, 0, -1):

            @pl.when((step >= hop) & (step - hop < seq_count))
            def move():
                spread_hop(step - hop, hop)

        @pl.when(step < seq_count)
        def work():
            attend(step)
            spread_hop(step, 0)

        @pl.when(step == seq_count)
        def places():
            tables()

        @pl.when(step == seq_count + 1)
        def rows():
            own_rows()

        return carry

    lax.fori_loop(0, seq_count + ends, time_step, 0)
    for seq in range(seq_count):
        spread_drain(seq)

    def finish(step, carry):
        cot_copy(step, lax.rem(me + step, experts)).wait()
        return carry

    lax.fori_loop(1, experts, finish, 0)


def head(
    tokens, norm_rows, flat_qkv, bias_row, segments, live, prio_col, rows, cotangent,
    experts, capacity, stride, half, part_half, head_parts,
):
    tok_count, model_width = tokens.shape
    seq_count, seqlen = segments.shape
    part = seqlen // head_parts
    wide = flat_qkv.shape[1]
    width = wide // 3
    dma = pltpu.SemaphoreType.DMA
    own = (head_parts, seq_count, part + part_half, LANES)
    slots = (experts, stride + half, LANES)
    return pl.pallas_call(
        partial(head_kernel, experts, capacity, stride, half, part_half, seq_count, head_parts),
        in_specs=[whole()] * 9,
        out_specs=[whole()] * 9,
        out_shape=[
            shaped((tok_count, model_width), BF16),
            shaped((tok_count, wide), BF16),
            shaped((tok_count, width), BF16),
            shaped((tok_count, LANES), F32),
            shaped((head_parts, seq_count, seqlen + seqlen // 2, LANES), BF16),
            shaped((8, tok_count), jnp.int32),
            shaped(slots, BF16),
            shaped(own, BF16),
            shaped((seq_count, part, model_width), BF16),
        ],
        scratch_shapes=[
            pltpu.VMEM(slots, BF16),
            dma((seq_count, head_parts)),
            dma((seq_count, head_parts, 2)),
            dma((experts,)),
            dma((experts,)),
        ],
        compiler_params=params(collective_id=3, has_side_effects=True),
        cost_estimate=cost(6e10, 1e7),
        name="head",
    )(tokens, norm_rows, flat_qkv, bias_row, segments, live, prio_col, rows, cotangent)


def gelu_parts(pre):
    root = math.sqrt(2.0 / math.pi)
    square = pre * pre
    wave = jnp.tanh(root * (pre + 0.044715 * pre * square))
    half_sum = 0.5 * (1.0 + wave)
    slope = half_sum + 0.5 * pre * (1.0 - wave * wave) * (
        root * (1.0 + 3.0 * 0.044715 * square)
    )
    return pre * half_sum, slope


def forward_kernel(
    experts, stride, half, seq_count, head_parts,
    gathered_ref, tokens_ref, vectors_ref, out_weight_ref, router_ref, rows_ref, ids_ref,
    up_ref, up_bias_ref, down_ref, down_bias_ref, cot_hbm,
    own_residual_ref, own_second_ref, own_columns_ref, gates_ref, arrived_ref, hidden_ref, result_ref,
    gate_col_ref, cot_all, residual_ref, context_scr, second_scr, logit_scr, send_scr, gate_send, gate_recv,
    send_sem, recv_sem, gate_send_sem, gate_recv_sem, cot_sem, cot_out, local_sem,
):
    me = lax.axis_index("exp")
    here = lax.axis_index("head")
    barrier = greet_both(experts, head_parts)
    ends = head_parts - 1
    pieces = cot_sem.shape[1]
    piece_rows = experts // pieces
    tok_count = tokens_ref.shape[0]

    def cot_copy(shard, piece, side, own=False):
        span = pl.ds(piece * piece_rows, piece_rows)
        return pltpu.make_async_remote_copy(
            src_ref=cot_hbm.at[span] if own else cot_all.at[shard, span],
            dst_ref=cot_all.at[shard, span],
            send_sem=cot_out.at[shard, piece, side],
            recv_sem=cot_sem.at[shard, piece],
            device_id=(me, here + 1 - 2 * side),
            device_id_type=MESH,
        )

    def cot_side(hop, side):
        shard = here - hop if side == 0 else here + hop
        there = shard >= 0 if side == 0 else shard <= ends
        onward = here < ends if side == 0 else here > 0
        return shard, there, onward

    def cot_hop(hop, piece):
        for side in range(2):
            shard, there, onward = cot_side(hop, side)

            @pl.when(there)
            def arrived():
                if hop > 0:
                    cot_copy(shard, piece, side).wait_recv()
                if hop < ends:

                    @pl.when(onward)
                    def pass_on():
                        cot_copy(shard, piece, side, hop == 0).start()

    def cot_drain(hop, piece):
        for side in range(2):
            shard, there, onward = cot_side(hop, side)

            @pl.when(there & onward)
            def sent():
                cot_copy(shard, piece, side, hop == 0).wait_send()

    local = pltpu.make_async_copy(cot_hbm, cot_all.at[here], local_sem.at[0])
    local.start()
    pl.semaphore_wait(barrier, experts - 1 + ends)
    for piece in range(pieces):
        cot_hop(0, piece)
    seqlen = tok_count // seq_count
    for seq in range(seq_count):
        span = slice(seq * seqlen, (seq + 1) * seqlen)
        unpack_rows(lambda z: gathered_ref[z, seq], context_scr, head_parts, seqlen, seqlen // 2)
        residual = (
            tokens_ref[span].astype(F32)
            + dot(context_scr[...], out_weight_ref[...])
            + vectors_ref[0:1]
        )
        residual_ref[span] = residual
        normal, ignored = standard(residual)
        second = (normal * vectors_ref[1:2] + vectors_ref[2:3]).astype(BF16)
        second_scr[span] = second
        logit_scr[:, span] = dot(second, router_ref[...]).T[:experts]
    part = seqlen // head_parts
    for seq in range(seq_count):
        own = pl.ds(pl.multiple_of(seq * seqlen + here * part, part), part)
        own_residual_ref[seq] = residual_ref[own]
        own_second_ref[seq] = second_scr[own]
    width = residual_ref.shape[1] // head_parts
    for z in range(head_parts):

        @pl.when(here == z)
        def columns():
            own_columns_ref[...] = residual_ref[:, z * width : (z + 1) * width]


    logits = logit_scr[...]
    powers = jnp.exp(logits - jnp.max(logits, axis=0, keepdims=True))
    chances = powers / jnp.sum(powers, axis=0, keepdims=True)
    numbers = lax.broadcasted_iota(jnp.int32, (experts, 1), 0)
    for pick in range(2):
        chosen = jnp.where(rows_ref[pick : pick + 1] == numbers, chances, 0.0)
        gate = jnp.where(ids_ref[pick : pick + 1] >= 0, jnp.sum(chosen, axis=0, keepdims=True), 0.0)
        gates_ref[pick : pick + 1] = gate
    gates_ref[2:8] = jnp.zeros((6, tok_count), F32)

    def copies(target, step):
        to = dict(device_id=(target, here), device_id_type=MESH)
        return (
            pltpu.make_async_remote_copy(
                src_ref=send_scr.at[step],
                dst_ref=arrived_ref.at[me],
                send_sem=send_sem.at[step],
                recv_sem=recv_sem.at[step],
                **to,
            ),
            pltpu.make_async_remote_copy(
                src_ref=gate_send.at[step],
                dst_ref=gate_recv.at[me],
                send_sem=gate_send_sem.at[step],
                recv_sem=gate_recv_sem.at[step],
                **to,
            ),
        )

    def fill(target):
        slots = target * stride + lax.broadcasted_iota(jnp.int32, (stride, 1), 0)
        first = ids_ref[0:1] == slots
        second = ids_ref[1:2] == slots
        block = dot(jnp.where(first | second, 1.0, 0.0).astype(BF16), second_scr[...]).astype(BF16)
        gate = jnp.sum(
            jnp.where(first, gates_ref[0:1], jnp.where(second, gates_ref[1:2], 0.0)),
            axis=1,
            keepdims=True,
        )
        return block, jnp.broadcast_to(gate, (stride, LANES)).T[:8]

    def send(step, carry):
        target = lax.rem(me + step, experts)
        block, gate = fill(target)
        send_scr[step] = block
        gate_send[step] = gate
        for copy in copies(target, step):
            copy.start()
        return carry

    lax.fori_loop(1, experts, send, 0)
    block, gate = fill(me)
    arrived_ref[me] = block
    gate_recv[me] = gate

    def work(source):
        pre = dot(arrived_ref[source], up_ref[...]) + up_bias_ref[...]
        hidden = gelu_parts(pre)[0].astype(BF16)
        hidden_ref[source] = hidden
        result = (dot(hidden, down_ref[...]) + down_bias_ref[...]).astype(BF16)
        for z in range(head_parts):
            wide, tail = pack_rows(result[:, z * width : (z + 1) * width], half)
            result_ref[z, source, :stride] = wide
            result_ref[z, source, stride:] = tail

    work(me)
    moves = [(hop, piece) for hop in range(1, ends) for piece in range(pieces)]
    early = len(moves) - min(experts - 2, len(moves))
    for move in moves[:early]:
        cot_hop(*move)

    def receive(step, carry):
        for place, move in enumerate(moves[early:]):

            @pl.when(step == place + 1)
            def pass_on():
                cot_hop(*move)

        source = lax.rem(me + experts - step, experts)
        wide, narrow = copies(source, step)
        wide.wait_recv()
        narrow.wait_recv()
        work(source)
        return carry

    lax.fori_loop(1, experts, receive, 0)

    def finish(step, carry):
        for copy in copies(lax.rem(me + step, experts), step):
            copy.wait_send()
        return carry

    lax.fori_loop(1, experts, finish, 0)
    for piece in range(pieces):
        cot_hop(ends, piece)
        for hop in range(ends):
            cot_drain(hop, piece)
    local.wait()
    lane = lax.broadcasted_iota(jnp.int32, (LANES, stride), 0)
    square = jnp.zeros((LANES, stride), F32)
    for source in range(experts):
        square = jnp.where(lane == source, gate_recv[source, 0:1], square)
    gate_col_ref[...] = square.T


def forward(
    gathered, tokens, vectors, out_weight, router, rows, ids, up, up_bias, down, down_bias, cot_slots,
    experts, stride, half, seq_count, head_parts,
):
    tok_count, model_width = tokens.shape
    seqlen = tok_count // seq_count
    part = seqlen // head_parts
    return pl.pallas_call(
        partial(forward_kernel, experts, stride, half, seq_count, head_parts),
        in_specs=[whole()] * 11 + [anywhere()],
        out_specs=[whole()] * 8 + [anywhere()],
        out_shape=[
            shaped((seq_count, part, model_width), F32),
            shaped((seq_count, part, model_width), BF16),
            shaped((tok_count, model_width // head_parts), F32),
            shaped((8, tok_count), F32),
            shaped((experts, stride, model_width), BF16),
            shaped((experts, stride, up.shape[1]), BF16),
            shaped((head_parts, experts, stride + half, LANES), BF16),
            shaped((stride, LANES), F32),
            shaped((head_parts, experts, stride + half, LANES), BF16),
        ],
        scratch_shapes=[
            pltpu.VMEM((tok_count, model_width), F32),
            pltpu.VMEM((seqlen, model_width), BF16),
            pltpu.VMEM((tok_count, model_width), BF16),
            pltpu.VMEM((experts, tok_count), F32),
            pltpu.VMEM((experts, stride, model_width), BF16),
            pltpu.VMEM((experts, 8, stride), F32),
            pltpu.VMEM((experts, 8, stride), F32),
            pltpu.SemaphoreType.DMA((experts,)),
            pltpu.SemaphoreType.DMA((experts,)),
            pltpu.SemaphoreType.DMA((experts,)),
            pltpu.SemaphoreType.DMA((experts,)),
            pltpu.SemaphoreType.DMA((head_parts, 4)),
            pltpu.SemaphoreType.DMA((head_parts, 4, 2)),
            pltpu.SemaphoreType.DMA((1,)),
        ],
        compiler_params=params(collective_id=0, has_side_effects=True),
        cost_estimate=cost(8e10, 1e8),
        name="forward",
    )(gathered, tokens, vectors, out_weight, router, rows, ids, up, up_bias, down, down_bias, cot_slots)


def backward_kernel(
    experts, stride, half, head_parts, chunk,
    arrived_hbm, hidden_hbm, result_hbm, cot_hbm, gate_col_ref, ids_ref, up_ref, up_bias_ref, down_ref,
    sums_ref, grad_up_ref, grad_up_bias_ref, grad_down_ref, grad_down_bias_ref,
    rows_scr, result_scr, cot_scr, cot_wide, result_wide, hidden_scr, pre_grad_scr, out_grad_scr,
    send_scr, recv_scr, gate_send, gate_recv, total_scr,
    load_sem, send_sem, recv_sem, gate_send_sem, gate_recv_sem,
):
    me = lax.axis_index("exp")
    here = lax.axis_index("head")
    barrier = greet(experts)
    tok_count = ids_ref.shape[0]
    model_width = up_ref.shape[0]

    def loads(step):
        home = lax.rem(me + step, experts)
        slot = lax.rem(step, 2)
        return (
            pltpu.make_async_copy(arrived_hbm.at[home], rows_scr.at[slot], load_sem.at[slot, 0]),
            pltpu.make_async_copy(result_hbm.at[:, home], result_scr.at[slot], load_sem.at[slot, 1]),
            pltpu.make_async_copy(cot_hbm.at[:, home], cot_scr.at[slot], load_sem.at[slot, 2]),
        )

    def copies(target, step):
        to = dict(device_id=(target, here), device_id_type=MESH)
        return (
            pltpu.make_async_remote_copy(
                src_ref=send_scr.at[step],
                dst_ref=recv_scr.at[me],
                send_sem=send_sem.at[step],
                recv_sem=recv_sem.at[step],
                **to,
            ),
            pltpu.make_async_remote_copy(
                src_ref=gate_send.at[step],
                dst_ref=gate_recv.at[me],
                send_sem=gate_send_sem.at[step],
                recv_sem=gate_recv_sem.at[step],
                **to,
            ),
        )

    for copy in loads(1):
        copy.start()
    grad_up_ref[...] = jnp.zeros_like(grad_up_ref)
    grad_down_ref[...] = jnp.zeros_like(grad_down_ref)
    grad_up_bias_ref[...] = jnp.zeros_like(grad_up_bias_ref)
    grad_down_bias_ref[...] = jnp.zeros_like(grad_down_bias_ref)
    total_scr[...] = jnp.zeros_like(total_scr)
    pl.semaphore_wait(barrier, experts - 1)

    def work(step):
        home = lax.rem(me + step, experts)
        slot = lax.rem(step, 2)
        for copy in loads(step):
            copy.wait()
        unpack_rows(lambda z: cot_scr[slot, z], cot_wide, head_parts, stride, half)
        unpack_rows(lambda z: result_scr[slot, z], result_wide, head_parts, stride, half)
        out_rows = cot_wide[...].astype(F32)
        pre = dot(rows_scr[slot], up_ref[...]) + up_bias_ref[...]
        slope = gelu_parts(pre)[1]
        lane = lax.broadcasted_iota(jnp.int32, (stride, LANES), 1)
        gate = jnp.sum(jnp.where(lane == home, gate_col_ref[...], 0.0), axis=1, keepdims=True)
        out_grad = (gate * out_rows).astype(BF16)
        out_grad_scr[step] = out_grad
        grad_down_bias_ref[0:1] += jnp.sum(out_grad.astype(F32), axis=0, keepdims=True)
        pre_grad = (dot_last(out_grad, down_ref[...]) * slope).astype(BF16)
        pre_grad_scr[step] = pre_grad
        grad_up_bias_ref[0:1] += jnp.sum(pre_grad.astype(F32), axis=0, keepdims=True)
        gate_grad = jnp.sum(result_wide[...].astype(F32) * out_rows, axis=1, keepdims=True)
        return (
            dot_last(pre_grad, up_ref[...]).astype(BF16),
            jnp.broadcast_to(gate_grad, (stride, LANES)).T[:8],
        )

    def send(step, carry):
        for copy in loads(lax.rem(step + 1, experts)):
            copy.start()
        block, gate = work(step)
        send_scr[step] = block
        gate_send[step] = gate
        for copy in copies(lax.rem(me + step, experts), step):
            copy.start()
        return carry

    lax.fori_loop(1, experts, send, 0)
    block, gate = work(0)
    recv_scr[me] = block
    gate_recv[me] = gate

    def row_loads(step):
        home = lax.rem(me + step, experts)
        slot = lax.rem(step, 2)
        return (
            pltpu.make_async_copy(arrived_hbm.at[home], rows_scr.at[slot], load_sem.at[slot, 0]),
            pltpu.make_async_copy(hidden_hbm.at[home], hidden_scr.at[slot], load_sem.at[slot, 1]),
        )

    def weigh(step):
        slot = lax.rem(step, 2)
        for copy in row_loads(step):
            copy.wait()
        grad_up_ref[...] += dot_first(rows_scr[slot], pre_grad_scr[step])
        grad_down_ref[...] += dot_first(hidden_scr[slot], out_grad_scr[step])

    def weigh_some(step, carry):
        for copy in row_loads(step + 1):
            copy.start()
        weigh(step)
        return carry

    for copy in row_loads(0):
        copy.start()
    lax.fori_loop(0, experts - 1, weigh_some, 0)
    weigh(experts - 1)

    def gather(source):
        slots = source * stride + lax.broadcasted_iota(jnp.int32, (1, stride), 1)
        lane = lax.broadcasted_iota(jnp.int32, (chunk, LANES), 1)

        def part(index, carry):
            span = pl.ds(pl.multiple_of(index * chunk, chunk), chunk)
            hit = (ids_ref[span, 0:1] == slots) | (ids_ref[span, 1:2] == slots)
            total_scr[span, :model_width] += dot(
                jnp.where(hit, 1.0, 0.0).astype(BF16), recv_scr[source]
            )
            gate = jnp.sum(jnp.where(hit, gate_recv[source, 0:1], 0.0), axis=1, keepdims=True)
            total_scr[span, model_width:] = jnp.where(
                lane == source, gate, total_scr[span, model_width:]
            )
            return carry

        lax.fori_loop(0, tok_count // chunk, part, 0)

    gather(me)

    def receive(step, carry):
        source = lax.rem(me + experts - step, experts)
        for copy in copies(source, step):
            copy.wait_recv()
        gather(source)
        return carry

    lax.fori_loop(1, experts, receive, 0)
    sums_ref[...] = total_scr[...].astype(BF16)

    def finish(step, carry):
        for copy in copies(lax.rem(me + step, experts), step):
            copy.wait_send()
        return carry

    lax.fori_loop(1, experts, finish, 0)


def backward(
    arrived, hidden, result, cot_rows, gate_col, id_cols, up, up_bias, down, half, head_parts, chunk
):
    tok_count = id_cols.shape[0]
    experts, stride, model_width = arrived.shape
    inner = up.shape[1]
    rows = (experts, stride, model_width)
    return pl.pallas_call(
        partial(backward_kernel, experts, stride, half, head_parts, chunk),
        in_specs=[anywhere()] * 4 + [whole()] * 5,
        out_specs=[whole()] * 5,
        out_shape=[
            shaped((tok_count, model_width + LANES), BF16),
            shaped((model_width, inner), F32),
            shaped((8, inner), F32),
            shaped((inner, model_width), F32),
            shaped((8, model_width), F32),
        ],
        scratch_shapes=[
            pltpu.VMEM((2, stride, model_width), BF16),
            pltpu.VMEM((2, head_parts, stride + half, LANES), BF16),
            pltpu.VMEM((2, head_parts, stride + half, LANES), BF16),
            pltpu.VMEM((stride, model_width), BF16),
            pltpu.VMEM((stride, model_width), BF16),
            pltpu.VMEM((2, stride, inner), BF16),
            pltpu.VMEM((experts, stride, inner), BF16),
            pltpu.VMEM(rows, BF16),
            pltpu.VMEM(rows, BF16),
            pltpu.VMEM(rows, BF16),
            pltpu.VMEM((experts, 8, stride), F32),
            pltpu.VMEM((experts, 8, stride), F32),
            pltpu.VMEM((tok_count, model_width + LANES), F32),
            pltpu.SemaphoreType.DMA((2, 3)),
            pltpu.SemaphoreType.DMA((experts,)),
            pltpu.SemaphoreType.DMA((experts,)),
            pltpu.SemaphoreType.DMA((experts,)),
            pltpu.SemaphoreType.DMA((experts,)),
        ],
        compiler_params=params(collective_id=1, has_side_effects=True),
        cost_estimate=cost(8e10, 1e8),
        name="backward",
    )(arrived, hidden, result, cot_rows, gate_col, id_cols, up, up_bias, down)


def tail_kernel(
    experts, stride, half, part_half, seq_count, head_parts, gap,
    sums_ref, id_cols_ref, gate_cols_ref, own_residual_ref, own_second_ref, cot_own_hbm,
    own_columns_hbm, router_ref, vectors_ref, own_tokens_ref, norm_ref, result_hbm,
    context_hbm, first_hbm, qkv_hbm, totals_hbm, weight_ref, out_weight_ref,
    seg_ref, live_ref,
    tokens_hbm, block_ref, qkv_sum_ref, out_sum_ref, bias_sum_ref, small_ref,
    own_recv, cot_wide, columns_scr, part_two, down_one, up_one, down_two, up_two, own_scr,
    full_one, full_two, grad_scr,
    context_scr, first_scr, qkv_scr, totals_scr, back_scr, joined_scr,
    qkv_grad, out_grad, bias_grad, rows_acc, router_acc,
    result_home, result_wide,
    qkv_send, qkv_recv, qkv_all, out_send, out_recv, out_all, bias_recv, small_head, small_recv,
    own_send_sem, own_recv_sem, columns_sem, load_sem, stage_sem, result_send_sem, result_recv_sem,
    down_one_sem, up_one_sem, down_two_sem, up_two_sem, down_one_out, up_one_out, down_two_out, up_two_out,
    full_one_sem, full_two_sem, full_one_out, full_two_out,
    sum_send_sem, sum_recv_sem, all_send_sem, all_recv_sem,
    bias_send_sem, bias_recv_sem, head_send_sem, head_recv_sem, small_send_sem, small_recv_sem,
):
    me = lax.axis_index("exp")
    here = lax.axis_index("head")
    ends = head_parts - 1
    seqlen = seg_ref.shape[1]
    part = seqlen // head_parts
    model_width = vectors_ref.shape[1]
    width = out_weight_ref.shape[0]
    factor = 1.0 / math.sqrt(HEAD_DIM)

    barrier = greet_both(experts, head_parts)

    def chunk_loads(seq):
        span = pl.ds(pl.multiple_of(seq * seqlen, seqlen), seqlen)
        return (
            pltpu.make_async_copy(context_hbm.at[span], context_scr, load_sem.at[0]),
            pltpu.make_async_copy(first_hbm.at[span], first_scr, load_sem.at[1]),
            pltpu.make_async_copy(qkv_hbm.at[span], qkv_scr, load_sem.at[2]),
            pltpu.make_async_copy(totals_hbm.at[span], totals_scr, load_sem.at[3]),
        )

    for copy in chunk_loads(0):
        copy.start()
    qkv_grad[...] = jnp.zeros_like(qkv_grad)
    out_grad[...] = jnp.zeros_like(out_grad)
    bias_grad[...] = jnp.zeros_like(bias_grad)
    rows_acc[...] = jnp.zeros_like(rows_acc)
    router_acc[...] = jnp.zeros_like(router_acc)
    pl.semaphore_wait(barrier, experts - 1 + ends)

    def to_exp(target):
        return dict(device_id=(target, here), device_id_type=MESH)

    def to_head(target):
        return dict(device_id=(me, target), device_id_type=MESH)

    def each_peer(action):
        def one(step, carry):
            action(step, lax.rem(me + step, experts), lax.rem(me + experts - step, experts))
            return carry

        lax.fori_loop(1, experts, one, 0)

    def result_copy(step, target):
        return pltpu.make_async_remote_copy(
            src_ref=result_hbm.at[target],
            dst_ref=result_home.at[me],
            send_sem=result_send_sem.at[step],
            recv_sem=result_recv_sem.at[step],
            **to_exp(target),
        )

    def own_copy(seq, step):
        target = lax.rem(here + step, head_parts)
        return pltpu.make_async_remote_copy(
            src_ref=cot_own_hbm.at[target, seq],
            dst_ref=own_recv.at[here, seq],
            send_sem=own_send_sem.at[seq, step],
            recv_sem=own_recv_sem.at[seq, step],
            **to_head(target),
        )

    own_local = pltpu.make_async_copy(cot_own_hbm.at[here], own_recv.at[here], columns_sem.at[1])
    own_local.start()
    own_local.wait()

    def down_copy(buffer, sems, outs, seq, shard):
        return pltpu.make_async_remote_copy(
            src_ref=buffer.at[seq, shard],
            dst_ref=buffer.at[seq, shard],
            send_sem=outs.at[seq, shard],
            recv_sem=sems.at[seq, shard],
            **to_head(here - 1),
        )

    def up_copy(buffer, sems, outs, seq, shard):
        return pltpu.make_async_remote_copy(
            src_ref=buffer.at[seq, shard - 1],
            dst_ref=buffer.at[seq, shard - 1],
            send_sem=outs.at[seq, shard - 1],
            recv_sem=sems.at[seq, shard - 1],
            **to_head(here + 1),
        )

    one_down = (down_one, down_one_sem, down_one_out)
    one_up = (up_one, up_one_sem, up_one_out)
    two_down = (down_two, down_two_sem, down_two_out)
    two_up = (up_two, up_two_sem, up_two_out)

    def reduce_hop(partial_ref, base, down, up, seq, hop):
        low = hop - ends + here
        high = ends - hop + here

        @pl.when((low >= 0) & (low < here))
        def downward():
            rows = partial_ref[pl.ds(pl.multiple_of(base + low * part, part), part)]

            @pl.when(here < ends)
            def add():
                down_copy(*down, seq, low).wait_recv()
                down[0][seq, low] = (down[0][seq, low].astype(F32) + rows.astype(F32)).astype(BF16)

            @pl.when(here == ends)
            def begin():
                down[0][seq, low] = rows

            down_copy(*down, seq, low).start()

        @pl.when((high > here) & (high <= ends))
        def upward():
            rows = partial_ref[pl.ds(pl.multiple_of(base + high * part, part), part)]

            @pl.when(here > 0)
            def add():
                up_copy(*up, seq, high).wait_recv()
                up[0][seq, high - 1] = (
                    up[0][seq, high - 1].astype(F32) + rows.astype(F32)
                ).astype(BF16)

            @pl.when(here == 0)
            def begin():
                up[0][seq, high - 1] = rows

            up_copy(*up, seq, high).start()

    def reduce_end(partial_ref, base, down, up, seq, columns):
        own = pl.ds(pl.multiple_of(base + here * part, part), part)
        own_scr[:, :columns] = partial_ref[own].astype(F32)

        @pl.when(here < ends)
        def below():
            down_copy(*down, seq, here).wait_recv()
            own_scr[:, :columns] += down[0][seq, here].astype(F32)

        @pl.when(here > 0)
        def above():
            up_copy(*up, seq, here).wait_recv()
            own_scr[:, :columns] += up[0][seq, here - 1].astype(F32)

    def reduce_drain(down, up, seq):
        for shard in range(ends):

            @pl.when(shard < here)
            def downward():
                down_copy(*down, seq, shard).wait_send()

            @pl.when(shard + 1 > here)
            def upward():
                up_copy(*up, seq, shard + 1).wait_send()

    def full_copy(buffer, sems, outs, seq, shard, side):
        rows = pl.ds(pl.multiple_of(shard * part, part), part)
        return pltpu.make_async_remote_copy(
            src_ref=buffer.at[seq, rows],
            dst_ref=buffer.at[seq, rows],
            send_sem=outs.at[seq, shard, side],
            recv_sem=sems.at[seq, shard],
            **to_head(here + 1 - 2 * side),
        )

    one_full = (full_one, full_one_sem, full_one_out)
    two_full = (full_two, full_two_sem, full_two_out)

    def spread_hop(full, seq, hop):
        for side in range(2):
            shard = here - hop if side == 0 else here + hop
            there = shard >= 0 if side == 0 else shard <= ends
            onward = here < ends if side == 0 else here > 0

            @pl.when(there)
            def arrived():
                if hop > 0:
                    full_copy(*full, seq, shard, side).wait_recv()
                if hop < ends:

                    @pl.when(onward)
                    def pass_on():
                        full_copy(*full, seq, shard, side).start()

    def spread_drain(full, seq):
        for hop in range(ends):
            for side in range(2):
                shard = here - hop if side == 0 else here + hop
                there = shard >= 0 if side == 0 else shard <= ends
                onward = here < ends if side == 0 else here > 0

                @pl.when(there & onward)
                def sent():
                    full_copy(*full, seq, shard, side).wait_send()

    def middle(seq):
        second = own_second_ref[seq]
        lane = lax.broadcasted_iota(jnp.int32, (part, LANES), 1)
        logits = jnp.where(lane < experts, dot(second, router_ref[...]), NEGATIVE)
        powers = jnp.exp(logits - jnp.max(logits, axis=1, keepdims=True))
        chances = powers / jnp.sum(powers, axis=1, keepdims=True)
        route_grad = own_scr[:, model_width:]
        logit_grad = (
            chances * (route_grad - jnp.sum(chances * route_grad, axis=1, keepdims=True))
        ).astype(BF16)
        router_acc[...] += dot_first(second, logit_grad)
        grad = own_scr[:, :model_width] + dot_last(logit_grad, router_ref[...])
        normal, scale = standard(own_residual_ref[seq])
        rows_acc[0:1] += jnp.sum(grad * normal, axis=0, keepdims=True)
        rows_acc[1:2] += jnp.sum(grad, axis=0, keepdims=True)
        for other in range(1, head_parts):
            own_copy(seq, other).wait_recv()
        unpack_rows(lambda z: own_recv[z, seq], cot_wide, head_parts, part, part_half)
        total = cot_wide[...].astype(F32) + norm_back(grad, vectors_ref[1:2], normal, scale)
        rows_acc[2:3] += jnp.sum(total, axis=0, keepdims=True)
        grad_scr[seq] = total
        full_one[seq, pl.ds(pl.multiple_of(here * part, part), part)] = total.astype(BF16)

    def attend_start(seq):
        for copy in chunk_loads(seq):
            copy.wait()
        grad = full_one[seq]
        back_scr[...] = dot_last(grad, out_weight_ref[...]).astype(BF16)
        out_grad[...] += dot_first(context_scr[...], grad)
        return mask_penalty(seg_ref[pl.ds(seq, 1)], live_ref[pl.ds(seq, 1)])

    def attend_head(head, penalty):
        lo = head * HEAD_DIM
        hi = lo + HEAD_DIM
        query = qkv_scr[:, lo:hi] * BF16(factor)
        keys = qkv_scr[:, width + lo : width + hi]
        values = qkv_scr[:, 2 * width + lo : 2 * width + hi]
        back = back_scr[:, lo:hi]
        weights = jnp.exp(
            dot_last(query, keys) + penalty - totals_scr[:, head : head + 1]
        )
        joined_scr[:, 2 * width + lo : 2 * width + hi] = dot_first(
            weights.astype(BF16), back
        ).astype(BF16)
        inner = jnp.sum(
            back.astype(F32) * context_scr[:, lo:hi].astype(F32), axis=-1, keepdims=True
        )
        score_grad = (weights * (dot_last(back, values) - inner)).astype(BF16)
        joined_scr[:, lo:hi] = (dot(score_grad, keys) * factor).astype(BF16)
        joined_scr[:, width + lo : width + hi] = dot_first(score_grad, query).astype(BF16)

    def attend_end(seq):
        joined = joined_scr[...]
        span = pl.ds(pl.multiple_of(lax.rem(seq, 2) * seqlen, seqlen), seqlen)
        part_two[span] = dot_last(joined, weight_ref[...]).astype(BF16)
        qkv_grad[...] += dot_first(first_scr[...], joined)
        bias_grad[0:1] += jnp.sum(joined.astype(F32), axis=0, keepdims=True)

        @pl.when(seq + 1 < seq_count)
        def more():
            for copy in chunk_loads(seq + 1):
                copy.start()

    def last(seq):
        grad = own_scr[:, :model_width]
        normal, scale = standard(own_tokens_ref[seq].astype(F32))
        rows_acc[3:4] += jnp.sum(grad * normal, axis=0, keepdims=True)
        rows_acc[4:5] += jnp.sum(grad, axis=0, keepdims=True)
        total = grad_scr[seq] + norm_back(grad, norm_ref[0:1], normal, scale)
        full_two[seq, pl.ds(pl.multiple_of(here * part, part), part)] = total.astype(BF16)

    def stage_copy(seq):
        span = pl.ds(pl.multiple_of(seq * seqlen, seqlen), seqlen)
        return pltpu.make_async_copy(full_two.at[seq], tokens_hbm.at[span], stage_sem.at[seq])

    def open_results():
        each_peer(lambda step, target, source: result_copy(step, target).wait_recv())

        def one(expert, carry):
            packed = result_home[expert]
            result_wide[expert, :, :LANES] = packed[:stride]
            tail = packed[stride:]
            result_wide[expert, :half, LANES:] = tail[:, :HEAD_DIM]
            result_wide[expert, half:, LANES:] = tail[2 * half - stride :, HEAD_DIM:]
            return carry

        lax.fori_loop(0, experts, one, 0)

    def combine(seq):
        span = pl.ds(pl.multiple_of(seq * seqlen, seqlen), seqlen)
        first = id_cols_ref[span, 0:1]
        second = id_cols_ref[span, 1:2]
        pltpu.make_async_copy(own_columns_hbm.at[span], columns_scr, columns_sem.at[0]).start()
        pltpu.make_async_copy(own_columns_hbm.at[span], columns_scr, columns_sem.at[0]).wait()
        first_gate = gate_cols_ref[span, 0:1]
        second_gate = gate_cols_ref[span, 1:2]

        def one(expert, total):
            slots = expert * stride + lax.broadcasted_iota(jnp.int32, (1, stride), 1)
            weights = jnp.where(
                first == slots, first_gate, jnp.where(second == slots, second_gate, 0.0)
            )
            return total + dot(weights.astype(BF16), result_wide[expert])

        block_ref[span] = lax.fori_loop(0, experts, one, columns_scr[...]).astype(BF16)

    qkv_rows = qkv_grad.shape[0] // experts
    out_rows = out_grad.shape[0] // experts

    def sum_copies(step, target):
        return (
            pltpu.make_async_remote_copy(
                src_ref=qkv_send.at[target],
                dst_ref=qkv_recv.at[me],
                send_sem=sum_send_sem.at[step, 0],
                recv_sem=sum_recv_sem.at[step, 0],
                **to_exp(target),
            ),
            pltpu.make_async_remote_copy(
                src_ref=out_send.at[target],
                dst_ref=out_recv.at[me],
                send_sem=sum_send_sem.at[step, 1],
                recv_sem=sum_recv_sem.at[step, 1],
                **to_exp(target),
            ),
        )

    def all_copies(step, target):
        return (
            pltpu.make_async_remote_copy(
                src_ref=qkv_all.at[me],
                dst_ref=qkv_all.at[me],
                send_sem=all_send_sem.at[step, 0],
                recv_sem=all_recv_sem.at[step, 0],
                **to_exp(target),
            ),
            pltpu.make_async_remote_copy(
                src_ref=out_all.at[me],
                dst_ref=out_all.at[me],
                send_sem=all_send_sem.at[step, 1],
                recv_sem=all_recv_sem.at[step, 1],
                **to_exp(target),
            ),
        )

    def all_arrivals(step, source):
        return (
            pltpu.make_async_remote_copy(
                src_ref=qkv_all.at[source],
                dst_ref=qkv_all.at[source],
                send_sem=all_send_sem.at[step, 0],
                recv_sem=all_recv_sem.at[step, 0],
                **to_exp(source),
            ),
            pltpu.make_async_remote_copy(
                src_ref=out_all.at[source],
                dst_ref=out_all.at[source],
                send_sem=all_send_sem.at[step, 1],
                recv_sem=all_recv_sem.at[step, 1],
                **to_exp(source),
            ),
        )

    def bias_copy(step, target):
        return pltpu.make_async_remote_copy(
            src_ref=bias_grad,
            dst_ref=bias_recv.at[me],
            send_sem=bias_send_sem.at[step],
            recv_sem=bias_recv_sem.at[step],
            **to_exp(target),
        )

    def start_sums():
        for block in range(experts):
            qkv_send[block] = qkv_grad[block * qkv_rows : (block + 1) * qkv_rows].astype(BF16)
            out_send[block] = out_grad[block * out_rows : (block + 1) * out_rows].astype(BF16)

        def begin(step, target, source):
            for copy in sum_copies(step, target):
                copy.start()
            bias_copy(step, target).start()

        each_peer(begin)
        qkv_recv[me] = qkv_send[me]
        out_recv[me] = out_send[me]
        bias_recv[me] = bias_grad[...]

    def spread_sums():
        def arrive(step, target, source):
            for copy in sum_copies(step, target):
                copy.wait_recv()
            bias_copy(step, target).wait_recv()

        each_peer(arrive)

        def add(source, totals):
            return (
                totals[0] + qkv_recv[source].astype(F32),
                totals[1] + out_recv[source].astype(F32),
                totals[2] + bias_recv[source],
            )

        qkv_total, out_total, bias_total = lax.fori_loop(
            1,
            experts,
            add,
            (qkv_recv[0].astype(F32), out_recv[0].astype(F32), bias_recv[0]),
        )
        qkv_all[me] = qkv_total.astype(BF16)
        out_all[me] = out_total.astype(BF16)
        bias_sum_ref[...] = bias_total

        def begin(step, target, source):
            for copy in all_copies(step, target):
                copy.start()

        each_peer(begin)

    def end_sums():
        def arrive(step, target, source):
            for copy in all_arrivals(step, source):
                copy.wait_recv()

        each_peer(arrive)
        for block in range(experts):
            qkv_sum_ref[block * qkv_rows : (block + 1) * qkv_rows] = qkv_all[block].astype(F32)
            out_sum_ref[block * out_rows : (block + 1) * out_rows] = out_all[block].astype(F32)

    def head_copy(step):
        return pltpu.make_async_remote_copy(
            src_ref=small_head.at[here],
            dst_ref=small_head.at[here],
            send_sem=head_send_sem.at[step],
            recv_sem=head_recv_sem.at[step],
            **to_head(lax.rem(here + step, head_parts)),
        )

    def head_arrival(step):
        source = lax.rem(here + head_parts - step, head_parts)
        return pltpu.make_async_remote_copy(
            src_ref=small_head.at[source],
            dst_ref=small_head.at[source],
            send_sem=head_send_sem.at[step],
            recv_sem=head_recv_sem.at[step],
            **to_head(source),
        )

    def small_copy(step, target):
        return pltpu.make_async_remote_copy(
            src_ref=small_recv.at[me],
            dst_ref=small_recv.at[me],
            send_sem=small_send_sem.at[step],
            recv_sem=small_recv_sem.at[step],
            **to_exp(target),
        )

    def small_arrival(step, source):
        return pltpu.make_async_remote_copy(
            src_ref=small_recv.at[source],
            dst_ref=small_recv.at[source],
            send_sem=small_send_sem.at[step],
            recv_sem=small_recv_sem.at[step],
            **to_exp(source),
        )

    heads = width // HEAD_DIM
    router_rows = small_head.shape[1] - 8

    second_start = 2 * ends
    spread_start = second_start + ends
    ticks = spread_start + ends + 1 + gap * (seq_count - 1)
    final = gap * (seq_count - 1)

    def tick(now, carry):
        def on(offset, action):
            since = now - offset

            @pl.when((since >= 0) & (lax.rem(since, gap) == 0) & (since < gap * seq_count))
            def run():
                action(since // gap)

        def first_end(seq):
            reduce_end(sums_ref, seq * seqlen, one_down, one_up, seq, model_width + LANES)
            middle(seq)

        def attend(seq):
            spread_hop(one_full, seq, ends)
            penalty = attend_start(seq)
            for head in range(heads):
                attend_head(head, penalty)
            attend_end(seq)

        def second_end(seq):
            reduce_end(part_two, lax.rem(seq, 2) * seqlen, two_down, two_up, seq, model_width)
            last(seq)

        def tokens_end(seq):
            spread_hop(two_full, seq, ends)
            stage_copy(seq).start()

        def own_begin(seq):
            for other in range(1, head_parts):
                own_copy(seq, other).start()

        on(ends, first_end)
        on(spread_start, second_end)
        for hop in range(ends):
            on(hop, lambda seq: reduce_hop(sums_ref, seq * seqlen, one_down, one_up, seq, hop))
            on(ends + hop, lambda seq: spread_hop(one_full, seq, hop))
            if hop > 0:
                on(
                    second_start + hop,
                    lambda seq: reduce_hop(
                        part_two, lax.rem(seq, 2) * seqlen, two_down, two_up, seq, hop
                    ),
                )
            on(spread_start + hop, lambda seq: spread_hop(two_full, seq, hop))
        on(0, own_begin)
        on(second_start, attend)
        on(
            second_start,
            lambda seq: reduce_hop(part_two, lax.rem(seq, 2) * seqlen, two_down, two_up, seq, 0),
        )

        @pl.when(now == 0)
        def send_results():
            each_peer(lambda step, target, source: result_copy(step, target).start())
            local = pltpu.make_async_copy(result_hbm.at[me], result_home.at[me], columns_sem.at[1])
            local.start()
            local.wait()

        @pl.when(now == ends + 1)
        def results():
            open_results()

        on(ends + 2, combine)

        @pl.when(now == final + second_start)
        def sums():
            start_sums()

        @pl.when(now == final + spread_start)
        def small():
            small_head[here, :8] = rows_acc[...]
            small_head[here, 8:] = router_acc[...].T[:router_rows]
            for other in range(1, head_parts):
                head_copy(other).start()

        @pl.when(now == final + spread_start + 1)
        def share():
            spread_sums()

        on(spread_start + ends, tokens_end)
        return carry

    lax.fori_loop(0, ticks, tick, 0)

    for other in range(1, head_parts):
        head_arrival(other).wait_recv()
    total = small_head[0]
    for other in range(1, head_parts):
        total = total + small_head[other]
    small_recv[me] = total
    each_peer(lambda step, target, source: small_copy(step, target).start())
    end_sums()
    each_peer(lambda step, target, source: small_arrival(step, source).wait_recv())
    small_ref[...] = lax.fori_loop(
        1, experts, lambda source, total: total + small_recv[source], small_recv[0]
    )
    for seq in range(seq_count):
        stage_copy(seq).wait()
        reduce_drain(one_down, one_up, seq)
        reduce_drain(two_down, two_up, seq)
        spread_drain(one_full, seq)
        spread_drain(two_full, seq)
    for other in range(1, head_parts):
        head_copy(other).wait_send()
        for seq in range(seq_count):
            own_copy(seq, other).wait_send()

    def sent(step, target, source):
        result_copy(step, target).wait_send()
        for copy in sum_copies(step, target):
            copy.wait_send()
        bias_copy(step, target).wait_send()
        for copy in all_copies(step, target):
            copy.wait_send()
        small_copy(step, target).wait_send()

    each_peer(sent)


def tail(
    sums, id_cols, gate_cols, own_residual, own_second, cot_own, own_columns, router, vectors,
    own_tokens, norm_rows, result, context, first, qkv, totals, flat_qkv, out_weight,
    segments, live, stride, half, part_half, head_parts,
):
    experts = result.shape[0]
    model_width = first.shape[1]
    seq_count, part = own_residual.shape[:2]
    seqlen = part * head_parts
    tok_count = seq_count * seqlen
    wide = flat_qkv.shape[1]
    width = wide // 3
    ends = head_parts - 1
    small_rows = 8 + round_up(experts, 8)
    dma = pltpu.SemaphoreType.DMA
    return pl.pallas_call(
        partial(tail_kernel, experts, stride, half, part_half, seq_count, head_parts, 2),
        in_specs=[whole()] * 5 + [anywhere()] * 2 + [whole()] * 4 + [anywhere()] * 5 + [whole()] * 4,
        out_specs=[anywhere()] + [whole()] * 5,
        out_shape=[
            shaped((tok_count, model_width), BF16),
            shaped((tok_count, width), BF16),
            shaped((model_width, wide), F32),
            shaped((width, model_width), F32),
            shaped((8, wide), F32),
            shaped((small_rows, model_width), F32),
        ],
        scratch_shapes=[
            pltpu.VMEM(cot_own.shape, BF16),
            pltpu.VMEM((part, model_width), BF16),
            pltpu.VMEM((seqlen, width), F32),
            pltpu.VMEM((2 * seqlen, model_width), BF16),
            pltpu.VMEM((seq_count, ends, part, model_width + LANES), BF16),
            pltpu.VMEM((seq_count, ends, part, model_width + LANES), BF16),
            pltpu.VMEM((seq_count, ends, part, model_width), BF16),
            pltpu.VMEM((seq_count, ends, part, model_width), BF16),
            pltpu.VMEM((part, model_width + LANES), F32),
            pltpu.VMEM((seq_count, seqlen, model_width), BF16),
            pltpu.VMEM((seq_count, seqlen, model_width), BF16),
            pltpu.VMEM((seq_count, part, model_width), F32),
            pltpu.VMEM((seqlen, width), BF16),
            pltpu.VMEM((seqlen, model_width), BF16),
            pltpu.VMEM((seqlen, wide), BF16),
            pltpu.VMEM((seqlen, LANES), F32),
            pltpu.VMEM((seqlen, width), BF16),
            pltpu.VMEM((seqlen, wide), BF16),
            pltpu.VMEM((model_width, wide), F32),
            pltpu.VMEM((width, model_width), F32),
            pltpu.VMEM((8, wide), F32),
            pltpu.VMEM((8, model_width), F32),
            pltpu.VMEM((model_width, LANES), F32),
            pltpu.VMEM((experts, stride + half, LANES), BF16),
            pltpu.VMEM((experts, stride, width), BF16),
            pltpu.VMEM((experts, model_width // experts, wide), BF16),
            pltpu.VMEM((experts, model_width // experts, wide), BF16),
            pltpu.VMEM((experts, model_width // experts, wide), BF16),
            pltpu.VMEM((experts, width // experts, model_width), BF16),
            pltpu.VMEM((experts, width // experts, model_width), BF16),
            pltpu.VMEM((experts, width // experts, model_width), BF16),
            pltpu.VMEM((experts, 8, wide), F32),
            pltpu.VMEM((head_parts, small_rows, model_width), F32),
            pltpu.VMEM((experts, small_rows, model_width), F32),
            dma((seq_count, head_parts)),
            dma((seq_count, head_parts)),
            dma((2,)),
            dma((4,)),
            dma((seq_count,)),
            dma((experts,)),
            dma((experts,)),
        ]
        + [dma((seq_count, ends))] * 8
        + [dma((seq_count, head_parts))] * 2
        + [dma((seq_count, head_parts, 2))] * 2
        + [dma((experts, 2))] * 4
        + [dma((experts,))] * 2
        + [dma((head_parts,))] * 2
        + [dma((experts,))] * 2,
        compiler_params=params(collective_id=2, has_side_effects=True),
        cost_estimate=cost(1e11, 1e8),
        name="tail",
    )(
        sums, id_cols, gate_cols, own_residual, own_second, cot_own, own_columns, router, vectors,
        own_tokens, norm_rows, result, context, first, qkv, totals, flat_qkv, out_weight,
        segments, live,
    )


def body(
    tokens,
    segments,
    live_mask,
    routes,
    priority,
    norm1_gain,
    norm1_bias,
    qkv_weight,
    qv_bias,
    out_weight,
    out_bias,
    norm2_gain,
    norm2_bias,
    router,
    up_weight,
    up_bias,
    down_weight,
    down_bias,
    cotangent,
):
    tok_count, model_width = tokens.shape
    seq_count, seqlen = segments.shape
    experts = lax.axis_size("exp")
    head_parts = lax.axis_size("head")
    head_index = lax.axis_index("head")
    quarter = model_width // head_parts
    capacity = (21 * tok_count + 10 * experts - 1) // (10 * experts)
    stride = round_up(capacity, 16)
    half = round_up(stride // 2, 16)
    local_width = qkv_weight.shape[2]

    def vector_rows(*vectors):
        rows = [v.astype(F32).reshape(1, -1) for v in vectors]
        rows.append(jnp.zeros((8 - len(rows), model_width), F32))
        return jnp.concatenate(rows, axis=0)

    norm_rows = vector_rows(norm1_gain, norm1_bias)
    vectors = vector_rows(out_bias, norm2_gain, norm2_bias)
    flat_qkv = qkv_weight.reshape(model_width, 3 * local_width)
    bias_row = jnp.concatenate(
        [qv_bias[0], jnp.zeros((local_width,), qv_bias.dtype), qv_bias[1]]
    ).astype(F32)[None]
    router_wide = jnp.pad(router, ((0, 0), (0, LANES - experts)))
    down_bias_row = lax.dynamic_update_slice_in_dim(
        jnp.zeros((1, model_width), F32), down_bias.astype(F32), head_index * quarter, 1
    )
    up, down = up_weight[0], down_weight[0]
    up_bias_row = up_bias.astype(F32)

    out_full_weight = lax.all_gather(out_weight, "head", axis=0, tiled=True)
    int_rows = jnp.concatenate(
        [
            routes.T,
            live_mask.reshape(1, tok_count),
            priority,
            jnp.zeros((4, tok_count), jnp.int32),
        ],
        axis=0,
    )
    part_half = round_up(seqlen // head_parts // 2, 16)
    first, qkv, context, totals, gathered, ids, cot_slots, cot_own, own_tokens = head(
        tokens, norm_rows, flat_qkv, bias_row, segments, live_mask, priority.reshape(tok_count, 1),
        int_rows, cotangent, experts, capacity, stride, half, part_half, head_parts,
    )
    id_cols = ids.T
    own_residual, own_second, own_columns, gates, arrived, hidden, result, gate_col, cot_rows = forward(
        gathered, tokens, vectors, out_full_weight, router_wide, int_rows, ids,
        up, up_bias_row, down, down_bias_row, cot_slots, experts, stride, half, seq_count, head_parts,
    )
    gate_cols = gates.T
    own_result = lax.psum_scatter(result, "head", scatter_dimension=0, tiled=True)[0]
    sums, grad_up, grad_up_bias, grad_down, grad_down_bias = backward(
        arrived, hidden, result, cot_rows, gate_col, id_cols, up, up_bias_row, down, half, head_parts,
        seqlen,
    )
    grad_tokens, block_out, qkv_grad, out_grad, bias_grad, small = tail(
        sums, id_cols, gate_cols, own_residual, own_second, cot_own, own_columns,
        router_wide, vectors, own_tokens, norm_rows, own_result, context, first, qkv, totals,
        flat_qkv, out_weight, segments, live_mask, stride, half, part_half, head_parts,
    )
    grad_qv_bias = jnp.concatenate(
        [bias_grad[0:1, :local_width], bias_grad[0:1, 2 * local_width :]], axis=0
    )
    return (
        block_out,
        grad_tokens.astype(F32),
        small[3],
        small[4],
        qkv_grad.reshape(model_width, 3, local_width),
        grad_qv_bias,
        out_grad,
        small[2],
        small[0],
        small[1],
        small[8 : 8 + experts].T,
        grad_up[None],
        grad_up_bias[0:1],
        grad_down[None],
        lax.dynamic_slice_in_dim(grad_down_bias[0:1], head_index * quarter, quarter, 1),
    )


def solution(mesh):
    in_specs = (
        P("exp", None),
        P("exp", None),
        P("exp", None),
        P("exp", None),
        P("exp", None),
        P(),
        P(),
        P(None, None, "head"),
        P(None, "head"),
        P("head", None),
        P(),
        P(),
        P(),
        P(),
        P("exp", None, "head"),
        P("exp", "head"),
        P("exp", "head", None),
        P("exp", "head"),
        P("exp", "head"),
    )
    out_specs = (
        P("exp", "head"),
        P("exp", None),
        P(),
        P(),
        P(None, None, "head"),
        P(None, "head"),
        P("head", None),
        P(),
        P(),
        P(),
        P(),
        P("exp", None, "head"),
        P("exp", "head"),
        P("exp", "head", None),
        P("exp", "head"),
    )
    return jax.shard_map(body, mesh=mesh, in_specs=in_specs, out_specs=out_specs, check_vma=False)
```

```python
from functools import partial
import math

import jax
import jax.numpy as jnp
from jax import lax
from jax.experimental import pallas as pl
from jax.experimental.pallas import tpu as pltpu
from jax.sharding import PartitionSpec as P

HEAD_DIM = 64
LANES = 128
EPSILON = 1e-06
NEGATIVE = -1e30
CONTRACT_FIRST = (((0,), (0,)), ((), ()))
CONTRACT_LAST = (((1,), (1,)), ((), ()))
F32 = jnp.float32
BF16 = jnp.bfloat16
MESH = pl.DeviceIdType.MESH
VMEM_LIMIT = 54 * 1024 * 1024


def round_up(number, step):
    return (number + step - 1) // step * step


def whole():
    return pl.BlockSpec(memory_space=pltpu.VMEM)


def anywhere():
    return pl.BlockSpec(memory_space=pl.ANY)


def shaped(shape, dtype):
    return jax.ShapeDtypeStruct(shape, dtype)


def params(**more):
    return pltpu.CompilerParams(vmem_limit_bytes=VMEM_LIMIT, **more)


def cost(flops, moved):
    return pl.CostEstimate(flops=int(flops), bytes_accessed=int(moved), transcendentals=0)


def dot(left, right):
    return jnp.dot(left, right, preferred_element_type=F32)


def dot_last(left, right):
    return lax.dot_general(left, right, CONTRACT_LAST, preferred_element_type=F32)


def dot_first(left, right):
    return lax.dot_general(left, right, CONTRACT_FIRST, preferred_element_type=F32)


def standard(values):
    centred = values - jnp.mean(values, axis=-1, keepdims=True)
    scale = lax.rsqrt(jnp.mean(centred * centred, axis=-1, keepdims=True) + EPSILON)
    return centred * scale, scale


def norm_back(grad_rows, gain_row, normal, scale):
    inner = grad_rows * gain_row
    return scale * (
        inner
        - jnp.mean(inner, axis=-1, keepdims=True)
        - normal * jnp.mean(inner * normal, axis=-1, keepdims=True)
    )


def diagonal_of(count):
    return lax.broadcasted_iota(jnp.int32, (count, count), 0) == lax.broadcasted_iota(
        jnp.int32, (count, count), 1
    )


def as_column(row, diagonal):
    return jnp.sum(jnp.where(diagonal, row.astype(F32), 0.0), axis=1, keepdims=True)


def mask_penalty(seg_row, live_row):
    diagonal = diagonal_of(seg_row.shape[1])
    same = as_column(seg_row, diagonal) == seg_row.astype(F32)
    return jnp.where(same & ((live_row > 0) | diagonal), 0.0, NEGATIVE)


def pack_rows(rows, half):
    count = rows.shape[0]
    third = rows[:, LANES:]
    return rows[:, :LANES], jnp.concatenate([third[:half], third[count - half :]], axis=1)


def unpack_rows(parts_of, into, head_parts, count, half):
    extra = HEAD_DIM
    width = LANES + extra
    for z in range(head_parts):
        packed = parts_of(z)
        into[:, z * width : z * width + LANES] = packed[:count]
        tail = packed[count : count + half]
        into[:half, z * width + LANES : (z + 1) * width] = tail[:, :extra]
        into[half:, z * width + LANES : (z + 1) * width] = tail[2 * half - count :, extra:]


def greet(peers):
    barrier = pltpu.get_barrier_semaphore()
    me = lax.axis_index("exp")
    here = lax.axis_index("head")

    def call(step, carry):
        other = lax.rem(me + step, peers)
        pl.semaphore_signal(barrier, inc=1, device_id=(other, here), device_id_type=MESH)
        return carry

    lax.fori_loop(1, peers, call, 0)
    return barrier


def greet_both(peers, head_parts):
    barrier = greet(peers)
    me = lax.axis_index("exp")
    here = lax.axis_index("head")

    def call(step, carry):
        other = lax.rem(here + step, head_parts)
        pl.semaphore_signal(barrier, inc=1, device_id=(me, other), device_id_type=MESH)
        return carry

    lax.fori_loop(1, head_parts, call, 0)
    return barrier


def head_kernel(
    experts, capacity, stride, half, part_half, seq_count, head_parts,
    tokens_ref, norm_ref, weight_ref, bias_ref, seg_ref, live_ref, rows_ref, cot_ref, out_weight_ref,
    first_hbm, qkv_hbm, context_hbm, total_hbm, out_full_ref, gathered_ref, ids_ref, cot_recv, own_send, own_tokens_ref,
    cot_send, first_scr, qkv_scr, context_scr, total_scr,
    gather_sem, gather_out, cot_send_sem, cot_recv_sem, store_sem,
    weight_sem, weight_out, pair_send_sem, pair_recv_sem,
):
    me = lax.axis_index("exp")
    here = lax.axis_index("head")
    barrier = greet_both(experts, head_parts)
    ends = head_parts - 1
    tok_count = tokens_ref.shape[0]
    seqlen = tok_count // seq_count
    part = seqlen // head_parts
    pl.semaphore_wait(barrier, experts - 1 + ends)

    def own_rows():
        for seq in range(seq_count):
            own = pl.ds(pl.multiple_of(seq * seqlen + here * part, part), part)
            own_tokens_ref[seq] = tokens_ref[own]
            for z in range(head_parts):
                start = seq * seqlen + z * part
                wide, tail = pack_rows(cot_ref[start : start + part], part_half)
                own_send[z, seq, :part] = wide
                own_send[z, seq, part:] = tail

    core = lax.rem(me, 2)
    weight_rows = out_weight_ref.shape[0]
    half_rows = weight_rows // 2

    def weight_span(shard, which):
        start = pl.multiple_of(shard * weight_rows + which * half_rows, 16)
        return pl.ds(start, half_rows)

    def weight_copy(shard, side):
        rows = weight_span(shard, core)
        return pltpu.make_async_remote_copy(
            src_ref=out_full_ref.at[rows],
            dst_ref=out_full_ref.at[rows],
            send_sem=weight_out.at[shard, side],
            recv_sem=weight_sem.at[shard],
            device_id=(me, here + 1 - 2 * side),
            device_id_type=MESH,
        )

    def pair_copy(step, which):
        rows = weight_span(lax.rem(here + step, head_parts), which)
        return pltpu.make_async_remote_copy(
            src_ref=out_full_ref.at[rows],
            dst_ref=out_full_ref.at[rows],
            send_sem=pair_send_sem.at[step],
            recv_sem=pair_recv_sem.at[step],
            device_id=(me + 1 - 2 * core, here),
            device_id_type=MESH,
        )

    def weight_hop(hop):
        def one(side, shard, there, onward):
            @pl.when(there)
            def arrived():
                if hop > 0:
                    weight_copy(shard, side).wait_recv()
                if hop < ends:

                    @pl.when(onward)
                    def pass_on():
                        weight_copy(shard, side).start()

        each_side(hop, one)
        if hop == ends:
            for step in range(1, head_parts):
                pair_copy(step, core).start()

    def stores(seq):
        slot = lax.rem(seq, 2)
        span = pl.ds(pl.multiple_of(seq * seqlen, seqlen), seqlen)
        return (
            pltpu.make_async_copy(first_scr.at[slot], first_hbm.at[span], store_sem.at[slot, 0]),
            pltpu.make_async_copy(qkv_scr.at[slot], qkv_hbm.at[span], store_sem.at[slot, 1]),
            pltpu.make_async_copy(context_scr.at[slot], context_hbm.at[span], store_sem.at[slot, 2]),
            pltpu.make_async_copy(total_scr.at[slot], total_hbm.at[span], store_sem.at[slot, 3]),
        )

    def attend(seq):
        slot = lax.rem(seq, 2)
        span = pl.ds(pl.multiple_of(seq * seqlen, seqlen), seqlen)

        @pl.when(seq >= 2)
        def free():
            for copy in stores(seq - 2):
                copy.wait()

        normal, ignored = standard(tokens_ref[span].astype(F32))
        first = (normal * norm_ref[0:1] + norm_ref[1:2]).astype(BF16)
        first_scr[slot] = first
        bias = bias_ref[...].astype(F32)
        bias_row = jnp.concatenate([bias[0:1], jnp.zeros_like(bias[0:1]), bias[1:2]], axis=1)
        rows = (dot(first, weight_ref[...]) + bias_row).astype(BF16)
        qkv_scr[slot] = rows
        penalty = mask_penalty(seg_ref[pl.ds(seq, 1)], live_ref[pl.ds(seq, 1)])
        width = rows.shape[1] // 3
        parts = []
        for head in range(width // HEAD_DIM):
            lo = head * HEAD_DIM
            hi = lo + HEAD_DIM
            query = rows[:, lo:hi] * BF16(1.0 / math.sqrt(HEAD_DIM))
            scores = dot_last(query, rows[:, width + lo : width + hi]) + penalty
            largest = jnp.max(scores, axis=-1, keepdims=True)
            weights = jnp.exp(scores - largest)
            total = jnp.sum(weights, axis=-1, keepdims=True)
            values = rows[:, 2 * width + lo : 2 * width + hi]
            parts.append((dot(weights.astype(BF16), values) / total).astype(BF16))
            total_scr[slot, :, head : head + 1] = largest + jnp.log(total)
        context = jnp.concatenate(parts, axis=1)
        context_scr[slot] = context
        for copy in stores(seq):
            copy.start()
        wide, tail = pack_rows(context, seqlen // 2)
        gathered_ref[here, seq, :seqlen] = wide
        gathered_ref[here, seq, seqlen:] = tail

    def full_copy(seq, shard, side):
        return pltpu.make_async_remote_copy(
            src_ref=gathered_ref.at[shard, seq],
            dst_ref=gathered_ref.at[shard, seq],
            send_sem=gather_out.at[seq, shard, side],
            recv_sem=gather_sem.at[seq, shard],
            device_id=(me, here + 1 - 2 * side),
            device_id_type=MESH,
        )

    def each_side(hop, action):
        for side in range(2):
            shard = here - hop if side == 0 else here + hop
            there = shard >= 0 if side == 0 else shard <= ends
            onward = here < ends if side == 0 else here > 0
            action(side, shard, there, onward)

    def spread_hop(seq, hop):
        def one(side, shard, there, onward):
            @pl.when(there)
            def arrived():
                if hop > 0:
                    full_copy(seq, shard, side).wait_recv()
                if hop < ends:

                    @pl.when(onward)
                    def pass_on():
                        full_copy(seq, shard, side).start()

        each_side(hop, one)

    def spread_drain(seq):
        def one(side, shard, there, onward):
            @pl.when(there & onward)
            def sent():
                full_copy(seq, shard, side).wait_send()

        for hop in range(ends):
            each_side(hop, one)

    numbers = lax.broadcasted_iota(jnp.int32, (experts, 1), 0)

    def hot(rows):
        live = rows[2:3] > 0
        first = jnp.where((rows[0:1] == numbers) & live, 1.0, 0.0)
        second = jnp.where((rows[1:2] == numbers) & live, 1.0, 0.0)
        return first, second

    def tables():
        rank_row = rows_ref[3:4].astype(F32)
        diagonal = diagonal_of(seqlen)
        counts = jnp.zeros((2 * experts, tok_count), F32)
        for start in range(0, tok_count, seqlen):
            first, second = hot(rows_ref[:, start : start + seqlen])
            rank_col = as_column(rank_row[:, start : start + seqlen], diagonal)
            earlier = jnp.where(rank_col < rank_row, 1.0, 0.0)
            both = jnp.concatenate([first, second], axis=0)
            counts = counts + dot(both.astype(BF16), earlier.astype(BF16))
        first, second = hot(rows_ref[...])
        total = jnp.sum(first, axis=1, keepdims=True)
        places = [
            jnp.sum(first * counts[:experts], axis=0, keepdims=True),
            jnp.sum(second * (counts[experts:] + total), axis=0, keepdims=True),
        ]
        for pick in range(2):
            place = places[pick].astype(jnp.int32)
            kept = (place < capacity) & (rows_ref[2:3] > 0)
            ids_ref[pick : pick + 1] = jnp.where(
                kept, rows_ref[pick : pick + 1] * stride + place, -1
            )
        ids_ref[2:8] = jnp.full((6, tok_count), -1, jnp.int32)

    def cot_copy(step, target):
        return pltpu.make_async_remote_copy(
            src_ref=cot_send.at[target],
            dst_ref=cot_recv.at[me],
            send_sem=cot_send_sem.at[step],
            recv_sem=cot_recv_sem.at[step],
            device_id=(target, here),
            device_id_type=MESH,
        )

    def fill(target):
        slots = target * stride + lax.broadcasted_iota(jnp.int32, (stride, 1), 0)
        hit = (ids_ref[0:1] == slots) | (ids_ref[1:2] == slots)
        block = dot(jnp.where(hit, 1.0, 0.0).astype(BF16), cot_ref[...]).astype(BF16)
        return pack_rows(block, half)

    def dispatch():
        def one(step, carry):
            target = lax.rem(me + step, experts)
            wide, tail = fill(target)
            cot_send[target, :stride] = wide
            cot_send[target, stride:] = tail
            cot_copy(step, target).start()
            return carry

        lax.fori_loop(1, experts, one, 0)
        wide, tail = fill(me)
        cot_recv[me, :stride] = wide
        cot_recv[me, stride:] = tail

    out_full_ref[pl.ds(pl.multiple_of(here * weight_rows, 16), weight_rows)] = out_weight_ref[...]
    weight_hop(0)

    def time_step(step, carry):
        for hop in range(1, ends + 1):

            @pl.when(step == hop)
            def weights():
                weight_hop(hop)

        @pl.when(step == seq_count + 1)
        def send():
            dispatch()

        for hop in range(ends, 0, -1):

            @pl.when((step >= hop) & (step - hop < seq_count))
            def move():
                spread_hop(step - hop, hop)

        @pl.when(step < seq_count)
        def work():
            attend(step)
            spread_hop(step, 0)

        @pl.when(step == seq_count)
        def places():
            tables()

        @pl.when(step == seq_count + 1)
        def rows():
            own_rows()

        return carry

    lax.fori_loop(0, seq_count + ends, time_step, 0)
    for seq in range(seq_count):
        spread_drain(seq)
    for seq in range(max(seq_count - 2, 0), seq_count):
        for copy in stores(seq):
            copy.wait()

    def sent(side, shard, there, onward):
        @pl.when(there & onward)
        def drain():
            weight_copy(shard, side).wait_send()

    for hop in range(ends):
        each_side(hop, sent)
    for step in range(1, head_parts):
        pair_copy(step, core).wait_send()
        pair_copy(step, 1 - core).wait_recv()

    def finish(step, carry):
        cot_copy(step, lax.rem(me + step, experts)).wait()
        return carry

    lax.fori_loop(1, experts, finish, 0)


def head(
    tokens, vectors, flat_qkv, qv_bias, segments, live, rows, cotangent, out_weight,
    experts, capacity, stride, half, part_half, head_parts,
):
    tok_count, model_width = tokens.shape
    seq_count, seqlen = segments.shape
    part = seqlen // head_parts
    wide = flat_qkv.shape[1]
    width = wide // 3
    dma = pltpu.SemaphoreType.DMA
    own = (head_parts, seq_count, part + part_half, LANES)
    slots = (experts, stride + half, LANES)
    return pl.pallas_call(
        partial(head_kernel, experts, capacity, stride, half, part_half, seq_count, head_parts),
        in_specs=[whole()] * 9,
        out_specs=[anywhere()] * 4 + [whole()] * 6,
        out_shape=[
            shaped((tok_count, model_width), BF16),
            shaped((tok_count, wide), BF16),
            shaped((tok_count, width), BF16),
            shaped((tok_count, LANES), F32),
            shaped((head_parts * out_weight.shape[0], model_width), BF16),
            shaped((head_parts, seq_count, seqlen + seqlen // 2, LANES), BF16),
            shaped((8, tok_count), jnp.int32),
            shaped(slots, BF16),
            shaped(own, BF16),
            shaped((seq_count, part, model_width), BF16),
        ],
        scratch_shapes=[
            pltpu.VMEM(slots, BF16),
            pltpu.VMEM((2, seqlen, model_width), BF16),
            pltpu.VMEM((2, seqlen, wide), BF16),
            pltpu.VMEM((2, seqlen, width), BF16),
            pltpu.VMEM((2, seqlen, LANES), F32),
            dma((seq_count, head_parts)),
            dma((seq_count, head_parts, 2)),
            dma((experts,)),
            dma((experts,)),
            dma((2, 4)),
            dma((head_parts,)),
            dma((head_parts, 2)),
            dma((head_parts,)),
            dma((head_parts,)),
        ],
        compiler_params=params(collective_id=3, has_side_effects=True),
        cost_estimate=cost(6e10, 1e7),
        name="head",
    )(tokens, vectors, flat_qkv, qv_bias, segments, live, rows, cotangent, out_weight)


def gelu_parts(pre):
    root = math.sqrt(2.0 / math.pi)
    square = pre * pre
    wave = jnp.tanh(root * (pre + 0.044715 * pre * square))
    half_sum = 0.5 * (1.0 + wave)
    slope = half_sum + 0.5 * pre * (1.0 - wave * wave) * (
        root * (1.0 + 3.0 * 0.044715 * square)
    )
    return pre * half_sum, slope


def forward_kernel(
    experts, stride, half, seq_count, head_parts,
    gathered_ref, tokens_ref, vectors_ref, out_weight_ref, router_ref, rows_ref, ids_ref,
    up_ref, up_bias_ref, down_ref, down_bias_ref, cot_hbm,
    own_residual_ref, own_second_ref, own_columns_ref, gates_ref, arrived_hbm, hidden_hbm, result_hbm,
    gate_col_ref, cot_all, arrived_ref, hidden_scr, result_scr, residual_ref, context_scr, second_scr, logit_scr, send_scr, gate_send, gate_recv,
    send_sem, recv_sem, gate_send_sem, gate_recv_sem, cot_sem, cot_out, local_sem,
    arrived_sem, store_sem,
):
    me = lax.axis_index("exp")
    here = lax.axis_index("head")
    barrier = greet_both(experts, head_parts)
    ends = head_parts - 1
    pieces = cot_sem.shape[1]
    piece_rows = experts // pieces
    tok_count = tokens_ref.shape[0]

    def cot_copy(shard, piece, side, own=False):
        span = pl.ds(piece * piece_rows, piece_rows)
        return pltpu.make_async_remote_copy(
            src_ref=cot_hbm.at[span] if own else cot_all.at[shard, span],
            dst_ref=cot_all.at[shard, span],
            send_sem=cot_out.at[shard, piece, side],
            recv_sem=cot_sem.at[shard, piece],
            device_id=(me, here + 1 - 2 * side),
            device_id_type=MESH,
        )

    def cot_side(hop, side):
        shard = here - hop if side == 0 else here + hop
        there = shard >= 0 if side == 0 else shard <= ends
        onward = here < ends if side == 0 else here > 0
        return shard, there, onward

    def cot_hop(hop, piece):
        for side in range(2):
            shard, there, onward = cot_side(hop, side)

            @pl.when(there)
            def arrived():
                if hop > 0:
                    cot_copy(shard, piece, side).wait_recv()
                if hop < ends:

                    @pl.when(onward)
                    def pass_on():
                        cot_copy(shard, piece, side, hop == 0).start()

    def cot_drain(hop, piece):
        for side in range(2):
            shard, there, onward = cot_side(hop, side)

            @pl.when(there & onward)
            def sent():
                cot_copy(shard, piece, side, hop == 0).wait_send()

    local = pltpu.make_async_copy(cot_hbm, cot_all.at[here], local_sem.at[0])
    local.start()
    pl.semaphore_wait(barrier, experts - 1 + ends)
    for piece in range(pieces):
        cot_hop(0, piece)
    seqlen = tok_count // seq_count
    for seq in range(seq_count):
        span = slice(seq * seqlen, (seq + 1) * seqlen)
        unpack_rows(lambda z: gathered_ref[z, seq], context_scr, head_parts, seqlen, seqlen // 2)
        residual = (
            tokens_ref[span].astype(F32)
            + dot(context_scr[...], out_weight_ref[...])
            + vectors_ref[2:3]
        )
        residual_ref[span] = residual
        normal, ignored = standard(residual)
        second = (normal * vectors_ref[3:4] + vectors_ref[4:5]).astype(BF16)
        second_scr[span] = second
        logit_scr[:, span] = dot(second, router_ref[...]).T[:experts]
    part = seqlen // head_parts
    for seq in range(seq_count):
        own = pl.ds(pl.multiple_of(seq * seqlen + here * part, part), part)
        own_residual_ref[seq] = residual_ref[own]
        own_second_ref[seq] = second_scr[own]
    width = residual_ref.shape[1] // head_parts
    for z in range(head_parts):

        @pl.when(here == z)
        def columns():
            own_columns_ref[...] = residual_ref[:, z * width : (z + 1) * width]


    logits = logit_scr[...]
    powers = jnp.exp(logits - jnp.max(logits, axis=0, keepdims=True))
    chances = powers / jnp.sum(powers, axis=0, keepdims=True)
    numbers = lax.broadcasted_iota(jnp.int32, (experts, 1), 0)
    for pick in range(2):
        chosen = jnp.where(rows_ref[pick : pick + 1] == numbers, chances, 0.0)
        gate = jnp.where(ids_ref[pick : pick + 1] >= 0, jnp.sum(chosen, axis=0, keepdims=True), 0.0)
        gates_ref[pick : pick + 1] = gate
    gates_ref[2:8] = jnp.zeros((6, tok_count), F32)

    def copies(target, step):
        to = dict(device_id=(target, here), device_id_type=MESH)
        return (
            pltpu.make_async_remote_copy(
                src_ref=send_scr.at[step],
                dst_ref=arrived_ref.at[me],
                send_sem=send_sem.at[step],
                recv_sem=recv_sem.at[step],
                **to,
            ),
            pltpu.make_async_remote_copy(
                src_ref=gate_send.at[step],
                dst_ref=gate_recv.at[me],
                send_sem=gate_send_sem.at[step],
                recv_sem=gate_recv_sem.at[step],
                **to,
            ),
        )

    def fill(target):
        slots = target * stride + lax.broadcasted_iota(jnp.int32, (stride, 1), 0)
        first = ids_ref[0:1] == slots
        second = ids_ref[1:2] == slots
        block = dot(jnp.where(first | second, 1.0, 0.0).astype(BF16), second_scr[...]).astype(BF16)
        gate = jnp.sum(
            jnp.where(first, gates_ref[0:1], jnp.where(second, gates_ref[1:2], 0.0)),
            axis=1,
            keepdims=True,
        )
        return block, jnp.broadcast_to(gate, (stride, LANES)).T[:8]

    def send(step, carry):
        target = lax.rem(me + step, experts)
        block, gate = fill(target)
        send_scr[step] = block
        gate_send[step] = gate
        for copy in copies(target, step):
            copy.start()
        return carry

    lax.fori_loop(1, experts, send, 0)
    block, gate = fill(me)
    arrived_ref[me] = block
    gate_recv[me] = gate

    def source_of(step):
        return lax.rem(me + experts - step, experts)

    def arrived_store(step):
        source = source_of(step)
        return pltpu.make_async_copy(
            arrived_ref.at[source], arrived_hbm.at[source], arrived_sem.at[step]
        )

    def stores(step):
        source = source_of(step)
        slot = lax.rem(step, 2)
        return (
            pltpu.make_async_copy(hidden_scr.at[slot], hidden_hbm.at[source], store_sem.at[slot, 0]),
            pltpu.make_async_copy(result_scr.at[slot], result_hbm.at[:, source], store_sem.at[slot, 1]),
        )

    def work(step):
        source = source_of(step)
        slot = lax.rem(step, 2)
        arrived_store(step).start()
        pre = dot(arrived_ref[source], up_ref[...]) + up_bias_ref[...].astype(F32)
        hidden = gelu_parts(pre)[0].astype(BF16)
        result = dot(hidden, down_ref[...])
        down_bias = down_bias_ref[...].astype(F32)

        @pl.when(step >= 2)
        def free():
            for copy in stores(step - 2):
                copy.wait()

        hidden_scr[slot] = hidden
        for z in range(head_parts):
            columns = result[:, z * width : (z + 1) * width] + jnp.where(here == z, down_bias, 0.0)
            wide, tail = pack_rows(columns.astype(BF16), half)
            result_scr[slot, z, :stride] = wide
            result_scr[slot, z, stride:] = tail
        for copy in stores(step):
            copy.start()

    work(0)
    moves = [(hop, piece) for hop in range(1, ends) for piece in range(pieces)]
    early = len(moves) - min(experts - 2, len(moves))
    for move in moves[:early]:
        cot_hop(*move)

    def receive(step, carry):
        for place, move in enumerate(moves[early:]):

            @pl.when(step == place + 1)
            def pass_on():
                cot_hop(*move)

        source = lax.rem(me + experts - step, experts)
        wide, narrow = copies(source, step)
        wide.wait_recv()
        narrow.wait_recv()
        work(step)
        return carry

    lax.fori_loop(1, experts, receive, 0)

    for step in (experts - 2, experts - 1):
        for copy in stores(step):
            copy.wait()

    def stored(step, carry):
        arrived_store(step).wait()
        return carry

    lax.fori_loop(0, experts, stored, 0)

    def finish(step, carry):
        for copy in copies(lax.rem(me + step, experts), step):
            copy.wait_send()
        return carry

    lax.fori_loop(1, experts, finish, 0)
    for piece in range(pieces):
        cot_hop(ends, piece)
        for hop in range(ends):
            cot_drain(hop, piece)
    local.wait()
    lane = lax.broadcasted_iota(jnp.int32, (LANES, stride), 0)
    square = jnp.zeros((LANES, stride), F32)
    for source in range(experts):
        square = jnp.where(lane == source, gate_recv[source, 0:1], square)
    gate_col_ref[...] = square.T


def forward(
    gathered, tokens, vectors, out_weight, router, rows, ids, up, up_bias, down, down_bias, cot_slots,
    experts, stride, half, seq_count, head_parts,
):
    tok_count, model_width = tokens.shape
    seqlen = tok_count // seq_count
    part = seqlen // head_parts
    return pl.pallas_call(
        partial(forward_kernel, experts, stride, half, seq_count, head_parts),
        in_specs=[whole()] * 11 + [anywhere()],
        out_specs=[whole()] * 4 + [anywhere()] * 3 + [whole()] + [anywhere()],
        out_shape=[
            shaped((seq_count, part, model_width), F32),
            shaped((seq_count, part, model_width), BF16),
            shaped((tok_count, model_width // head_parts), F32),
            shaped((8, tok_count), F32),
            shaped((experts, stride, model_width), BF16),
            shaped((experts, stride, up.shape[1]), BF16),
            shaped((head_parts, experts, stride + half, LANES), BF16),
            shaped((stride, LANES), F32),
            shaped((head_parts, experts, stride + half, LANES), BF16),
        ],
        scratch_shapes=[
            pltpu.VMEM((experts, stride, model_width), BF16),
            pltpu.VMEM((2, stride, up.shape[1]), BF16),
            pltpu.VMEM((2, head_parts, stride + half, LANES), BF16),
            pltpu.VMEM((tok_count, model_width), F32),
            pltpu.VMEM((seqlen, model_width), BF16),
            pltpu.VMEM((tok_count, model_width), BF16),
            pltpu.VMEM((experts, tok_count), F32),
            pltpu.VMEM((experts, stride, model_width), BF16),
            pltpu.VMEM((experts, 8, stride), F32),
            pltpu.VMEM((experts, 8, stride), F32),
            pltpu.SemaphoreType.DMA((experts,)),
            pltpu.SemaphoreType.DMA((experts,)),
            pltpu.SemaphoreType.DMA((experts,)),
            pltpu.SemaphoreType.DMA((experts,)),
            pltpu.SemaphoreType.DMA((head_parts, 4)),
            pltpu.SemaphoreType.DMA((head_parts, 4, 2)),
            pltpu.SemaphoreType.DMA((1,)),
            pltpu.SemaphoreType.DMA((experts,)),
            pltpu.SemaphoreType.DMA((2, 2)),
        ],
        compiler_params=params(collective_id=0, has_side_effects=True),
        cost_estimate=cost(8e10, 1e8),
        name="forward",
    )(gathered, tokens, vectors, out_weight, router, rows, ids, up, up_bias, down, down_bias, cot_slots)


def backward_kernel(
    experts, stride, half, head_parts, chunk,
    arrived_hbm, hidden_hbm, result_hbm, cot_hbm, gate_col_ref, ids_ref, up_ref, up_bias_ref, down_ref,
    sums_ref, grad_up_ref, grad_up_bias_ref, grad_down_ref, grad_down_bias_ref,
    rows_scr, result_scr, cot_scr, cot_wide, result_wide, hidden_scr, pre_grad_scr, out_grad_scr,
    send_scr, recv_scr, gate_send, gate_recv, total_scr,
    load_sem, send_sem, recv_sem, gate_send_sem, gate_recv_sem,
):
    me = lax.axis_index("exp")
    here = lax.axis_index("head")
    barrier = greet(experts)
    tok_count = ids_ref.shape[0]
    model_width = up_ref.shape[0]

    def loads(step):
        home = lax.rem(me + step, experts)
        slot = lax.rem(step, 2)
        return (
            pltpu.make_async_copy(arrived_hbm.at[home], rows_scr.at[slot], load_sem.at[slot, 0]),
            pltpu.make_async_copy(result_hbm.at[:, home], result_scr.at[slot], load_sem.at[slot, 1]),
            pltpu.make_async_copy(cot_hbm.at[:, home], cot_scr.at[slot], load_sem.at[slot, 2]),
        )

    def copies(target, step):
        to = dict(device_id=(target, here), device_id_type=MESH)
        return (
            pltpu.make_async_remote_copy(
                src_ref=send_scr.at[step],
                dst_ref=recv_scr.at[me],
                send_sem=send_sem.at[step],
                recv_sem=recv_sem.at[step],
                **to,
            ),
            pltpu.make_async_remote_copy(
                src_ref=gate_send.at[step],
                dst_ref=gate_recv.at[me],
                send_sem=gate_send_sem.at[step],
                recv_sem=gate_recv_sem.at[step],
                **to,
            ),
        )

    for copy in loads(1):
        copy.start()
    grad_up_ref[...] = jnp.zeros_like(grad_up_ref)
    grad_down_ref[...] = jnp.zeros_like(grad_down_ref)
    grad_up_bias_ref[...] = jnp.zeros_like(grad_up_bias_ref)
    grad_down_bias_ref[...] = jnp.zeros_like(grad_down_bias_ref)
    total_scr[...] = jnp.zeros_like(total_scr)
    pl.semaphore_wait(barrier, experts - 1)

    def work(step):
        home = lax.rem(me + step, experts)
        slot = lax.rem(step, 2)
        for copy in loads(step):
            copy.wait()
        unpack_rows(lambda z: cot_scr[slot, z], cot_wide, head_parts, stride, half)
        unpack_rows(lambda z: result_scr[slot, z], result_wide, head_parts, stride, half)
        out_rows = cot_wide[...].astype(F32)
        pre = dot(rows_scr[slot], up_ref[...]) + up_bias_ref[...].astype(F32)
        slope = gelu_parts(pre)[1]
        lane = lax.broadcasted_iota(jnp.int32, (stride, LANES), 1)
        gate = jnp.sum(jnp.where(lane == home, gate_col_ref[...], 0.0), axis=1, keepdims=True)
        out_grad = (gate * out_rows).astype(BF16)
        out_grad_scr[step] = out_grad
        grad_down_bias_ref[0:1] += jnp.sum(out_grad.astype(F32), axis=0, keepdims=True)
        pre_grad = (dot_last(out_grad, down_ref[...]) * slope).astype(BF16)
        pre_grad_scr[step] = pre_grad
        grad_up_bias_ref[0:1] += jnp.sum(pre_grad.astype(F32), axis=0, keepdims=True)
        gate_grad = jnp.sum(result_wide[...].astype(F32) * out_rows, axis=1, keepdims=True)
        return (
            dot_last(pre_grad, up_ref[...]).astype(BF16),
            jnp.broadcast_to(gate_grad, (stride, LANES)).T[:8],
        )

    def send(step, carry):
        for copy in loads(lax.rem(step + 1, experts)):
            copy.start()
        block, gate = work(step)
        send_scr[step] = block
        gate_send[step] = gate
        for copy in copies(lax.rem(me + step, experts), step):
            copy.start()
        return carry

    lax.fori_loop(1, experts, send, 0)
    block, gate = work(0)
    recv_scr[me] = block
    gate_recv[me] = gate

    def row_loads(step):
        home = lax.rem(me + step, experts)
        slot = lax.rem(step, 2)
        return (
            pltpu.make_async_copy(arrived_hbm.at[home], rows_scr.at[slot], load_sem.at[slot, 0]),
            pltpu.make_async_copy(hidden_hbm.at[home], hidden_scr.at[slot], load_sem.at[slot, 1]),
        )

    def weigh(step):
        slot = lax.rem(step, 2)
        for copy in row_loads(step):
            copy.wait()
        grad_up_ref[...] += dot_first(rows_scr[slot], pre_grad_scr[step])
        grad_down_ref[...] += dot_first(hidden_scr[slot], out_grad_scr[step])

    def weigh_some(step, carry):
        for copy in row_loads(step + 1):
            copy.start()
        weigh(step)
        return carry

    for copy in row_loads(0):
        copy.start()
    lax.fori_loop(0, experts - 1, weigh_some, 0)
    weigh(experts - 1)

    def gather(source):
        slots = source * stride + lax.broadcasted_iota(jnp.int32, (1, stride), 1)
        lane = lax.broadcasted_iota(jnp.int32, (chunk, LANES), 1)

        def part(index, carry):
            span = pl.ds(pl.multiple_of(index * chunk, chunk), chunk)
            hit = (ids_ref[span, 0:1] == slots) | (ids_ref[span, 1:2] == slots)
            total_scr[span, :model_width] += dot(
                jnp.where(hit, 1.0, 0.0).astype(BF16), recv_scr[source]
            )
            gate = jnp.sum(jnp.where(hit, gate_recv[source, 0:1], 0.0), axis=1, keepdims=True)
            total_scr[span, model_width:] = jnp.where(
                lane == source, gate, total_scr[span, model_width:]
            )
            return carry

        lax.fori_loop(0, tok_count // chunk, part, 0)

    gather(me)

    def receive(step, carry):
        source = lax.rem(me + experts - step, experts)
        for copy in copies(source, step):
            copy.wait_recv()
        gather(source)
        return carry

    lax.fori_loop(1, experts, receive, 0)
    sums_ref[...] = total_scr[...].astype(BF16)

    def finish(step, carry):
        for copy in copies(lax.rem(me + step, experts), step):
            copy.wait_send()
        return carry

    lax.fori_loop(1, experts, finish, 0)


def backward(
    arrived, hidden, result, cot_rows, gate_col, id_cols, up, up_bias, down, half, head_parts, chunk
):
    tok_count = id_cols.shape[0]
    experts, stride, model_width = arrived.shape
    inner = up.shape[1]
    rows = (experts, stride, model_width)
    return pl.pallas_call(
        partial(backward_kernel, experts, stride, half, head_parts, chunk),
        in_specs=[anywhere()] * 4 + [whole()] * 5,
        out_specs=[whole()] * 5,
        out_shape=[
            shaped((tok_count, model_width + LANES), BF16),
            shaped((model_width, inner), F32),
            shaped((8, inner), F32),
            shaped((inner, model_width), F32),
            shaped((8, model_width), F32),
        ],
        scratch_shapes=[
            pltpu.VMEM((2, stride, model_width), BF16),
            pltpu.VMEM((2, head_parts, stride + half, LANES), BF16),
            pltpu.VMEM((2, head_parts, stride + half, LANES), BF16),
            pltpu.VMEM((stride, model_width), BF16),
            pltpu.VMEM((stride, model_width), BF16),
            pltpu.VMEM((2, stride, inner), BF16),
            pltpu.VMEM((experts, stride, inner), BF16),
            pltpu.VMEM(rows, BF16),
            pltpu.VMEM(rows, BF16),
            pltpu.VMEM(rows, BF16),
            pltpu.VMEM((experts, 8, stride), F32),
            pltpu.VMEM((experts, 8, stride), F32),
            pltpu.VMEM((tok_count, model_width + LANES), F32),
            pltpu.SemaphoreType.DMA((2, 3)),
            pltpu.SemaphoreType.DMA((experts,)),
            pltpu.SemaphoreType.DMA((experts,)),
            pltpu.SemaphoreType.DMA((experts,)),
            pltpu.SemaphoreType.DMA((experts,)),
        ],
        compiler_params=params(collective_id=1, has_side_effects=True),
        cost_estimate=cost(8e10, 1e8),
        name="backward",
    )(arrived, hidden, result, cot_rows, gate_col, id_cols, up, up_bias, down)


def copy_kernel(first_ref, second_ref, first_out, second_out):
    first_out[...] = first_ref[...]
    second_out[...] = second_ref[...]


def copies_of(first, second):
    rows = first.shape[0] // 4
    specs = [pl.BlockSpec((rows, a.shape[1]), lambda i: (i, 0)) for a in (first, second)]
    return pl.pallas_call(
        copy_kernel,
        grid=(4,),
        in_specs=specs,
        out_specs=specs,
        out_shape=[shaped(first.shape, F32), shaped(second.shape, F32)],
        compiler_params=params(),
        cost_estimate=cost(0, 1e7),
        name="copies",
    )(first, second)


def tail_kernel(
    experts, stride, half, part_half, seq_count, head_parts, gap,
    sums_ref, id_cols_ref, gate_cols_ref, own_residual_ref, own_second_ref, cot_own_hbm,
    own_columns_hbm, router_ref, vectors_ref, own_tokens_ref, result_hbm,
    context_hbm, first_hbm, qkv_hbm, totals_hbm, weight_ref, out_weight_ref,
    seg_ref, live_ref,
    tokens_hbm, block_ref, qkv_sum_ref, out_sum_ref, bias_sum_ref, small_ref,
    own_recv, cot_wide, columns_scr, part_two, down_one, up_one, down_two, up_two, own_scr,
    full_one, full_two, grad_scr,
    context_scr, first_scr, qkv_scr, totals_scr, back_scr, joined_scr,
    qkv_grad, out_grad, bias_grad, rows_acc, router_acc,
    result_home, result_wide,
    qkv_send, qkv_recv, qkv_all, out_send, out_recv, out_all, bias_recv, small_head, small_recv,
    own_send_sem, own_recv_sem, columns_sem, load_sem, stage_sem, result_send_sem, result_recv_sem,
    down_one_sem, up_one_sem, down_two_sem, up_two_sem, down_one_out, up_one_out, down_two_out, up_two_out,
    full_one_sem, full_two_sem, full_one_out, full_two_out,
    sum_send_sem, sum_recv_sem, all_send_sem, all_recv_sem,
    bias_send_sem, bias_recv_sem, head_send_sem, head_recv_sem, small_send_sem, small_recv_sem,
):
    me = lax.axis_index("exp")
    here = lax.axis_index("head")
    ends = head_parts - 1
    seqlen = seg_ref.shape[1]
    part = seqlen // head_parts
    model_width = vectors_ref.shape[1]
    width = out_weight_ref.shape[0]
    factor = 1.0 / math.sqrt(HEAD_DIM)

    barrier = greet_both(experts, head_parts)

    def chunk_loads(seq):
        span = pl.ds(pl.multiple_of(seq * seqlen, seqlen), seqlen)
        return (
            pltpu.make_async_copy(context_hbm.at[span], context_scr, load_sem.at[0]),
            pltpu.make_async_copy(first_hbm.at[span], first_scr, load_sem.at[1]),
            pltpu.make_async_copy(qkv_hbm.at[span], qkv_scr, load_sem.at[2]),
            pltpu.make_async_copy(totals_hbm.at[span], totals_scr, load_sem.at[3]),
        )

    for copy in chunk_loads(0):
        copy.start()
    qkv_grad[...] = jnp.zeros_like(qkv_grad)
    out_grad[...] = jnp.zeros_like(out_grad)
    bias_grad[...] = jnp.zeros_like(bias_grad)
    rows_acc[...] = jnp.zeros_like(rows_acc)
    router_acc[...] = jnp.zeros_like(router_acc)
    pl.semaphore_wait(barrier, experts - 1 + ends)

    def to_exp(target):
        return dict(device_id=(target, here), device_id_type=MESH)

    def to_head(target):
        return dict(device_id=(me, target), device_id_type=MESH)

    def each_peer(action):
        def one(step, carry):
            action(step, lax.rem(me + step, experts), lax.rem(me + experts - step, experts))
            return carry

        lax.fori_loop(1, experts, one, 0)

    def result_copy(step, target):
        return pltpu.make_async_remote_copy(
            src_ref=result_hbm.at[target],
            dst_ref=result_home.at[me],
            send_sem=result_send_sem.at[step],
            recv_sem=result_recv_sem.at[step],
            **to_exp(target),
        )

    def own_copy(seq, step):
        target = lax.rem(here + step, head_parts)
        return pltpu.make_async_remote_copy(
            src_ref=cot_own_hbm.at[target, seq],
            dst_ref=own_recv.at[here, seq],
            send_sem=own_send_sem.at[seq, step],
            recv_sem=own_recv_sem.at[seq, step],
            **to_head(target),
        )

    own_local = pltpu.make_async_copy(cot_own_hbm.at[here], own_recv.at[here], columns_sem.at[1])
    own_local.start()
    own_local.wait()

    def down_copy(buffer, sems, outs, seq, shard):
        return pltpu.make_async_remote_copy(
            src_ref=buffer.at[seq, shard],
            dst_ref=buffer.at[seq, shard],
            send_sem=outs.at[seq, shard],
            recv_sem=sems.at[seq, shard],
            **to_head(here - 1),
        )

    def up_copy(buffer, sems, outs, seq, shard):
        return pltpu.make_async_remote_copy(
            src_ref=buffer.at[seq, shard - 1],
            dst_ref=buffer.at[seq, shard - 1],
            send_sem=outs.at[seq, shard - 1],
            recv_sem=sems.at[seq, shard - 1],
            **to_head(here + 1),
        )

    one_down = (down_one, down_one_sem, down_one_out)
    one_up = (up_one, up_one_sem, up_one_out)
    two_down = (down_two, down_two_sem, down_two_out)
    two_up = (up_two, up_two_sem, up_two_out)

    def reduce_hop(partial_ref, base, down, up, seq, hop):
        low = hop - ends + here
        high = ends - hop + here

        @pl.when((low >= 0) & (low < here))
        def downward():
            rows = partial_ref[pl.ds(pl.multiple_of(base + low * part, part), part)]

            @pl.when(here < ends)
            def add():
                down_copy(*down, seq, low).wait_recv()
                down[0][seq, low] = (down[0][seq, low].astype(F32) + rows.astype(F32)).astype(BF16)

            @pl.when(here == ends)
            def begin():
                down[0][seq, low] = rows

            down_copy(*down, seq, low).start()

        @pl.when((high > here) & (high <= ends))
        def upward():
            rows = partial_ref[pl.ds(pl.multiple_of(base + high * part, part), part)]

            @pl.when(here > 0)
            def add():
                up_copy(*up, seq, high).wait_recv()
                up[0][seq, high - 1] = (
                    up[0][seq, high - 1].astype(F32) + rows.astype(F32)
                ).astype(BF16)

            @pl.when(here == 0)
            def begin():
                up[0][seq, high - 1] = rows

            up_copy(*up, seq, high).start()

    def reduce_end(partial_ref, base, down, up, seq, columns):
        own = pl.ds(pl.multiple_of(base + here * part, part), part)
        own_scr[:, :columns] = partial_ref[own].astype(F32)

        @pl.when(here < ends)
        def below():
            down_copy(*down, seq, here).wait_recv()
            own_scr[:, :columns] += down[0][seq, here].astype(F32)

        @pl.when(here > 0)
        def above():
            up_copy(*up, seq, here).wait_recv()
            own_scr[:, :columns] += up[0][seq, here - 1].astype(F32)

    def reduce_drain(down, up, seq):
        for shard in range(ends):

            @pl.when(shard < here)
            def downward():
                down_copy(*down, seq, shard).wait_send()

            @pl.when(shard + 1 > here)
            def upward():
                up_copy(*up, seq, shard + 1).wait_send()

    def full_copy(buffer, sems, outs, seq, shard, side):
        rows = pl.ds(pl.multiple_of(shard * part, part), part)
        return pltpu.make_async_remote_copy(
            src_ref=buffer.at[seq, rows],
            dst_ref=buffer.at[seq, rows],
            send_sem=outs.at[seq, shard, side],
            recv_sem=sems.at[seq, shard],
            **to_head(here + 1 - 2 * side),
        )

    one_full = (full_one, full_one_sem, full_one_out)
    two_full = (full_two, full_two_sem, full_two_out)

    def spread_hop(full, seq, hop):
        for side in range(2):
            shard = here - hop if side == 0 else here + hop
            there = shard >= 0 if side == 0 else shard <= ends
            onward = here < ends if side == 0 else here > 0

            @pl.when(there)
            def arrived():
                if hop > 0:
                    full_copy(*full, seq, shard, side).wait_recv()
                if hop < ends:

                    @pl.when(onward)
                    def pass_on():
                        full_copy(*full, seq, shard, side).start()

    def spread_drain(full, seq):
        for hop in range(ends):
            for side in range(2):
                shard = here - hop if side == 0 else here + hop
                there = shard >= 0 if side == 0 else shard <= ends
                onward = here < ends if side == 0 else here > 0

                @pl.when(there & onward)
                def sent():
                    full_copy(*full, seq, shard, side).wait_send()

    def middle(seq):
        second = own_second_ref[seq]
        lane = lax.broadcasted_iota(jnp.int32, (part, LANES), 1)
        logits = jnp.where(lane < experts, dot(second, router_ref[...]), NEGATIVE)
        powers = jnp.exp(logits - jnp.max(logits, axis=1, keepdims=True))
        chances = powers / jnp.sum(powers, axis=1, keepdims=True)
        route_grad = own_scr[:, model_width:]
        logit_grad = (
            chances * (route_grad - jnp.sum(chances * route_grad, axis=1, keepdims=True))
        ).astype(BF16)
        router_acc[...] += dot_first(second, logit_grad)
        grad = own_scr[:, :model_width] + dot_last(logit_grad, router_ref[...])
        normal, scale = standard(own_residual_ref[seq])
        rows_acc[0:1] += jnp.sum(grad * normal, axis=0, keepdims=True)
        rows_acc[1:2] += jnp.sum(grad, axis=0, keepdims=True)
        for other in range(1, head_parts):
            own_copy(seq, other).wait_recv()
        unpack_rows(lambda z: own_recv[z, seq], cot_wide, head_parts, part, part_half)
        total = cot_wide[...].astype(F32) + norm_back(grad, vectors_ref[3:4], normal, scale)
        rows_acc[2:3] += jnp.sum(total, axis=0, keepdims=True)
        grad_scr[seq] = total
        full_one[seq, pl.ds(pl.multiple_of(here * part, part), part)] = total.astype(BF16)

    def attend_start(seq):
        for copy in chunk_loads(seq):
            copy.wait()
        grad = full_one[seq]
        back_scr[...] = dot_last(grad, out_weight_ref[...]).astype(BF16)
        out_grad[...] += dot_first(context_scr[...], grad)
        return mask_penalty(seg_ref[pl.ds(seq, 1)], live_ref[pl.ds(seq, 1)])

    def attend_head(head, penalty):
        lo = head * HEAD_DIM
        hi = lo + HEAD_DIM
        query = qkv_scr[:, lo:hi] * BF16(factor)
        keys = qkv_scr[:, width + lo : width + hi]
        values = qkv_scr[:, 2 * width + lo : 2 * width + hi]
        back = back_scr[:, lo:hi]
        weights = jnp.exp(
            dot_last(query, keys) + penalty - totals_scr[:, head : head + 1]
        )
        joined_scr[:, 2 * width + lo : 2 * width + hi] = dot_first(
            weights.astype(BF16), back
        ).astype(BF16)
        inner = jnp.sum(
            back.astype(F32) * context_scr[:, lo:hi].astype(F32), axis=-1, keepdims=True
        )
        score_grad = (weights * (dot_last(back, values) - inner)).astype(BF16)
        joined_scr[:, lo:hi] = (dot(score_grad, keys) * factor).astype(BF16)
        joined_scr[:, width + lo : width + hi] = dot_first(score_grad, query).astype(BF16)

    def attend_end(seq):
        joined = joined_scr[...]
        span = pl.ds(pl.multiple_of(lax.rem(seq, 2) * seqlen, seqlen), seqlen)
        part_two[span] = dot_last(joined, weight_ref[...]).astype(BF16)
        qkv_grad[...] += dot_first(first_scr[...], joined)
        bias_grad[0:1] += jnp.sum(joined.astype(F32), axis=0, keepdims=True)

        @pl.when(seq + 1 < seq_count)
        def more():
            for copy in chunk_loads(seq + 1):
                copy.start()

    def last(seq):
        grad = own_scr[:, :model_width]
        normal, scale = standard(own_tokens_ref[seq].astype(F32))
        rows_acc[3:4] += jnp.sum(grad * normal, axis=0, keepdims=True)
        rows_acc[4:5] += jnp.sum(grad, axis=0, keepdims=True)
        total = grad_scr[seq] + norm_back(grad, vectors_ref[0:1], normal, scale)
        full_two[seq, pl.ds(pl.multiple_of(here * part, part), part)] = total.astype(BF16)

    def stage_copy(seq):
        span = pl.ds(pl.multiple_of(seq * seqlen, seqlen), seqlen)
        return pltpu.make_async_copy(full_two.at[seq], tokens_hbm.at[span], stage_sem.at[seq])

    def open_results():
        each_peer(lambda step, target, source: result_copy(step, target).wait_recv())

        def one(expert, carry):
            packed = result_home[expert]
            result_wide[expert, :, :LANES] = packed[:stride]
            tail = packed[stride:]
            result_wide[expert, :half, LANES:] = tail[:, :HEAD_DIM]
            result_wide[expert, half:, LANES:] = tail[2 * half - stride :, HEAD_DIM:]
            return carry

        lax.fori_loop(0, experts, one, 0)

    def combine(seq):
        span = pl.ds(pl.multiple_of(seq * seqlen, seqlen), seqlen)
        first = id_cols_ref[span, 0:1]
        second = id_cols_ref[span, 1:2]
        pltpu.make_async_copy(own_columns_hbm.at[span], columns_scr, columns_sem.at[0]).start()
        pltpu.make_async_copy(own_columns_hbm.at[span], columns_scr, columns_sem.at[0]).wait()
        first_gate = gate_cols_ref[span, 0:1]
        second_gate = gate_cols_ref[span, 1:2]

        def one(expert, total):
            slots = expert * stride + lax.broadcasted_iota(jnp.int32, (1, stride), 1)
            weights = jnp.where(
                first == slots, first_gate, jnp.where(second == slots, second_gate, 0.0)
            )
            return total + dot(weights.astype(BF16), result_wide[expert])

        block_ref[span] = lax.fori_loop(0, experts, one, columns_scr[...]).astype(BF16)

    qkv_rows = qkv_grad.shape[0] // experts
    out_rows = out_grad.shape[0] // experts

    def sum_copies(step, target):
        return (
            pltpu.make_async_remote_copy(
                src_ref=qkv_send.at[target],
                dst_ref=qkv_recv.at[me],
                send_sem=sum_send_sem.at[step, 0],
                recv_sem=sum_recv_sem.at[step, 0],
                **to_exp(target),
            ),
            pltpu.make_async_remote_copy(
                src_ref=out_send.at[target],
                dst_ref=out_recv.at[me],
                send_sem=sum_send_sem.at[step, 1],
                recv_sem=sum_recv_sem.at[step, 1],
                **to_exp(target),
            ),
        )

    def all_copies(step, target):
        return (
            pltpu.make_async_remote_copy(
                src_ref=qkv_all.at[me],
                dst_ref=qkv_all.at[me],
                send_sem=all_send_sem.at[step, 0],
                recv_sem=all_recv_sem.at[step, 0],
                **to_exp(target),
            ),
            pltpu.make_async_remote_copy(
                src_ref=out_all.at[me],
                dst_ref=out_all.at[me],
                send_sem=all_send_sem.at[step, 1],
                recv_sem=all_recv_sem.at[step, 1],
                **to_exp(target),
            ),
        )

    def all_arrivals(step, source):
        return (
            pltpu.make_async_remote_copy(
                src_ref=qkv_all.at[source],
                dst_ref=qkv_all.at[source],
                send_sem=all_send_sem.at[step, 0],
                recv_sem=all_recv_sem.at[step, 0],
                **to_exp(source),
            ),
            pltpu.make_async_remote_copy(
                src_ref=out_all.at[source],
                dst_ref=out_all.at[source],
                send_sem=all_send_sem.at[step, 1],
                recv_sem=all_recv_sem.at[step, 1],
                **to_exp(source),
            ),
        )

    def bias_copy(step, target):
        return pltpu.make_async_remote_copy(
            src_ref=bias_grad,
            dst_ref=bias_recv.at[me],
            send_sem=bias_send_sem.at[step],
            recv_sem=bias_recv_sem.at[step],
            **to_exp(target),
        )

    def start_sums():
        for block in range(experts):
            qkv_send[block] = qkv_grad[block * qkv_rows : (block + 1) * qkv_rows].astype(BF16)
            out_send[block] = out_grad[block * out_rows : (block + 1) * out_rows].astype(BF16)

        def begin(step, target, source):
            for copy in sum_copies(step, target):
                copy.start()
            bias_copy(step, target).start()

        each_peer(begin)
        qkv_recv[me] = qkv_send[me]
        out_recv[me] = out_send[me]
        bias_recv[me] = bias_grad[...]

    def spread_sums():
        def arrive(step, target, source):
            for copy in sum_copies(step, target):
                copy.wait_recv()
            bias_copy(step, target).wait_recv()

        each_peer(arrive)

        def add(source, totals):
            return (
                totals[0] + qkv_recv[source].astype(F32),
                totals[1] + out_recv[source].astype(F32),
                totals[2] + bias_recv[source],
            )

        qkv_total, out_total, bias_total = lax.fori_loop(
            1,
            experts,
            add,
            (qkv_recv[0].astype(F32), out_recv[0].astype(F32), bias_recv[0]),
        )
        qkv_all[me] = qkv_total.astype(BF16)
        out_all[me] = out_total.astype(BF16)
        bias_sum_ref[...] = bias_total

        def begin(step, target, source):
            for copy in all_copies(step, target):
                copy.start()

        each_peer(begin)

    def end_sums():
        def arrive(step, target, source):
            for copy in all_arrivals(step, source):
                copy.wait_recv()

        each_peer(arrive)
        for block in range(experts):
            qkv_sum_ref[block * qkv_rows : (block + 1) * qkv_rows] = qkv_all[block].astype(F32)
            out_sum_ref[block * out_rows : (block + 1) * out_rows] = out_all[block].astype(F32)

    def head_copy(step):
        return pltpu.make_async_remote_copy(
            src_ref=small_head.at[here],
            dst_ref=small_head.at[here],
            send_sem=head_send_sem.at[step],
            recv_sem=head_recv_sem.at[step],
            **to_head(lax.rem(here + step, head_parts)),
        )

    def head_arrival(step):
        source = lax.rem(here + head_parts - step, head_parts)
        return pltpu.make_async_remote_copy(
            src_ref=small_head.at[source],
            dst_ref=small_head.at[source],
            send_sem=head_send_sem.at[step],
            recv_sem=head_recv_sem.at[step],
            **to_head(source),
        )

    def small_copy(step, target):
        return pltpu.make_async_remote_copy(
            src_ref=small_recv.at[me],
            dst_ref=small_recv.at[me],
            send_sem=small_send_sem.at[step],
            recv_sem=small_recv_sem.at[step],
            **to_exp(target),
        )

    def small_arrival(step, source):
        return pltpu.make_async_remote_copy(
            src_ref=small_recv.at[source],
            dst_ref=small_recv.at[source],
            send_sem=small_send_sem.at[step],
            recv_sem=small_recv_sem.at[step],
            **to_exp(source),
        )

    heads = width // HEAD_DIM
    router_rows = small_head.shape[1] - 8

    second_start = 2 * ends
    spread_start = second_start + ends
    ticks = spread_start + ends + 1 + gap * (seq_count - 1)
    final = gap * (seq_count - 1)

    def tick(now, carry):
        def on(offset, action):
            since = now - offset

            @pl.when((since >= 0) & (lax.rem(since, gap) == 0) & (since < gap * seq_count))
            def run():
                action(since // gap)

        def first_end(seq):
            reduce_end(sums_ref, seq * seqlen, one_down, one_up, seq, model_width + LANES)
            middle(seq)

        def attend(seq):
            spread_hop(one_full, seq, ends)
            penalty = attend_start(seq)
            for head in range(heads):
                attend_head(head, penalty)
            attend_end(seq)

        def second_end(seq):
            reduce_end(part_two, lax.rem(seq, 2) * seqlen, two_down, two_up, seq, model_width)
            last(seq)

        def tokens_end(seq):
            spread_hop(two_full, seq, ends)
            stage_copy(seq).start()

        def own_begin(seq):
            for other in range(1, head_parts):
                own_copy(seq, other).start()

        on(ends, first_end)
        on(spread_start, second_end)
        for hop in range(ends):
            on(hop, lambda seq: reduce_hop(sums_ref, seq * seqlen, one_down, one_up, seq, hop))
            on(ends + hop, lambda seq: spread_hop(one_full, seq, hop))
            if hop > 0:
                on(
                    second_start + hop,
                    lambda seq: reduce_hop(
                        part_two, lax.rem(seq, 2) * seqlen, two_down, two_up, seq, hop
                    ),
                )
            on(spread_start + hop, lambda seq: spread_hop(two_full, seq, hop))
        on(0, own_begin)
        on(second_start, attend)
        on(
            second_start,
            lambda seq: reduce_hop(part_two, lax.rem(seq, 2) * seqlen, two_down, two_up, seq, 0),
        )

        @pl.when(now == 0)
        def send_results():
            each_peer(lambda step, target, source: result_copy(step, target).start())
            local = pltpu.make_async_copy(result_hbm.at[me], result_home.at[me], columns_sem.at[1])
            local.start()
            local.wait()

        @pl.when(now == ends + 1)
        def results():
            open_results()

        on(ends + 2, combine)

        @pl.when(now == final + second_start)
        def sums():
            start_sums()

        @pl.when(now == final + second_start + 2)
        def share():
            spread_sums()

        @pl.when(now == final + spread_start)
        def small():
            small_head[here, :8] = rows_acc[...]
            small_head[here, 8:] = router_acc[...].T[:router_rows]
            for other in range(1, head_parts):
                head_copy(other).start()

        @pl.when(now == final + spread_start + 1)
        def small_on():
            for other in range(1, head_parts):
                head_arrival(other).wait_recv()
            total = small_head[0]
            for other in range(1, head_parts):
                total = total + small_head[other]
            small_recv[me] = total
            each_peer(lambda step, target, source: small_copy(step, target).start())
            end_sums()

        on(spread_start + ends, tokens_end)
        return carry

    lax.fori_loop(0, ticks, tick, 0)

    each_peer(lambda step, target, source: small_arrival(step, source).wait_recv())
    small_ref[...] = lax.fori_loop(
        1, experts, lambda source, total: total + small_recv[source], small_recv[0]
    )
    for seq in range(seq_count):
        stage_copy(seq).wait()
        reduce_drain(one_down, one_up, seq)
        reduce_drain(two_down, two_up, seq)
        spread_drain(one_full, seq)
        spread_drain(two_full, seq)
    for other in range(1, head_parts):
        head_copy(other).wait_send()
        for seq in range(seq_count):
            own_copy(seq, other).wait_send()

    def sent(step, target, source):
        result_copy(step, target).wait_send()
        for copy in sum_copies(step, target):
            copy.wait_send()
        bias_copy(step, target).wait_send()
        for copy in all_copies(step, target):
            copy.wait_send()
        small_copy(step, target).wait_send()

    each_peer(sent)


def tail(
    sums, id_cols, gate_cols, own_residual, own_second, cot_own, own_columns, router, vectors,
    own_tokens, result, context, first, qkv, totals, flat_qkv, out_weight,
    segments, live, stride, half, part_half, head_parts,
):
    experts = result.shape[0]
    model_width = first.shape[1]
    seq_count, part = own_residual.shape[:2]
    seqlen = part * head_parts
    tok_count = seq_count * seqlen
    wide = flat_qkv.shape[1]
    width = wide // 3
    ends = head_parts - 1
    small_rows = 8 + round_up(experts, 8)
    dma = pltpu.SemaphoreType.DMA
    return pl.pallas_call(
        partial(tail_kernel, experts, stride, half, part_half, seq_count, head_parts, 2),
        in_specs=[whole()] * 5 + [anywhere()] * 2 + [whole()] * 3 + [anywhere()] * 5 + [whole()] * 4,
        out_specs=[anywhere()] + [whole()] * 5,
        out_shape=[
            shaped((tok_count, model_width), BF16),
            shaped((tok_count, width), BF16),
            shaped((model_width, wide), F32),
            shaped((width, model_width), F32),
            shaped((8, wide), F32),
            shaped((small_rows, model_width), F32),
        ],
        scratch_shapes=[
            pltpu.VMEM(cot_own.shape, BF16),
            pltpu.VMEM((part, model_width), BF16),
            pltpu.VMEM((seqlen, width), F32),
            pltpu.VMEM((2 * seqlen, model_width), BF16),
            pltpu.VMEM((seq_count, ends, part, model_width + LANES), BF16),
            pltpu.VMEM((seq_count, ends, part, model_width + LANES), BF16),
            pltpu.VMEM((seq_count, ends, part, model_width), BF16),
            pltpu.VMEM((seq_count, ends, part, model_width), BF16),
            pltpu.VMEM((part, model_width + LANES), F32),
            pltpu.VMEM((seq_count, seqlen, model_width), BF16),
            pltpu.VMEM((seq_count, seqlen, model_width), BF16),
            pltpu.VMEM((seq_count, part, model_width), F32),
            pltpu.VMEM((seqlen, width), BF16),
            pltpu.VMEM((seqlen, model_width), BF16),
            pltpu.VMEM((seqlen, wide), BF16),
            pltpu.VMEM((seqlen, LANES), F32),
            pltpu.VMEM((seqlen, width), BF16),
            pltpu.VMEM((seqlen, wide), BF16),
            pltpu.VMEM((model_width, wide), F32),
            pltpu.VMEM((width, model_width), F32),
            pltpu.VMEM((8, wide), F32),
            pltpu.VMEM((8, model_width), F32),
            pltpu.VMEM((model_width, LANES), F32),
            pltpu.VMEM((experts, stride + half, LANES), BF16),
            pltpu.VMEM((experts, stride, width), BF16),
            pltpu.VMEM((experts, model_width // experts, wide), BF16),
            pltpu.VMEM((experts, model_width // experts, wide), BF16),
            pltpu.VMEM((experts, model_width // experts, wide), BF16),
            pltpu.VMEM((experts, width // experts, model_width), BF16),
            pltpu.VMEM((experts, width // experts, model_width), BF16),
            pltpu.VMEM((experts, width // experts, model_width), BF16),
            pltpu.VMEM((experts, 8, wide), F32),
            pltpu.VMEM((head_parts, small_rows, model_width), F32),
            pltpu.VMEM((experts, small_rows, model_width), F32),
            dma((seq_count, head_parts)),
            dma((seq_count, head_parts)),
            dma((2,)),
            dma((4,)),
            dma((seq_count,)),
            dma((experts,)),
            dma((experts,)),
        ]
        + [dma((seq_count, ends))] * 8
        + [dma((seq_count, head_parts))] * 2
        + [dma((seq_count, head_parts, 2))] * 2
        + [dma((experts, 2))] * 4
        + [dma((experts,))] * 2
        + [dma((head_parts,))] * 2
        + [dma((experts,))] * 2,
        compiler_params=params(collective_id=2, has_side_effects=True),
        cost_estimate=cost(1e11, 1e8),
        name="tail",
    )(
        sums, id_cols, gate_cols, own_residual, own_second, cot_own, own_columns, router, vectors,
        own_tokens, result, context, first, qkv, totals, flat_qkv, out_weight,
        segments, live,
    )


def body(
    tokens,
    segments,
    live_mask,
    routes,
    priority,
    norm1_gain,
    norm1_bias,
    qkv_weight,
    qv_bias,
    out_weight,
    out_bias,
    norm2_gain,
    norm2_bias,
    router,
    up_weight,
    up_bias,
    down_weight,
    down_bias,
    cotangent,
):
    tok_count, model_width = tokens.shape
    seq_count, seqlen = segments.shape
    experts = lax.axis_size("exp")
    head_parts = lax.axis_size("head")
    head_index = lax.axis_index("head")
    quarter = model_width // head_parts
    capacity = (21 * tok_count + 10 * experts - 1) // (10 * experts)
    stride = round_up(capacity, 16)
    half = round_up(stride // 2, 16)
    local_width = qkv_weight.shape[2]

    rows_of = [norm1_gain, norm1_bias, out_bias, norm2_gain, norm2_bias]
    spare = jnp.zeros(((8 - len(rows_of)) * model_width,), BF16)
    vectors = jnp.concatenate(rows_of + [spare]).astype(F32).reshape(8, model_width)
    flat_qkv = qkv_weight.reshape(model_width, 3 * local_width)
    router_wide = jnp.pad(router, ((0, 0), (0, LANES - experts)))
    up, down = up_weight[0], down_weight[0]

    int_rows = jnp.concatenate(
        [
            routes.T,
            live_mask.reshape(1, tok_count),
            priority,
            jnp.zeros((4, tok_count), jnp.int32),
        ],
        axis=0,
    )
    part_half = round_up(seqlen // head_parts // 2, 16)
    first, qkv, context, totals, out_full_weight, gathered, ids, cot_slots, cot_own, own_tokens = head(
        tokens, vectors, flat_qkv, qv_bias, segments, live_mask, int_rows, cotangent, out_weight, experts, capacity, stride, half, part_half, head_parts,
    )
    id_cols = ids.T
    own_residual, own_second, own_columns, gates, arrived, hidden, result, gate_col, cot_rows = forward(
        gathered, tokens, vectors, out_full_weight, router_wide, int_rows, ids,
        up, up_bias, down, down_bias, cot_slots, experts, stride, half, seq_count, head_parts,
    )
    gate_cols = gates.T
    own_result = lax.psum_scatter(result, "head", scatter_dimension=0, tiled=True)[0]
    sums, grad_up, grad_up_bias, grad_down, grad_down_bias = backward(
        arrived, hidden, result, cot_rows, gate_col, id_cols, up, up_bias, down, half, head_parts,
        seqlen,
    )
    grad_up, grad_down, own_result = lax.optimization_barrier(
        (*copies_of(grad_up, grad_down), own_result)
    )
    grad_tokens, block_out, qkv_grad, out_grad, bias_grad, small = tail(
        sums, id_cols, gate_cols, own_residual, own_second, cot_own, own_columns,
        router_wide, vectors, own_tokens, own_result, context, first, qkv, totals,
        flat_qkv, out_weight, segments, live_mask, stride, half, part_half, head_parts,
    )
    grad_qv_bias = jnp.concatenate(
        [bias_grad[0:1, :local_width], bias_grad[0:1, 2 * local_width :]], axis=0
    )
    return (
        block_out,
        grad_tokens.astype(F32),
        small[3],
        small[4],
        qkv_grad.reshape(model_width, 3, local_width),
        grad_qv_bias,
        out_grad,
        small[2],
        small[0],
        small[1],
        small[8 : 8 + experts].T,
        grad_up[None],
        grad_up_bias[0:1],
        grad_down[None],
        lax.dynamic_slice_in_dim(grad_down_bias[0:1], head_index * quarter, quarter, 1),
    )


def solution(mesh):
    in_specs = (
        P("exp", None),
        P("exp", None),
        P("exp", None),
        P("exp", None),
        P("exp", None),
        P(),
        P(),
        P(None, None, "head"),
        P(None, "head"),
        P("head", None),
        P(),
        P(),
        P(),
        P(),
        P("exp", None, "head"),
        P("exp", "head"),
        P("exp", "head", None),
        P("exp", "head"),
        P("exp", "head"),
    )
    out_specs = (
        P("exp", "head"),
        P("exp", None),
        P(),
        P(),
        P(None, None, "head"),
        P(None, "head"),
        P("head", None),
        P(),
        P(),
        P(),
        P(),
        P("exp", None, "head"),
        P("exp", "head"),
        P("exp", "head", None),
        P("exp", "head"),
    )
    return jax.shard_map(body, mesh=mesh, in_specs=in_specs, out_specs=out_specs, check_vma=False)
```

```python
from functools import partial
import math

import jax
import jax.numpy as jnp
from jax import lax
from jax.experimental import pallas as pl
from jax.experimental.pallas import tpu as pltpu
from jax.sharding import PartitionSpec as P

HEAD_DIM = 64
LANES = 128
EPSILON = 1e-06
NEGATIVE = -1e30
CONTRACT_FIRST = (((0,), (0,)), ((), ()))
CONTRACT_LAST = (((1,), (1,)), ((), ()))
F32 = jnp.float32
BF16 = jnp.bfloat16
MESH = pl.DeviceIdType.MESH
VMEM_LIMIT = 54 * 1024 * 1024


def round_up(number, step):
    return (number + step - 1) // step * step


def whole():
    return pl.BlockSpec(memory_space=pltpu.VMEM)


def anywhere():
    return pl.BlockSpec(memory_space=pl.ANY)


def shaped(shape, dtype):
    return jax.ShapeDtypeStruct(shape, dtype)


def params(**more):
    return pltpu.CompilerParams(vmem_limit_bytes=VMEM_LIMIT, **more)


def cost(flops, moved):
    return pl.CostEstimate(flops=int(flops), bytes_accessed=int(moved), transcendentals=0)


def dot(left, right):
    return jnp.dot(left, right, preferred_element_type=F32)


def dot_last(left, right):
    return lax.dot_general(left, right, CONTRACT_LAST, preferred_element_type=F32)


def dot_first(left, right):
    return lax.dot_general(left, right, CONTRACT_FIRST, preferred_element_type=F32)


def standard(values):
    centred = values - jnp.mean(values, axis=-1, keepdims=True)
    scale = lax.rsqrt(jnp.mean(centred * centred, axis=-1, keepdims=True) + EPSILON)
    return centred * scale, scale


def norm_back(grad_rows, gain_row, normal, scale):
    inner = grad_rows * gain_row
    return scale * (
        inner
        - jnp.mean(inner, axis=-1, keepdims=True)
        - normal * jnp.mean(inner * normal, axis=-1, keepdims=True)
    )


def diagonal_of(count):
    return lax.broadcasted_iota(jnp.int32, (count, count), 0) == lax.broadcasted_iota(
        jnp.int32, (count, count), 1
    )


def as_column(row, diagonal):
    return jnp.sum(jnp.where(diagonal, row.astype(F32), 0.0), axis=1, keepdims=True)


def mask_penalty(seg_row, live_row):
    diagonal = diagonal_of(seg_row.shape[1])
    same = as_column(seg_row, diagonal) == seg_row.astype(F32)
    return jnp.where(same & ((live_row > 0) | diagonal), 0.0, NEGATIVE)


def pack_rows(rows, half):
    count = rows.shape[0]
    third = rows[:, LANES:]
    return rows[:, :LANES], jnp.concatenate([third[:half], third[count - half :]], axis=1)


def unpack_rows(parts_of, into, head_parts, count, half):
    extra = HEAD_DIM
    width = LANES + extra
    for z in range(head_parts):
        packed = parts_of(z)
        into[:, z * width : z * width + LANES] = packed[:count]
        tail = packed[count : count + half]
        into[:half, z * width + LANES : (z + 1) * width] = tail[:, :extra]
        into[half:, z * width + LANES : (z + 1) * width] = tail[2 * half - count :, extra:]


def greet(peers):
    barrier = pltpu.get_barrier_semaphore()
    me = lax.axis_index("exp")
    here = lax.axis_index("head")

    def call(step, carry):
        other = lax.rem(me + step, peers)
        pl.semaphore_signal(barrier, inc=1, device_id=(other, here), device_id_type=MESH)
        return carry

    lax.fori_loop(1, peers, call, 0)
    return barrier


def greet_both(peers, head_parts):
    barrier = greet(peers)
    me = lax.axis_index("exp")
    here = lax.axis_index("head")

    def call(step, carry):
        other = lax.rem(here + step, head_parts)
        pl.semaphore_signal(barrier, inc=1, device_id=(me, other), device_id_type=MESH)
        return carry

    lax.fori_loop(1, head_parts, call, 0)
    return barrier


def head_kernel(
    experts, capacity, stride, half, part_half, seq_count, head_parts,
    tokens_ref, gain1_ref, bias1_ref, out_bias_ref, gain2_ref, bias2_ref, weight_ref, bias_ref, seg_ref, live_ref, rows_ref, cot_ref, out_weight_ref,
    first_hbm, qkv_hbm, context_hbm, total_hbm, norm_ref, out_full_ref, gathered_ref, ids_ref, cot_recv, own_send, own_tokens_ref,
    cot_send, first_scr, qkv_scr, context_scr, total_scr,
    gather_sem, gather_out, cot_send_sem, cot_recv_sem, store_sem,
    weight_sem, weight_out, pair_send_sem, pair_recv_sem,
):
    me = lax.axis_index("exp")
    here = lax.axis_index("head")
    barrier = greet_both(experts, head_parts)
    ends = head_parts - 1
    tok_count = tokens_ref.shape[0]
    seqlen = tok_count // seq_count
    part = seqlen // head_parts
    pl.semaphore_wait(barrier, experts - 1 + ends)

    def own_rows():
        for seq in range(seq_count):
            own = pl.ds(pl.multiple_of(seq * seqlen + here * part, part), part)
            own_tokens_ref[seq] = tokens_ref[own]
            for z in range(head_parts):
                start = seq * seqlen + z * part
                wide, tail = pack_rows(cot_ref[start : start + part], part_half)
                own_send[z, seq, :part] = wide
                own_send[z, seq, part:] = tail

    for row, vector in enumerate((gain1_ref, bias1_ref, out_bias_ref, gain2_ref, bias2_ref)):
        norm_ref[row : row + 1] = vector[...].astype(F32).reshape(1, -1)
    norm_ref[5:8] = jnp.zeros((3, norm_ref.shape[1]), F32)
    core = lax.rem(me, 2)
    weight_rows = out_weight_ref.shape[0]
    half_rows = weight_rows // 2

    def weight_span(shard, which):
        start = pl.multiple_of(shard * weight_rows + which * half_rows, 16)
        return pl.ds(start, half_rows)

    def weight_copy(shard, side):
        rows = weight_span(shard, core)
        return pltpu.make_async_remote_copy(
            src_ref=out_full_ref.at[rows],
            dst_ref=out_full_ref.at[rows],
            send_sem=weight_out.at[shard, side],
            recv_sem=weight_sem.at[shard],
            device_id=(me, here + 1 - 2 * side),
            device_id_type=MESH,
        )

    def pair_copy(step, which):
        rows = weight_span(lax.rem(here + step, head_parts), which)
        return pltpu.make_async_remote_copy(
            src_ref=out_full_ref.at[rows],
            dst_ref=out_full_ref.at[rows],
            send_sem=pair_send_sem.at[step],
            recv_sem=pair_recv_sem.at[step],
            device_id=(me + 1 - 2 * core, here),
            device_id_type=MESH,
        )

    def weight_hop(hop):
        def one(side, shard, there, onward):
            @pl.when(there)
            def arrived():
                if hop > 0:
                    weight_copy(shard, side).wait_recv()
                if hop < ends:

                    @pl.when(onward)
                    def pass_on():
                        weight_copy(shard, side).start()

        each_side(hop, one)
        if hop == ends:
            for step in range(1, head_parts):
                pair_copy(step, core).start()

    def stores(seq):
        slot = lax.rem(seq, 2)
        span = pl.ds(pl.multiple_of(seq * seqlen, seqlen), seqlen)
        return (
            pltpu.make_async_copy(first_scr.at[slot], first_hbm.at[span], store_sem.at[slot, 0]),
            pltpu.make_async_copy(qkv_scr.at[slot], qkv_hbm.at[span], store_sem.at[slot, 1]),
            pltpu.make_async_copy(context_scr.at[slot], context_hbm.at[span], store_sem.at[slot, 2]),
            pltpu.make_async_copy(total_scr.at[slot], total_hbm.at[span], store_sem.at[slot, 3]),
        )

    def attend(seq):
        slot = lax.rem(seq, 2)
        span = pl.ds(pl.multiple_of(seq * seqlen, seqlen), seqlen)

        @pl.when(seq >= 2)
        def free():
            for copy in stores(seq - 2):
                copy.wait()

        normal, ignored = standard(tokens_ref[span].astype(F32))
        first = (normal * norm_ref[0:1] + norm_ref[1:2]).astype(BF16)
        first_scr[slot] = first
        bias = bias_ref[...].astype(F32)
        bias_row = jnp.concatenate([bias[0:1], jnp.zeros_like(bias[0:1]), bias[1:2]], axis=1)
        rows = (dot(first, weight_ref[...]) + bias_row).astype(BF16)
        qkv_scr[slot] = rows
        penalty = mask_penalty(seg_ref[pl.ds(seq, 1)], live_ref[pl.ds(seq, 1)])
        width = rows.shape[1] // 3
        parts = []
        for head in range(width // HEAD_DIM):
            lo = head * HEAD_DIM
            hi = lo + HEAD_DIM
            query = rows[:, lo:hi] * BF16(1.0 / math.sqrt(HEAD_DIM))
            scores = dot_last(query, rows[:, width + lo : width + hi]) + penalty
            largest = jnp.max(scores, axis=-1, keepdims=True)
            weights = jnp.exp(scores - largest)
            total = jnp.sum(weights, axis=-1, keepdims=True)
            values = rows[:, 2 * width + lo : 2 * width + hi]
            parts.append((dot(weights.astype(BF16), values) / total).astype(BF16))
            total_scr[slot, :, head : head + 1] = largest + jnp.log(total)
        context = jnp.concatenate(parts, axis=1)
        context_scr[slot] = context
        for copy in stores(seq):
            copy.start()
        wide, tail = pack_rows(context, seqlen // 2)
        gathered_ref[here, seq, :seqlen] = wide
        gathered_ref[here, seq, seqlen:] = tail

    def full_copy(seq, shard, side):
        return pltpu.make_async_remote_copy(
            src_ref=gathered_ref.at[shard, seq],
            dst_ref=gathered_ref.at[shard, seq],
            send_sem=gather_out.at[seq, shard, side],
            recv_sem=gather_sem.at[seq, shard],
            device_id=(me, here + 1 - 2 * side),
            device_id_type=MESH,
        )

    def each_side(hop, action):
        for side in range(2):
            shard = here - hop if side == 0 else here + hop
            there = shard >= 0 if side == 0 else shard <= ends
            onward = here < ends if side == 0 else here > 0
            action(side, shard, there, onward)

    def spread_hop(seq, hop):
        def one(side, shard, there, onward):
            @pl.when(there)
            def arrived():
                if hop > 0:
                    full_copy(seq, shard, side).wait_recv()
                if hop < ends:

                    @pl.when(onward)
                    def pass_on():
                        full_copy(seq, shard, side).start()

        each_side(hop, one)

    def spread_drain(seq):
        def one(side, shard, there, onward):
            @pl.when(there & onward)
            def sent():
                full_copy(seq, shard, side).wait_send()

        for hop in range(ends):
            each_side(hop, one)

    numbers = lax.broadcasted_iota(jnp.int32, (experts, 1), 0)

    def hot(rows):
        live = rows[2:3] > 0
        first = jnp.where((rows[0:1] == numbers) & live, 1.0, 0.0)
        second = jnp.where((rows[1:2] == numbers) & live, 1.0, 0.0)
        return first, second

    def tables():
        rank_row = rows_ref[3:4].astype(F32)
        diagonal = diagonal_of(seqlen)
        counts = jnp.zeros((2 * experts, tok_count), F32)
        for start in range(0, tok_count, seqlen):
            first, second = hot(rows_ref[:, start : start + seqlen])
            rank_col = as_column(rank_row[:, start : start + seqlen], diagonal)
            earlier = jnp.where(rank_col < rank_row, 1.0, 0.0)
            both = jnp.concatenate([first, second], axis=0)
            counts = counts + dot(both.astype(BF16), earlier.astype(BF16))
        first, second = hot(rows_ref[...])
        total = jnp.sum(first, axis=1, keepdims=True)
        places = [
            jnp.sum(first * counts[:experts], axis=0, keepdims=True),
            jnp.sum(second * (counts[experts:] + total), axis=0, keepdims=True),
        ]
        for pick in range(2):
            place = places[pick].astype(jnp.int32)
            kept = (place < capacity) & (rows_ref[2:3] > 0)
            ids_ref[pick : pick + 1] = jnp.where(
                kept, rows_ref[pick : pick + 1] * stride + place, -1
            )
        ids_ref[2:8] = jnp.full((6, tok_count), -1, jnp.int32)

    def cot_copy(step, target):
        return pltpu.make_async_remote_copy(
            src_ref=cot_send.at[target],
            dst_ref=cot_recv.at[me],
            send_sem=cot_send_sem.at[step],
            recv_sem=cot_recv_sem.at[step],
            device_id=(target, here),
            device_id_type=MESH,
        )

    def fill(target):
        slots = target * stride + lax.broadcasted_iota(jnp.int32, (stride, 1), 0)
        hit = (ids_ref[0:1] == slots) | (ids_ref[1:2] == slots)
        block = dot(jnp.where(hit, 1.0, 0.0).astype(BF16), cot_ref[...]).astype(BF16)
        return pack_rows(block, half)

    def dispatch():
        def one(step, carry):
            target = lax.rem(me + step, experts)
            wide, tail = fill(target)
            cot_send[target, :stride] = wide
            cot_send[target, stride:] = tail
            cot_copy(step, target).start()
            return carry

        lax.fori_loop(1, experts, one, 0)
        wide, tail = fill(me)
        cot_recv[me, :stride] = wide
        cot_recv[me, stride:] = tail

    out_full_ref[pl.ds(pl.multiple_of(here * weight_rows, 16), weight_rows)] = out_weight_ref[...]
    weight_hop(0)

    def time_step(step, carry):
        for hop in range(1, ends + 1):

            @pl.when(step == hop)
            def weights():
                weight_hop(hop)

        @pl.when(step == seq_count + 1)
        def send():
            dispatch()

        for hop in range(ends, 0, -1):

            @pl.when((step >= hop) & (step - hop < seq_count))
            def move():
                spread_hop(step - hop, hop)

        @pl.when(step < seq_count)
        def work():
            attend(step)
            spread_hop(step, 0)

        @pl.when(step == seq_count)
        def places():
            tables()

        @pl.when(step == seq_count + 1)
        def rows():
            own_rows()

        return carry

    lax.fori_loop(0, seq_count + ends, time_step, 0)
    for seq in range(seq_count):
        spread_drain(seq)
    for seq in range(max(seq_count - 2, 0), seq_count):
        for copy in stores(seq):
            copy.wait()

    def sent(side, shard, there, onward):
        @pl.when(there & onward)
        def drain():
            weight_copy(shard, side).wait_send()

    for hop in range(ends):
        each_side(hop, sent)
    for step in range(1, head_parts):
        pair_copy(step, core).wait_send()
        pair_copy(step, 1 - core).wait_recv()

    def finish(step, carry):
        cot_copy(step, lax.rem(me + step, experts)).wait()
        return carry

    lax.fori_loop(1, experts, finish, 0)


def head(
    tokens, norm_vectors, flat_qkv, qv_bias, segments, live, rows, cotangent, out_weight,
    experts, capacity, stride, half, part_half, head_parts,
):
    tok_count, model_width = tokens.shape
    seq_count, seqlen = segments.shape
    part = seqlen // head_parts
    wide = flat_qkv.shape[1]
    width = wide // 3
    dma = pltpu.SemaphoreType.DMA
    own = (head_parts, seq_count, part + part_half, LANES)
    slots = (experts, stride + half, LANES)
    return pl.pallas_call(
        partial(head_kernel, experts, capacity, stride, half, part_half, seq_count, head_parts),
        in_specs=[whole()] * 13,
        out_specs=[anywhere()] * 4 + [whole()] * 7,
        out_shape=[
            shaped((tok_count, model_width), BF16),
            shaped((tok_count, wide), BF16),
            shaped((tok_count, width), BF16),
            shaped((tok_count, LANES), F32),
            shaped((8, model_width), F32),
            shaped((head_parts * out_weight.shape[0], model_width), BF16),
            shaped((head_parts, seq_count, seqlen + seqlen // 2, LANES), BF16),
            shaped((8, tok_count), jnp.int32),
            shaped(slots, BF16),
            shaped(own, BF16),
            shaped((seq_count, part, model_width), BF16),
        ],
        scratch_shapes=[
            pltpu.VMEM(slots, BF16),
            pltpu.VMEM((2, seqlen, model_width), BF16),
            pltpu.VMEM((2, seqlen, wide), BF16),
            pltpu.VMEM((2, seqlen, width), BF16),
            pltpu.VMEM((2, seqlen, LANES), F32),
            dma((seq_count, head_parts)),
            dma((seq_count, head_parts, 2)),
            dma((experts,)),
            dma((experts,)),
            dma((2, 4)),
            dma((head_parts,)),
            dma((head_parts, 2)),
            dma((head_parts,)),
            dma((head_parts,)),
        ],
        compiler_params=params(collective_id=3, has_side_effects=True),
        cost_estimate=cost(6e10, 1e7),
        name="head",
    )(tokens, *norm_vectors, flat_qkv, qv_bias, segments, live, rows, cotangent, out_weight)


def gelu_parts(pre):
    root = math.sqrt(2.0 / math.pi)
    square = pre * pre
    wave = jnp.tanh(root * (pre + 0.044715 * pre * square))
    half_sum = 0.5 * (1.0 + wave)
    slope = half_sum + 0.5 * pre * (1.0 - wave * wave) * (
        root * (1.0 + 3.0 * 0.044715 * square)
    )
    return pre * half_sum, slope


def forward_kernel(
    experts, stride, half, seq_count, head_parts,
    gathered_ref, tokens_ref, vectors_ref, out_weight_ref, router_ref, rows_ref, ids_ref,
    up_ref, up_bias_ref, down_ref, down_bias_ref, cot_hbm,
    own_residual_ref, own_second_ref, own_columns_ref, gates_ref, arrived_hbm, hidden_hbm, result_hbm,
    gate_col_ref, cot_all, arrived_ref, hidden_scr, result_scr, residual_ref, context_scr, second_scr, logit_scr, send_scr, gate_send, gate_recv,
    send_sem, recv_sem, gate_send_sem, gate_recv_sem, cot_sem, cot_out, local_sem,
    arrived_sem, store_sem,
):
    me = lax.axis_index("exp")
    here = lax.axis_index("head")
    barrier = greet_both(experts, head_parts)
    ends = head_parts - 1
    pieces = cot_sem.shape[1]
    piece_rows = experts // pieces
    tok_count = tokens_ref.shape[0]

    def cot_copy(shard, piece, side, own=False):
        span = pl.ds(piece * piece_rows, piece_rows)
        return pltpu.make_async_remote_copy(
            src_ref=cot_hbm.at[span] if own else cot_all.at[shard, span],
            dst_ref=cot_all.at[shard, span],
            send_sem=cot_out.at[shard, piece, side],
            recv_sem=cot_sem.at[shard, piece],
            device_id=(me, here + 1 - 2 * side),
            device_id_type=MESH,
        )

    def cot_side(hop, side):
        shard = here - hop if side == 0 else here + hop
        there = shard >= 0 if side == 0 else shard <= ends
        onward = here < ends if side == 0 else here > 0
        return shard, there, onward

    def cot_hop(hop, piece):
        for side in range(2):
            shard, there, onward = cot_side(hop, side)

            @pl.when(there)
            def arrived():
                if hop > 0:
                    cot_copy(shard, piece, side).wait_recv()
                if hop < ends:

                    @pl.when(onward)
                    def pass_on():
                        cot_copy(shard, piece, side, hop == 0).start()

    def cot_drain(hop, piece):
        for side in range(2):
            shard, there, onward = cot_side(hop, side)

            @pl.when(there & onward)
            def sent():
                cot_copy(shard, piece, side, hop == 0).wait_send()

    local = pltpu.make_async_copy(cot_hbm, cot_all.at[here], local_sem.at[0])
    local.start()
    pl.semaphore_wait(barrier, experts - 1 + ends)
    for piece in range(pieces):
        cot_hop(0, piece)
    seqlen = tok_count // seq_count
    for seq in range(seq_count):
        span = slice(seq * seqlen, (seq + 1) * seqlen)
        unpack_rows(lambda z: gathered_ref[z, seq], context_scr, head_parts, seqlen, seqlen // 2)
        residual = (
            tokens_ref[span].astype(F32)
            + dot(context_scr[...], out_weight_ref[...])
            + vectors_ref[2:3]
        )
        residual_ref[span] = residual
        normal, ignored = standard(residual)
        second = (normal * vectors_ref[3:4] + vectors_ref[4:5]).astype(BF16)
        second_scr[span] = second
        logit_scr[:, span] = dot(second, router_ref[...]).T[:experts]
    part = seqlen // head_parts
    for seq in range(seq_count):
        own = pl.ds(pl.multiple_of(seq * seqlen + here * part, part), part)
        own_residual_ref[seq] = residual_ref[own]
        own_second_ref[seq] = second_scr[own]
    width = residual_ref.shape[1] // head_parts
    for z in range(head_parts):

        @pl.when(here == z)
        def columns():
            own_columns_ref[...] = residual_ref[:, z * width : (z + 1) * width]


    logits = logit_scr[...]
    powers = jnp.exp(logits - jnp.max(logits, axis=0, keepdims=True))
    chances = powers / jnp.sum(powers, axis=0, keepdims=True)
    numbers = lax.broadcasted_iota(jnp.int32, (experts, 1), 0)
    for pick in range(2):
        chosen = jnp.where(rows_ref[pick : pick + 1] == numbers, chances, 0.0)
        gate = jnp.where(ids_ref[pick : pick + 1] >= 0, jnp.sum(chosen, axis=0, keepdims=True), 0.0)
        gates_ref[pick : pick + 1] = gate
    gates_ref[2:8] = jnp.zeros((6, tok_count), F32)

    def copies(target, step):
        to = dict(device_id=(target, here), device_id_type=MESH)
        return (
            pltpu.make_async_remote_copy(
                src_ref=send_scr.at[step],
                dst_ref=arrived_ref.at[me],
                send_sem=send_sem.at[step],
                recv_sem=recv_sem.at[step],
                **to,
            ),
            pltpu.make_async_remote_copy(
                src_ref=gate_send.at[step],
                dst_ref=gate_recv.at[me],
                send_sem=gate_send_sem.at[step],
                recv_sem=gate_recv_sem.at[step],
                **to,
            ),
        )

    def fill(target):
        slots = target * stride + lax.broadcasted_iota(jnp.int32, (stride, 1), 0)
        first = ids_ref[0:1] == slots
        second = ids_ref[1:2] == slots
        block = dot(jnp.where(first | second, 1.0, 0.0).astype(BF16), second_scr[...]).astype(BF16)
        gate = jnp.sum(
            jnp.where(first, gates_ref[0:1], jnp.where(second, gates_ref[1:2], 0.0)),
            axis=1,
            keepdims=True,
        )
        return block, jnp.broadcast_to(gate, (stride, LANES)).T[:8]

    def send(step, carry):
        target = lax.rem(me + step, experts)
        block, gate = fill(target)
        send_scr[step] = block
        gate_send[step] = gate
        for copy in copies(target, step):
            copy.start()
        return carry

    lax.fori_loop(1, experts, send, 0)
    block, gate = fill(me)
    arrived_ref[me] = block
    gate_recv[me] = gate

    def source_of(step):
        return lax.rem(me + experts - step, experts)

    def arrived_store(step):
        source = source_of(step)
        return pltpu.make_async_copy(
            arrived_ref.at[source], arrived_hbm.at[source], arrived_sem.at[step]
        )

    def stores(step):
        source = source_of(step)
        slot = lax.rem(step, 2)
        return (
            pltpu.make_async_copy(hidden_scr.at[slot], hidden_hbm.at[source], store_sem.at[slot, 0]),
            pltpu.make_async_copy(result_scr.at[slot], result_hbm.at[:, source], store_sem.at[slot, 1]),
        )

    def work(step):
        source = source_of(step)
        slot = lax.rem(step, 2)
        arrived_store(step).start()
        pre = dot(arrived_ref[source], up_ref[...]) + up_bias_ref[...].astype(F32)
        hidden = gelu_parts(pre)[0].astype(BF16)
        result = dot(hidden, down_ref[...])
        down_bias = down_bias_ref[...].astype(F32)

        @pl.when(step >= 2)
        def free():
            for copy in stores(step - 2):
                copy.wait()

        hidden_scr[slot] = hidden
        for z in range(head_parts):
            columns = result[:, z * width : (z + 1) * width] + jnp.where(here == z, down_bias, 0.0)
            wide, tail = pack_rows(columns.astype(BF16), half)
            result_scr[slot, z, :stride] = wide
            result_scr[slot, z, stride:] = tail
        for copy in stores(step):
            copy.start()

    work(0)
    moves = [(hop, piece) for hop in range(1, ends) for piece in range(pieces)]
    early = len(moves) - min(experts - 2, len(moves))
    for move in moves[:early]:
        cot_hop(*move)

    def receive(step, carry):
        for place, move in enumerate(moves[early:]):

            @pl.when(step == place + 1)
            def pass_on():
                cot_hop(*move)

        source = lax.rem(me + experts - step, experts)
        wide, narrow = copies(source, step)
        wide.wait_recv()
        narrow.wait_recv()
        work(step)
        return carry

    lax.fori_loop(1, experts, receive, 0)

    for step in (experts - 2, experts - 1):
        for copy in stores(step):
            copy.wait()

    def stored(step, carry):
        arrived_store(step).wait()
        return carry

    lax.fori_loop(0, experts, stored, 0)

    def finish(step, carry):
        for copy in copies(lax.rem(me + step, experts), step):
            copy.wait_send()
        return carry

    lax.fori_loop(1, experts, finish, 0)
    for piece in range(pieces):
        cot_hop(ends, piece)
        for hop in range(ends):
            cot_drain(hop, piece)
    local.wait()
    lane = lax.broadcasted_iota(jnp.int32, (LANES, stride), 0)
    square = jnp.zeros((LANES, stride), F32)
    for source in range(experts):
        square = jnp.where(lane == source, gate_recv[source, 0:1], square)
    gate_col_ref[...] = square.T


def forward(
    gathered, tokens, vectors, out_weight, router, rows, ids, up, up_bias, down, down_bias, cot_slots,
    experts, stride, half, seq_count, head_parts,
):
    tok_count, model_width = tokens.shape
    seqlen = tok_count // seq_count
    part = seqlen // head_parts
    return pl.pallas_call(
        partial(forward_kernel, experts, stride, half, seq_count, head_parts),
        in_specs=[whole()] * 11 + [anywhere()],
        out_specs=[whole()] * 4 + [anywhere()] * 3 + [whole()] + [anywhere()],
        out_shape=[
            shaped((seq_count, part, model_width), F32),
            shaped((seq_count, part, model_width), BF16),
            shaped((tok_count, model_width // head_parts), F32),
            shaped((8, tok_count), F32),
            shaped((experts, stride, model_width), BF16),
            shaped((experts, stride, up.shape[1]), BF16),
            shaped((head_parts, experts, stride + half, LANES), BF16),
            shaped((stride, LANES), F32),
            shaped((head_parts, experts, stride + half, LANES), BF16),
        ],
        scratch_shapes=[
            pltpu.VMEM((experts, stride, model_width), BF16),
            pltpu.VMEM((2, stride, up.shape[1]), BF16),
            pltpu.VMEM((2, head_parts, stride + half, LANES), BF16),
            pltpu.VMEM((tok_count, model_width), F32),
            pltpu.VMEM((seqlen, model_width), BF16),
            pltpu.VMEM((tok_count, model_width), BF16),
            pltpu.VMEM((experts, tok_count), F32),
            pltpu.VMEM((experts, stride, model_width), BF16),
            pltpu.VMEM((experts, 8, stride), F32),
            pltpu.VMEM((experts, 8, stride), F32),
            pltpu.SemaphoreType.DMA((experts,)),
            pltpu.SemaphoreType.DMA((experts,)),
            pltpu.SemaphoreType.DMA((experts,)),
            pltpu.SemaphoreType.DMA((experts,)),
            pltpu.SemaphoreType.DMA((head_parts, 4)),
            pltpu.SemaphoreType.DMA((head_parts, 4, 2)),
            pltpu.SemaphoreType.DMA((1,)),
            pltpu.SemaphoreType.DMA((experts,)),
            pltpu.SemaphoreType.DMA((2, 2)),
        ],
        compiler_params=params(collective_id=0, has_side_effects=True),
        cost_estimate=cost(8e10, 1e8),
        name="forward",
    )(gathered, tokens, vectors, out_weight, router, rows, ids, up, up_bias, down, down_bias, cot_slots)


def backward_kernel(
    experts, stride, half, head_parts, chunk,
    arrived_hbm, hidden_hbm, result_hbm, cot_hbm, gate_col_ref, ids_ref, up_ref, up_bias_ref, down_ref,
    sums_ref, route_ref, grad_up_ref, grad_up_bias_ref, grad_down_ref, grad_down_bias_ref,
    rows_scr, result_scr, cot_scr, cot_wide, result_wide, hidden_scr, pre_grad_scr, out_grad_scr,
    send_scr, recv_scr, gate_send, gate_recv, total_scr,
    load_sem, send_sem, recv_sem, gate_send_sem, gate_recv_sem,
):
    me = lax.axis_index("exp")
    here = lax.axis_index("head")
    barrier = greet(experts)
    tok_count = ids_ref.shape[0]
    model_width = up_ref.shape[0]

    def loads(step):
        home = lax.rem(me + step, experts)
        slot = lax.rem(step, 2)
        return (
            pltpu.make_async_copy(arrived_hbm.at[home], rows_scr.at[slot], load_sem.at[slot, 0]),
            pltpu.make_async_copy(result_hbm.at[:, home], result_scr.at[slot], load_sem.at[slot, 1]),
            pltpu.make_async_copy(cot_hbm.at[:, home], cot_scr.at[slot], load_sem.at[slot, 2]),
        )

    def copies(target, step):
        to = dict(device_id=(target, here), device_id_type=MESH)
        return (
            pltpu.make_async_remote_copy(
                src_ref=send_scr.at[step],
                dst_ref=recv_scr.at[me],
                send_sem=send_sem.at[step],
                recv_sem=recv_sem.at[step],
                **to,
            ),
            pltpu.make_async_remote_copy(
                src_ref=gate_send.at[step],
                dst_ref=gate_recv.at[me],
                send_sem=gate_send_sem.at[step],
                recv_sem=gate_recv_sem.at[step],
                **to,
            ),
        )

    for copy in loads(1):
        copy.start()
    grad_up_ref[...] = jnp.zeros_like(grad_up_ref)
    grad_down_ref[...] = jnp.zeros_like(grad_down_ref)
    grad_up_bias_ref[...] = jnp.zeros_like(grad_up_bias_ref)
    grad_down_bias_ref[...] = jnp.zeros_like(grad_down_bias_ref)
    total_scr[...] = jnp.zeros_like(total_scr)
    pl.semaphore_wait(barrier, experts - 1)

    def work(step):
        home = lax.rem(me + step, experts)
        slot = lax.rem(step, 2)
        for copy in loads(step):
            copy.wait()
        unpack_rows(lambda z: cot_scr[slot, z], cot_wide, head_parts, stride, half)
        unpack_rows(lambda z: result_scr[slot, z], result_wide, head_parts, stride, half)
        out_rows = cot_wide[...].astype(F32)
        pre = dot(rows_scr[slot], up_ref[...]) + up_bias_ref[...].astype(F32)
        slope = gelu_parts(pre)[1]
        lane = lax.broadcasted_iota(jnp.int32, (stride, LANES), 1)
        gate = jnp.sum(jnp.where(lane == home, gate_col_ref[...], 0.0), axis=1, keepdims=True)
        out_grad = (gate * out_rows).astype(BF16)
        out_grad_scr[step] = out_grad
        grad_down_bias_ref[0:1] += jnp.sum(out_grad.astype(F32), axis=0, keepdims=True)
        pre_grad = (dot_last(out_grad, down_ref[...]) * slope).astype(BF16)
        pre_grad_scr[step] = pre_grad
        grad_up_bias_ref[0:1] += jnp.sum(pre_grad.astype(F32), axis=0, keepdims=True)
        gate_grad = jnp.sum(result_wide[...].astype(F32) * out_rows, axis=1, keepdims=True)
        return (
            dot_last(pre_grad, up_ref[...]).astype(BF16),
            jnp.broadcast_to(gate_grad, (stride, LANES)).T[:8],
        )

    def send(step, carry):
        for copy in loads(lax.rem(step + 1, experts)):
            copy.start()
        block, gate = work(step)
        send_scr[step] = block
        gate_send[step] = gate
        for copy in copies(lax.rem(me + step, experts), step):
            copy.start()
        return carry

    lax.fori_loop(1, experts, send, 0)
    block, gate = work(0)
    recv_scr[me] = block
    gate_recv[me] = gate

    def row_loads(step):
        home = lax.rem(me + step, experts)
        slot = lax.rem(step, 2)
        return (
            pltpu.make_async_copy(arrived_hbm.at[home], rows_scr.at[slot], load_sem.at[slot, 0]),
            pltpu.make_async_copy(hidden_hbm.at[home], hidden_scr.at[slot], load_sem.at[slot, 1]),
        )

    def weigh(step):
        slot = lax.rem(step, 2)
        for copy in row_loads(step):
            copy.wait()
        grad_up_ref[...] += dot_first(rows_scr[slot], pre_grad_scr[step])
        grad_down_ref[...] += dot_first(hidden_scr[slot], out_grad_scr[step])

    def weigh_some(step, carry):
        for copy in row_loads(step + 1):
            copy.start()
        weigh(step)
        return carry

    for copy in row_loads(0):
        copy.start()
    lax.fori_loop(0, experts - 1, weigh_some, 0)
    weigh(experts - 1)

    def gather(source):
        slots = source * stride + lax.broadcasted_iota(jnp.int32, (1, stride), 1)
        lane = lax.broadcasted_iota(jnp.int32, (chunk, LANES), 1)

        def part(index, carry):
            span = pl.ds(pl.multiple_of(index * chunk, chunk), chunk)
            hit = (ids_ref[span, 0:1] == slots) | (ids_ref[span, 1:2] == slots)
            total_scr[span, :model_width] += dot(
                jnp.where(hit, 1.0, 0.0).astype(BF16), recv_scr[source]
            )
            gate = jnp.sum(jnp.where(hit, gate_recv[source, 0:1], 0.0), axis=1, keepdims=True)
            total_scr[span, model_width:] = jnp.where(
                lane == source, gate, total_scr[span, model_width:]
            )
            return carry

        lax.fori_loop(0, tok_count // chunk, part, 0)

    gather(me)

    def receive(step, carry):
        source = lax.rem(me + experts - step, experts)
        for copy in copies(source, step):
            copy.wait_recv()
        gather(source)
        return carry

    lax.fori_loop(1, experts, receive, 0)
    sums_ref[...] = total_scr[:, :model_width].astype(BF16)
    parts, seqs, kinds, count = route_ref.shape
    for seq in range(seqs):
        for z in range(parts):
            start = (seq * parts + z) * count
            route_ref[z, seq] = total_scr[start : start + count, model_width:].T[:kinds]

    def finish(step, carry):
        for copy in copies(lax.rem(me + step, experts), step):
            copy.wait_send()
        return carry

    lax.fori_loop(1, experts, finish, 0)


def backward(
    arrived, hidden, result, cot_rows, gate_col, id_cols, up, up_bias, down, half, head_parts, chunk
):
    tok_count = id_cols.shape[0]
    experts, stride, model_width = arrived.shape
    inner = up.shape[1]
    rows = (experts, stride, model_width)
    return pl.pallas_call(
        partial(backward_kernel, experts, stride, half, head_parts, chunk),
        in_specs=[anywhere()] * 4 + [whole()] * 5,
        out_specs=[whole()] * 6,
        out_shape=[
            shaped((tok_count, model_width), BF16),
            shaped((head_parts, tok_count // chunk, round_up(experts, 8), chunk // head_parts), F32),
            shaped((model_width, inner), F32),
            shaped((8, inner), F32),
            shaped((inner, model_width), F32),
            shaped((8, model_width), F32),
        ],
        scratch_shapes=[
            pltpu.VMEM((2, stride, model_width), BF16),
            pltpu.VMEM((2, head_parts, stride + half, LANES), BF16),
            pltpu.VMEM((2, head_parts, stride + half, LANES), BF16),
            pltpu.VMEM((stride, model_width), BF16),
            pltpu.VMEM((stride, model_width), BF16),
            pltpu.VMEM((2, stride, inner), BF16),
            pltpu.VMEM((experts, stride, inner), BF16),
            pltpu.VMEM(rows, BF16),
            pltpu.VMEM(rows, BF16),
            pltpu.VMEM(rows, BF16),
            pltpu.VMEM((experts, 8, stride), F32),
            pltpu.VMEM((experts, 8, stride), F32),
            pltpu.VMEM((tok_count, model_width + LANES), F32),
            pltpu.SemaphoreType.DMA((2, 3)),
            pltpu.SemaphoreType.DMA((experts,)),
            pltpu.SemaphoreType.DMA((experts,)),
            pltpu.SemaphoreType.DMA((experts,)),
            pltpu.SemaphoreType.DMA((experts,)),
        ],
        compiler_params=params(collective_id=1, has_side_effects=True),
        cost_estimate=cost(8e10, 1e8),
        name="backward",
    )(arrived, hidden, result, cot_rows, gate_col, id_cols, up, up_bias, down)


def copy_kernel(first_ref, second_ref, first_out, second_out):
    first_out[...] = first_ref[...]
    second_out[...] = second_ref[...]


def copies_of(first, second):
    rows = first.shape[0] // 4
    specs = [pl.BlockSpec((rows, a.shape[1]), lambda i: (i, 0)) for a in (first, second)]
    return pl.pallas_call(
        copy_kernel,
        grid=(4,),
        in_specs=specs,
        out_specs=specs,
        out_shape=[shaped(first.shape, F32), shaped(second.shape, F32)],
        compiler_params=params(),
        cost_estimate=cost(0, 1e7),
        name="copies",
    )(first, second)


def tail_kernel(
    experts, stride, half, part_half, seq_count, head_parts, gap,
    sums_ref, route_hbm, id_cols_ref, gate_cols_ref, own_residual_ref, own_second_ref, cot_own_hbm,
    own_columns_hbm, router_ref, vectors_ref, own_tokens_ref, result_hbm,
    context_hbm, first_hbm, qkv_hbm, totals_hbm, weight_ref, out_weight_ref,
    seg_ref, live_ref,
    tokens_hbm, block_ref, qkv_sum_ref, out_sum_ref, bias_sum_ref, small_ref,
    route_recv, own_recv, cot_wide, columns_scr, part_two, down_one, up_one, down_two, up_two, own_scr,
    full_one, full_two, grad_scr,
    context_scr, first_scr, qkv_scr, totals_scr, back_scr, joined_scr,
    qkv_grad, out_grad, bias_grad, rows_acc, router_acc,
    result_home, result_wide,
    qkv_send, qkv_recv, qkv_all, out_send, out_recv, out_all, bias_recv, small_head, small_recv,
    route_send_sem, route_recv_sem, own_send_sem, own_recv_sem, columns_sem, load_sem, stage_sem, result_send_sem, result_recv_sem,
    down_one_sem, up_one_sem, down_two_sem, up_two_sem, down_one_out, up_one_out, down_two_out, up_two_out,
    full_one_sem, full_two_sem, full_one_out, full_two_out,
    sum_send_sem, sum_recv_sem, all_send_sem, all_recv_sem,
    bias_send_sem, bias_recv_sem, head_send_sem, head_recv_sem, small_send_sem, small_recv_sem,
):
    me = lax.axis_index("exp")
    here = lax.axis_index("head")
    ends = head_parts - 1
    seqlen = seg_ref.shape[1]
    part = seqlen // head_parts
    model_width = vectors_ref.shape[1]
    width = out_weight_ref.shape[0]
    factor = 1.0 / math.sqrt(HEAD_DIM)

    barrier = greet_both(experts, head_parts)

    def chunk_loads(seq):
        span = pl.ds(pl.multiple_of(seq * seqlen, seqlen), seqlen)
        return (
            pltpu.make_async_copy(context_hbm.at[span], context_scr, load_sem.at[0]),
            pltpu.make_async_copy(first_hbm.at[span], first_scr, load_sem.at[1]),
            pltpu.make_async_copy(qkv_hbm.at[span], qkv_scr, load_sem.at[2]),
            pltpu.make_async_copy(totals_hbm.at[span], totals_scr, load_sem.at[3]),
        )

    for copy in chunk_loads(0):
        copy.start()
    qkv_grad[...] = jnp.zeros_like(qkv_grad)
    out_grad[...] = jnp.zeros_like(out_grad)
    bias_grad[...] = jnp.zeros_like(bias_grad)
    rows_acc[...] = jnp.zeros_like(rows_acc)
    router_acc[...] = jnp.zeros_like(router_acc)
    pl.semaphore_wait(barrier, experts - 1 + ends)

    def to_exp(target):
        return dict(device_id=(target, here), device_id_type=MESH)

    def to_head(target):
        return dict(device_id=(me, target), device_id_type=MESH)

    def each_peer(action):
        def one(step, carry):
            action(step, lax.rem(me + step, experts), lax.rem(me + experts - step, experts))
            return carry

        lax.fori_loop(1, experts, one, 0)

    def result_copy(step, target):
        return pltpu.make_async_remote_copy(
            src_ref=result_hbm.at[target],
            dst_ref=result_home.at[me],
            send_sem=result_send_sem.at[step],
            recv_sem=result_recv_sem.at[step],
            **to_exp(target),
        )

    def own_copy(seq, step):
        target = lax.rem(here + step, head_parts)
        return pltpu.make_async_remote_copy(
            src_ref=cot_own_hbm.at[target, seq],
            dst_ref=own_recv.at[here, seq],
            send_sem=own_send_sem.at[seq, step],
            recv_sem=own_recv_sem.at[seq, step],
            **to_head(target),
        )

    def route_copy(step):
        target = lax.rem(here + step, head_parts)
        return pltpu.make_async_remote_copy(
            src_ref=route_hbm.at[target],
            dst_ref=route_recv.at[here],
            send_sem=route_send_sem.at[step],
            recv_sem=route_recv_sem.at[step],
            **to_head(target),
        )

    for other in range(1, head_parts):
        route_copy(other).start()
    route_local = pltpu.make_async_copy(route_hbm.at[here], route_recv.at[here], columns_sem.at[2])
    route_local.start()
    route_local.wait()
    own_local = pltpu.make_async_copy(cot_own_hbm.at[here], own_recv.at[here], columns_sem.at[1])
    own_local.start()
    own_local.wait()

    def down_copy(buffer, sems, outs, seq, shard):
        return pltpu.make_async_remote_copy(
            src_ref=buffer.at[seq, shard],
            dst_ref=buffer.at[seq, shard],
            send_sem=outs.at[seq, shard],
            recv_sem=sems.at[seq, shard],
            **to_head(here - 1),
        )

    def up_copy(buffer, sems, outs, seq, shard):
        return pltpu.make_async_remote_copy(
            src_ref=buffer.at[seq, shard - 1],
            dst_ref=buffer.at[seq, shard - 1],
            send_sem=outs.at[seq, shard - 1],
            recv_sem=sems.at[seq, shard - 1],
            **to_head(here + 1),
        )

    one_down = (down_one, down_one_sem, down_one_out)
    one_up = (up_one, up_one_sem, up_one_out)
    two_down = (down_two, down_two_sem, down_two_out)
    two_up = (up_two, up_two_sem, up_two_out)

    def reduce_hop(partial_ref, base, down, up, seq, hop):
        low = hop - ends + here
        high = ends - hop + here

        @pl.when((low >= 0) & (low < here))
        def downward():
            rows = partial_ref[pl.ds(pl.multiple_of(base + low * part, part), part)]

            @pl.when(here < ends)
            def add():
                down_copy(*down, seq, low).wait_recv()
                down[0][seq, low] = (down[0][seq, low].astype(F32) + rows.astype(F32)).astype(BF16)

            @pl.when(here == ends)
            def begin():
                down[0][seq, low] = rows

            down_copy(*down, seq, low).start()

        @pl.when((high > here) & (high <= ends))
        def upward():
            rows = partial_ref[pl.ds(pl.multiple_of(base + high * part, part), part)]

            @pl.when(here > 0)
            def add():
                up_copy(*up, seq, high).wait_recv()
                up[0][seq, high - 1] = (
                    up[0][seq, high - 1].astype(F32) + rows.astype(F32)
                ).astype(BF16)

            @pl.when(here == 0)
            def begin():
                up[0][seq, high - 1] = rows

            up_copy(*up, seq, high).start()

    def reduce_end(partial_ref, base, down, up, seq):
        own = pl.ds(pl.multiple_of(base + here * part, part), part)
        own_scr[...] = partial_ref[own].astype(F32)

        @pl.when(here < ends)
        def below():
            down_copy(*down, seq, here).wait_recv()
            own_scr[...] += down[0][seq, here].astype(F32)

        @pl.when(here > 0)
        def above():
            up_copy(*up, seq, here).wait_recv()
            own_scr[...] += up[0][seq, here - 1].astype(F32)

    def reduce_drain(down, up, seq):
        for shard in range(ends):

            @pl.when(shard < here)
            def downward():
                down_copy(*down, seq, shard).wait_send()

            @pl.when(shard + 1 > here)
            def upward():
                up_copy(*up, seq, shard + 1).wait_send()

    def full_copy(buffer, sems, outs, seq, shard, side):
        rows = pl.ds(pl.multiple_of(shard * part, part), part)
        return pltpu.make_async_remote_copy(
            src_ref=buffer.at[seq, rows],
            dst_ref=buffer.at[seq, rows],
            send_sem=outs.at[seq, shard, side],
            recv_sem=sems.at[seq, shard],
            **to_head(here + 1 - 2 * side),
        )

    one_full = (full_one, full_one_sem, full_one_out)
    two_full = (full_two, full_two_sem, full_two_out)

    def spread_hop(full, seq, hop):
        for side in range(2):
            shard = here - hop if side == 0 else here + hop
            there = shard >= 0 if side == 0 else shard <= ends
            onward = here < ends if side == 0 else here > 0

            @pl.when(there)
            def arrived():
                if hop > 0:
                    full_copy(*full, seq, shard, side).wait_recv()
                if hop < ends:

                    @pl.when(onward)
                    def pass_on():
                        full_copy(*full, seq, shard, side).start()

    def spread_drain(full, seq):
        for hop in range(ends):
            for side in range(2):
                shard = here - hop if side == 0 else here + hop
                there = shard >= 0 if side == 0 else shard <= ends
                onward = here < ends if side == 0 else here > 0

                @pl.when(there & onward)
                def sent():
                    full_copy(*full, seq, shard, side).wait_send()

    def middle(seq):
        second = own_second_ref[seq]
        lane = lax.broadcasted_iota(jnp.int32, (part, LANES), 1)
        logits = jnp.where(lane < experts, dot(second, router_ref[...]), NEGATIVE)
        powers = jnp.exp(logits - jnp.max(logits, axis=1, keepdims=True))
        chances = powers / jnp.sum(powers, axis=1, keepdims=True)
        @pl.when(seq == 0)
        def routes():
            for other in range(1, head_parts):
                route_copy(other).wait_recv()

        route = route_recv[0, seq]
        for other in range(1, head_parts):
            route = route + route_recv[other, seq]
        blank = jnp.zeros((LANES - route.shape[0], part), F32)
        route_grad = jnp.concatenate([route, blank], axis=0).T
        logit_grad = (
            chances * (route_grad - jnp.sum(chances * route_grad, axis=1, keepdims=True))
        ).astype(BF16)
        router_acc[...] += dot_first(second, logit_grad)
        grad = own_scr[...] + dot_last(logit_grad, router_ref[...])
        normal, scale = standard(own_residual_ref[seq])
        rows_acc[0:1] += jnp.sum(grad * normal, axis=0, keepdims=True)
        rows_acc[1:2] += jnp.sum(grad, axis=0, keepdims=True)
        for other in range(1, head_parts):
            own_copy(seq, other).wait_recv()
        unpack_rows(lambda z: own_recv[z, seq], cot_wide, head_parts, part, part_half)
        total = cot_wide[...].astype(F32) + norm_back(grad, vectors_ref[3:4], normal, scale)
        rows_acc[2:3] += jnp.sum(total, axis=0, keepdims=True)
        grad_scr[seq] = total
        full_one[seq, pl.ds(pl.multiple_of(here * part, part), part)] = total.astype(BF16)

    def attend_start(seq):
        for copy in chunk_loads(seq):
            copy.wait()
        grad = full_one[seq]
        back_scr[...] = dot_last(grad, out_weight_ref[...]).astype(BF16)
        out_grad[...] += dot_first(context_scr[...], grad)
        return mask_penalty(seg_ref[pl.ds(seq, 1)], live_ref[pl.ds(seq, 1)])

    def attend_head(head, penalty):
        lo = head * HEAD_DIM
        hi = lo + HEAD_DIM
        query = qkv_scr[:, lo:hi] * BF16(factor)
        keys = qkv_scr[:, width + lo : width + hi]
        values = qkv_scr[:, 2 * width + lo : 2 * width + hi]
        back = back_scr[:, lo:hi]
        weights = jnp.exp(
            dot_last(query, keys) + penalty - totals_scr[:, head : head + 1]
        )
        joined_scr[:, 2 * width + lo : 2 * width + hi] = dot_first(
            weights.astype(BF16), back
        ).astype(BF16)
        inner = jnp.sum(
            back.astype(F32) * context_scr[:, lo:hi].astype(F32), axis=-1, keepdims=True
        )
        score_grad = (weights * (dot_last(back, values) - inner)).astype(BF16)
        joined_scr[:, lo:hi] = (dot(score_grad, keys) * factor).astype(BF16)
        joined_scr[:, width + lo : width + hi] = dot_first(score_grad, query).astype(BF16)

    def attend_end(seq):
        joined = joined_scr[...]
        span = pl.ds(pl.multiple_of(lax.rem(seq, 2) * seqlen, seqlen), seqlen)
        part_two[span] = dot_last(joined, weight_ref[...]).astype(BF16)
        qkv_grad[...] += dot_first(first_scr[...], joined)
        bias_grad[0:1] += jnp.sum(joined.astype(F32), axis=0, keepdims=True)

        @pl.when(seq + 1 < seq_count)
        def more():
            for copy in chunk_loads(seq + 1):
                copy.start()

    def last(seq):
        grad = own_scr[...]
        normal, scale = standard(own_tokens_ref[seq].astype(F32))
        rows_acc[3:4] += jnp.sum(grad * normal, axis=0, keepdims=True)
        rows_acc[4:5] += jnp.sum(grad, axis=0, keepdims=True)
        total = grad_scr[seq] + norm_back(grad, vectors_ref[0:1], normal, scale)
        full_two[seq, pl.ds(pl.multiple_of(here * part, part), part)] = total.astype(BF16)

    def stage_copy(seq):
        span = pl.ds(pl.multiple_of(seq * seqlen, seqlen), seqlen)
        return pltpu.make_async_copy(full_two.at[seq], tokens_hbm.at[span], stage_sem.at[seq])

    def open_results():
        each_peer(lambda step, target, source: result_copy(step, target).wait_recv())

        def one(expert, carry):
            packed = result_home[expert]
            result_wide[expert, :, :LANES] = packed[:stride]
            tail = packed[stride:]
            result_wide[expert, :half, LANES:] = tail[:, :HEAD_DIM]
            result_wide[expert, half:, LANES:] = tail[2 * half - stride :, HEAD_DIM:]
            return carry

        lax.fori_loop(0, experts, one, 0)

    def combine(seq):
        span = pl.ds(pl.multiple_of(seq * seqlen, seqlen), seqlen)
        first = id_cols_ref[span, 0:1]
        second = id_cols_ref[span, 1:2]
        pltpu.make_async_copy(own_columns_hbm.at[span], columns_scr, columns_sem.at[0]).start()
        pltpu.make_async_copy(own_columns_hbm.at[span], columns_scr, columns_sem.at[0]).wait()
        first_gate = gate_cols_ref[span, 0:1]
        second_gate = gate_cols_ref[span, 1:2]

        def one(expert, total):
            slots = expert * stride + lax.broadcasted_iota(jnp.int32, (1, stride), 1)
            weights = jnp.where(
                first == slots, first_gate, jnp.where(second == slots, second_gate, 0.0)
            )
            return total + dot(weights.astype(BF16), result_wide[expert])

        block_ref[span] = lax.fori_loop(0, experts, one, columns_scr[...]).astype(BF16)

    qkv_rows = qkv_grad.shape[0] // experts
    out_rows = out_grad.shape[0] // experts

    def sum_copies(step, target):
        return (
            pltpu.make_async_remote_copy(
                src_ref=qkv_send.at[target],
                dst_ref=qkv_recv.at[me],
                send_sem=sum_send_sem.at[step, 0],
                recv_sem=sum_recv_sem.at[step, 0],
                **to_exp(target),
            ),
            pltpu.make_async_remote_copy(
                src_ref=out_send.at[target],
                dst_ref=out_recv.at[me],
                send_sem=sum_send_sem.at[step, 1],
                recv_sem=sum_recv_sem.at[step, 1],
                **to_exp(target),
            ),
        )

    def all_copies(step, target):
        return (
            pltpu.make_async_remote_copy(
                src_ref=qkv_all.at[me],
                dst_ref=qkv_all.at[me],
                send_sem=all_send_sem.at[step, 0],
                recv_sem=all_recv_sem.at[step, 0],
                **to_exp(target),
            ),
            pltpu.make_async_remote_copy(
                src_ref=out_all.at[me],
                dst_ref=out_all.at[me],
                send_sem=all_send_sem.at[step, 1],
                recv_sem=all_recv_sem.at[step, 1],
                **to_exp(target),
            ),
        )

    def all_arrivals(step, source):
        return (
            pltpu.make_async_remote_copy(
                src_ref=qkv_all.at[source],
                dst_ref=qkv_all.at[source],
                send_sem=all_send_sem.at[step, 0],
                recv_sem=all_recv_sem.at[step, 0],
                **to_exp(source),
            ),
            pltpu.make_async_remote_copy(
                src_ref=out_all.at[source],
                dst_ref=out_all.at[source],
                send_sem=all_send_sem.at[step, 1],
                recv_sem=all_recv_sem.at[step, 1],
                **to_exp(source),
            ),
        )

    def bias_copy(step, target):
        return pltpu.make_async_remote_copy(
            src_ref=bias_grad,
            dst_ref=bias_recv.at[me],
            send_sem=bias_send_sem.at[step],
            recv_sem=bias_recv_sem.at[step],
            **to_exp(target),
        )

    def start_sums():
        for block in range(experts):
            qkv_send[block] = qkv_grad[block * qkv_rows : (block + 1) * qkv_rows].astype(BF16)
            out_send[block] = out_grad[block * out_rows : (block + 1) * out_rows].astype(BF16)

        def begin(step, target, source):
            for copy in sum_copies(step, target):
                copy.start()
            bias_copy(step, target).start()

        each_peer(begin)
        qkv_recv[me] = qkv_send[me]
        out_recv[me] = out_send[me]
        bias_recv[me] = bias_grad[...]

    def spread_sums():
        def arrive(step, target, source):
            for copy in sum_copies(step, target):
                copy.wait_recv()
            bias_copy(step, target).wait_recv()

        each_peer(arrive)

        def add(source, totals):
            return (
                totals[0] + qkv_recv[source].astype(F32),
                totals[1] + out_recv[source].astype(F32),
                totals[2] + bias_recv[source],
            )

        qkv_total, out_total, bias_total = lax.fori_loop(
            1,
            experts,
            add,
            (qkv_recv[0].astype(F32), out_recv[0].astype(F32), bias_recv[0]),
        )
        qkv_all[me] = qkv_total.astype(BF16)
        out_all[me] = out_total.astype(BF16)
        bias_sum_ref[...] = bias_total

        def begin(step, target, source):
            for copy in all_copies(step, target):
                copy.start()

        each_peer(begin)

    def end_sums():
        def arrive(step, target, source):
            for copy in all_arrivals(step, source):
                copy.wait_recv()

        each_peer(arrive)
        for block in range(experts):
            qkv_sum_ref[block * qkv_rows : (block + 1) * qkv_rows] = qkv_all[block].astype(F32)
            out_sum_ref[block * out_rows : (block + 1) * out_rows] = out_all[block].astype(F32)

    def head_copy(step):
        return pltpu.make_async_remote_copy(
            src_ref=small_head.at[here],
            dst_ref=small_head.at[here],
            send_sem=head_send_sem.at[step],
            recv_sem=head_recv_sem.at[step],
            **to_head(lax.rem(here + step, head_parts)),
        )

    def head_arrival(step):
        source = lax.rem(here + head_parts - step, head_parts)
        return pltpu.make_async_remote_copy(
            src_ref=small_head.at[source],
            dst_ref=small_head.at[source],
            send_sem=head_send_sem.at[step],
            recv_sem=head_recv_sem.at[step],
            **to_head(source),
        )

    def small_copy(step, target):
        return pltpu.make_async_remote_copy(
            src_ref=small_recv.at[me],
            dst_ref=small_recv.at[me],
            send_sem=small_send_sem.at[step],
            recv_sem=small_recv_sem.at[step],
            **to_exp(target),
        )

    def small_arrival(step, source):
        return pltpu.make_async_remote_copy(
            src_ref=small_recv.at[source],
            dst_ref=small_recv.at[source],
            send_sem=small_send_sem.at[step],
            recv_sem=small_recv_sem.at[step],
            **to_exp(source),
        )

    heads = width // HEAD_DIM
    router_rows = small_head.shape[1] - 8

    second_start = 2 * ends
    spread_start = second_start + ends
    ticks = spread_start + ends + 1 + gap * (seq_count - 1)
    final = gap * (seq_count - 1)

    def tick(now, carry):
        def on(offset, action):
            since = now - offset

            @pl.when((since >= 0) & (lax.rem(since, gap) == 0) & (since < gap * seq_count))
            def run():
                action(since // gap)

        def first_end(seq):
            reduce_end(sums_ref, seq * seqlen, one_down, one_up, seq)
            middle(seq)

        def attend(seq):
            spread_hop(one_full, seq, ends)
            penalty = attend_start(seq)
            for head in range(heads):
                attend_head(head, penalty)
            attend_end(seq)

        def second_end(seq):
            reduce_end(part_two, lax.rem(seq, 2) * seqlen, two_down, two_up, seq)
            last(seq)

        def tokens_end(seq):
            spread_hop(two_full, seq, ends)
            stage_copy(seq).start()

        def own_begin(seq):
            for other in range(1, head_parts):
                own_copy(seq, other).start()

        on(ends, first_end)
        on(spread_start, second_end)
        for hop in range(ends):
            on(hop, lambda seq: reduce_hop(sums_ref, seq * seqlen, one_down, one_up, seq, hop))
            on(ends + hop, lambda seq: spread_hop(one_full, seq, hop))
            if hop > 0:
                on(
                    second_start + hop,
                    lambda seq: reduce_hop(
                        part_two, lax.rem(seq, 2) * seqlen, two_down, two_up, seq, hop
                    ),
                )
            on(spread_start + hop, lambda seq: spread_hop(two_full, seq, hop))
        on(0, own_begin)
        on(second_start, attend)
        on(
            second_start,
            lambda seq: reduce_hop(part_two, lax.rem(seq, 2) * seqlen, two_down, two_up, seq, 0),
        )

        @pl.when(now == 0)
        def send_results():
            each_peer(lambda step, target, source: result_copy(step, target).start())
            local = pltpu.make_async_copy(result_hbm.at[me], result_home.at[me], columns_sem.at[1])
            local.start()
            local.wait()

        @pl.when(now == ends + 1)
        def results():
            open_results()

        on(ends + 2, combine)

        @pl.when(now == final + second_start)
        def sums():
            start_sums()

        @pl.when(now == final + second_start + 2)
        def share():
            spread_sums()

        @pl.when(now == final + spread_start)
        def small():
            small_head[here, :8] = rows_acc[...]
            small_head[here, 8:] = router_acc[...].T[:router_rows]
            for other in range(1, head_parts):
                head_copy(other).start()

        @pl.when(now == final + spread_start + 1)
        def small_on():
            for other in range(1, head_parts):
                head_arrival(other).wait_recv()
            total = small_head[0]
            for other in range(1, head_parts):
                total = total + small_head[other]
            small_recv[me] = total
            each_peer(lambda step, target, source: small_copy(step, target).start())
            end_sums()

        on(spread_start + ends, tokens_end)
        return carry

    lax.fori_loop(0, ticks, tick, 0)

    each_peer(lambda step, target, source: small_arrival(step, source).wait_recv())
    small_ref[...] = lax.fori_loop(
        1, experts, lambda source, total: total + small_recv[source], small_recv[0]
    )
    for seq in range(seq_count):
        stage_copy(seq).wait()
        reduce_drain(one_down, one_up, seq)
        reduce_drain(two_down, two_up, seq)
        spread_drain(one_full, seq)
        spread_drain(two_full, seq)
    for other in range(1, head_parts):
        head_copy(other).wait_send()
        route_copy(other).wait_send()
        for seq in range(seq_count):
            own_copy(seq, other).wait_send()

    def sent(step, target, source):
        result_copy(step, target).wait_send()
        for copy in sum_copies(step, target):
            copy.wait_send()
        bias_copy(step, target).wait_send()
        for copy in all_copies(step, target):
            copy.wait_send()
        small_copy(step, target).wait_send()

    each_peer(sent)


def tail(
    sums, route, id_cols, gate_cols, own_residual, own_second, cot_own, own_columns, router, vectors,
    own_tokens, result, context, first, qkv, totals, flat_qkv, out_weight,
    segments, live, stride, half, part_half, head_parts,
):
    experts = result.shape[0]
    model_width = first.shape[1]
    seq_count, part = own_residual.shape[:2]
    seqlen = part * head_parts
    tok_count = seq_count * seqlen
    wide = flat_qkv.shape[1]
    width = wide // 3
    ends = head_parts - 1
    small_rows = 8 + round_up(experts, 8)
    dma = pltpu.SemaphoreType.DMA
    return pl.pallas_call(
        partial(tail_kernel, experts, stride, half, part_half, seq_count, head_parts, 2),
        in_specs=[whole(), anywhere()] + [whole()] * 4 + [anywhere()] * 2 + [whole()] * 3 + [anywhere()] * 5 + [whole()] * 4,
        out_specs=[anywhere()] + [whole()] * 5,
        out_shape=[
            shaped((tok_count, model_width), BF16),
            shaped((tok_count, width), BF16),
            shaped((model_width, wide), F32),
            shaped((width, model_width), F32),
            shaped((8, wide), F32),
            shaped((small_rows, model_width), F32),
        ],
        scratch_shapes=[
            pltpu.VMEM(route.shape, F32),
            pltpu.VMEM(cot_own.shape, BF16),
            pltpu.VMEM((part, model_width), BF16),
            pltpu.VMEM((seqlen, width), F32),
            pltpu.VMEM((2 * seqlen, model_width), BF16),
            pltpu.VMEM((seq_count, ends, part, model_width), BF16),
            pltpu.VMEM((seq_count, ends, part, model_width), BF16),
            pltpu.VMEM((seq_count, ends, part, model_width), BF16),
            pltpu.VMEM((seq_count, ends, part, model_width), BF16),
            pltpu.VMEM((part, model_width), F32),
            pltpu.VMEM((seq_count, seqlen, model_width), BF16),
            pltpu.VMEM((seq_count, seqlen, model_width), BF16),
            pltpu.VMEM((seq_count, part, model_width), F32),
            pltpu.VMEM((seqlen, width), BF16),
            pltpu.VMEM((seqlen, model_width), BF16),
            pltpu.VMEM((seqlen, wide), BF16),
            pltpu.VMEM((seqlen, LANES), F32),
            pltpu.VMEM((seqlen, width), BF16),
            pltpu.VMEM((seqlen, wide), BF16),
            pltpu.VMEM((model_width, wide), F32),
            pltpu.VMEM((width, model_width), F32),
            pltpu.VMEM((8, wide), F32),
            pltpu.VMEM((8, model_width), F32),
            pltpu.VMEM((model_width, LANES), F32),
            pltpu.VMEM((experts, stride + half, LANES), BF16),
            pltpu.VMEM((experts, stride, width), BF16),
            pltpu.VMEM((experts, model_width // experts, wide), BF16),
            pltpu.VMEM((experts, model_width // experts, wide), BF16),
            pltpu.VMEM((experts, model_width // experts, wide), BF16),
            pltpu.VMEM((experts, width // experts, model_width), BF16),
            pltpu.VMEM((experts, width // experts, model_width), BF16),
            pltpu.VMEM((experts, width // experts, model_width), BF16),
            pltpu.VMEM((experts, 8, wide), F32),
            pltpu.VMEM((head_parts, small_rows, model_width), F32),
            pltpu.VMEM((experts, small_rows, model_width), F32),
            dma((head_parts,)),
            dma((head_parts,)),
            dma((seq_count, head_parts)),
            dma((seq_count, head_parts)),
            dma((3,)),
            dma((4,)),
            dma((seq_count,)),
            dma((experts,)),
            dma((experts,)),
        ]
        + [dma((seq_count, ends))] * 8
        + [dma((seq_count, head_parts))] * 2
        + [dma((seq_count, head_parts, 2))] * 2
        + [dma((experts, 2))] * 4
        + [dma((experts,))] * 2
        + [dma((head_parts,))] * 2
        + [dma((experts,))] * 2,
        compiler_params=params(collective_id=2, has_side_effects=True),
        cost_estimate=cost(1e11, 1e8),
        name="tail",
    )(
        sums, route, id_cols, gate_cols, own_residual, own_second, cot_own, own_columns, router, vectors,
        own_tokens, result, context, first, qkv, totals, flat_qkv, out_weight,
        segments, live,
    )


def body(
    tokens,
    segments,
    live_mask,
    routes,
    priority,
    norm1_gain,
    norm1_bias,
    qkv_weight,
    qv_bias,
    out_weight,
    out_bias,
    norm2_gain,
    norm2_bias,
    router,
    up_weight,
    up_bias,
    down_weight,
    down_bias,
    cotangent,
):
    tok_count, model_width = tokens.shape
    seq_count, seqlen = segments.shape
    experts = lax.axis_size("exp")
    head_parts = lax.axis_size("head")
    head_index = lax.axis_index("head")
    quarter = model_width // head_parts
    capacity = (21 * tok_count + 10 * experts - 1) // (10 * experts)
    stride = round_up(capacity, 16)
    half = round_up(stride // 2, 16)
    local_width = qkv_weight.shape[2]

    norm_vectors = [norm1_gain, norm1_bias, out_bias, norm2_gain, norm2_bias]
    flat_qkv = qkv_weight.reshape(model_width, 3 * local_width)
    router_wide = jnp.pad(router, ((0, 0), (0, LANES - experts)))
    up, down = up_weight[0], down_weight[0]

    int_rows = jnp.concatenate(
        [
            routes.T,
            live_mask.reshape(1, tok_count),
            priority,
            jnp.zeros((4, tok_count), jnp.int32),
        ],
        axis=0,
    )
    part_half = round_up(seqlen // head_parts // 2, 16)
    first, qkv, context, totals, vectors, out_full_weight, gathered, ids, cot_slots, cot_own, own_tokens = head(
        tokens, norm_vectors, flat_qkv, qv_bias, segments, live_mask, int_rows, cotangent, out_weight, experts, capacity, stride, half, part_half, head_parts,
    )
    id_cols = ids.T
    own_residual, own_second, own_columns, gates, arrived, hidden, result, gate_col, cot_rows = forward(
        gathered, tokens, vectors, out_full_weight, router_wide, int_rows, ids,
        up, up_bias, down, down_bias, cot_slots, experts, stride, half, seq_count, head_parts,
    )
    gate_cols = gates.T
    own_result = lax.psum_scatter(result, "head", scatter_dimension=0, tiled=True)[0]
    sums, route_terms, grad_up, grad_up_bias, grad_down, grad_down_bias = backward(
        arrived, hidden, result, cot_rows, gate_col, id_cols, up, up_bias, down, half, head_parts,
        seqlen,
    )
    grad_up, grad_down, own_result = lax.optimization_barrier(
        (*copies_of(grad_up, grad_down), own_result)
    )
    grad_tokens, block_out, qkv_grad, out_grad, bias_grad, small = tail(
        sums, route_terms, id_cols, gate_cols, own_residual, own_second, cot_own, own_columns,
        router_wide, vectors, own_tokens, own_result, context, first, qkv, totals,
        flat_qkv, out_weight, segments, live_mask, stride, half, part_half, head_parts,
    )
    grad_qv_bias = jnp.concatenate(
        [bias_grad[0:1, :local_width], bias_grad[0:1, 2 * local_width :]], axis=0
    )
    return (
        block_out,
        grad_tokens.astype(F32),
        small[3],
        small[4],
        qkv_grad.reshape(model_width, 3, local_width),
        grad_qv_bias,
        out_grad,
        small[2],
        small[0],
        small[1],
        small[8 : 8 + experts].T,
        grad_up[None],
        grad_up_bias[0:1],
        grad_down[None],
        lax.dynamic_slice_in_dim(grad_down_bias[0:1], head_index * quarter, quarter, 1),
    )


def solution(mesh):
    in_specs = (
        P("exp", None),
        P("exp", None),
        P("exp", None),
        P("exp", None),
        P("exp", None),
        P(),
        P(),
        P(None, None, "head"),
        P(None, "head"),
        P("head", None),
        P(),
        P(),
        P(),
        P(),
        P("exp", None, "head"),
        P("exp", "head"),
        P("exp", "head", None),
        P("exp", "head"),
        P("exp", "head"),
    )
    out_specs = (
        P("exp", "head"),
        P("exp", None),
        P(),
        P(),
        P(None, None, "head"),
        P(None, "head"),
        P("head", None),
        P(),
        P(),
        P(),
        P(),
        P("exp", None, "head"),
        P("exp", "head"),
        P("exp", "head", None),
        P("exp", "head"),
    )
    return jax.shard_map(body, mesh=mesh, in_specs=in_specs, out_specs=out_specs, check_vma=False)
```

```python
from functools import partial
import math

import jax
import jax.numpy as jnp
from jax import lax
from jax.experimental import pallas as pl
from jax.experimental.pallas import tpu as pltpu
from jax.sharding import PartitionSpec as P

HEAD_DIM = 64
LANES = 128
EPSILON = 1e-06
NEGATIVE = -1e30
CONTRACT_FIRST = (((0,), (0,)), ((), ()))
CONTRACT_LAST = (((1,), (1,)), ((), ()))
F32 = jnp.float32
BF16 = jnp.bfloat16
MESH = pl.DeviceIdType.MESH
VMEM_LIMIT = 54 * 1024 * 1024


def round_up(number, step):
    return (number + step - 1) // step * step


def whole():
    return pl.BlockSpec(memory_space=pltpu.VMEM)


def anywhere():
    return pl.BlockSpec(memory_space=pl.ANY)


def shaped(shape, dtype):
    return jax.ShapeDtypeStruct(shape, dtype)


def params(**more):
    return pltpu.CompilerParams(vmem_limit_bytes=VMEM_LIMIT, **more)


def cost(flops, moved):
    return pl.CostEstimate(flops=int(flops), bytes_accessed=int(moved), transcendentals=0)


def dot(left, right):
    return jnp.dot(left, right, preferred_element_type=F32)


def dot_last(left, right):
    return lax.dot_general(left, right, CONTRACT_LAST, preferred_element_type=F32)


def dot_first(left, right):
    return lax.dot_general(left, right, CONTRACT_FIRST, preferred_element_type=F32)


def standard(values):
    centred = values - jnp.mean(values, axis=-1, keepdims=True)
    scale = lax.rsqrt(jnp.mean(centred * centred, axis=-1, keepdims=True) + EPSILON)
    return centred * scale, scale


def norm_back(grad_rows, gain_row, normal, scale):
    inner = grad_rows * gain_row
    return scale * (
        inner
        - jnp.mean(inner, axis=-1, keepdims=True)
        - normal * jnp.mean(inner * normal, axis=-1, keepdims=True)
    )


def diagonal_of(count):
    return lax.broadcasted_iota(jnp.int32, (count, count), 0) == lax.broadcasted_iota(
        jnp.int32, (count, count), 1
    )


def as_column(row, diagonal):
    return jnp.sum(jnp.where(diagonal, row.astype(F32), 0.0), axis=1, keepdims=True)


def mask_penalty(seg_row, live_row):
    diagonal = diagonal_of(seg_row.shape[1])
    same = as_column(seg_row, diagonal) == seg_row.astype(F32)
    return jnp.where(same & ((live_row > 0) | diagonal), 0.0, NEGATIVE)


def pack_rows(rows, half):
    count = rows.shape[0]
    third = rows[:, LANES:]
    return rows[:, :LANES], jnp.concatenate([third[:half], third[count - half :]], axis=1)


def unpack_rows(parts_of, into, head_parts, count, half):
    extra = HEAD_DIM
    width = LANES + extra
    for z in range(head_parts):
        packed = parts_of(z)
        into[:, z * width : z * width + LANES] = packed[:count]
        tail = packed[count : count + half]
        into[:half, z * width + LANES : (z + 1) * width] = tail[:, :extra]
        into[half:, z * width + LANES : (z + 1) * width] = tail[2 * half - count :, extra:]


def greet(peers):
    barrier = pltpu.get_barrier_semaphore()
    me = lax.axis_index("exp")
    here = lax.axis_index("head")

    def call(step, carry):
        other = lax.rem(me + step, peers)
        pl.semaphore_signal(barrier, inc=1, device_id=(other, here), device_id_type=MESH)
        return carry

    lax.fori_loop(1, peers, call, 0)
    return barrier


def greet_both(peers, head_parts):
    barrier = greet(peers)
    me = lax.axis_index("exp")
    here = lax.axis_index("head")

    def call(step, carry):
        other = lax.rem(here + step, head_parts)
        pl.semaphore_signal(barrier, inc=1, device_id=(me, other), device_id_type=MESH)
        return carry

    lax.fori_loop(1, head_parts, call, 0)
    return barrier


def head_kernel(
    experts, capacity, stride, half, part_half, seq_count, head_parts,
    tokens_ref, gain1_ref, bias1_ref, out_bias_ref, gain2_ref, bias2_ref, weight_ref, bias_ref, seg_ref, live_ref, routes_ref, prio_ref, cot_ref, out_weight_ref,
    first_hbm, qkv_hbm, context_hbm, total_hbm, norm_ref, out_full_ref, gathered_ref, ids_ref, id_cols_ref, cot_recv, own_send, own_tokens_ref,
    rows_scr, cot_send, first_scr, qkv_scr, context_scr, total_scr,
    gather_sem, gather_out, cot_send_sem, cot_recv_sem, store_sem,
    weight_sem, weight_out, pair_send_sem, pair_recv_sem,
):
    me = lax.axis_index("exp")
    here = lax.axis_index("head")
    barrier = greet_both(experts, head_parts)
    ends = head_parts - 1
    tok_count = tokens_ref.shape[0]
    seqlen = tok_count // seq_count
    part = seqlen // head_parts
    pl.semaphore_wait(barrier, experts - 1 + ends)

    def own_rows():
        diagonal = diagonal_of(seqlen)
        for start in range(0, tok_count, seqlen):
            for pick in range(2):
                row = ids_ref[pick : pick + 1, start : start + seqlen]
                id_cols_ref[start : start + seqlen, pick : pick + 1] = as_column(
                    row, diagonal
                ).astype(jnp.int32)
        for seq in range(seq_count):
            own = pl.ds(pl.multiple_of(seq * seqlen + here * part, part), part)
            own_tokens_ref[seq] = tokens_ref[own]
            for z in range(head_parts):
                start = seq * seqlen + z * part
                block = cot_ref[:, start : start + part].astype(F32).T.astype(BF16)
                wide, tail = pack_rows(block, part_half)
                own_send[z, seq, :part] = wide
                own_send[z, seq, part:] = tail

    for row, vector in enumerate((gain1_ref, bias1_ref, out_bias_ref, gain2_ref, bias2_ref)):
        norm_ref[row : row + 1] = vector[...].astype(F32).reshape(1, -1)
    norm_ref[5:8] = jnp.zeros((3, norm_ref.shape[1]), F32)
    rows_scr[0:2] = routes_ref[...]
    rows_scr[3:4] = prio_ref[...]
    rows_scr[4:8] = jnp.zeros((4, tok_count), jnp.int32)
    for seq in range(seq_count):
        rows_scr[2:3, seq * seqlen : (seq + 1) * seqlen] = live_ref[seq : seq + 1]
    core = lax.rem(me, 2)
    weight_rows = out_weight_ref.shape[0]
    half_rows = weight_rows // 2

    def weight_span(shard, which):
        start = pl.multiple_of(shard * weight_rows + which * half_rows, 16)
        return pl.ds(start, half_rows)

    def weight_copy(shard, side):
        rows = weight_span(shard, core)
        return pltpu.make_async_remote_copy(
            src_ref=out_full_ref.at[rows],
            dst_ref=out_full_ref.at[rows],
            send_sem=weight_out.at[shard, side],
            recv_sem=weight_sem.at[shard],
            device_id=(me, here + 1 - 2 * side),
            device_id_type=MESH,
        )

    def pair_copy(step, which):
        rows = weight_span(lax.rem(here + step, head_parts), which)
        return pltpu.make_async_remote_copy(
            src_ref=out_full_ref.at[rows],
            dst_ref=out_full_ref.at[rows],
            send_sem=pair_send_sem.at[step],
            recv_sem=pair_recv_sem.at[step],
            device_id=(me + 1 - 2 * core, here),
            device_id_type=MESH,
        )

    def weight_hop(hop):
        def one(side, shard, there, onward):
            @pl.when(there)
            def arrived():
                if hop > 0:
                    weight_copy(shard, side).wait_recv()
                if hop < ends:

                    @pl.when(onward)
                    def pass_on():
                        weight_copy(shard, side).start()

        each_side(hop, one)
        if hop == ends:
            for step in range(1, head_parts):
                pair_copy(step, core).start()

    def stores(seq):
        slot = lax.rem(seq, 2)
        span = pl.ds(pl.multiple_of(seq * seqlen, seqlen), seqlen)
        return (
            pltpu.make_async_copy(first_scr.at[slot], first_hbm.at[span], store_sem.at[slot, 0]),
            pltpu.make_async_copy(qkv_scr.at[slot], qkv_hbm.at[span], store_sem.at[slot, 1]),
            pltpu.make_async_copy(context_scr.at[slot], context_hbm.at[span], store_sem.at[slot, 2]),
            pltpu.make_async_copy(total_scr.at[slot], total_hbm.at[span], store_sem.at[slot, 3]),
        )

    def attend(seq):
        slot = lax.rem(seq, 2)
        span = pl.ds(pl.multiple_of(seq * seqlen, seqlen), seqlen)

        @pl.when(seq >= 2)
        def free():
            for copy in stores(seq - 2):
                copy.wait()

        normal, ignored = standard(tokens_ref[span].astype(F32))
        first = (normal * norm_ref[0:1] + norm_ref[1:2]).astype(BF16)
        first_scr[slot] = first
        bias = bias_ref[...].astype(F32)
        bias_row = jnp.concatenate([bias[0:1], jnp.zeros_like(bias[0:1]), bias[1:2]], axis=1)
        rows = (dot(first, weight_ref[...]) + bias_row).astype(BF16)
        qkv_scr[slot] = rows
        penalty = mask_penalty(seg_ref[pl.ds(seq, 1)], live_ref[pl.ds(seq, 1)])
        width = rows.shape[1] // 3
        parts = []
        for head in range(width // HEAD_DIM):
            lo = head * HEAD_DIM
            hi = lo + HEAD_DIM
            query = rows[:, lo:hi] * BF16(1.0 / math.sqrt(HEAD_DIM))
            scores = dot_last(query, rows[:, width + lo : width + hi]) + penalty
            largest = jnp.max(scores, axis=-1, keepdims=True)
            weights = jnp.exp(scores - largest)
            total = jnp.sum(weights, axis=-1, keepdims=True)
            values = rows[:, 2 * width + lo : 2 * width + hi]
            parts.append((dot(weights.astype(BF16), values) / total).astype(BF16))
            total_scr[slot, :, head : head + 1] = largest + jnp.log(total)
        context = jnp.concatenate(parts, axis=1)
        context_scr[slot] = context
        for copy in stores(seq):
            copy.start()
        wide, tail = pack_rows(context, seqlen // 2)
        gathered_ref[here, seq, :seqlen] = wide
        gathered_ref[here, seq, seqlen:] = tail

    def full_copy(seq, shard, side):
        return pltpu.make_async_remote_copy(
            src_ref=gathered_ref.at[shard, seq],
            dst_ref=gathered_ref.at[shard, seq],
            send_sem=gather_out.at[seq, shard, side],
            recv_sem=gather_sem.at[seq, shard],
            device_id=(me, here + 1 - 2 * side),
            device_id_type=MESH,
        )

    def each_side(hop, action):
        for side in range(2):
            shard = here - hop if side == 0 else here + hop
            there = shard >= 0 if side == 0 else shard <= ends
            onward = here < ends if side == 0 else here > 0
            action(side, shard, there, onward)

    def spread_hop(seq, hop):
        def one(side, shard, there, onward):
            @pl.when(there)
            def arrived():
                if hop > 0:
                    full_copy(seq, shard, side).wait_recv()
                if hop < ends:

                    @pl.when(onward)
                    def pass_on():
                        full_copy(seq, shard, side).start()

        each_side(hop, one)

    def spread_drain(seq):
        def one(side, shard, there, onward):
            @pl.when(there & onward)
            def sent():
                full_copy(seq, shard, side).wait_send()

        for hop in range(ends):
            each_side(hop, one)

    numbers = lax.broadcasted_iota(jnp.int32, (experts, 1), 0)

    def hot(rows):
        live = rows[2:3] > 0
        first = jnp.where((rows[0:1] == numbers) & live, 1.0, 0.0)
        second = jnp.where((rows[1:2] == numbers) & live, 1.0, 0.0)
        return first, second

    def tables():
        rank_row = rows_scr[3:4].astype(F32)
        diagonal = diagonal_of(seqlen)
        counts = jnp.zeros((2 * experts, tok_count), F32)
        for start in range(0, tok_count, seqlen):
            first, second = hot(rows_scr[:, start : start + seqlen])
            rank_col = as_column(rank_row[:, start : start + seqlen], diagonal)
            earlier = jnp.where(rank_col < rank_row, 1.0, 0.0)
            both = jnp.concatenate([first, second], axis=0)
            counts = counts + dot(both.astype(BF16), earlier.astype(BF16))
        first, second = hot(rows_scr[...])
        total = jnp.sum(first, axis=1, keepdims=True)
        places = [
            jnp.sum(first * counts[:experts], axis=0, keepdims=True),
            jnp.sum(second * (counts[experts:] + total), axis=0, keepdims=True),
        ]
        for pick in range(2):
            place = places[pick].astype(jnp.int32)
            kept = (place < capacity) & (rows_scr[2:3] > 0)
            ids_ref[pick : pick + 1] = jnp.where(
                kept, rows_scr[pick : pick + 1] * stride + place, -1
            )
        ids_ref[2:8] = jnp.full((6, tok_count), -1, jnp.int32)

    def cot_copy(step, target):
        return pltpu.make_async_remote_copy(
            src_ref=cot_send.at[target],
            dst_ref=cot_recv.at[me],
            send_sem=cot_send_sem.at[step],
            recv_sem=cot_recv_sem.at[step],
            device_id=(target, here),
            device_id_type=MESH,
        )

    def fill(target):
        slots = target * stride + lax.broadcasted_iota(jnp.int32, (stride, 1), 0)
        hit = (ids_ref[0:1] == slots) | (ids_ref[1:2] == slots)
        block = dot_last(jnp.where(hit, 1.0, 0.0).astype(BF16), cot_ref[...]).astype(BF16)
        return pack_rows(block, half)

    def dispatch():
        def one(step, carry):
            target = lax.rem(me + step, experts)
            wide, tail = fill(target)
            cot_send[target, :stride] = wide
            cot_send[target, stride:] = tail
            cot_copy(step, target).start()
            return carry

        lax.fori_loop(1, experts, one, 0)
        wide, tail = fill(me)
        cot_recv[me, :stride] = wide
        cot_recv[me, stride:] = tail

    out_full_ref[pl.ds(pl.multiple_of(here * weight_rows, 16), weight_rows)] = out_weight_ref[...]
    weight_hop(0)

    def time_step(step, carry):
        for hop in range(1, ends + 1):

            @pl.when(step == hop)
            def weights():
                weight_hop(hop)

        @pl.when(step == seq_count + 1)
        def send():
            dispatch()

        for hop in range(ends, 0, -1):

            @pl.when((step >= hop) & (step - hop < seq_count))
            def move():
                spread_hop(step - hop, hop)

        @pl.when(step < seq_count)
        def work():
            attend(step)
            spread_hop(step, 0)

        @pl.when(step == seq_count)
        def places():
            tables()

        @pl.when(step == seq_count + 1)
        def rows():
            own_rows()

        return carry

    lax.fori_loop(0, seq_count + ends, time_step, 0)
    for seq in range(seq_count):
        spread_drain(seq)
    for seq in range(max(seq_count - 2, 0), seq_count):
        for copy in stores(seq):
            copy.wait()

    def sent(side, shard, there, onward):
        @pl.when(there & onward)
        def drain():
            weight_copy(shard, side).wait_send()

    for hop in range(ends):
        each_side(hop, sent)
    for step in range(1, head_parts):
        pair_copy(step, core).wait_send()
        pair_copy(step, 1 - core).wait_recv()

    def finish(step, carry):
        cot_copy(step, lax.rem(me + step, experts)).wait()
        return carry

    lax.fori_loop(1, experts, finish, 0)


def head(
    tokens, norm_vectors, flat_qkv, qv_bias, segments, live, routes_t, priority, cotangent, out_weight,
    experts, capacity, stride, half, part_half, head_parts,
):
    tok_count, model_width = tokens.shape
    seq_count, seqlen = segments.shape
    part = seqlen // head_parts
    wide = flat_qkv.shape[1]
    width = wide // 3
    dma = pltpu.SemaphoreType.DMA
    own = (head_parts, seq_count, part + part_half, LANES)
    slots = (experts, stride + half, LANES)
    return pl.pallas_call(
        partial(head_kernel, experts, capacity, stride, half, part_half, seq_count, head_parts),
        in_specs=[whole()] * 14,
        out_specs=[anywhere()] * 4 + [whole()] * 8,
        out_shape=[
            shaped((tok_count, model_width), BF16),
            shaped((tok_count, wide), BF16),
            shaped((tok_count, width), BF16),
            shaped((tok_count, LANES), F32),
            shaped((8, model_width), F32),
            shaped((head_parts * out_weight.shape[0], model_width), BF16),
            shaped((head_parts, seq_count, seqlen + seqlen // 2, LANES), BF16),
            shaped((8, tok_count), jnp.int32),
            shaped((tok_count, 8), jnp.int32),
            shaped(slots, BF16),
            shaped(own, BF16),
            shaped((seq_count, part, model_width), BF16),
        ],
        scratch_shapes=[
            pltpu.VMEM((8, tok_count), jnp.int32),
            pltpu.VMEM(slots, BF16),
            pltpu.VMEM((2, seqlen, model_width), BF16),
            pltpu.VMEM((2, seqlen, wide), BF16),
            pltpu.VMEM((2, seqlen, width), BF16),
            pltpu.VMEM((2, seqlen, LANES), F32),
            dma((seq_count, head_parts)),
            dma((seq_count, head_parts, 2)),
            dma((experts,)),
            dma((experts,)),
            dma((2, 4)),
            dma((head_parts,)),
            dma((head_parts, 2)),
            dma((head_parts,)),
            dma((head_parts,)),
        ],
        compiler_params=params(collective_id=3, has_side_effects=True),
        cost_estimate=cost(6e10, 1e7),
        name="head",
    )(tokens, *norm_vectors, flat_qkv, qv_bias, segments, live, routes_t, priority, cotangent, out_weight)


def gelu_parts(pre):
    root = math.sqrt(2.0 / math.pi)
    square = pre * pre
    wave = jnp.tanh(root * (pre + 0.044715 * pre * square))
    half_sum = 0.5 * (1.0 + wave)
    slope = half_sum + 0.5 * pre * (1.0 - wave * wave) * (
        root * (1.0 + 3.0 * 0.044715 * square)
    )
    return pre * half_sum, slope


def forward_kernel(
    experts, stride, half, seq_count, head_parts,
    gathered_ref, tokens_ref, vectors_ref, out_weight_ref, router_ref, rows_ref, ids_ref,
    up_ref, up_bias_ref, down_ref, down_bias_ref, cot_hbm,
    own_residual_ref, own_second_ref, own_columns_ref, gate_cols_ref, arrived_hbm, hidden_hbm, result_hbm,
    gate_col_ref, cot_all, gates_ref, arrived_ref, hidden_scr, result_scr, residual_ref, context_scr, second_scr, logit_scr, send_scr, gate_send, gate_recv,
    send_sem, recv_sem, gate_send_sem, gate_recv_sem, cot_sem, cot_out, local_sem,
    arrived_sem, store_sem,
):
    me = lax.axis_index("exp")
    here = lax.axis_index("head")
    barrier = greet_both(experts, head_parts)
    ends = head_parts - 1
    pieces = cot_sem.shape[1]
    piece_rows = experts // pieces
    tok_count = tokens_ref.shape[0]

    def cot_copy(shard, piece, side, own=False):
        span = pl.ds(piece * piece_rows, piece_rows)
        return pltpu.make_async_remote_copy(
            src_ref=cot_hbm.at[span] if own else cot_all.at[shard, span],
            dst_ref=cot_all.at[shard, span],
            send_sem=cot_out.at[shard, piece, side],
            recv_sem=cot_sem.at[shard, piece],
            device_id=(me, here + 1 - 2 * side),
            device_id_type=MESH,
        )

    def cot_side(hop, side):
        shard = here - hop if side == 0 else here + hop
        there = shard >= 0 if side == 0 else shard <= ends
        onward = here < ends if side == 0 else here > 0
        return shard, there, onward

    def cot_hop(hop, piece):
        for side in range(2):
            shard, there, onward = cot_side(hop, side)

            @pl.when(there)
            def arrived():
                if hop > 0:
                    cot_copy(shard, piece, side).wait_recv()
                if hop < ends:

                    @pl.when(onward)
                    def pass_on():
                        cot_copy(shard, piece, side, hop == 0).start()

    def cot_drain(hop, piece):
        for side in range(2):
            shard, there, onward = cot_side(hop, side)

            @pl.when(there & onward)
            def sent():
                cot_copy(shard, piece, side, hop == 0).wait_send()

    local = pltpu.make_async_copy(cot_hbm, cot_all.at[here], local_sem.at[0])
    local.start()
    pl.semaphore_wait(barrier, experts - 1 + ends)
    for piece in range(pieces):
        cot_hop(0, piece)
    seqlen = tok_count // seq_count
    for seq in range(seq_count):
        span = slice(seq * seqlen, (seq + 1) * seqlen)
        unpack_rows(lambda z: gathered_ref[z, seq], context_scr, head_parts, seqlen, seqlen // 2)
        residual = (
            tokens_ref[span].astype(F32)
            + dot(context_scr[...], out_weight_ref[...])
            + vectors_ref[2:3]
        )
        residual_ref[span] = residual
        normal, ignored = standard(residual)
        second = (normal * vectors_ref[3:4] + vectors_ref[4:5]).astype(BF16)
        second_scr[span] = second
        logit_scr[:, span] = dot(second, router_ref[...]).T[:experts]
    part = seqlen // head_parts
    for seq in range(seq_count):
        own = pl.ds(pl.multiple_of(seq * seqlen + here * part, part), part)
        own_residual_ref[seq] = residual_ref[own]
        own_second_ref[seq] = second_scr[own]
    width = residual_ref.shape[1] // head_parts
    for z in range(head_parts):

        @pl.when(here == z)
        def columns():
            own_columns_ref[...] = residual_ref[:, z * width : (z + 1) * width]


    logits = logit_scr[...]
    powers = jnp.exp(logits - jnp.max(logits, axis=0, keepdims=True))
    chances = powers / jnp.sum(powers, axis=0, keepdims=True)
    numbers = lax.broadcasted_iota(jnp.int32, (experts, 1), 0)
    for pick in range(2):
        chosen = jnp.where(rows_ref[pick : pick + 1] == numbers, chances, 0.0)
        gate = jnp.where(ids_ref[pick : pick + 1] >= 0, jnp.sum(chosen, axis=0, keepdims=True), 0.0)
        gates_ref[pick : pick + 1] = gate
    gates_ref[2:8] = jnp.zeros((6, tok_count), F32)

    def copies(target, step):
        to = dict(device_id=(target, here), device_id_type=MESH)
        return (
            pltpu.make_async_remote_copy(
                src_ref=send_scr.at[step],
                dst_ref=arrived_ref.at[me],
                send_sem=send_sem.at[step],
                recv_sem=recv_sem.at[step],
                **to,
            ),
            pltpu.make_async_remote_copy(
                src_ref=gate_send.at[step],
                dst_ref=gate_recv.at[me],
                send_sem=gate_send_sem.at[step],
                recv_sem=gate_recv_sem.at[step],
                **to,
            ),
        )

    def fill(target):
        slots = target * stride + lax.broadcasted_iota(jnp.int32, (stride, 1), 0)
        first = ids_ref[0:1] == slots
        second = ids_ref[1:2] == slots
        block = dot(jnp.where(first | second, 1.0, 0.0).astype(BF16), second_scr[...]).astype(BF16)
        gate = jnp.sum(
            jnp.where(first, gates_ref[0:1], jnp.where(second, gates_ref[1:2], 0.0)),
            axis=1,
            keepdims=True,
        )
        return block, jnp.broadcast_to(gate, (stride, LANES)).T[:8]

    def send(step, carry):
        target = lax.rem(me + step, experts)
        block, gate = fill(target)
        send_scr[step] = block
        gate_send[step] = gate
        for copy in copies(target, step):
            copy.start()
        return carry

    lax.fori_loop(1, experts, send, 0)
    block, gate = fill(me)
    arrived_ref[me] = block
    gate_recv[me] = gate

    def source_of(step):
        return lax.rem(me + experts - step, experts)

    def arrived_store(step):
        source = source_of(step)
        return pltpu.make_async_copy(
            arrived_ref.at[source], arrived_hbm.at[source], arrived_sem.at[step]
        )

    def stores(step):
        source = source_of(step)
        slot = lax.rem(step, 2)
        return (
            pltpu.make_async_copy(hidden_scr.at[slot], hidden_hbm.at[source], store_sem.at[slot, 0]),
            pltpu.make_async_copy(result_scr.at[slot], result_hbm.at[:, source], store_sem.at[slot, 1]),
        )

    def work(step):
        source = source_of(step)
        slot = lax.rem(step, 2)
        arrived_store(step).start()
        pre = dot(arrived_ref[source], up_ref[...]) + up_bias_ref[...].astype(F32)
        hidden = gelu_parts(pre)[0].astype(BF16)
        result = dot(hidden, down_ref[...])
        down_bias = down_bias_ref[...].astype(F32)

        @pl.when(step >= 2)
        def free():
            for copy in stores(step - 2):
                copy.wait()

        hidden_scr[slot] = hidden
        for z in range(head_parts):
            columns = result[:, z * width : (z + 1) * width] + jnp.where(here == z, down_bias, 0.0)
            wide, tail = pack_rows(columns.astype(BF16), half)
            result_scr[slot, z, :stride] = wide
            result_scr[slot, z, stride:] = tail
        for copy in stores(step):
            copy.start()

    diagonal = diagonal_of(seqlen)
    for start in range(0, tok_count, seqlen):
        for pick in range(2):
            gate_cols_ref[start : start + seqlen, pick : pick + 1] = as_column(
                gates_ref[pick : pick + 1, start : start + seqlen], diagonal
            )
    work(0)
    moves = [(hop, piece) for hop in range(1, ends) for piece in range(pieces)]
    early = len(moves) - min(experts - 2, len(moves))
    for move in moves[:early]:
        cot_hop(*move)

    def receive(step, carry):
        for place, move in enumerate(moves[early:]):

            @pl.when(step == place + 1)
            def pass_on():
                cot_hop(*move)

        source = lax.rem(me + experts - step, experts)
        wide, narrow = copies(source, step)
        wide.wait_recv()
        narrow.wait_recv()
        work(step)
        return carry

    lax.fori_loop(1, experts, receive, 0)

    for step in (experts - 2, experts - 1):
        for copy in stores(step):
            copy.wait()

    def stored(step, carry):
        arrived_store(step).wait()
        return carry

    lax.fori_loop(0, experts, stored, 0)

    def finish(step, carry):
        for copy in copies(lax.rem(me + step, experts), step):
            copy.wait_send()
        return carry

    lax.fori_loop(1, experts, finish, 0)
    for piece in range(pieces):
        cot_hop(ends, piece)
        for hop in range(ends):
            cot_drain(hop, piece)
    local.wait()
    lane = lax.broadcasted_iota(jnp.int32, (LANES, stride), 0)
    square = jnp.zeros((LANES, stride), F32)
    for source in range(experts):
        square = jnp.where(lane == source, gate_recv[source, 0:1], square)
    gate_col_ref[...] = square.T


def forward(
    gathered, tokens, vectors, out_weight, router, rows, ids, up, up_bias, down, down_bias, cot_slots,
    experts, stride, half, seq_count, head_parts,
):
    tok_count, model_width = tokens.shape
    seqlen = tok_count // seq_count
    part = seqlen // head_parts
    return pl.pallas_call(
        partial(forward_kernel, experts, stride, half, seq_count, head_parts),
        in_specs=[whole()] * 11 + [anywhere()],
        out_specs=[whole()] * 4 + [anywhere()] * 3 + [whole()] + [anywhere()],
        out_shape=[
            shaped((seq_count, part, model_width), F32),
            shaped((seq_count, part, model_width), BF16),
            shaped((tok_count, model_width // head_parts), F32),
            shaped((tok_count, 8), F32),
            shaped((experts, stride, model_width), BF16),
            shaped((experts, stride, up.shape[1]), BF16),
            shaped((head_parts, experts, stride + half, LANES), BF16),
            shaped((stride, LANES), F32),
            shaped((head_parts, experts, stride + half, LANES), BF16),
        ],
        scratch_shapes=[
            pltpu.VMEM((8, tok_count), F32),
            pltpu.VMEM((experts, stride, model_width), BF16),
            pltpu.VMEM((2, stride, up.shape[1]), BF16),
            pltpu.VMEM((2, head_parts, stride + half, LANES), BF16),
            pltpu.VMEM((tok_count, model_width), F32),
            pltpu.VMEM((seqlen, model_width), BF16),
            pltpu.VMEM((tok_count, model_width), BF16),
            pltpu.VMEM((experts, tok_count), F32),
            pltpu.VMEM((experts, stride, model_width), BF16),
            pltpu.VMEM((experts, 8, stride), F32),
            pltpu.VMEM((experts, 8, stride), F32),
            pltpu.SemaphoreType.DMA((experts,)),
            pltpu.SemaphoreType.DMA((experts,)),
            pltpu.SemaphoreType.DMA((experts,)),
            pltpu.SemaphoreType.DMA((experts,)),
            pltpu.SemaphoreType.DMA((head_parts, 4)),
            pltpu.SemaphoreType.DMA((head_parts, 4, 2)),
            pltpu.SemaphoreType.DMA((1,)),
            pltpu.SemaphoreType.DMA((experts,)),
            pltpu.SemaphoreType.DMA((2, 2)),
        ],
        compiler_params=params(collective_id=0, has_side_effects=True),
        cost_estimate=cost(8e10, 1e8),
        name="forward",
    )(gathered, tokens, vectors, out_weight, router, rows, ids, up, up_bias, down, down_bias, cot_slots)


def backward_kernel(
    experts, stride, half, head_parts, chunk,
    arrived_hbm, hidden_hbm, result_hbm, cot_hbm, gate_col_ref, ids_ref, up_ref, up_bias_ref, down_ref,
    sums_ref, route_ref, grad_up_ref, grad_up_bias_ref, grad_down_ref, grad_down_bias_ref,
    rows_scr, result_scr, cot_scr, cot_wide, result_wide, hidden_scr, pre_grad_scr, out_grad_scr,
    send_scr, recv_scr, gate_send, gate_recv, total_scr,
    load_sem, send_sem, recv_sem, gate_send_sem, gate_recv_sem,
):
    me = lax.axis_index("exp")
    here = lax.axis_index("head")
    barrier = greet(experts)
    tok_count = ids_ref.shape[0]
    model_width = up_ref.shape[0]

    def loads(step):
        home = lax.rem(me + step, experts)
        slot = lax.rem(step, 2)
        return (
            pltpu.make_async_copy(arrived_hbm.at[home], rows_scr.at[slot], load_sem.at[slot, 0]),
            pltpu.make_async_copy(result_hbm.at[:, home], result_scr.at[slot], load_sem.at[slot, 1]),
            pltpu.make_async_copy(cot_hbm.at[:, home], cot_scr.at[slot], load_sem.at[slot, 2]),
        )

    def copies(target, step):
        to = dict(device_id=(target, here), device_id_type=MESH)
        return (
            pltpu.make_async_remote_copy(
                src_ref=send_scr.at[step],
                dst_ref=recv_scr.at[me],
                send_sem=send_sem.at[step],
                recv_sem=recv_sem.at[step],
                **to,
            ),
            pltpu.make_async_remote_copy(
                src_ref=gate_send.at[step],
                dst_ref=gate_recv.at[me],
                send_sem=gate_send_sem.at[step],
                recv_sem=gate_recv_sem.at[step],
                **to,
            ),
        )

    for copy in loads(1):
        copy.start()
    grad_up_ref[...] = jnp.zeros_like(grad_up_ref)
    grad_down_ref[...] = jnp.zeros_like(grad_down_ref)
    grad_up_bias_ref[...] = jnp.zeros_like(grad_up_bias_ref)
    grad_down_bias_ref[...] = jnp.zeros_like(grad_down_bias_ref)
    total_scr[...] = jnp.zeros_like(total_scr)
    pl.semaphore_wait(barrier, experts - 1)

    def work(step):
        home = lax.rem(me + step, experts)
        slot = lax.rem(step, 2)
        for copy in loads(step):
            copy.wait()
        unpack_rows(lambda z: cot_scr[slot, z], cot_wide, head_parts, stride, half)
        unpack_rows(lambda z: result_scr[slot, z], result_wide, head_parts, stride, half)
        out_rows = cot_wide[...].astype(F32)
        pre = dot(rows_scr[slot], up_ref[...]) + up_bias_ref[...].astype(F32)
        slope = gelu_parts(pre)[1]
        lane = lax.broadcasted_iota(jnp.int32, (stride, LANES), 1)
        gate = jnp.sum(jnp.where(lane == home, gate_col_ref[...], 0.0), axis=1, keepdims=True)
        out_grad = (gate * out_rows).astype(BF16)
        out_grad_scr[step] = out_grad
        grad_down_bias_ref[0:1] += jnp.sum(out_grad.astype(F32), axis=0, keepdims=True)
        pre_grad = (dot_last(out_grad, down_ref[...]) * slope).astype(BF16)
        pre_grad_scr[step] = pre_grad
        grad_up_bias_ref[0:1] += jnp.sum(pre_grad.astype(F32), axis=0, keepdims=True)
        gate_grad = jnp.sum(result_wide[...].astype(F32) * out_rows, axis=1, keepdims=True)
        return (
            dot_last(pre_grad, up_ref[...]).astype(BF16),
            jnp.broadcast_to(gate_grad, (stride, LANES)).T[:8],
        )

    def send(step, carry):
        for copy in loads(lax.rem(step + 1, experts)):
            copy.start()
        block, gate = work(step)
        send_scr[step] = block
        gate_send[step] = gate
        for copy in copies(lax.rem(me + step, experts), step):
            copy.start()
        return carry

    lax.fori_loop(1, experts, send, 0)
    block, gate = work(0)
    recv_scr[me] = block
    gate_recv[me] = gate

    def row_loads(step):
        home = lax.rem(me + step, experts)
        slot = lax.rem(step, 2)
        return (
            pltpu.make_async_copy(arrived_hbm.at[home], rows_scr.at[slot], load_sem.at[slot, 0]),
            pltpu.make_async_copy(hidden_hbm.at[home], hidden_scr.at[slot], load_sem.at[slot, 1]),
        )

    def weigh(step):
        slot = lax.rem(step, 2)
        for copy in row_loads(step):
            copy.wait()
        grad_up_ref[...] += dot_first(rows_scr[slot], pre_grad_scr[step])
        grad_down_ref[...] += dot_first(hidden_scr[slot], out_grad_scr[step])

    def weigh_some(step, carry):
        for copy in row_loads(step + 1):
            copy.start()
        weigh(step)
        return carry

    for copy in row_loads(0):
        copy.start()
    lax.fori_loop(0, experts - 1, weigh_some, 0)
    weigh(experts - 1)

    def gather(source):
        slots = source * stride + lax.broadcasted_iota(jnp.int32, (1, stride), 1)
        lane = lax.broadcasted_iota(jnp.int32, (chunk, LANES), 1)

        def part(index, carry):
            span = pl.ds(pl.multiple_of(index * chunk, chunk), chunk)
            hit = (ids_ref[span, 0:1] == slots) | (ids_ref[span, 1:2] == slots)
            total_scr[span, :model_width] += dot(
                jnp.where(hit, 1.0, 0.0).astype(BF16), recv_scr[source]
            )
            gate = jnp.sum(jnp.where(hit, gate_recv[source, 0:1], 0.0), axis=1, keepdims=True)
            total_scr[span, model_width:] = jnp.where(
                lane == source, gate, total_scr[span, model_width:]
            )
            return carry

        lax.fori_loop(0, tok_count // chunk, part, 0)

    gather(me)

    def receive(step, carry):
        source = lax.rem(me + experts - step, experts)
        for copy in copies(source, step):
            copy.wait_recv()
        gather(source)
        return carry

    lax.fori_loop(1, experts, receive, 0)
    sums_ref[...] = total_scr[:, :model_width].astype(BF16)
    parts, seqs, kinds, count = route_ref.shape
    for seq in range(seqs):
        for z in range(parts):
            start = (seq * parts + z) * count
            route_ref[z, seq] = total_scr[start : start + count, model_width:].T[:kinds]

    def finish(step, carry):
        for copy in copies(lax.rem(me + step, experts), step):
            copy.wait_send()
        return carry

    lax.fori_loop(1, experts, finish, 0)


def backward(
    arrived, hidden, result, cot_rows, gate_col, id_cols, up, up_bias, down, half, head_parts, chunk
):
    tok_count = id_cols.shape[0]
    experts, stride, model_width = arrived.shape
    inner = up.shape[1]
    rows = (experts, stride, model_width)
    return pl.pallas_call(
        partial(backward_kernel, experts, stride, half, head_parts, chunk),
        in_specs=[anywhere()] * 4 + [whole()] * 5,
        out_specs=[whole()] * 6,
        out_shape=[
            shaped((tok_count, model_width), BF16),
            shaped((head_parts, tok_count // chunk, round_up(experts, 8), chunk // head_parts), F32),
            shaped((model_width, inner), F32),
            shaped((8, inner), F32),
            shaped((inner, model_width), F32),
            shaped((8, model_width), F32),
        ],
        scratch_shapes=[
            pltpu.VMEM((2, stride, model_width), BF16),
            pltpu.VMEM((2, head_parts, stride + half, LANES), BF16),
            pltpu.VMEM((2, head_parts, stride + half, LANES), BF16),
            pltpu.VMEM((stride, model_width), BF16),
            pltpu.VMEM((stride, model_width), BF16),
            pltpu.VMEM((2, stride, inner), BF16),
            pltpu.VMEM((experts, stride, inner), BF16),
            pltpu.VMEM(rows, BF16),
            pltpu.VMEM(rows, BF16),
            pltpu.VMEM(rows, BF16),
            pltpu.VMEM((experts, 8, stride), F32),
            pltpu.VMEM((experts, 8, stride), F32),
            pltpu.VMEM((tok_count, model_width + LANES), F32),
            pltpu.SemaphoreType.DMA((2, 3)),
            pltpu.SemaphoreType.DMA((experts,)),
            pltpu.SemaphoreType.DMA((experts,)),
            pltpu.SemaphoreType.DMA((experts,)),
            pltpu.SemaphoreType.DMA((experts,)),
        ],
        compiler_params=params(collective_id=1, has_side_effects=True),
        cost_estimate=cost(8e10, 1e8),
        name="backward",
    )(arrived, hidden, result, cot_rows, gate_col, id_cols, up, up_bias, down)


def copy_kernel(first_ref, second_ref, first_out, second_out):
    first_out[...] = first_ref[...]
    second_out[...] = second_ref[...]


def copies_of(first, second):
    rows = first.shape[0] // 4
    specs = [pl.BlockSpec((rows, a.shape[1]), lambda i: (i, 0)) for a in (first, second)]
    return pl.pallas_call(
        copy_kernel,
        grid=(4,),
        in_specs=specs,
        out_specs=specs,
        out_shape=[shaped(first.shape, F32), shaped(second.shape, F32)],
        compiler_params=params(),
        cost_estimate=cost(0, 1e7),
        name="copies",
    )(first, second)


def widen_kernel(rows_ref, out_ref):
    out_ref[...] = rows_ref[...].astype(F32)


def widened(rows):
    spec = pl.BlockSpec((rows.shape[0] // 4, rows.shape[1]), lambda i: (i, 0))
    return pl.pallas_call(
        widen_kernel,
        grid=(4,),
        in_specs=[spec],
        out_specs=spec,
        out_shape=shaped(rows.shape, F32),
        compiler_params=params(),
        cost_estimate=cost(0, 8e6),
        name="widen",
    )(rows)


def tail_kernel(
    experts, stride, half, part_half, seq_count, head_parts, gap,
    sums_ref, route_hbm, id_cols_ref, gate_cols_ref, own_residual_ref, own_second_ref, cot_own_hbm,
    own_columns_hbm, router_ref, vectors_ref, own_tokens_ref, result_hbm,
    context_hbm, first_hbm, qkv_hbm, totals_hbm, weight_ref, out_weight_ref,
    seg_ref, live_ref,
    tokens_hbm, block_ref, qkv_sum_ref, out_sum_ref, bias_sum_ref, small_ref,
    route_recv, own_recv, cot_wide, columns_scr, part_two, down_one, up_one, down_two, up_two, own_scr,
    full_one, full_two, grad_scr,
    context_scr, first_scr, qkv_scr, totals_scr, back_scr, joined_scr,
    qkv_grad, out_grad, bias_grad, rows_acc, router_acc,
    result_home, result_wide,
    qkv_send, qkv_recv, qkv_all, out_send, out_recv, out_all, bias_recv, small_head, small_recv,
    route_send_sem, route_recv_sem, own_send_sem, own_recv_sem, columns_sem, load_sem, stage_sem, result_send_sem, result_recv_sem,
    down_one_sem, up_one_sem, down_two_sem, up_two_sem, down_one_out, up_one_out, down_two_out, up_two_out,
    full_one_sem, full_two_sem, full_one_out, full_two_out,
    sum_send_sem, sum_recv_sem, all_send_sem, all_recv_sem,
    bias_send_sem, bias_recv_sem, head_send_sem, head_recv_sem, small_send_sem, small_recv_sem,
):
    me = lax.axis_index("exp")
    here = lax.axis_index("head")
    ends = head_parts - 1
    seqlen = seg_ref.shape[1]
    part = seqlen // head_parts
    model_width = vectors_ref.shape[1]
    width = out_weight_ref.shape[0]
    factor = 1.0 / math.sqrt(HEAD_DIM)

    barrier = greet_both(experts, head_parts)

    def chunk_loads(seq):
        span = pl.ds(pl.multiple_of(seq * seqlen, seqlen), seqlen)
        return (
            pltpu.make_async_copy(context_hbm.at[span], context_scr, load_sem.at[0]),
            pltpu.make_async_copy(first_hbm.at[span], first_scr, load_sem.at[1]),
            pltpu.make_async_copy(qkv_hbm.at[span], qkv_scr, load_sem.at[2]),
            pltpu.make_async_copy(totals_hbm.at[span], totals_scr, load_sem.at[3]),
        )

    for copy in chunk_loads(0):
        copy.start()
    qkv_grad[...] = jnp.zeros_like(qkv_grad)
    out_grad[...] = jnp.zeros_like(out_grad)
    bias_grad[...] = jnp.zeros_like(bias_grad)
    rows_acc[...] = jnp.zeros_like(rows_acc)
    router_acc[...] = jnp.zeros_like(router_acc)
    pl.semaphore_wait(barrier, experts - 1 + ends)

    def to_exp(target):
        return dict(device_id=(target, here), device_id_type=MESH)

    def to_head(target):
        return dict(device_id=(me, target), device_id_type=MESH)

    def each_peer(action):
        def one(step, carry):
            action(step, lax.rem(me + step, experts), lax.rem(me + experts - step, experts))
            return carry

        lax.fori_loop(1, experts, one, 0)

    def result_copy(step, target):
        return pltpu.make_async_remote_copy(
            src_ref=result_hbm.at[target],
            dst_ref=result_home.at[me],
            send_sem=result_send_sem.at[step],
            recv_sem=result_recv_sem.at[step],
            **to_exp(target),
        )

    def own_copy(seq, step):
        target = lax.rem(here + step, head_parts)
        return pltpu.make_async_remote_copy(
            src_ref=cot_own_hbm.at[target, seq],
            dst_ref=own_recv.at[here, seq],
            send_sem=own_send_sem.at[seq, step],
            recv_sem=own_recv_sem.at[seq, step],
            **to_head(target),
        )

    def route_copy(step):
        target = lax.rem(here + step, head_parts)
        return pltpu.make_async_remote_copy(
            src_ref=route_hbm.at[target],
            dst_ref=route_recv.at[here],
            send_sem=route_send_sem.at[step],
            recv_sem=route_recv_sem.at[step],
            **to_head(target),
        )

    for other in range(1, head_parts):
        route_copy(other).start()
    route_local = pltpu.make_async_copy(route_hbm.at[here], route_recv.at[here], columns_sem.at[2])
    route_local.start()
    route_local.wait()
    own_local = pltpu.make_async_copy(cot_own_hbm.at[here], own_recv.at[here], columns_sem.at[1])
    own_local.start()
    own_local.wait()

    def down_copy(buffer, sems, outs, seq, shard):
        return pltpu.make_async_remote_copy(
            src_ref=buffer.at[seq, shard],
            dst_ref=buffer.at[seq, shard],
            send_sem=outs.at[seq, shard],
            recv_sem=sems.at[seq, shard],
            **to_head(here - 1),
        )

    def up_copy(buffer, sems, outs, seq, shard):
        return pltpu.make_async_remote_copy(
            src_ref=buffer.at[seq, shard - 1],
            dst_ref=buffer.at[seq, shard - 1],
            send_sem=outs.at[seq, shard - 1],
            recv_sem=sems.at[seq, shard - 1],
            **to_head(here + 1),
        )

    one_down = (down_one, down_one_sem, down_one_out)
    one_up = (up_one, up_one_sem, up_one_out)
    two_down = (down_two, down_two_sem, down_two_out)
    two_up = (up_two, up_two_sem, up_two_out)

    def reduce_hop(partial_ref, base, down, up, seq, hop):
        low = hop - ends + here
        high = ends - hop + here

        @pl.when((low >= 0) & (low < here))
        def downward():
            rows = partial_ref[pl.ds(pl.multiple_of(base + low * part, part), part)]

            @pl.when(here < ends)
            def add():
                down_copy(*down, seq, low).wait_recv()
                down[0][seq, low] = (down[0][seq, low].astype(F32) + rows.astype(F32)).astype(BF16)

            @pl.when(here == ends)
            def begin():
                down[0][seq, low] = rows

            down_copy(*down, seq, low).start()

        @pl.when((high > here) & (high <= ends))
        def upward():
            rows = partial_ref[pl.ds(pl.multiple_of(base + high * part, part), part)]

            @pl.when(here > 0)
            def add():
                up_copy(*up, seq, high).wait_recv()
                up[0][seq, high - 1] = (
                    up[0][seq, high - 1].astype(F32) + rows.astype(F32)
                ).astype(BF16)

            @pl.when(here == 0)
            def begin():
                up[0][seq, high - 1] = rows

            up_copy(*up, seq, high).start()

    def reduce_end(partial_ref, base, down, up, seq):
        own = pl.ds(pl.multiple_of(base + here * part, part), part)
        own_scr[...] = partial_ref[own].astype(F32)

        @pl.when(here < ends)
        def below():
            down_copy(*down, seq, here).wait_recv()
            own_scr[...] += down[0][seq, here].astype(F32)

        @pl.when(here > 0)
        def above():
            up_copy(*up, seq, here).wait_recv()
            own_scr[...] += up[0][seq, here - 1].astype(F32)

    def reduce_drain(down, up, seq):
        for shard in range(ends):

            @pl.when(shard < here)
            def downward():
                down_copy(*down, seq, shard).wait_send()

            @pl.when(shard + 1 > here)
            def upward():
                up_copy(*up, seq, shard + 1).wait_send()

    def full_copy(buffer, sems, outs, seq, shard, side):
        rows = pl.ds(pl.multiple_of(shard * part, part), part)
        return pltpu.make_async_remote_copy(
            src_ref=buffer.at[seq, rows],
            dst_ref=buffer.at[seq, rows],
            send_sem=outs.at[seq, shard, side],
            recv_sem=sems.at[seq, shard],
            **to_head(here + 1 - 2 * side),
        )

    one_full = (full_one, full_one_sem, full_one_out)
    two_full = (full_two, full_two_sem, full_two_out)

    def spread_hop(full, seq, hop):
        for side in range(2):
            shard = here - hop if side == 0 else here + hop
            there = shard >= 0 if side == 0 else shard <= ends
            onward = here < ends if side == 0 else here > 0

            @pl.when(there)
            def arrived():
                if hop > 0:
                    full_copy(*full, seq, shard, side).wait_recv()
                if hop < ends:

                    @pl.when(onward)
                    def pass_on():
                        full_copy(*full, seq, shard, side).start()

    def spread_drain(full, seq):
        for hop in range(ends):
            for side in range(2):
                shard = here - hop if side == 0 else here + hop
                there = shard >= 0 if side == 0 else shard <= ends
                onward = here < ends if side == 0 else here > 0

                @pl.when(there & onward)
                def sent():
                    full_copy(*full, seq, shard, side).wait_send()

    def middle(seq):
        second = own_second_ref[seq]
        lane = lax.broadcasted_iota(jnp.int32, (part, LANES), 1)
        logits = jnp.where(lane < experts, dot(second, router_ref[...]), NEGATIVE)
        powers = jnp.exp(logits - jnp.max(logits, axis=1, keepdims=True))
        chances = powers / jnp.sum(powers, axis=1, keepdims=True)
        @pl.when(seq == 0)
        def routes():
            for other in range(1, head_parts):
                route_copy(other).wait_recv()

        route = route_recv[0, seq]
        for other in range(1, head_parts):
            route = route + route_recv[other, seq]
        blank = jnp.zeros((LANES - route.shape[0], part), F32)
        route_grad = jnp.concatenate([route, blank], axis=0).T
        logit_grad = (
            chances * (route_grad - jnp.sum(chances * route_grad, axis=1, keepdims=True))
        ).astype(BF16)
        router_acc[...] += dot_first(second, logit_grad)
        grad = own_scr[...] + dot_last(logit_grad, router_ref[...])
        normal, scale = standard(own_residual_ref[seq])
        rows_acc[0:1] += jnp.sum(grad * normal, axis=0, keepdims=True)
        rows_acc[1:2] += jnp.sum(grad, axis=0, keepdims=True)
        for other in range(1, head_parts):
            own_copy(seq, other).wait_recv()
        unpack_rows(lambda z: own_recv[z, seq], cot_wide, head_parts, part, part_half)
        total = cot_wide[...].astype(F32) + norm_back(grad, vectors_ref[3:4], normal, scale)
        rows_acc[2:3] += jnp.sum(total, axis=0, keepdims=True)
        grad_scr[seq] = total
        full_one[seq, pl.ds(pl.multiple_of(here * part, part), part)] = total.astype(BF16)

    def attend_start(seq):
        for copy in chunk_loads(seq):
            copy.wait()
        grad = full_one[seq]
        back_scr[...] = dot_last(grad, out_weight_ref[...]).astype(BF16)
        out_grad[...] += dot_first(context_scr[...], grad)
        return mask_penalty(seg_ref[pl.ds(seq, 1)], live_ref[pl.ds(seq, 1)])

    def attend_head(head, penalty):
        lo = head * HEAD_DIM
        hi = lo + HEAD_DIM
        query = qkv_scr[:, lo:hi] * BF16(factor)
        keys = qkv_scr[:, width + lo : width + hi]
        values = qkv_scr[:, 2 * width + lo : 2 * width + hi]
        back = back_scr[:, lo:hi]
        weights = jnp.exp(
            dot_last(query, keys) + penalty - totals_scr[:, head : head + 1]
        )
        joined_scr[:, 2 * width + lo : 2 * width + hi] = dot_first(
            weights.astype(BF16), back
        ).astype(BF16)
        inner = jnp.sum(
            back.astype(F32) * context_scr[:, lo:hi].astype(F32), axis=-1, keepdims=True
        )
        score_grad = (weights * (dot_last(back, values) - inner)).astype(BF16)
        joined_scr[:, lo:hi] = (dot(score_grad, keys) * factor).astype(BF16)
        joined_scr[:, width + lo : width + hi] = dot_first(score_grad, query).astype(BF16)

    def attend_end(seq):
        joined = joined_scr[...]
        span = pl.ds(pl.multiple_of(lax.rem(seq, 2) * seqlen, seqlen), seqlen)
        part_two[span] = dot_last(joined, weight_ref[...]).astype(BF16)
        qkv_grad[...] += dot_first(first_scr[...], joined)
        bias_grad[0:1] += jnp.sum(joined.astype(F32), axis=0, keepdims=True)

        @pl.when(seq + 1 < seq_count)
        def more():
            for copy in chunk_loads(seq + 1):
                copy.start()

    def last(seq):
        grad = own_scr[...]
        normal, scale = standard(own_tokens_ref[seq].astype(F32))
        rows_acc[3:4] += jnp.sum(grad * normal, axis=0, keepdims=True)
        rows_acc[4:5] += jnp.sum(grad, axis=0, keepdims=True)
        total = grad_scr[seq] + norm_back(grad, vectors_ref[0:1], normal, scale)
        full_two[seq, pl.ds(pl.multiple_of(here * part, part), part)] = total.astype(BF16)

    def stage_copy(seq):
        span = pl.ds(pl.multiple_of(seq * seqlen, seqlen), seqlen)
        return pltpu.make_async_copy(full_two.at[seq], tokens_hbm.at[span], stage_sem.at[seq])

    def open_results():
        each_peer(lambda step, target, source: result_copy(step, target).wait_recv())

        def one(expert, carry):
            packed = result_home[expert]
            result_wide[expert, :, :LANES] = packed[:stride]
            tail = packed[stride:]
            result_wide[expert, :half, LANES:] = tail[:, :HEAD_DIM]
            result_wide[expert, half:, LANES:] = tail[2 * half - stride :, HEAD_DIM:]
            return carry

        lax.fori_loop(0, experts, one, 0)

    def combine(seq):
        span = pl.ds(pl.multiple_of(seq * seqlen, seqlen), seqlen)
        first = id_cols_ref[span, 0:1]
        second = id_cols_ref[span, 1:2]
        pltpu.make_async_copy(own_columns_hbm.at[span], columns_scr, columns_sem.at[0]).start()
        pltpu.make_async_copy(own_columns_hbm.at[span], columns_scr, columns_sem.at[0]).wait()
        first_gate = gate_cols_ref[span, 0:1]
        second_gate = gate_cols_ref[span, 1:2]

        def one(expert, total):
            slots = expert * stride + lax.broadcasted_iota(jnp.int32, (1, stride), 1)
            weights = jnp.where(
                first == slots, first_gate, jnp.where(second == slots, second_gate, 0.0)
            )
            return total + dot(weights.astype(BF16), result_wide[expert])

        block_ref[span] = lax.fori_loop(0, experts, one, columns_scr[...]).astype(BF16)

    qkv_rows = qkv_grad.shape[0] // experts
    out_rows = out_grad.shape[0] // experts

    def sum_copies(step, target):
        return (
            pltpu.make_async_remote_copy(
                src_ref=qkv_send.at[target],
                dst_ref=qkv_recv.at[me],
                send_sem=sum_send_sem.at[step, 0],
                recv_sem=sum_recv_sem.at[step, 0],
                **to_exp(target),
            ),
            pltpu.make_async_remote_copy(
                src_ref=out_send.at[target],
                dst_ref=out_recv.at[me],
                send_sem=sum_send_sem.at[step, 1],
                recv_sem=sum_recv_sem.at[step, 1],
                **to_exp(target),
            ),
        )

    def all_copies(step, target):
        return (
            pltpu.make_async_remote_copy(
                src_ref=qkv_all.at[me],
                dst_ref=qkv_all.at[me],
                send_sem=all_send_sem.at[step, 0],
                recv_sem=all_recv_sem.at[step, 0],
                **to_exp(target),
            ),
            pltpu.make_async_remote_copy(
                src_ref=out_all.at[me],
                dst_ref=out_all.at[me],
                send_sem=all_send_sem.at[step, 1],
                recv_sem=all_recv_sem.at[step, 1],
                **to_exp(target),
            ),
        )

    def all_arrivals(step, source):
        return (
            pltpu.make_async_remote_copy(
                src_ref=qkv_all.at[source],
                dst_ref=qkv_all.at[source],
                send_sem=all_send_sem.at[step, 0],
                recv_sem=all_recv_sem.at[step, 0],
                **to_exp(source),
            ),
            pltpu.make_async_remote_copy(
                src_ref=out_all.at[source],
                dst_ref=out_all.at[source],
                send_sem=all_send_sem.at[step, 1],
                recv_sem=all_recv_sem.at[step, 1],
                **to_exp(source),
            ),
        )

    def bias_copy(step, target):
        return pltpu.make_async_remote_copy(
            src_ref=bias_grad,
            dst_ref=bias_recv.at[me],
            send_sem=bias_send_sem.at[step],
            recv_sem=bias_recv_sem.at[step],
            **to_exp(target),
        )

    def start_sums():
        for block in range(experts):
            qkv_send[block] = qkv_grad[block * qkv_rows : (block + 1) * qkv_rows].astype(BF16)
            out_send[block] = out_grad[block * out_rows : (block + 1) * out_rows].astype(BF16)

        def begin(step, target, source):
            for copy in sum_copies(step, target):
                copy.start()
            bias_copy(step, target).start()

        each_peer(begin)
        qkv_recv[me] = qkv_send[me]
        out_recv[me] = out_send[me]
        bias_recv[me] = bias_grad[...]

    def spread_sums():
        def arrive(step, target, source):
            for copy in sum_copies(step, target):
                copy.wait_recv()
            bias_copy(step, target).wait_recv()

        each_peer(arrive)

        def add(source, totals):
            return (
                totals[0] + qkv_recv[source].astype(F32),
                totals[1] + out_recv[source].astype(F32),
                totals[2] + bias_recv[source],
            )

        qkv_total, out_total, bias_total = lax.fori_loop(
            1,
            experts,
            add,
            (qkv_recv[0].astype(F32), out_recv[0].astype(F32), bias_recv[0]),
        )
        qkv_all[me] = qkv_total.astype(BF16)
        out_all[me] = out_total.astype(BF16)
        bias_sum_ref[...] = bias_total

        def begin(step, target, source):
            for copy in all_copies(step, target):
                copy.start()

        each_peer(begin)

    def end_sums():
        def arrive(step, target, source):
            for copy in all_arrivals(step, source):
                copy.wait_recv()

        each_peer(arrive)
        for block in range(experts):
            qkv_sum_ref[block * qkv_rows : (block + 1) * qkv_rows] = qkv_all[block].astype(F32)
            out_sum_ref[block * out_rows : (block + 1) * out_rows] = out_all[block].astype(F32)

    def head_copy(step):
        return pltpu.make_async_remote_copy(
            src_ref=small_head.at[here],
            dst_ref=small_head.at[here],
            send_sem=head_send_sem.at[step],
            recv_sem=head_recv_sem.at[step],
            **to_head(lax.rem(here + step, head_parts)),
        )

    def head_arrival(step):
        source = lax.rem(here + head_parts - step, head_parts)
        return pltpu.make_async_remote_copy(
            src_ref=small_head.at[source],
            dst_ref=small_head.at[source],
            send_sem=head_send_sem.at[step],
            recv_sem=head_recv_sem.at[step],
            **to_head(source),
        )

    def small_copy(step, target):
        return pltpu.make_async_remote_copy(
            src_ref=small_recv.at[me],
            dst_ref=small_recv.at[me],
            send_sem=small_send_sem.at[step],
            recv_sem=small_recv_sem.at[step],
            **to_exp(target),
        )

    def small_arrival(step, source):
        return pltpu.make_async_remote_copy(
            src_ref=small_recv.at[source],
            dst_ref=small_recv.at[source],
            send_sem=small_send_sem.at[step],
            recv_sem=small_recv_sem.at[step],
            **to_exp(source),
        )

    heads = width // HEAD_DIM
    router_rows = small_head.shape[1] - 8

    second_start = 2 * ends
    spread_start = second_start + ends
    ticks = spread_start + ends + 1 + gap * (seq_count - 1)
    final = gap * (seq_count - 1)

    def tick(now, carry):
        def on(offset, action):
            since = now - offset

            @pl.when((since >= 0) & (lax.rem(since, gap) == 0) & (since < gap * seq_count))
            def run():
                action(since // gap)

        def first_end(seq):
            reduce_end(sums_ref, seq * seqlen, one_down, one_up, seq)
            middle(seq)

        def attend(seq):
            spread_hop(one_full, seq, ends)
            penalty = attend_start(seq)
            for head in range(heads):
                attend_head(head, penalty)
            attend_end(seq)

        def second_end(seq):
            reduce_end(part_two, lax.rem(seq, 2) * seqlen, two_down, two_up, seq)
            last(seq)

        def tokens_end(seq):
            spread_hop(two_full, seq, ends)
            stage_copy(seq).start()

        def own_begin(seq):
            for other in range(1, head_parts):
                own_copy(seq, other).start()

        on(ends, first_end)
        on(spread_start, second_end)
        for hop in range(ends):
            on(hop, lambda seq: reduce_hop(sums_ref, seq * seqlen, one_down, one_up, seq, hop))
            on(ends + hop, lambda seq: spread_hop(one_full, seq, hop))
            if hop > 0:
                on(
                    second_start + hop,
                    lambda seq: reduce_hop(
                        part_two, lax.rem(seq, 2) * seqlen, two_down, two_up, seq, hop
                    ),
                )
            on(spread_start + hop, lambda seq: spread_hop(two_full, seq, hop))
        on(0, own_begin)
        on(second_start, attend)
        on(
            second_start,
            lambda seq: reduce_hop(part_two, lax.rem(seq, 2) * seqlen, two_down, two_up, seq, 0),
        )

        @pl.when(now == 0)
        def send_results():
            each_peer(lambda step, target, source: result_copy(step, target).start())
            local = pltpu.make_async_copy(result_hbm.at[me], result_home.at[me], columns_sem.at[1])
            local.start()
            local.wait()

        @pl.when(now == ends + 1)
        def results():
            open_results()

        on(ends + 2, combine)

        @pl.when(now == final + second_start)
        def sums():
            start_sums()

        @pl.when(now == final + second_start + 2)
        def share():
            spread_sums()

        @pl.when(now == final + spread_start)
        def small():
            small_head[here, :8] = rows_acc[...]
            small_head[here, 8:] = router_acc[...].T[:router_rows]
            for other in range(1, head_parts):
                head_copy(other).start()

        @pl.when(now == final + spread_start + 1)
        def small_on():
            for other in range(1, head_parts):
                head_arrival(other).wait_recv()
            total = small_head[0]
            for other in range(1, head_parts):
                total = total + small_head[other]
            small_recv[me] = total
            each_peer(lambda step, target, source: small_copy(step, target).start())
            end_sums()

        on(spread_start + ends, tokens_end)
        return carry

    lax.fori_loop(0, ticks, tick, 0)

    each_peer(lambda step, target, source: small_arrival(step, source).wait_recv())
    small_ref[...] = lax.fori_loop(
        1, experts, lambda source, total: total + small_recv[source], small_recv[0]
    )
    for seq in range(seq_count):
        stage_copy(seq).wait()
        reduce_drain(one_down, one_up, seq)
        reduce_drain(two_down, two_up, seq)
        spread_drain(one_full, seq)
        spread_drain(two_full, seq)
    for other in range(1, head_parts):
        head_copy(other).wait_send()
        route_copy(other).wait_send()
        for seq in range(seq_count):
            own_copy(seq, other).wait_send()

    def sent(step, target, source):
        result_copy(step, target).wait_send()
        for copy in sum_copies(step, target):
            copy.wait_send()
        bias_copy(step, target).wait_send()
        for copy in all_copies(step, target):
            copy.wait_send()
        small_copy(step, target).wait_send()

    each_peer(sent)


def tail(
    sums, route, id_cols, gate_cols, own_residual, own_second, cot_own, own_columns, router, vectors,
    own_tokens, result, context, first, qkv, totals, flat_qkv, out_weight,
    segments, live, stride, half, part_half, head_parts,
):
    experts = result.shape[0]
    model_width = first.shape[1]
    seq_count, part = own_residual.shape[:2]
    seqlen = part * head_parts
    tok_count = seq_count * seqlen
    wide = flat_qkv.shape[1]
    width = wide // 3
    ends = head_parts - 1
    small_rows = 8 + round_up(experts, 8)
    dma = pltpu.SemaphoreType.DMA
    return pl.pallas_call(
        partial(tail_kernel, experts, stride, half, part_half, seq_count, head_parts, 2),
        in_specs=[whole(), anywhere()] + [whole()] * 4 + [anywhere()] * 2 + [whole()] * 3 + [anywhere()] * 5 + [whole()] * 4,
        out_specs=[anywhere()] + [whole()] * 5,
        out_shape=[
            shaped((tok_count, model_width), BF16),
            shaped((tok_count, width), BF16),
            shaped((model_width, wide), F32),
            shaped((width, model_width), F32),
            shaped((8, wide), F32),
            shaped((small_rows, model_width), F32),
        ],
        scratch_shapes=[
            pltpu.VMEM(route.shape, F32),
            pltpu.VMEM(cot_own.shape, BF16),
            pltpu.VMEM((part, model_width), BF16),
            pltpu.VMEM((seqlen, width), F32),
            pltpu.VMEM((2 * seqlen, model_width), BF16),
            pltpu.VMEM((seq_count, ends, part, model_width), BF16),
            pltpu.VMEM((seq_count, ends, part, model_width), BF16),
            pltpu.VMEM((seq_count, ends, part, model_width), BF16),
            pltpu.VMEM((seq_count, ends, part, model_width), BF16),
            pltpu.VMEM((part, model_width), F32),
            pltpu.VMEM((seq_count, seqlen, model_width), BF16),
            pltpu.VMEM((seq_count, seqlen, model_width), BF16),
            pltpu.VMEM((seq_count, part, model_width), F32),
            pltpu.VMEM((seqlen, width), BF16),
            pltpu.VMEM((seqlen, model_width), BF16),
            pltpu.VMEM((seqlen, wide), BF16),
            pltpu.VMEM((seqlen, LANES), F32),
            pltpu.VMEM((seqlen, width), BF16),
            pltpu.VMEM((seqlen, wide), BF16),
            pltpu.VMEM((model_width, wide), F32),
            pltpu.VMEM((width, model_width), F32),
            pltpu.VMEM((8, wide), F32),
            pltpu.VMEM((8, model_width), F32),
            pltpu.VMEM((model_width, LANES), F32),
            pltpu.VMEM((experts, stride + half, LANES), BF16),
            pltpu.VMEM((experts, stride, width), BF16),
            pltpu.VMEM((experts, model_width // experts, wide), BF16),
            pltpu.VMEM((experts, model_width // experts, wide), BF16),
            pltpu.VMEM((experts, model_width // experts, wide), BF16),
            pltpu.VMEM((experts, width // experts, model_width), BF16),
            pltpu.VMEM((experts, width // experts, model_width), BF16),
            pltpu.VMEM((experts, width // experts, model_width), BF16),
            pltpu.VMEM((experts, 8, wide), F32),
            pltpu.VMEM((head_parts, small_rows, model_width), F32),
            pltpu.VMEM((experts, small_rows, model_width), F32),
            dma((head_parts,)),
            dma((head_parts,)),
            dma((seq_count, head_parts)),
            dma((seq_count, head_parts)),
            dma((3,)),
            dma((4,)),
            dma((seq_count,)),
            dma((experts,)),
            dma((experts,)),
        ]
        + [dma((seq_count, ends))] * 8
        + [dma((seq_count, head_parts))] * 2
        + [dma((seq_count, head_parts, 2))] * 2
        + [dma((experts, 2))] * 4
        + [dma((experts,))] * 2
        + [dma((head_parts,))] * 2
        + [dma((experts,))] * 2,
        compiler_params=params(collective_id=2, has_side_effects=True),
        cost_estimate=cost(1e11, 1e8),
        name="tail",
    )(
        sums, route, id_cols, gate_cols, own_residual, own_second, cot_own, own_columns, router, vectors,
        own_tokens, result, context, first, qkv, totals, flat_qkv, out_weight,
        segments, live,
    )


def body(
    tokens,
    segments,
    live_mask,
    routes,
    priority,
    norm1_gain,
    norm1_bias,
    qkv_weight,
    qv_bias,
    out_weight,
    out_bias,
    norm2_gain,
    norm2_bias,
    router,
    up_weight,
    up_bias,
    down_weight,
    down_bias,
    cotangent,
):
    tok_count, model_width = tokens.shape
    seq_count, seqlen = segments.shape
    experts = lax.axis_size("exp")
    head_parts = lax.axis_size("head")
    head_index = lax.axis_index("head")
    quarter = model_width // head_parts
    capacity = (21 * tok_count + 10 * experts - 1) // (10 * experts)
    stride = round_up(capacity, 16)
    half = round_up(stride // 2, 16)
    local_width = qkv_weight.shape[2]

    norm_vectors = [norm1_gain, norm1_bias, out_bias, norm2_gain, norm2_bias]
    flat_qkv = qkv_weight.reshape(model_width, 3 * local_width)
    router_wide = jnp.pad(router, ((0, 0), (0, LANES - experts)))
    up, down = up_weight[0], down_weight[0]

    routes_t = routes.T
    part_half = round_up(seqlen // head_parts // 2, 16)
    first, qkv, context, totals, vectors, out_full_weight, gathered, ids, id_cols, cot_slots, cot_own, own_tokens = head(
        tokens, norm_vectors, flat_qkv, qv_bias, segments, live_mask, routes_t, priority, cotangent.T, out_weight, experts, capacity, stride, half, part_half, head_parts,
    )
    own_residual, own_second, own_columns, gate_cols, arrived, hidden, result, gate_col, cot_rows = forward(
        gathered, tokens, vectors, out_full_weight, router_wide, routes_t, ids,
        up, up_bias, down, down_bias, cot_slots, experts, stride, half, seq_count, head_parts,
    )
    own_result = lax.psum_scatter(result, "head", scatter_dimension=0, tiled=True)[0]
    sums, route_terms, grad_up, grad_up_bias, grad_down, grad_down_bias = backward(
        arrived, hidden, result, cot_rows, gate_col, id_cols, up, up_bias, down, half, head_parts,
        seqlen,
    )
    grad_up, grad_down, own_result = lax.optimization_barrier(
        (*copies_of(grad_up, grad_down), own_result)
    )
    grad_tokens, block_out, qkv_grad, out_grad, bias_grad, small = tail(
        sums, route_terms, id_cols, gate_cols, own_residual, own_second, cot_own, own_columns,
        router_wide, vectors, own_tokens, own_result, context, first, qkv, totals,
        flat_qkv, out_weight, segments, live_mask, stride, half, part_half, head_parts,
    )
    grad_qv_bias = jnp.concatenate(
        [bias_grad[0:1, :local_width], bias_grad[0:1, 2 * local_width :]], axis=0
    )
    return (
        block_out,
        widened(grad_tokens),
        small[3],
        small[4],
        qkv_grad.reshape(model_width, 3, local_width),
        grad_qv_bias,
        out_grad,
        small[2],
        small[0],
        small[1],
        small[8 : 8 + experts].T,
        grad_up[None],
        grad_up_bias[0:1],
        grad_down[None],
        lax.dynamic_slice_in_dim(grad_down_bias[0:1], head_index * quarter, quarter, 1),
    )


def solution(mesh):
    in_specs = (
        P("exp", None),
        P("exp", None),
        P("exp", None),
        P("exp", None),
        P("exp", None),
        P(),
        P(),
        P(None, None, "head"),
        P(None, "head"),
        P("head", None),
        P(),
        P(),
        P(),
        P(),
        P("exp", None, "head"),
        P("exp", "head"),
        P("exp", "head", None),
        P("exp", "head"),
        P("exp", "head"),
    )
    out_specs = (
        P("exp", "head"),
        P("exp", None),
        P(),
        P(),
        P(None, None, "head"),
        P(None, "head"),
        P("head", None),
        P(),
        P(),
        P(),
        P(),
        P("exp", None, "head"),
        P("exp", "head"),
        P("exp", "head", None),
        P("exp", "head"),
    )
    return jax.shard_map(body, mesh=mesh, in_specs=in_specs, out_specs=out_specs, check_vma=False)
```

```python
from functools import partial
import math

import jax
import jax.numpy as jnp
from jax import lax
from jax.experimental import pallas as pl
from jax.experimental.pallas import tpu as pltpu
from jax.sharding import PartitionSpec as P

HEAD_DIM = 64
LANES = 128
EPSILON = 1e-06
NEGATIVE = -1e30
CONTRACT_FIRST = (((0,), (0,)), ((), ()))
CONTRACT_LAST = (((1,), (1,)), ((), ()))
F32 = jnp.float32
BF16 = jnp.bfloat16
MESH = pl.DeviceIdType.MESH
VMEM_LIMIT = 54 * 1024 * 1024


def round_up(number, step):
    return (number + step - 1) // step * step


def whole():
    return pl.BlockSpec(memory_space=pltpu.VMEM)


def anywhere():
    return pl.BlockSpec(memory_space=pl.ANY)


def shaped(shape, dtype):
    return jax.ShapeDtypeStruct(shape, dtype)


def params(**more):
    return pltpu.CompilerParams(vmem_limit_bytes=VMEM_LIMIT, **more)


def cost(flops, moved):
    return pl.CostEstimate(flops=int(flops), bytes_accessed=int(moved), transcendentals=0)


def dot(left, right):
    return jnp.dot(left, right, preferred_element_type=F32)


def dot_last(left, right):
    return lax.dot_general(left, right, CONTRACT_LAST, preferred_element_type=F32)


def dot_first(left, right):
    return lax.dot_general(left, right, CONTRACT_FIRST, preferred_element_type=F32)


def standard(values):
    centred = values - jnp.mean(values, axis=-1, keepdims=True)
    scale = lax.rsqrt(jnp.mean(centred * centred, axis=-1, keepdims=True) + EPSILON)
    return centred * scale, scale


def norm_back(grad_rows, gain_row, normal, scale):
    inner = grad_rows * gain_row
    return scale * (
        inner
        - jnp.mean(inner, axis=-1, keepdims=True)
        - normal * jnp.mean(inner * normal, axis=-1, keepdims=True)
    )


def diagonal_of(count):
    return lax.broadcasted_iota(jnp.int32, (count, count), 0) == lax.broadcasted_iota(
        jnp.int32, (count, count), 1
    )


def as_column(row, diagonal):
    return jnp.sum(jnp.where(diagonal, row.astype(F32), 0.0), axis=1, keepdims=True)


def mask_penalty(seg_row, live_row):
    diagonal = diagonal_of(seg_row.shape[1])
    same = as_column(seg_row, diagonal) == seg_row.astype(F32)
    return jnp.where(same & ((live_row > 0) | diagonal), 0.0, NEGATIVE)


def pack_rows(rows, half):
    count = rows.shape[0]
    third = rows[:, LANES:]
    return rows[:, :LANES], jnp.concatenate([third[:half], third[count - half :]], axis=1)


def unpack_rows(parts_of, into, head_parts, count, half):
    extra = HEAD_DIM
    width = LANES + extra
    for z in range(head_parts):
        packed = parts_of(z)
        into[:, z * width : z * width + LANES] = packed[:count]
        tail = packed[count : count + half]
        into[:half, z * width + LANES : (z + 1) * width] = tail[:, :extra]
        into[half:, z * width + LANES : (z + 1) * width] = tail[2 * half - count :, extra:]


def greet(peers):
    barrier = pltpu.get_barrier_semaphore()
    me = lax.axis_index("exp")
    here = lax.axis_index("head")

    def call(step, carry):
        other = lax.rem(me + step, peers)
        pl.semaphore_signal(barrier, inc=1, device_id=(other, here), device_id_type=MESH)
        return carry

    lax.fori_loop(1, peers, call, 0)
    return barrier


def greet_both(peers, head_parts):
    barrier = greet(peers)
    me = lax.axis_index("exp")
    here = lax.axis_index("head")

    def call(step, carry):
        other = lax.rem(here + step, head_parts)
        pl.semaphore_signal(barrier, inc=1, device_id=(me, other), device_id_type=MESH)
        return carry

    lax.fori_loop(1, head_parts, call, 0)
    return barrier


def head_kernel(
    experts, capacity, stride, half, part_half, seq_count, head_parts,
    tokens_ref, gain1_ref, bias1_ref, out_bias_ref, gain2_ref, bias2_ref, weight_ref, bias_ref, seg_ref, live_ref, routes_ref, prio_ref, cot_ref, out_weight_ref,
    first_hbm, qkv_hbm, context_hbm, total_hbm, norm_ref, out_full_ref, gathered_ref, ids_ref, id_cols_ref, cot_recv, own_send, own_tokens_ref,
    rows_scr, cot_send, first_scr, qkv_scr, context_scr, total_scr,
    gather_sem, gather_out, cot_send_sem, cot_recv_sem, store_sem,
    weight_sem, weight_out, pair_send_sem, pair_recv_sem,
):
    me = lax.axis_index("exp")
    here = lax.axis_index("head")
    barrier = greet_both(experts, head_parts)
    ends = head_parts - 1
    tok_count = tokens_ref.shape[0]
    seqlen = tok_count // seq_count
    part = seqlen // head_parts
    pl.semaphore_wait(barrier, experts - 1 + ends)

    def own_rows():
        diagonal = diagonal_of(seqlen)
        for start in range(0, tok_count, seqlen):
            for pick in range(2):
                row = ids_ref[pick : pick + 1, start : start + seqlen]
                id_cols_ref[start : start + seqlen, pick : pick + 1] = as_column(
                    row, diagonal
                ).astype(jnp.int32)
        for seq in range(seq_count):
            own = pl.ds(pl.multiple_of(seq * seqlen + here * part, part), part)
            own_tokens_ref[seq] = tokens_ref[own]
            for z in range(head_parts):
                start = seq * seqlen + z * part
                block = cot_ref[:, start : start + part].astype(F32).T.astype(BF16)
                wide, tail = pack_rows(block, part_half)
                own_send[z, seq, :part] = wide
                own_send[z, seq, part:] = tail

    for row, vector in enumerate((gain1_ref, bias1_ref, out_bias_ref, gain2_ref, bias2_ref)):
        norm_ref[row : row + 1] = vector[...].astype(F32).reshape(1, -1)
    norm_ref[5:8] = jnp.zeros((3, norm_ref.shape[1]), F32)
    rows_scr[0:2] = routes_ref[...]
    rows_scr[3:4] = prio_ref[...]
    rows_scr[4:8] = jnp.zeros((4, tok_count), jnp.int32)
    for seq in range(seq_count):
        rows_scr[2:3, seq * seqlen : (seq + 1) * seqlen] = live_ref[seq : seq + 1]
    core = lax.rem(me, 2)
    weight_rows = out_weight_ref.shape[0]
    half_rows = weight_rows // 2

    def weight_span(shard, which):
        start = pl.multiple_of(shard * weight_rows + which * half_rows, 16)
        return pl.ds(start, half_rows)

    def weight_copy(shard, side):
        rows = weight_span(shard, core)
        return pltpu.make_async_remote_copy(
            src_ref=out_full_ref.at[rows],
            dst_ref=out_full_ref.at[rows],
            send_sem=weight_out.at[shard, side],
            recv_sem=weight_sem.at[shard],
            device_id=(me, here + 1 - 2 * side),
            device_id_type=MESH,
        )

    def pair_copy(step, which):
        rows = weight_span(lax.rem(here + step, head_parts), which)
        return pltpu.make_async_remote_copy(
            src_ref=out_full_ref.at[rows],
            dst_ref=out_full_ref.at[rows],
            send_sem=pair_send_sem.at[step],
            recv_sem=pair_recv_sem.at[step],
            device_id=(me + 1 - 2 * core, here),
            device_id_type=MESH,
        )

    def weight_hop(hop):
        def one(side, shard, there, onward):
            @pl.when(there)
            def arrived():
                if hop > 0:
                    weight_copy(shard, side).wait_recv()
                if hop < ends:

                    @pl.when(onward)
                    def pass_on():
                        weight_copy(shard, side).start()

        each_side(hop, one)
        if hop == ends:
            for step in range(1, head_parts):
                pair_copy(step, core).start()

    def stores(seq):
        slot = lax.rem(seq, 2)
        span = pl.ds(pl.multiple_of(seq * seqlen, seqlen), seqlen)
        return (
            pltpu.make_async_copy(first_scr.at[slot], first_hbm.at[span], store_sem.at[slot, 0]),
            pltpu.make_async_copy(qkv_scr.at[slot], qkv_hbm.at[span], store_sem.at[slot, 1]),
            pltpu.make_async_copy(context_scr.at[slot], context_hbm.at[span], store_sem.at[slot, 2]),
            pltpu.make_async_copy(total_scr.at[slot], total_hbm.at[span], store_sem.at[slot, 3]),
        )

    def attend(seq):
        slot = lax.rem(seq, 2)
        span = pl.ds(pl.multiple_of(seq * seqlen, seqlen), seqlen)

        @pl.when(seq >= 2)
        def free():
            for copy in stores(seq - 2):
                copy.wait()

        normal, ignored = standard(tokens_ref[span].astype(F32))
        first = (normal * norm_ref[0:1] + norm_ref[1:2]).astype(BF16)
        first_scr[slot] = first
        bias = bias_ref[...].astype(F32)
        bias_row = jnp.concatenate([bias[0:1], jnp.zeros_like(bias[0:1]), bias[1:2]], axis=1)
        rows = (dot(first, weight_ref[...]) + bias_row).astype(BF16)
        qkv_scr[slot] = rows
        penalty = mask_penalty(seg_ref[pl.ds(seq, 1)], live_ref[pl.ds(seq, 1)])
        width = rows.shape[1] // 3
        parts = []
        for head in range(width // HEAD_DIM):
            lo = head * HEAD_DIM
            hi = lo + HEAD_DIM
            query = rows[:, lo:hi] * BF16(1.0 / math.sqrt(HEAD_DIM))
            scores = dot_last(query, rows[:, width + lo : width + hi]) + penalty
            largest = jnp.max(scores, axis=-1, keepdims=True)
            weights = jnp.exp(scores - largest)
            total = jnp.sum(weights, axis=-1, keepdims=True)
            values = rows[:, 2 * width + lo : 2 * width + hi]
            parts.append((dot(weights.astype(BF16), values) / total).astype(BF16))
            total_scr[slot, :, head : head + 1] = largest + jnp.log(total)
        context = jnp.concatenate(parts, axis=1)
        context_scr[slot] = context
        for copy in stores(seq):
            copy.start()
        wide, tail = pack_rows(context, seqlen // 2)
        gathered_ref[here, seq, :seqlen] = wide
        gathered_ref[here, seq, seqlen:] = tail

    def full_copy(seq, shard, side):
        return pltpu.make_async_remote_copy(
            src_ref=gathered_ref.at[shard, seq],
            dst_ref=gathered_ref.at[shard, seq],
            send_sem=gather_out.at[seq, shard, side],
            recv_sem=gather_sem.at[seq, shard],
            device_id=(me, here + 1 - 2 * side),
            device_id_type=MESH,
        )

    def each_side(hop, action):
        for side in range(2):
            shard = here - hop if side == 0 else here + hop
            there = shard >= 0 if side == 0 else shard <= ends
            onward = here < ends if side == 0 else here > 0
            action(side, shard, there, onward)

    def spread_hop(seq, hop):
        def one(side, shard, there, onward):
            @pl.when(there)
            def arrived():
                if hop > 0:
                    full_copy(seq, shard, side).wait_recv()
                if hop < ends:

                    @pl.when(onward)
                    def pass_on():
                        full_copy(seq, shard, side).start()

        each_side(hop, one)

    def spread_drain(seq):
        def one(side, shard, there, onward):
            @pl.when(there & onward)
            def sent():
                full_copy(seq, shard, side).wait_send()

        for hop in range(ends):
            each_side(hop, one)

    numbers = lax.broadcasted_iota(jnp.int32, (experts, 1), 0)

    def hot(rows):
        live = rows[2:3] > 0
        first = jnp.where((rows[0:1] == numbers) & live, 1.0, 0.0)
        second = jnp.where((rows[1:2] == numbers) & live, 1.0, 0.0)
        return first, second

    def tables():
        rank_row = rows_scr[3:4].astype(F32)
        diagonal = diagonal_of(seqlen)
        counts = jnp.zeros((2 * experts, tok_count), F32)
        for start in range(0, tok_count, seqlen):
            first, second = hot(rows_scr[:, start : start + seqlen])
            rank_col = as_column(rank_row[:, start : start + seqlen], diagonal)
            earlier = jnp.where(rank_col < rank_row, 1.0, 0.0)
            both = jnp.concatenate([first, second], axis=0)
            counts = counts + dot(both.astype(BF16), earlier.astype(BF16))
        first, second = hot(rows_scr[...])
        total = jnp.sum(first, axis=1, keepdims=True)
        places = [
            jnp.sum(first * counts[:experts], axis=0, keepdims=True),
            jnp.sum(second * (counts[experts:] + total), axis=0, keepdims=True),
        ]
        for pick in range(2):
            place = places[pick].astype(jnp.int32)
            kept = (place < capacity) & (rows_scr[2:3] > 0)
            ids_ref[pick : pick + 1] = jnp.where(
                kept, rows_scr[pick : pick + 1] * stride + place, -1
            )
        ids_ref[2:8] = jnp.full((6, tok_count), -1, jnp.int32)

    def cot_copy(step, target):
        return pltpu.make_async_remote_copy(
            src_ref=cot_send.at[target],
            dst_ref=cot_recv.at[me],
            send_sem=cot_send_sem.at[step],
            recv_sem=cot_recv_sem.at[step],
            device_id=(target, here),
            device_id_type=MESH,
        )

    def fill(target):
        slots = target * stride + lax.broadcasted_iota(jnp.int32, (stride, 1), 0)
        hit = (ids_ref[0:1] == slots) | (ids_ref[1:2] == slots)
        block = dot_last(jnp.where(hit, 1.0, 0.0).astype(BF16), cot_ref[...]).astype(BF16)
        return pack_rows(block, half)

    def dispatch():
        def one(step, carry):
            target = lax.rem(me + step, experts)
            wide, tail = fill(target)
            cot_send[target, :stride] = wide
            cot_send[target, stride:] = tail
            cot_copy(step, target).start()
            return carry

        lax.fori_loop(1, experts, one, 0)
        wide, tail = fill(me)
        cot_recv[me, :stride] = wide
        cot_recv[me, stride:] = tail

    out_full_ref[pl.ds(pl.multiple_of(here * weight_rows, 16), weight_rows)] = out_weight_ref[...]
    weight_hop(0)

    def time_step(step, carry):
        for hop in range(1, ends + 1):

            @pl.when(step == hop)
            def weights():
                weight_hop(hop)

        @pl.when(step == seq_count + 1)
        def send():
            dispatch()

        for hop in range(ends, 0, -1):

            @pl.when((step >= hop) & (step - hop < seq_count))
            def move():
                spread_hop(step - hop, hop)

        @pl.when(step < seq_count)
        def work():
            attend(step)
            spread_hop(step, 0)

        @pl.when(step == seq_count)
        def places():
            tables()

        @pl.when(step == seq_count + 1)
        def rows():
            own_rows()

        return carry

    lax.fori_loop(0, seq_count + ends, time_step, 0)
    for seq in range(seq_count):
        spread_drain(seq)
    for seq in range(max(seq_count - 2, 0), seq_count):
        for copy in stores(seq):
            copy.wait()

    def sent(side, shard, there, onward):
        @pl.when(there & onward)
        def drain():
            weight_copy(shard, side).wait_send()

    for hop in range(ends):
        each_side(hop, sent)
    for step in range(1, head_parts):
        pair_copy(step, core).wait_send()
        pair_copy(step, 1 - core).wait_recv()

    def finish(step, carry):
        cot_copy(step, lax.rem(me + step, experts)).wait()
        return carry

    lax.fori_loop(1, experts, finish, 0)


def head(
    tokens, norm_vectors, flat_qkv, qv_bias, segments, live, routes_t, priority, cotangent, out_weight,
    experts, capacity, stride, half, part_half, head_parts,
):
    tok_count, model_width = tokens.shape
    seq_count, seqlen = segments.shape
    part = seqlen // head_parts
    wide = flat_qkv.shape[1]
    width = wide // 3
    dma = pltpu.SemaphoreType.DMA
    own = (head_parts, seq_count, part + part_half, LANES)
    slots = (experts, stride + half, LANES)
    return pl.pallas_call(
        partial(head_kernel, experts, capacity, stride, half, part_half, seq_count, head_parts),
        in_specs=[whole()] * 14,
        out_specs=[anywhere()] * 4 + [whole()] * 8,
        out_shape=[
            shaped((tok_count, model_width), BF16),
            shaped((tok_count, wide), BF16),
            shaped((tok_count, width), BF16),
            shaped((tok_count, LANES), F32),
            shaped((8, model_width), F32),
            shaped((head_parts * out_weight.shape[0], model_width), BF16),
            shaped((head_parts, seq_count, seqlen + seqlen // 2, LANES), BF16),
            shaped((8, tok_count), jnp.int32),
            shaped((tok_count, 8), jnp.int32),
            shaped(slots, BF16),
            shaped(own, BF16),
            shaped((seq_count, part, model_width), BF16),
        ],
        scratch_shapes=[
            pltpu.VMEM((8, tok_count), jnp.int32),
            pltpu.VMEM(slots, BF16),
            pltpu.VMEM((2, seqlen, model_width), BF16),
            pltpu.VMEM((2, seqlen, wide), BF16),
            pltpu.VMEM((2, seqlen, width), BF16),
            pltpu.VMEM((2, seqlen, LANES), F32),
            dma((seq_count, head_parts)),
            dma((seq_count, head_parts, 2)),
            dma((experts,)),
            dma((experts,)),
            dma((2, 4)),
            dma((head_parts,)),
            dma((head_parts, 2)),
            dma((head_parts,)),
            dma((head_parts,)),
        ],
        compiler_params=params(collective_id=3, has_side_effects=True),
        cost_estimate=cost(6e10, 1e7),
        name="head",
    )(tokens, *norm_vectors, flat_qkv, qv_bias, segments, live, routes_t, priority, cotangent, out_weight)


def gelu_parts(pre):
    root = math.sqrt(2.0 / math.pi)
    square = pre * pre
    wave = jnp.tanh(root * (pre + 0.044715 * pre * square))
    half_sum = 0.5 * (1.0 + wave)
    slope = half_sum + 0.5 * pre * (1.0 - wave * wave) * (
        root * (1.0 + 3.0 * 0.044715 * square)
    )
    return pre * half_sum, slope


def forward_kernel(
    experts, stride, half, seq_count, head_parts,
    gathered_ref, tokens_ref, vectors_ref, out_weight_ref, router_ref, rows_ref, ids_ref,
    up_ref, up_bias_ref, down_ref, down_bias_ref, cot_hbm,
    own_residual_ref, own_second_ref, own_columns_ref, gate_cols_ref, arrived_hbm, hidden_hbm, result_hbm,
    gate_col_ref, cot_all, gates_ref, arrived_ref, hidden_scr, result_scr, residual_ref, context_scr, second_scr, logit_scr, send_scr, gate_send, gate_recv,
    send_sem, recv_sem, gate_send_sem, gate_recv_sem, cot_sem, cot_out, local_sem,
    arrived_sem, store_sem,
):
    me = lax.axis_index("exp")
    here = lax.axis_index("head")
    barrier = greet_both(experts, head_parts)
    ends = head_parts - 1
    pieces = cot_sem.shape[1]
    piece_rows = experts // pieces
    tok_count = tokens_ref.shape[0]

    def cot_copy(shard, piece, side, own=False):
        span = pl.ds(piece * piece_rows, piece_rows)
        return pltpu.make_async_remote_copy(
            src_ref=cot_hbm.at[span] if own else cot_all.at[shard, span],
            dst_ref=cot_all.at[shard, span],
            send_sem=cot_out.at[shard, piece, side],
            recv_sem=cot_sem.at[shard, piece],
            device_id=(me, here + 1 - 2 * side),
            device_id_type=MESH,
        )

    def cot_side(hop, side):
        shard = here - hop if side == 0 else here + hop
        there = shard >= 0 if side == 0 else shard <= ends
        onward = here < ends if side == 0 else here > 0
        return shard, there, onward

    def cot_hop(hop, piece):
        for side in range(2):
            shard, there, onward = cot_side(hop, side)

            @pl.when(there)
            def arrived():
                if hop > 0:
                    cot_copy(shard, piece, side).wait_recv()
                if hop < ends:

                    @pl.when(onward)
                    def pass_on():
                        cot_copy(shard, piece, side, hop == 0).start()

    def cot_drain(hop, piece):
        for side in range(2):
            shard, there, onward = cot_side(hop, side)

            @pl.when(there & onward)
            def sent():
                cot_copy(shard, piece, side, hop == 0).wait_send()

    local = pltpu.make_async_copy(cot_hbm, cot_all.at[here], local_sem.at[0])
    local.start()
    pl.semaphore_wait(barrier, experts - 1 + ends)
    for piece in range(pieces):
        cot_hop(0, piece)
    seqlen = tok_count // seq_count
    for seq in range(seq_count):
        span = slice(seq * seqlen, (seq + 1) * seqlen)
        unpack_rows(lambda z: gathered_ref[z, seq], context_scr, head_parts, seqlen, seqlen // 2)
        residual = (
            tokens_ref[span].astype(F32)
            + dot(context_scr[...], out_weight_ref[...])
            + vectors_ref[2:3]
        )
        residual_ref[span] = residual
        normal, ignored = standard(residual)
        second = (normal * vectors_ref[3:4] + vectors_ref[4:5]).astype(BF16)
        second_scr[span] = second
        logit_scr[:, span] = dot(second, router_ref[...]).T[:experts]
    part = seqlen // head_parts
    for seq in range(seq_count):
        own = pl.ds(pl.multiple_of(seq * seqlen + here * part, part), part)
        own_residual_ref[seq] = residual_ref[own]
        own_second_ref[seq] = second_scr[own]
    width = residual_ref.shape[1] // head_parts
    for z in range(head_parts):

        @pl.when(here == z)
        def columns():
            own_columns_ref[...] = residual_ref[:, z * width : (z + 1) * width]


    logits = logit_scr[...]
    powers = jnp.exp(logits - jnp.max(logits, axis=0, keepdims=True))
    chances = powers / jnp.sum(powers, axis=0, keepdims=True)
    numbers = lax.broadcasted_iota(jnp.int32, (experts, 1), 0)
    for pick in range(2):
        chosen = jnp.where(rows_ref[pick : pick + 1] == numbers, chances, 0.0)
        gate = jnp.where(ids_ref[pick : pick + 1] >= 0, jnp.sum(chosen, axis=0, keepdims=True), 0.0)
        gates_ref[pick : pick + 1] = gate
    gates_ref[2:8] = jnp.zeros((6, tok_count), F32)

    def copies(target, step):
        to = dict(device_id=(target, here), device_id_type=MESH)
        return (
            pltpu.make_async_remote_copy(
                src_ref=send_scr.at[step],
                dst_ref=arrived_ref.at[me],
                send_sem=send_sem.at[step],
                recv_sem=recv_sem.at[step],
                **to,
            ),
            pltpu.make_async_remote_copy(
                src_ref=gate_send.at[step],
                dst_ref=gate_recv.at[me],
                send_sem=gate_send_sem.at[step],
                recv_sem=gate_recv_sem.at[step],
                **to,
            ),
        )

    def fill(target):
        slots = target * stride + lax.broadcasted_iota(jnp.int32, (stride, 1), 0)
        first = ids_ref[0:1] == slots
        second = ids_ref[1:2] == slots
        block = dot(jnp.where(first | second, 1.0, 0.0).astype(BF16), second_scr[...]).astype(BF16)
        gate = jnp.sum(
            jnp.where(first, gates_ref[0:1], jnp.where(second, gates_ref[1:2], 0.0)),
            axis=1,
            keepdims=True,
        )
        return block, jnp.broadcast_to(gate, (stride, LANES)).T[:8]

    def send(step, carry):
        target = lax.rem(me + step, experts)
        block, gate = fill(target)
        send_scr[step] = block
        gate_send[step] = gate
        for copy in copies(target, step):
            copy.start()
        return carry

    lax.fori_loop(1, experts, send, 0)
    block, gate = fill(me)
    arrived_ref[me] = block
    gate_recv[me] = gate

    def source_of(step):
        return lax.rem(me + experts - step, experts)

    def arrived_store(step):
        source = source_of(step)
        return pltpu.make_async_copy(
            arrived_ref.at[source], arrived_hbm.at[source], arrived_sem.at[step]
        )

    def stores(step):
        source = source_of(step)
        slot = lax.rem(step, 2)
        return (
            pltpu.make_async_copy(hidden_scr.at[slot], hidden_hbm.at[source], store_sem.at[slot, 0]),
            pltpu.make_async_copy(result_scr.at[slot], result_hbm.at[:, source], store_sem.at[slot, 1]),
        )

    def work(step):
        source = source_of(step)
        slot = lax.rem(step, 2)
        arrived_store(step).start()
        pre = dot(arrived_ref[source], up_ref[...]) + up_bias_ref[...].astype(F32)
        hidden = gelu_parts(pre)[0].astype(BF16)
        result = dot(hidden, down_ref[...])
        down_bias = down_bias_ref[...].astype(F32)

        @pl.when(step >= 2)
        def free():
            for copy in stores(step - 2):
                copy.wait()

        hidden_scr[slot] = hidden
        for z in range(head_parts):
            columns = result[:, z * width : (z + 1) * width] + jnp.where(here == z, down_bias, 0.0)
            wide, tail = pack_rows(columns.astype(BF16), half)
            result_scr[slot, z, :stride] = wide
            result_scr[slot, z, stride:] = tail
        for copy in stores(step):
            copy.start()

    diagonal = diagonal_of(seqlen)
    for start in range(0, tok_count, seqlen):
        for pick in range(2):
            gate_cols_ref[start : start + seqlen, pick : pick + 1] = as_column(
                gates_ref[pick : pick + 1, start : start + seqlen], diagonal
            )
    work(0)
    moves = [(hop, piece) for hop in range(1, ends) for piece in range(pieces)]
    early = len(moves) - min(experts - 2, len(moves))
    for move in moves[:early]:
        cot_hop(*move)

    def receive(step, carry):
        for place, move in enumerate(moves[early:]):

            @pl.when(step == place + 1)
            def pass_on():
                cot_hop(*move)

        source = lax.rem(me + experts - step, experts)
        wide, narrow = copies(source, step)
        wide.wait_recv()
        narrow.wait_recv()
        work(step)
        return carry

    lax.fori_loop(1, experts, receive, 0)

    for step in (experts - 2, experts - 1):
        for copy in stores(step):
            copy.wait()

    def stored(step, carry):
        arrived_store(step).wait()
        return carry

    lax.fori_loop(0, experts, stored, 0)

    def finish(step, carry):
        for copy in copies(lax.rem(me + step, experts), step):
            copy.wait_send()
        return carry

    lax.fori_loop(1, experts, finish, 0)
    for piece in range(pieces):
        cot_hop(ends, piece)
        for hop in range(ends):
            cot_drain(hop, piece)
    local.wait()
    lane = lax.broadcasted_iota(jnp.int32, (LANES, stride), 0)
    square = jnp.zeros((LANES, stride), F32)
    for source in range(experts):
        square = jnp.where(lane == source, gate_recv[source, 0:1], square)
    gate_col_ref[...] = square.T


def forward(
    gathered, tokens, vectors, out_weight, router, rows, ids, up, up_bias, down, down_bias, cot_slots,
    experts, stride, half, seq_count, head_parts,
):
    tok_count, model_width = tokens.shape
    seqlen = tok_count // seq_count
    part = seqlen // head_parts
    return pl.pallas_call(
        partial(forward_kernel, experts, stride, half, seq_count, head_parts),
        in_specs=[whole()] * 11 + [anywhere()],
        out_specs=[whole()] * 4 + [anywhere()] * 3 + [whole()] + [anywhere()],
        out_shape=[
            shaped((seq_count, part, model_width), F32),
            shaped((seq_count, part, model_width), BF16),
            shaped((tok_count, model_width // head_parts), F32),
            shaped((tok_count, 8), F32),
            shaped((experts, stride, model_width), BF16),
            shaped((experts, stride, up.shape[1]), BF16),
            shaped((head_parts, experts, stride + half, LANES), BF16),
            shaped((stride, LANES), F32),
            shaped((head_parts, experts, stride + half, LANES), BF16),
        ],
        scratch_shapes=[
            pltpu.VMEM((8, tok_count), F32),
            pltpu.VMEM((experts, stride, model_width), BF16),
            pltpu.VMEM((2, stride, up.shape[1]), BF16),
            pltpu.VMEM((2, head_parts, stride + half, LANES), BF16),
            pltpu.VMEM((tok_count, model_width), F32),
            pltpu.VMEM((seqlen, model_width), BF16),
            pltpu.VMEM((tok_count, model_width), BF16),
            pltpu.VMEM((experts, tok_count), F32),
            pltpu.VMEM((experts, stride, model_width), BF16),
            pltpu.VMEM((experts, 8, stride), F32),
            pltpu.VMEM((experts, 8, stride), F32),
            pltpu.SemaphoreType.DMA((experts,)),
            pltpu.SemaphoreType.DMA((experts,)),
            pltpu.SemaphoreType.DMA((experts,)),
            pltpu.SemaphoreType.DMA((experts,)),
            pltpu.SemaphoreType.DMA((head_parts, 4)),
            pltpu.SemaphoreType.DMA((head_parts, 4, 2)),
            pltpu.SemaphoreType.DMA((1,)),
            pltpu.SemaphoreType.DMA((experts,)),
            pltpu.SemaphoreType.DMA((2, 2)),
        ],
        compiler_params=params(collective_id=0, has_side_effects=True),
        cost_estimate=cost(8e10, 1e8),
        name="forward",
    )(gathered, tokens, vectors, out_weight, router, rows, ids, up, up_bias, down, down_bias, cot_slots)


def backward_kernel(
    experts, stride, half, head_parts, chunk,
    arrived_hbm, hidden_hbm, result_hbm, cot_hbm, gate_col_ref, ids_ref, up_ref, up_bias_ref, down_ref,
    sums_ref, route_ref, grad_up_ref, grad_up_bias_ref, grad_down_ref, grad_down_bias_ref,
    rows_scr, result_scr, cot_scr, cot_wide, result_wide, hidden_scr, pre_grad_scr, out_grad_scr,
    send_scr, recv_scr, gate_send, gate_recv, total_scr,
    load_sem, send_sem, recv_sem, gate_send_sem, gate_recv_sem,
):
    me = lax.axis_index("exp")
    here = lax.axis_index("head")
    barrier = greet(experts)
    tok_count = ids_ref.shape[0]
    model_width = up_ref.shape[0]

    def loads(step):
        home = lax.rem(me + step, experts)
        slot = lax.rem(step, 2)
        return (
            pltpu.make_async_copy(arrived_hbm.at[home], rows_scr.at[slot], load_sem.at[slot, 0]),
            pltpu.make_async_copy(result_hbm.at[:, home], result_scr.at[slot], load_sem.at[slot, 1]),
            pltpu.make_async_copy(cot_hbm.at[:, home], cot_scr.at[slot], load_sem.at[slot, 2]),
        )

    def copies(target, step):
        to = dict(device_id=(target, here), device_id_type=MESH)
        return (
            pltpu.make_async_remote_copy(
                src_ref=send_scr.at[step],
                dst_ref=recv_scr.at[me],
                send_sem=send_sem.at[step],
                recv_sem=recv_sem.at[step],
                **to,
            ),
            pltpu.make_async_remote_copy(
                src_ref=gate_send.at[step],
                dst_ref=gate_recv.at[me],
                send_sem=gate_send_sem.at[step],
                recv_sem=gate_recv_sem.at[step],
                **to,
            ),
        )

    for copy in loads(1):
        copy.start()
    grad_up_ref[...] = jnp.zeros_like(grad_up_ref)
    grad_down_ref[...] = jnp.zeros_like(grad_down_ref)
    grad_up_bias_ref[...] = jnp.zeros_like(grad_up_bias_ref)
    grad_down_bias_ref[...] = jnp.zeros_like(grad_down_bias_ref)
    total_scr[...] = jnp.zeros_like(total_scr)
    pl.semaphore_wait(barrier, experts - 1)

    def work(step):
        home = lax.rem(me + step, experts)
        slot = lax.rem(step, 2)
        for copy in loads(step):
            copy.wait()
        unpack_rows(lambda z: cot_scr[slot, z], cot_wide, head_parts, stride, half)
        unpack_rows(lambda z: result_scr[slot, z], result_wide, head_parts, stride, half)
        out_rows = cot_wide[...].astype(F32)
        pre = dot(rows_scr[slot], up_ref[...]) + up_bias_ref[...].astype(F32)
        slope = gelu_parts(pre)[1]
        lane = lax.broadcasted_iota(jnp.int32, (stride, LANES), 1)
        gate = jnp.sum(jnp.where(lane == home, gate_col_ref[...], 0.0), axis=1, keepdims=True)
        out_grad = (gate * out_rows).astype(BF16)
        out_grad_scr[step] = out_grad
        grad_down_bias_ref[0:1] += jnp.sum(out_grad.astype(F32), axis=0, keepdims=True)
        pre_grad = (dot_last(out_grad, down_ref[...]) * slope).astype(BF16)
        pre_grad_scr[step] = pre_grad
        grad_up_bias_ref[0:1] += jnp.sum(pre_grad.astype(F32), axis=0, keepdims=True)
        gate_grad = jnp.sum(result_wide[...].astype(F32) * out_rows, axis=1, keepdims=True)
        return (
            dot_last(pre_grad, up_ref[...]).astype(BF16),
            jnp.broadcast_to(gate_grad, (stride, LANES)).T[:8],
        )

    def send(step, carry):
        for copy in loads(lax.rem(step + 1, experts)):
            copy.start()
        block, gate = work(step)
        send_scr[step] = block
        gate_send[step] = gate
        for copy in copies(lax.rem(me + step, experts), step):
            copy.start()
        return carry

    lax.fori_loop(1, experts, send, 0)
    block, gate = work(0)
    recv_scr[me] = block
    gate_recv[me] = gate

    def row_loads(step):
        home = lax.rem(me + step, experts)
        slot = lax.rem(step, 2)
        return (
            pltpu.make_async_copy(arrived_hbm.at[home], rows_scr.at[slot], load_sem.at[slot, 0]),
            pltpu.make_async_copy(hidden_hbm.at[home], hidden_scr.at[slot], load_sem.at[slot, 1]),
        )

    def weigh(step):
        slot = lax.rem(step, 2)
        for copy in row_loads(step):
            copy.wait()
        grad_up_ref[...] += dot_first(rows_scr[slot], pre_grad_scr[step])
        grad_down_ref[...] += dot_first(hidden_scr[slot], out_grad_scr[step])

    def weigh_some(step, carry):
        for copy in row_loads(step + 1):
            copy.start()
        weigh(step)
        return carry

    for copy in row_loads(0):
        copy.start()
    lax.fori_loop(0, experts - 1, weigh_some, 0)
    weigh(experts - 1)

    def gather(source):
        slots = source * stride + lax.broadcasted_iota(jnp.int32, (1, stride), 1)
        lane = lax.broadcasted_iota(jnp.int32, (chunk, LANES), 1)

        def part(index, carry):
            span = pl.ds(pl.multiple_of(index * chunk, chunk), chunk)
            hit = (ids_ref[span, 0:1] == slots) | (ids_ref[span, 1:2] == slots)
            total_scr[span, :model_width] += dot(
                jnp.where(hit, 1.0, 0.0).astype(BF16), recv_scr[source]
            )
            gate = jnp.sum(jnp.where(hit, gate_recv[source, 0:1], 0.0), axis=1, keepdims=True)
            total_scr[span, model_width:] = jnp.where(
                lane == source, gate, total_scr[span, model_width:]
            )
            return carry

        lax.fori_loop(0, tok_count // chunk, part, 0)

    gather(me)

    def receive(step, carry):
        source = lax.rem(me + experts - step, experts)
        for copy in copies(source, step):
            copy.wait_recv()
        gather(source)
        return carry

    lax.fori_loop(1, experts, receive, 0)
    sums_ref[...] = total_scr[:, :model_width].astype(BF16)
    parts, seqs, kinds, count = route_ref.shape
    for seq in range(seqs):
        for z in range(parts):
            start = (seq * parts + z) * count
            route_ref[z, seq] = total_scr[start : start + count, model_width:].T[:kinds]

    def finish(step, carry):
        for copy in copies(lax.rem(me + step, experts), step):
            copy.wait_send()
        return carry

    lax.fori_loop(1, experts, finish, 0)


def backward(
    arrived, hidden, result, cot_rows, gate_col, id_cols, up, up_bias, down, half, head_parts, chunk
):
    tok_count = id_cols.shape[0]
    experts, stride, model_width = arrived.shape
    inner = up.shape[1]
    rows = (experts, stride, model_width)
    return pl.pallas_call(
        partial(backward_kernel, experts, stride, half, head_parts, chunk),
        in_specs=[anywhere()] * 4 + [whole()] * 5,
        out_specs=[whole()] * 6,
        out_shape=[
            shaped((tok_count, model_width), BF16),
            shaped((head_parts, tok_count // chunk, round_up(experts, 8), chunk // head_parts), F32),
            shaped((model_width, inner), F32),
            shaped((8, inner), F32),
            shaped((inner, model_width), F32),
            shaped((8, model_width), F32),
        ],
        scratch_shapes=[
            pltpu.VMEM((2, stride, model_width), BF16),
            pltpu.VMEM((2, head_parts, stride + half, LANES), BF16),
            pltpu.VMEM((2, head_parts, stride + half, LANES), BF16),
            pltpu.VMEM((stride, model_width), BF16),
            pltpu.VMEM((stride, model_width), BF16),
            pltpu.VMEM((2, stride, inner), BF16),
            pltpu.VMEM((experts, stride, inner), BF16),
            pltpu.VMEM(rows, BF16),
            pltpu.VMEM(rows, BF16),
            pltpu.VMEM(rows, BF16),
            pltpu.VMEM((experts, 8, stride), F32),
            pltpu.VMEM((experts, 8, stride), F32),
            pltpu.VMEM((tok_count, model_width + LANES), F32),
            pltpu.SemaphoreType.DMA((2, 3)),
            pltpu.SemaphoreType.DMA((experts,)),
            pltpu.SemaphoreType.DMA((experts,)),
            pltpu.SemaphoreType.DMA((experts,)),
            pltpu.SemaphoreType.DMA((experts,)),
        ],
        compiler_params=params(collective_id=1, has_side_effects=True),
        cost_estimate=cost(8e10, 1e8),
        name="backward",
    )(arrived, hidden, result, cot_rows, gate_col, id_cols, up, up_bias, down)


def copy_kernel(first_ref, second_ref, first_out, second_out):
    first_out[...] = first_ref[...]
    second_out[...] = second_ref[...]


def copies_of(first, second):
    rows = first.shape[0] // 4
    specs = [pl.BlockSpec((rows, a.shape[1]), lambda i: (i, 0)) for a in (first, second)]
    return pl.pallas_call(
        copy_kernel,
        grid=(4,),
        in_specs=specs,
        out_specs=specs,
        out_shape=[shaped(first.shape, F32), shaped(second.shape, F32)],
        compiler_params=params(),
        cost_estimate=cost(0, 1e7),
        name="copies",
    )(first, second)


def widen_kernel(rows_ref, out_ref):
    out_ref[...] = rows_ref[...].astype(F32)


def widened(rows):
    spec = pl.BlockSpec((rows.shape[0] // 4, rows.shape[1]), lambda i: (i, 0))
    return pl.pallas_call(
        widen_kernel,
        grid=(4,),
        in_specs=[spec],
        out_specs=spec,
        out_shape=shaped(rows.shape, F32),
        compiler_params=params(),
        cost_estimate=cost(0, 8e6),
        name="widen",
    )(rows)


def tail_kernel(
    experts, stride, half, part_half, seq_count, head_parts, gap,
    sums_ref, route_hbm, id_cols_ref, gate_cols_ref, own_residual_ref, own_second_ref, cot_own_hbm,
    own_columns_hbm, router_ref, vectors_ref, own_tokens_ref, result_hbm,
    context_hbm, first_hbm, qkv_hbm, totals_hbm, weight_ref, out_weight_ref,
    seg_ref, live_ref,
    tokens_hbm, block_ref, qkv_sum_ref, out_sum_ref, bias_sum_ref, small_ref,
    route_recv, own_recv, cot_wide, columns_scr, part_two, down_one, up_one, down_two, up_two, own_scr,
    full_one, full_two, grad_scr,
    context_scr, first_scr, qkv_scr, totals_scr, back_scr, joined_scr,
    qkv_grad, out_grad, bias_grad, rows_acc, router_acc,
    result_home, result_wide,
    qkv_send, qkv_recv, qkv_all, out_send, out_recv, out_all, bias_recv, small_head, small_recv,
    route_send_sem, route_recv_sem, own_send_sem, own_recv_sem, columns_sem, load_sem, stage_sem, result_send_sem, result_recv_sem,
    down_one_sem, up_one_sem, down_two_sem, up_two_sem, down_one_out, up_one_out, down_two_out, up_two_out,
    full_one_sem, full_two_sem, full_one_out, full_two_out,
    sum_send_sem, sum_recv_sem, all_send_sem, all_recv_sem,
    bias_send_sem, bias_recv_sem, head_send_sem, head_recv_sem, small_send_sem, small_recv_sem,
):
    me = lax.axis_index("exp")
    here = lax.axis_index("head")
    ends = head_parts - 1
    seqlen = seg_ref.shape[1]
    part = seqlen // head_parts
    model_width = vectors_ref.shape[1]
    width = out_weight_ref.shape[0]
    factor = 1.0 / math.sqrt(HEAD_DIM)

    barrier = greet_both(experts, head_parts)

    def chunk_loads(seq):
        span = pl.ds(pl.multiple_of(seq * seqlen, seqlen), seqlen)
        return (
            pltpu.make_async_copy(context_hbm.at[span], context_scr, load_sem.at[0]),
            pltpu.make_async_copy(first_hbm.at[span], first_scr, load_sem.at[1]),
            pltpu.make_async_copy(qkv_hbm.at[span], qkv_scr, load_sem.at[2]),
            pltpu.make_async_copy(totals_hbm.at[span], totals_scr, load_sem.at[3]),
        )

    for copy in chunk_loads(0):
        copy.start()
    qkv_grad[...] = jnp.zeros_like(qkv_grad)
    out_grad[...] = jnp.zeros_like(out_grad)
    bias_grad[...] = jnp.zeros_like(bias_grad)
    rows_acc[...] = jnp.zeros_like(rows_acc)
    router_acc[...] = jnp.zeros_like(router_acc)
    pl.semaphore_wait(barrier, experts - 1 + ends)

    def to_exp(target):
        return dict(device_id=(target, here), device_id_type=MESH)

    def to_head(target):
        return dict(device_id=(me, target), device_id_type=MESH)

    def each_peer(action):
        def one(step, carry):
            action(step, lax.rem(me + step, experts), lax.rem(me + experts - step, experts))
            return carry

        lax.fori_loop(1, experts, one, 0)

    def result_copy(step, target):
        return pltpu.make_async_remote_copy(
            src_ref=result_hbm.at[target],
            dst_ref=result_home.at[me],
            send_sem=result_send_sem.at[step],
            recv_sem=result_recv_sem.at[step],
            **to_exp(target),
        )

    def own_copy(seq, step):
        target = lax.rem(here + step, head_parts)
        return pltpu.make_async_remote_copy(
            src_ref=cot_own_hbm.at[target, seq],
            dst_ref=own_recv.at[here, seq],
            send_sem=own_send_sem.at[seq, step],
            recv_sem=own_recv_sem.at[seq, step],
            **to_head(target),
        )

    def route_copy(step):
        target = lax.rem(here + step, head_parts)
        return pltpu.make_async_remote_copy(
            src_ref=route_hbm.at[target],
            dst_ref=route_recv.at[here],
            send_sem=route_send_sem.at[step],
            recv_sem=route_recv_sem.at[step],
            **to_head(target),
        )

    for other in range(1, head_parts):
        route_copy(other).start()
    route_local = pltpu.make_async_copy(route_hbm.at[here], route_recv.at[here], columns_sem.at[2])
    route_local.start()
    own_local = pltpu.make_async_copy(cot_own_hbm.at[here], own_recv.at[here], columns_sem.at[3])
    own_local.start()

    def down_copy(buffer, sems, outs, seq, shard):
        return pltpu.make_async_remote_copy(
            src_ref=buffer.at[seq, shard],
            dst_ref=buffer.at[seq, shard],
            send_sem=outs.at[seq, shard],
            recv_sem=sems.at[seq, shard],
            **to_head(here - 1),
        )

    def up_copy(buffer, sems, outs, seq, shard):
        return pltpu.make_async_remote_copy(
            src_ref=buffer.at[seq, shard - 1],
            dst_ref=buffer.at[seq, shard - 1],
            send_sem=outs.at[seq, shard - 1],
            recv_sem=sems.at[seq, shard - 1],
            **to_head(here + 1),
        )

    one_down = (down_one, down_one_sem, down_one_out)
    one_up = (up_one, up_one_sem, up_one_out)
    two_down = (down_two, down_two_sem, down_two_out)
    two_up = (up_two, up_two_sem, up_two_out)

    def reduce_hop(partial_ref, base, down, up, seq, hop):
        low = hop - ends + here
        high = ends - hop + here

        @pl.when((low >= 0) & (low < here))
        def downward():
            rows = partial_ref[pl.ds(pl.multiple_of(base + low * part, part), part)]

            @pl.when(here < ends)
            def add():
                down_copy(*down, seq, low).wait_recv()
                down[0][seq, low] = (down[0][seq, low].astype(F32) + rows.astype(F32)).astype(BF16)

            @pl.when(here == ends)
            def begin():
                down[0][seq, low] = rows

            down_copy(*down, seq, low).start()

        @pl.when((high > here) & (high <= ends))
        def upward():
            rows = partial_ref[pl.ds(pl.multiple_of(base + high * part, part), part)]

            @pl.when(here > 0)
            def add():
                up_copy(*up, seq, high).wait_recv()
                up[0][seq, high - 1] = (
                    up[0][seq, high - 1].astype(F32) + rows.astype(F32)
                ).astype(BF16)

            @pl.when(here == 0)
            def begin():
                up[0][seq, high - 1] = rows

            up_copy(*up, seq, high).start()

    def reduce_end(partial_ref, base, down, up, seq):
        own = pl.ds(pl.multiple_of(base + here * part, part), part)
        own_scr[...] = partial_ref[own].astype(F32)

        @pl.when(here < ends)
        def below():
            down_copy(*down, seq, here).wait_recv()
            own_scr[...] += down[0][seq, here].astype(F32)

        @pl.when(here > 0)
        def above():
            up_copy(*up, seq, here).wait_recv()
            own_scr[...] += up[0][seq, here - 1].astype(F32)

    def reduce_drain(down, up, seq):
        for shard in range(ends):

            @pl.when(shard < here)
            def downward():
                down_copy(*down, seq, shard).wait_send()

            @pl.when(shard + 1 > here)
            def upward():
                up_copy(*up, seq, shard + 1).wait_send()

    def full_copy(buffer, sems, outs, seq, shard, side):
        rows = pl.ds(pl.multiple_of(shard * part, part), part)
        return pltpu.make_async_remote_copy(
            src_ref=buffer.at[seq, rows],
            dst_ref=buffer.at[seq, rows],
            send_sem=outs.at[seq, shard, side],
            recv_sem=sems.at[seq, shard],
            **to_head(here + 1 - 2 * side),
        )

    one_full = (full_one, full_one_sem, full_one_out)
    two_full = (full_two, full_two_sem, full_two_out)

    def spread_hop(full, seq, hop):
        for side in range(2):
            shard = here - hop if side == 0 else here + hop
            there = shard >= 0 if side == 0 else shard <= ends
            onward = here < ends if side == 0 else here > 0

            @pl.when(there)
            def arrived():
                if hop > 0:
                    full_copy(*full, seq, shard, side).wait_recv()
                if hop < ends:

                    @pl.when(onward)
                    def pass_on():
                        full_copy(*full, seq, shard, side).start()

    def spread_drain(full, seq):
        for hop in range(ends):
            for side in range(2):
                shard = here - hop if side == 0 else here + hop
                there = shard >= 0 if side == 0 else shard <= ends
                onward = here < ends if side == 0 else here > 0

                @pl.when(there & onward)
                def sent():
                    full_copy(*full, seq, shard, side).wait_send()

    def middle(seq):
        second = own_second_ref[seq]
        lane = lax.broadcasted_iota(jnp.int32, (part, LANES), 1)
        logits = jnp.where(lane < experts, dot(second, router_ref[...]), NEGATIVE)
        powers = jnp.exp(logits - jnp.max(logits, axis=1, keepdims=True))
        chances = powers / jnp.sum(powers, axis=1, keepdims=True)
        @pl.when(seq == 0)
        def routes():
            route_local.wait()
            own_local.wait()
            for other in range(1, head_parts):
                route_copy(other).wait_recv()

        route = route_recv[0, seq]
        for other in range(1, head_parts):
            route = route + route_recv[other, seq]
        blank = jnp.zeros((LANES - route.shape[0], part), F32)
        route_grad = jnp.concatenate([route, blank], axis=0).T
        logit_grad = (
            chances * (route_grad - jnp.sum(chances * route_grad, axis=1, keepdims=True))
        ).astype(BF16)
        router_acc[...] += dot_first(second, logit_grad)
        grad = own_scr[...] + dot_last(logit_grad, router_ref[...])
        normal, scale = standard(own_residual_ref[seq])
        rows_acc[0:1] += jnp.sum(grad * normal, axis=0, keepdims=True)
        rows_acc[1:2] += jnp.sum(grad, axis=0, keepdims=True)
        for other in range(1, head_parts):
            own_copy(seq, other).wait_recv()
        unpack_rows(lambda z: own_recv[z, seq], cot_wide, head_parts, part, part_half)
        total = cot_wide[...].astype(F32) + norm_back(grad, vectors_ref[3:4], normal, scale)
        rows_acc[2:3] += jnp.sum(total, axis=0, keepdims=True)
        grad_scr[seq] = total
        full_one[seq, pl.ds(pl.multiple_of(here * part, part), part)] = total.astype(BF16)

    def attend_start(seq):
        for copy in chunk_loads(seq):
            copy.wait()
        grad = full_one[seq]
        back_scr[...] = dot_last(grad, out_weight_ref[...]).astype(BF16)
        out_grad[...] += dot_first(context_scr[...], grad)
        return mask_penalty(seg_ref[pl.ds(seq, 1)], live_ref[pl.ds(seq, 1)])

    def attend_head(head, penalty):
        lo = head * HEAD_DIM
        hi = lo + HEAD_DIM
        query = qkv_scr[:, lo:hi] * BF16(factor)
        keys = qkv_scr[:, width + lo : width + hi]
        values = qkv_scr[:, 2 * width + lo : 2 * width + hi]
        back = back_scr[:, lo:hi]
        weights = jnp.exp(
            dot_last(query, keys) + penalty - totals_scr[:, head : head + 1]
        )
        joined_scr[:, 2 * width + lo : 2 * width + hi] = dot_first(
            weights.astype(BF16), back
        ).astype(BF16)
        inner = jnp.sum(
            back.astype(F32) * context_scr[:, lo:hi].astype(F32), axis=-1, keepdims=True
        )
        score_grad = (weights * (dot_last(back, values) - inner)).astype(BF16)
        joined_scr[:, lo:hi] = (dot(score_grad, keys) * factor).astype(BF16)
        joined_scr[:, width + lo : width + hi] = dot_first(score_grad, query).astype(BF16)

    def attend_end(seq):
        joined = joined_scr[...]
        span = pl.ds(pl.multiple_of(lax.rem(seq, 2) * seqlen, seqlen), seqlen)
        part_two[span] = dot_last(joined, weight_ref[...]).astype(BF16)
        qkv_grad[...] += dot_first(first_scr[...], joined)
        bias_grad[0:1] += jnp.sum(joined.astype(F32), axis=0, keepdims=True)

        @pl.when(seq + 1 < seq_count)
        def more():
            for copy in chunk_loads(seq + 1):
                copy.start()

    def last(seq):
        grad = own_scr[...]
        normal, scale = standard(own_tokens_ref[seq].astype(F32))
        rows_acc[3:4] += jnp.sum(grad * normal, axis=0, keepdims=True)
        rows_acc[4:5] += jnp.sum(grad, axis=0, keepdims=True)
        total = grad_scr[seq] + norm_back(grad, vectors_ref[0:1], normal, scale)
        full_two[seq, pl.ds(pl.multiple_of(here * part, part), part)] = total.astype(BF16)

    def stage_copy(seq):
        span = pl.ds(pl.multiple_of(seq * seqlen, seqlen), seqlen)
        return pltpu.make_async_copy(full_two.at[seq], tokens_hbm.at[span], stage_sem.at[seq])

    def open_results():
        each_peer(lambda step, target, source: result_copy(step, target).wait_recv())

        def one(expert, carry):
            packed = result_home[expert]
            result_wide[expert, :, :LANES] = packed[:stride]
            tail = packed[stride:]
            result_wide[expert, :half, LANES:] = tail[:, :HEAD_DIM]
            result_wide[expert, half:, LANES:] = tail[2 * half - stride :, HEAD_DIM:]
            return carry

        lax.fori_loop(0, experts, one, 0)

    def combine(seq):
        span = pl.ds(pl.multiple_of(seq * seqlen, seqlen), seqlen)
        first = id_cols_ref[span, 0:1]
        second = id_cols_ref[span, 1:2]
        pltpu.make_async_copy(own_columns_hbm.at[span], columns_scr, columns_sem.at[0]).start()
        pltpu.make_async_copy(own_columns_hbm.at[span], columns_scr, columns_sem.at[0]).wait()
        first_gate = gate_cols_ref[span, 0:1]
        second_gate = gate_cols_ref[span, 1:2]

        def one(expert, total):
            slots = expert * stride + lax.broadcasted_iota(jnp.int32, (1, stride), 1)
            weights = jnp.where(
                first == slots, first_gate, jnp.where(second == slots, second_gate, 0.0)
            )
            return total + dot(weights.astype(BF16), result_wide[expert])

        block_ref[span] = lax.fori_loop(0, experts, one, columns_scr[...]).astype(BF16)

    qkv_rows = qkv_grad.shape[0] // experts
    out_rows = out_grad.shape[0] // experts

    def sum_copies(step, target):
        return (
            pltpu.make_async_remote_copy(
                src_ref=qkv_send.at[target],
                dst_ref=qkv_recv.at[me],
                send_sem=sum_send_sem.at[step, 0],
                recv_sem=sum_recv_sem.at[step, 0],
                **to_exp(target),
            ),
            pltpu.make_async_remote_copy(
                src_ref=out_send.at[target],
                dst_ref=out_recv.at[me],
                send_sem=sum_send_sem.at[step, 1],
                recv_sem=sum_recv_sem.at[step, 1],
                **to_exp(target),
            ),
        )

    def all_copies(step, target):
        return (
            pltpu.make_async_remote_copy(
                src_ref=qkv_all.at[me],
                dst_ref=qkv_all.at[me],
                send_sem=all_send_sem.at[step, 0],
                recv_sem=all_recv_sem.at[step, 0],
                **to_exp(target),
            ),
            pltpu.make_async_remote_copy(
                src_ref=out_all.at[me],
                dst_ref=out_all.at[me],
                send_sem=all_send_sem.at[step, 1],
                recv_sem=all_recv_sem.at[step, 1],
                **to_exp(target),
            ),
        )

    def all_arrivals(step, source):
        return (
            pltpu.make_async_remote_copy(
                src_ref=qkv_all.at[source],
                dst_ref=qkv_all.at[source],
                send_sem=all_send_sem.at[step, 0],
                recv_sem=all_recv_sem.at[step, 0],
                **to_exp(source),
            ),
            pltpu.make_async_remote_copy(
                src_ref=out_all.at[source],
                dst_ref=out_all.at[source],
                send_sem=all_send_sem.at[step, 1],
                recv_sem=all_recv_sem.at[step, 1],
                **to_exp(source),
            ),
        )

    def bias_copy(step, target):
        return pltpu.make_async_remote_copy(
            src_ref=bias_grad,
            dst_ref=bias_recv.at[me],
            send_sem=bias_send_sem.at[step],
            recv_sem=bias_recv_sem.at[step],
            **to_exp(target),
        )

    def start_sums():
        for block in range(experts):
            qkv_send[block] = qkv_grad[block * qkv_rows : (block + 1) * qkv_rows].astype(BF16)
            out_send[block] = out_grad[block * out_rows : (block + 1) * out_rows].astype(BF16)

        def begin(step, target, source):
            for copy in sum_copies(step, target):
                copy.start()
            bias_copy(step, target).start()

        each_peer(begin)
        qkv_recv[me] = qkv_send[me]
        out_recv[me] = out_send[me]
        bias_recv[me] = bias_grad[...]

    def spread_sums():
        def arrive(step, target, source):
            for copy in sum_copies(step, target):
                copy.wait_recv()
            bias_copy(step, target).wait_recv()

        each_peer(arrive)

        def add(source, totals):
            return (
                totals[0] + qkv_recv[source].astype(F32),
                totals[1] + out_recv[source].astype(F32),
                totals[2] + bias_recv[source],
            )

        qkv_total, out_total, bias_total = lax.fori_loop(
            1,
            experts,
            add,
            (qkv_recv[0].astype(F32), out_recv[0].astype(F32), bias_recv[0]),
        )
        qkv_all[me] = qkv_total.astype(BF16)
        out_all[me] = out_total.astype(BF16)
        bias_sum_ref[...] = bias_total

        def begin(step, target, source):
            for copy in all_copies(step, target):
                copy.start()

        each_peer(begin)

    def end_sums():
        def arrive(step, target, source):
            for copy in all_arrivals(step, source):
                copy.wait_recv()

        each_peer(arrive)
        for block in range(experts):
            qkv_sum_ref[block * qkv_rows : (block + 1) * qkv_rows] = qkv_all[block].astype(F32)
            out_sum_ref[block * out_rows : (block + 1) * out_rows] = out_all[block].astype(F32)

    def head_copy(step):
        return pltpu.make_async_remote_copy(
            src_ref=small_head.at[here],
            dst_ref=small_head.at[here],
            send_sem=head_send_sem.at[step],
            recv_sem=head_recv_sem.at[step],
            **to_head(lax.rem(here + step, head_parts)),
        )

    def head_arrival(step):
        source = lax.rem(here + head_parts - step, head_parts)
        return pltpu.make_async_remote_copy(
            src_ref=small_head.at[source],
            dst_ref=small_head.at[source],
            send_sem=head_send_sem.at[step],
            recv_sem=head_recv_sem.at[step],
            **to_head(source),
        )

    def small_copy(step, target):
        return pltpu.make_async_remote_copy(
            src_ref=small_recv.at[me],
            dst_ref=small_recv.at[me],
            send_sem=small_send_sem.at[step],
            recv_sem=small_recv_sem.at[step],
            **to_exp(target),
        )

    def small_arrival(step, source):
        return pltpu.make_async_remote_copy(
            src_ref=small_recv.at[source],
            dst_ref=small_recv.at[source],
            send_sem=small_send_sem.at[step],
            recv_sem=small_recv_sem.at[step],
            **to_exp(source),
        )

    heads = width // HEAD_DIM
    router_rows = small_head.shape[1] - 8

    second_start = 2 * ends
    spread_start = second_start + ends
    ticks = spread_start + ends + 1 + gap * (seq_count - 1)
    final = gap * (seq_count - 1)

    def tick(now, carry):
        def on(offset, action):
            since = now - offset

            @pl.when((since >= 0) & (lax.rem(since, gap) == 0) & (since < gap * seq_count))
            def run():
                action(since // gap)

        def first_end(seq):
            reduce_end(sums_ref, seq * seqlen, one_down, one_up, seq)
            middle(seq)

        def attend(seq):
            spread_hop(one_full, seq, ends)
            penalty = attend_start(seq)
            for head in range(heads):
                attend_head(head, penalty)
            attend_end(seq)

        def second_end(seq):
            reduce_end(part_two, lax.rem(seq, 2) * seqlen, two_down, two_up, seq)
            last(seq)

        def tokens_end(seq):
            spread_hop(two_full, seq, ends)
            stage_copy(seq).start()

        def own_begin(seq):
            for other in range(1, head_parts):
                own_copy(seq, other).start()

        on(ends, first_end)
        on(spread_start, second_end)
        for hop in range(ends):
            on(hop, lambda seq: reduce_hop(sums_ref, seq * seqlen, one_down, one_up, seq, hop))
            on(ends + hop, lambda seq: spread_hop(one_full, seq, hop))
            if hop > 0:
                on(
                    second_start + hop,
                    lambda seq: reduce_hop(
                        part_two, lax.rem(seq, 2) * seqlen, two_down, two_up, seq, hop
                    ),
                )
            on(spread_start + hop, lambda seq: spread_hop(two_full, seq, hop))
        on(0, own_begin)
        on(second_start, attend)
        on(
            second_start,
            lambda seq: reduce_hop(part_two, lax.rem(seq, 2) * seqlen, two_down, two_up, seq, 0),
        )

        @pl.when(now == 0)
        def send_results():
            each_peer(lambda step, target, source: result_copy(step, target).start())
            local = pltpu.make_async_copy(result_hbm.at[me], result_home.at[me], columns_sem.at[1])
            local.start()
            local.wait()

        @pl.when(now == ends + 1)
        def results():
            open_results()

        on(ends + 2, combine)

        @pl.when(now == final + second_start)
        def sums():
            start_sums()

        @pl.when(now == final + second_start + 2)
        def share():
            spread_sums()

        @pl.when(now == final + spread_start)
        def small():
            small_head[here, :8] = rows_acc[...]
            small_head[here, 8:] = router_acc[...].T[:router_rows]
            for other in range(1, head_parts):
                head_copy(other).start()

        @pl.when(now == final + spread_start + 1)
        def small_on():
            for other in range(1, head_parts):
                head_arrival(other).wait_recv()
            total = small_head[0]
            for other in range(1, head_parts):
                total = total + small_head[other]
            small_recv[me] = total
            each_peer(lambda step, target, source: small_copy(step, target).start())
            end_sums()

        on(spread_start + ends, tokens_end)
        return carry

    lax.fori_loop(0, ticks, tick, 0)

    each_peer(lambda step, target, source: small_arrival(step, source).wait_recv())
    small_ref[...] = lax.fori_loop(
        1, experts, lambda source, total: total + small_recv[source], small_recv[0]
    )
    for seq in range(seq_count):
        stage_copy(seq).wait()
        reduce_drain(one_down, one_up, seq)
        reduce_drain(two_down, two_up, seq)
        spread_drain(one_full, seq)
        spread_drain(two_full, seq)
    for other in range(1, head_parts):
        head_copy(other).wait_send()
        route_copy(other).wait_send()
        for seq in range(seq_count):
            own_copy(seq, other).wait_send()

    def sent(step, target, source):
        result_copy(step, target).wait_send()
        for copy in sum_copies(step, target):
            copy.wait_send()
        bias_copy(step, target).wait_send()
        for copy in all_copies(step, target):
            copy.wait_send()
        small_copy(step, target).wait_send()

    each_peer(sent)


def tail(
    sums, route, id_cols, gate_cols, own_residual, own_second, cot_own, own_columns, router, vectors,
    own_tokens, result, context, first, qkv, totals, flat_qkv, out_weight,
    segments, live, stride, half, part_half, head_parts,
):
    experts = result.shape[0]
    model_width = first.shape[1]
    seq_count, part = own_residual.shape[:2]
    seqlen = part * head_parts
    tok_count = seq_count * seqlen
    wide = flat_qkv.shape[1]
    width = wide // 3
    ends = head_parts - 1
    small_rows = 8 + round_up(experts, 8)
    dma = pltpu.SemaphoreType.DMA
    return pl.pallas_call(
        partial(tail_kernel, experts, stride, half, part_half, seq_count, head_parts, 2),
        in_specs=[whole(), anywhere()] + [whole()] * 4 + [anywhere()] * 2 + [whole()] * 3 + [anywhere()] * 5 + [whole()] * 4,
        out_specs=[anywhere()] + [whole()] * 5,
        out_shape=[
            shaped((tok_count, model_width), BF16),
            shaped((tok_count, width), BF16),
            shaped((model_width, wide), F32),
            shaped((width, model_width), F32),
            shaped((8, wide), F32),
            shaped((small_rows, model_width), F32),
        ],
        scratch_shapes=[
            pltpu.VMEM(route.shape, F32),
            pltpu.VMEM(cot_own.shape, BF16),
            pltpu.VMEM((part, model_width), BF16),
            pltpu.VMEM((seqlen, width), F32),
            pltpu.VMEM((2 * seqlen, model_width), BF16),
            pltpu.VMEM((seq_count, ends, part, model_width), BF16),
            pltpu.VMEM((seq_count, ends, part, model_width), BF16),
            pltpu.VMEM((seq_count, ends, part, model_width), BF16),
            pltpu.VMEM((seq_count, ends, part, model_width), BF16),
            pltpu.VMEM((part, model_width), F32),
            pltpu.VMEM((seq_count, seqlen, model_width), BF16),
            pltpu.VMEM((seq_count, seqlen, model_width), BF16),
            pltpu.VMEM((seq_count, part, model_width), F32),
            pltpu.VMEM((seqlen, width), BF16),
            pltpu.VMEM((seqlen, model_width), BF16),
            pltpu.VMEM((seqlen, wide), BF16),
            pltpu.VMEM((seqlen, LANES), F32),
            pltpu.VMEM((seqlen, width), BF16),
            pltpu.VMEM((seqlen, wide), BF16),
            pltpu.VMEM((model_width, wide), F32),
            pltpu.VMEM((width, model_width), F32),
            pltpu.VMEM((8, wide), F32),
            pltpu.VMEM((8, model_width), F32),
            pltpu.VMEM((model_width, LANES), F32),
            pltpu.VMEM((experts, stride + half, LANES), BF16),
            pltpu.VMEM((experts, stride, width), BF16),
            pltpu.VMEM((experts, model_width // experts, wide), BF16),
            pltpu.VMEM((experts, model_width // experts, wide), BF16),
            pltpu.VMEM((experts, model_width // experts, wide), BF16),
            pltpu.VMEM((experts, width // experts, model_width), BF16),
            pltpu.VMEM((experts, width // experts, model_width), BF16),
            pltpu.VMEM((experts, width // experts, model_width), BF16),
            pltpu.VMEM((experts, 8, wide), F32),
            pltpu.VMEM((head_parts, small_rows, model_width), F32),
            pltpu.VMEM((experts, small_rows, model_width), F32),
            dma((head_parts,)),
            dma((head_parts,)),
            dma((seq_count, head_parts)),
            dma((seq_count, head_parts)),
            dma((4,)),
            dma((4,)),
            dma((seq_count,)),
            dma((experts,)),
            dma((experts,)),
        ]
        + [dma((seq_count, ends))] * 8
        + [dma((seq_count, head_parts))] * 2
        + [dma((seq_count, head_parts, 2))] * 2
        + [dma((experts, 2))] * 4
        + [dma((experts,))] * 2
        + [dma((head_parts,))] * 2
        + [dma((experts,))] * 2,
        compiler_params=params(collective_id=2, has_side_effects=True),
        cost_estimate=cost(1e11, 1e8),
        name="tail",
    )(
        sums, route, id_cols, gate_cols, own_residual, own_second, cot_own, own_columns, router, vectors,
        own_tokens, result, context, first, qkv, totals, flat_qkv, out_weight,
        segments, live,
    )


def body(
    tokens,
    segments,
    live_mask,
    routes,
    priority,
    norm1_gain,
    norm1_bias,
    qkv_weight,
    qv_bias,
    out_weight,
    out_bias,
    norm2_gain,
    norm2_bias,
    router,
    up_weight,
    up_bias,
    down_weight,
    down_bias,
    cotangent,
):
    tok_count, model_width = tokens.shape
    seq_count, seqlen = segments.shape
    experts = lax.axis_size("exp")
    head_parts = lax.axis_size("head")
    head_index = lax.axis_index("head")
    quarter = model_width // head_parts
    capacity = (21 * tok_count + 10 * experts - 1) // (10 * experts)
    stride = round_up(capacity, 16)
    half = round_up(stride // 2, 16)
    local_width = qkv_weight.shape[2]

    norm_vectors = [norm1_gain, norm1_bias, out_bias, norm2_gain, norm2_bias]
    flat_qkv = qkv_weight.reshape(model_width, 3 * local_width)
    router_wide = jnp.pad(router, ((0, 0), (0, LANES - experts)))
    up, down = up_weight[0], down_weight[0]

    routes_t = routes.T
    part_half = round_up(seqlen // head_parts // 2, 16)
    first, qkv, context, totals, vectors, out_full_weight, gathered, ids, id_cols, cot_slots, cot_own, own_tokens = head(
        tokens, norm_vectors, flat_qkv, qv_bias, segments, live_mask, routes_t, priority, cotangent.T, out_weight, experts, capacity, stride, half, part_half, head_parts,
    )
    own_residual, own_second, own_columns, gate_cols, arrived, hidden, result, gate_col, cot_rows = forward(
        gathered, tokens, vectors, out_full_weight, router_wide, routes_t, ids,
        up, up_bias, down, down_bias, cot_slots, experts, stride, half, seq_count, head_parts,
    )
    own_result = lax.psum_scatter(result, "head", scatter_dimension=0, tiled=True)[0]
    sums, route_terms, grad_up, grad_up_bias, grad_down, grad_down_bias = backward(
        arrived, hidden, result, cot_rows, gate_col, id_cols, up, up_bias, down, half, head_parts,
        seqlen,
    )
    grad_up, grad_down, own_result = lax.optimization_barrier(
        (*copies_of(grad_up, grad_down), own_result)
    )
    grad_tokens, block_out, qkv_grad, out_grad, bias_grad, small = tail(
        sums, route_terms, id_cols, gate_cols, own_residual, own_second, cot_own, own_columns,
        router_wide, vectors, own_tokens, own_result, context, first, qkv, totals,
        flat_qkv, out_weight, segments, live_mask, stride, half, part_half, head_parts,
    )
    grad_qv_bias = jnp.concatenate(
        [bias_grad[0:1, :local_width], bias_grad[0:1, 2 * local_width :]], axis=0
    )
    return (
        block_out,
        widened(grad_tokens),
        small[3],
        small[4],
        qkv_grad.reshape(model_width, 3, local_width),
        grad_qv_bias,
        out_grad,
        small[2],
        small[0],
        small[1],
        small[8 : 8 + experts].T,
        grad_up[None],
        grad_up_bias[0:1],
        grad_down[None],
        lax.dynamic_slice_in_dim(grad_down_bias[0:1], head_index * quarter, quarter, 1),
    )


def solution(mesh):
    in_specs = (
        P("exp", None),
        P("exp", None),
        P("exp", None),
        P("exp", None),
        P("exp", None),
        P(),
        P(),
        P(None, None, "head"),
        P(None, "head"),
        P("head", None),
        P(),
        P(),
        P(),
        P(),
        P("exp", None, "head"),
        P("exp", "head"),
        P("exp", "head", None),
        P("exp", "head"),
        P("exp", "head"),
    )
    out_specs = (
        P("exp", "head"),
        P("exp", None),
        P(),
        P(),
        P(None, None, "head"),
        P(None, "head"),
        P("head", None),
        P(),
        P(),
        P(),
        P(),
        P("exp", None, "head"),
        P("exp", "head"),
        P("exp", "head", None),
        P("exp", "head"),
    )
    return jax.shard_map(body, mesh=mesh, in_specs=in_specs, out_specs=out_specs, check_vma=False)
```
